32 devices in a mesh: grp: 2 (over y), sec: 4 (over z), op: 2 (over x), rep: 2 (over core).
Axes of the slice: x: 2, y: 2, z: 4, core: 2. Of those that a mesh axis runs over, the one named last changes fastest.
Arguments:
- psi: bfloat16 [32, 256, 256], P(('grp', 'sec'), 'rep'), parts along dimension 0, may hold values from -6 to 6
- left_env: bfloat16 [32, 16, 256, 256], P(('grp', 'op'), 'sec', 'rep'), parts along dimension 0, may hold values from -0.09375 to 0.09375
- right_env: bfloat16 [32, 256, 256], P(('grp', 'op')), parts along dimension 0, may hold values from -0.375 to 0.375
- pairing: int32 [32, 16], P(('grp', 'op'), 'sec'), parts along dimension 0, may hold values from 0 to 15, as said below
- block_rows: int32 [32], P(('grp', 'sec')), parts along dimension 0, may hold values from 64 to 256, as said below
- block_cols: int32 [32], P(('grp', 'sec')), parts along dimension 0, may hold values from 64 to 256, as said below
- energy: float32 [32, 256], P(('grp', 'sec'), 'rep'), parts along dimension 0, may hold values from 1 to 4
Outputs:
- sigma_first: bfloat16 [32, 256, 256], P(('grp', 'sec'), 'rep'), parts along dimension 0
- sigma_second: bfloat16 [32, 256, 256], P(('grp', 'sec'), 'rep'), parts along dimension 0
The draws below stay inside these ranges and needn't reach their ends.
There are 2 independent parts, one for each index of `grp`. The reference program is written for one: setup_inputs(seed, part) draws one part's arguments, and reference() takes and returns one part's arrays. A program takes and returns all parts, laid end to end along the dimension named above; each array names one. Nothing has to cross between parts.
Inputs may be any that keep to these rules, and one draw needn't show every extreme that they name: `pairing`: the 8 x 4 entries of one op index and one sec index name sectors of any one sec index at most 9 times, and all of them that name sectors of one sec index name the same sector; in every op index some sec index is named exactly 9 times from every sec index. `block_rows`: some sector has exactly 256 live rows. `block_cols`: some sector has exactly 256 live columns.
All inputs are finite; a program needn't handle non-finite values.
Results may differ from the reference program's by a relative error of at most 0.0085.
Values may be sent and summed in bfloat16 or wider, within the bound.
No kernel may reach another device: no remote copies, remote signals or barrier semaphores. Data moves between devices by JAX's collectives and lax.ppermute only.
A program may use at most 64 MiB of HBM per device.

```python
import math
import jax
import jax.numpy as jnp
from jax import lax

B = 256
SEC_DEV = 4
TERMS_DEV = 8
S = 16
TERMS = 16
CAP = 9


def draw_pairing(key, part):
    key = jax.random.fold_in(key, 11)
    groups = TERMS // TERMS_DEV
    owners = S // SEC_DEV
    pair_count = TERMS_DEV * SEC_DEV
    full_owner = jax.random.randint(jax.random.fold_in(key, 1), (groups,), 0, owners)

    def one_block(block_id):
        block_key = jax.random.fold_in(key, block_id + 7)
        first_key = jax.random.fold_in(block_key, 1)
        second_key = jax.random.fold_in(block_key, 2)
        third_key = jax.random.fold_in(block_key, 3)
        chosen_owner = full_owner[block_id // owners]
        others = jax.random.permutation(first_key, (owners - 1) * CAP)[:pair_count - CAP].astype(jnp.int32)
        other_ids = (chosen_owner + 1 + others // CAP) % owners
        owner_ids = jnp.concatenate([jnp.zeros((CAP,), jnp.int32) + chosen_owner, other_ids.astype(jnp.int32)])
        owner_ids = jax.random.permutation(second_key, owner_ids)
        slot_table = jax.random.randint(third_key, (owners,), 0, SEC_DEV).astype(jnp.int32)
        slot_ids = slot_table[owner_ids]
        return (owner_ids * SEC_DEV + slot_ids).astype(jnp.int32).reshape(TERMS_DEV, SEC_DEV)
    block_ids = jnp.arange(groups * owners, dtype=jnp.int32)
    blocks = jax.vmap(one_block)(block_ids).reshape(groups, owners, TERMS_DEV, SEC_DEV)
    return blocks.transpose(0, 2, 1, 3).reshape(TERMS, S)


def block_dims(key):
    value_key = jax.random.fold_in(key, 1)
    place_key = jax.random.fold_in(key, 2)
    values = jax.random.randint(value_key, (S,), B // 4, B + 1)
    chosen_pos = jax.random.randint(place_key, (), 0, S)
    return values.at[chosen_pos].set(B).astype(jnp.int32)


def draw_block_rows(key, part):
    key = jax.random.fold_in(key, 13)
    return block_dims(key)


def draw_block_cols(key, part):
    key = jax.random.fold_in(key, 17)
    return block_dims(key)


def block_scale(rng, shape, pieces, least, high):
    loudness = 1.0
    for axis_at, shards_of in pieces:
        heights = jax.random.uniform(jax.random.fold_in(jax.random.fold_in(rng, 6), axis_at), (shards_of,), jnp.float32, least / len(pieces), high / len(pieces))
        loudness = loudness * jnp.repeat(jnp.exp(heights), shape[axis_at] // shards_of).reshape((-1,) + (1,) * (len(shape) - 1 - axis_at))
    return loudness


def centred(key, shape, deviation, limit, shards=(), kind=jnp.bfloat16):
    gain = block_scale(key, shape, shards, -0.22, 0.18) if shards else 1.0
    entries = jax.random.normal(key, shape, jnp.float32) * deviation * gain
    return jnp.minimum(jnp.maximum(entries, -limit), limit).astype(kind)


def setup_inputs(seed: int = 0, part: int = 0) -> dict:
    seeds = jax.random.split(jax.random.key(seed), 8)
    own_keys = jax.random.split(jax.random.fold_in(seeds[7], part), 8)
    psi = centred(own_keys[0], (S, B, B), 1.0, 6.0, ((0, 4), (1, 2)))
    left_env = centred(own_keys[1], (TERMS, S, B, B), (B * TERMS) ** -0.5, 0.09375, ((0, 2), (1, 4), (2, 2)))
    right_env = centred(own_keys[2], (TERMS, B, B), B ** -0.5, 0.375, ((0, 2),))
    pairing = draw_pairing(jax.random.fold_in(jax.random.fold_in(seeds[7], part), 71), part)
    block_rows = draw_block_rows(jax.random.fold_in(jax.random.fold_in(seeds[7], part), 71), part)
    block_cols = draw_block_cols(jax.random.fold_in(jax.random.fold_in(seeds[7], part), 71), part)
    energy = jnp.clip(jnp.exp(math.log(4.0) - 1.3862944 * jax.random.uniform(own_keys[6], (S, B), jnp.float32) ** block_scale(own_keys[6], (S, B), ((0, 4), (1, 2)), -0.2, 0.2)), 1.0, 4.0)
    return dict(psi=psi, left_env=left_env, right_env=right_env, pairing=pairing, block_rows=block_rows, block_cols=block_cols, energy=energy)


def reference(psi, left_env, right_env, pairing, block_rows, block_cols, energy):
    row_index = lax.broadcasted_iota(jnp.int32, (S, B, B), 1)
    col_index = lax.broadcasted_iota(jnp.int32, (S, B, B), 2)
    live_mask = (row_index < block_rows[:, None, None]) & (col_index < block_cols[:, None, None])
    start_vec = jnp.where(live_mask, psi, jnp.zeros_like(psi))
    op_groups = TERMS // TERMS_DEV
    sec_groups = S // SEC_DEV
    left_groups = left_env.reshape(op_groups, TERMS_DEV, sec_groups, SEC_DEV, B, B).transpose(0, 2, 1, 3, 4, 5)
    right_groups = right_env.reshape(op_groups, TERMS_DEV, B, B)
    pair_groups = pairing.reshape(op_groups, TERMS_DEV, sec_groups, SEC_DEV).transpose(0, 2, 1, 3)

    def sigma_map(vector):
        widened = vector.astype(jnp.float32)
        vec_groups = widened.reshape(sec_groups, SEC_DEV, B, B)

        def op_step(running, op_inputs):
            left_all, right, target_all = op_inputs
            right_wide = right.astype(jnp.float32)

            def sec_step(inner_running, sec_inputs):
                left, target, vec = sec_inputs
                inner_block = jnp.einsum('tsij,sjk->tsik', left.astype(jnp.float32), vec).astype(jnp.bfloat16)
                outer_block = jnp.einsum('tsik,tkl->tsil', inner_block.astype(jnp.float32), right_wide).astype(jnp.bfloat16)
                flat_target = target.reshape(TERMS_DEV * SEC_DEV).astype(jnp.int32)
                block_sum = jnp.zeros((S, B, B), jnp.float32).at[flat_target].add(outer_block.reshape(TERMS_DEV * SEC_DEV, B, B).astype(jnp.float32))
                group_sum = lax.optimization_barrier(block_sum.astype(jnp.bfloat16))
                return (inner_running + group_sum.astype(jnp.float32), None)
            running, _ = lax.scan(sec_step, running, (left_all, target_all, vec_groups))
            return (running, None)
        running, _ = lax.scan(op_step, jnp.zeros((S, B, B), jnp.float32), (left_groups, right_groups, pair_groups))
        return jnp.where(live_mask, running + energy[:, :, None] * widened, jnp.zeros_like(running))
    sigma_one = sigma_map(start_vec)
    start_wide = start_vec.astype(jnp.float32)
    norm_sq = jnp.sum(start_wide * start_wide)
    correlation = jnp.sum(start_wide * sigma_one)
    rayleigh = correlation / norm_sq
    residual = sigma_one - rayleigh * start_wide
    resid_sq = jnp.sum(residual * residual)
    update = (residual * lax.rsqrt(resid_sq / (S * B * B) + 1e-06)).astype(jnp.bfloat16)
    sigma_two = sigma_map(update)
    return (sigma_one.astype(jnp.bfloat16), sigma_two.astype(jnp.bfloat16))
```

```python
import functools

import jax
import jax.numpy as jnp
from jax import lax
from jax.experimental import pallas as pl
from jax.experimental.pallas import tpu as pltpu
from jax.sharding import PartitionSpec as P

EPSILON = 1e-06
HEAD = 16
PARTS = 3
LANES = 128
VMEM_BYTES = 24 * 1024 * 1024
F32 = jnp.float32
BF16 = jnp.bfloat16


def whole(space):
    return pl.BlockSpec(memory_space=space)


def live(rows, cols, first_row, shape):
    row_ids = first_row + lax.broadcasted_iota(jnp.int32, shape, 0)
    col_ids = lax.broadcasted_iota(jnp.int32, shape, 1)
    return (row_ids < rows) & (col_ids < cols)


def total(array):
    return jnp.sum(jnp.sum(array, axis=0, keepdims=True), axis=1, keepdims=True)


def header(slot, scalars):
    row_ids = lax.broadcasted_iota(jnp.int32, (HEAD, LANES), 0)
    head = jnp.where(row_ids == 0, slot.astype(F32), 0.0)
    row = 1
    for scalar in scalars:
        rest = jnp.broadcast_to(scalar, (HEAD, LANES))
        for _ in range(PARTS):
            piece = rest.astype(BF16).astype(F32)
            head = jnp.where(row_ids == row, piece, head)
            rest = rest - piece
            row += 1
    return head.astype(BF16)


def head_scalar(head_sum, index):
    first = 1 + PARTS * index
    return jnp.sum(head_sum[first:first + PARTS], axis=0, keepdims=True)


def product_kernel(is_first, split, rep_count, sec_count, *refs):
    refs = list(refs)
    take = lambda count: [refs.pop(0) for _ in range(count)]
    pairing_ref, rows_ref, cols_ref, left_ref, right_ref = take(5)
    psi_refs = take(rep_count)
    other_refs = take(rep_count)
    out_refs = take(sec_count if split else 1)
    vec_ref, inner_ref, sum_ref, slot_ref = refs
    terms, sec_dev, half, width = left_ref.shape
    rep = lax.axis_index("rep")
    sec = lax.axis_index("sec")

    scalar_a = jnp.zeros((1, 1), F32)
    scalar_b = jnp.zeros((1, 1), F32)
    for step in range(rep_count):
        first_row = pl.multiple_of(lax.rem(rep + step, rep_count) * half, half)
        for s in range(sec_dev):
            psi = psi_refs[step][s].astype(F32)
            if is_first:
                vector = jnp.where(
                    live(rows_ref[s], cols_ref[s], first_row, (half, width)), psi, 0.0
                )
                by_row = jnp.sum(vector * vector, axis=1, keepdims=True)
                scalar_a += jnp.sum(by_row, axis=0, keepdims=True)
                energy = other_refs[step][:, s:s + 1]
                scalar_b += jnp.sum(by_row * energy, axis=0, keepdims=True)
                vec_ref[s, pl.ds(first_row, half), :] = vector.astype(BF16)
            else:
                vector = other_refs[step][s].astype(F32)
                scalar_a += total(psi * vector)
                scalar_b += total(vector * vector)
                vec_ref[s, pl.ds(first_row, half), :] = other_refs[step][s]

    for d in range(sec_count):
        slot_ref[d] = 0
        sum_ref[d] = jnp.zeros((half, width), F32)
    for s in range(sec_dev):
        inner = jnp.dot(
            left_ref[:, s].reshape(terms * half, width), vec_ref[s], preferred_element_type=F32
        )
        inner_ref[s] = inner.astype(BF16).reshape(terms, half, width)
    for t in range(terms):
        outer = jnp.dot(
            inner_ref[:, t].reshape(sec_dev * half, width),
            right_ref[t],
            preferred_element_type=F32,
        )
        for s in range(sec_dev):
            target = pairing_ref[s, t]
            owner = lax.div(target, sec_dev)
            place = lax.rem(owner - sec + sec_count, sec_count) if split else owner
            slot_ref[place] = lax.rem(target, sec_dev)
            sum_ref[place] += outer[s * half:(s + 1) * half]
    for d in range(sec_count):
        out = out_refs[d] if split else out_refs[0].at[d]
        for column in range(width // LANES):
            out[column * half:(column + 1) * half, :] = sum_ref[
                d, :, column * LANES:(column + 1) * LANES
            ].astype(BF16)
        out[width // LANES * half:, :] = header(slot_ref[d], (scalar_a, scalar_b))


def sigma_packets(is_first, split, pairing, rows, cols, left_env, right_env, psi_all, others):
    terms, sec_dev, half, width = left_env.shape
    sec_count = lax.axis_size("sec")
    rep_count = len(psi_all)
    packet = (width // LANES * half + HEAD, LANES)
    if split:
        outs = [jax.ShapeDtypeStruct(packet, BF16)] * sec_count
    else:
        outs = [jax.ShapeDtypeStruct((sec_count,) + packet, BF16)]
    pair_flops = 2 * half * width * width * 2
    return pl.pallas_call(
        functools.partial(product_kernel, is_first, split, rep_count, sec_count),
        out_shape=outs,
        in_specs=[whole(pltpu.SMEM)] * 3 + [whole(pltpu.VMEM)] * (2 + 2 * rep_count),
        out_specs=[whole(pltpu.VMEM)] * len(outs),
        scratch_shapes=[
            pltpu.VMEM((sec_dev, rep_count * half, width), BF16),
            pltpu.VMEM((sec_dev, terms, half, width), BF16),
            pltpu.VMEM((sec_count, half, width), F32),
            pltpu.SMEM((sec_count,), jnp.int32),
        ],
        compiler_params=pltpu.CompilerParams(vmem_limit_bytes=VMEM_BYTES),
        cost_estimate=pl.CostEstimate(
            flops=terms * sec_dev * pair_flops,
            bytes_accessed=2 * (left_env.size + right_env.size),
            transcendentals=0,
        ),
        name="products_first" if is_first else "products_second",
    )(pairing, rows, cols, left_env, right_env, *psi_all, *others)


def exchange(packets, split):
    sec_count = lax.axis_size("sec")
    op_count = lax.axis_size("op")
    if not split:
        arrived = lax.all_to_all(packets[0], "sec", split_axis=0, concat_axis=0, tiled=True)
        gathered = [arrived]
        for step in range(1, op_count):
            turn = [(i, (i + step) % op_count) for i in range(op_count)]
            gathered.append(lax.ppermute(arrived, "op", turn))
        return gathered
    arrived = [packets[0]]
    for step in range(1, sec_count):
        turn = [(i, (i + step) % sec_count) for i in range(sec_count)]
        arrived.append(lax.ppermute(packets[step], "sec", turn))
    gathered = list(arrived)
    for step in range(1, op_count):
        turn = [(i, (i + step) % op_count) for i in range(op_count)]
        gathered += [lax.ppermute(packet, "op", turn) for packet in arrived]
    return gathered


def add_packets(packet_refs, split, sec_dev, half, width, sum_ref):
    own = lax.axis_size("sec") if split else 1
    body_rows = width // LANES * half
    sum_ref[...] = jnp.zeros_like(sum_ref)
    if split:
        heads = [ref[body_rows:].astype(F32) for ref in packet_refs]
        for column in range(width // LANES):
            for s in range(sec_dev):
                part = jnp.zeros((half, LANES), F32)
                for ref, head in zip(packet_refs, heads):
                    body = ref[column * half:(column + 1) * half].astype(F32)
                    part += jnp.where(head[0:1] == s, body, 0.0)
                sum_ref[s, :, column * LANES:(column + 1) * LANES] = part
        return sum(heads[1:own], heads[0])

    head_sum = jnp.zeros((HEAD, LANES), F32)
    for index, ref in enumerate(packet_refs):
        def add_one(p, carry):
            head = ref[p, body_rows:, :].astype(F32)
            for column in range(width // LANES):
                body = ref[p, column * half:(column + 1) * half, :].astype(F32)
                lanes = slice(column * LANES, (column + 1) * LANES)
                for s in range(sec_dev):
                    sum_ref[s, :, lanes] += jnp.where(head[0:1] == s, body, 0.0)
            return carry + head
        result = lax.fori_loop(0, ref.shape[0], add_one, jnp.zeros((HEAD, LANES), F32))
        if index < own:
            head_sum = head_sum + result
    return head_sum


def first_kernel(split, count, *refs):
    rows_ref, cols_ref = refs[:2]
    packet_refs = refs[2:2 + count]
    psi_ref, energy_ref, first_ref, one_ref, vec_ref, norm_ref, sum_ref = refs[2 + count:]
    sec_dev, half, width = psi_ref.shape
    head_sum = add_packets(packet_refs, split, sec_dev, half, width, sum_ref)
    norm = head_scalar(head_sum, 0)
    shift = head_scalar(head_sum, 1) / norm
    norm_ref[...] = jnp.broadcast_to(norm, norm_ref.shape)
    shift = jnp.concatenate([shift] * (width // LANES), axis=1)
    first_row = lax.axis_index("rep") * half
    for s in range(sec_dev):
        mask = live(rows_ref[s], cols_ref[s], first_row, (half, width))
        start = jnp.where(mask, psi_ref[s].astype(F32), 0.0)
        one = jnp.where(mask, sum_ref[s] + energy_ref[:, s:s + 1] * start, 0.0)
        one_ref[s] = one
        first_ref[s] = one.astype(BF16)
        vec_ref[s] = (one - shift * start).astype(BF16)


def second_kernel(split, count, entries, *refs):
    rows_ref, cols_ref = refs[:2]
    packet_refs = refs[2:2 + count]
    vec_ref, energy_ref, one_ref, norm_ref, second_ref, sum_ref = refs[2 + count:]
    sec_dev, half, width = vec_ref.shape
    head_sum = add_packets(packet_refs, split, sec_dev, half, width, sum_ref)
    cross = head_scalar(head_sum, 0)
    square = head_scalar(head_sum, 1)
    excess = cross / norm_ref[0:1]
    resid_sq = jnp.maximum(square - excess * cross, 0.0)
    scale = lax.rsqrt(resid_sq / entries + EPSILON)
    excess = jnp.concatenate([excess] * (width // LANES), axis=1)
    scale = jnp.concatenate([scale] * (width // LANES), axis=1)
    first_row = lax.axis_index("rep") * half
    for s in range(sec_dev):
        mask = live(rows_ref[s], cols_ref[s], first_row, (half, width))
        mapped = sum_ref[s] + energy_ref[:, s:s + 1] * vec_ref[s].astype(F32)
        value = jnp.where(mask, scale * (mapped - excess * one_ref[s]), 0.0)
        second_ref[s] = value.astype(BF16)


def body(psi, left_env, right_env, pairing, block_rows, block_cols, energy):
    sec_count = lax.axis_size("sec")
    op_count = lax.axis_size("op")
    rep_count = lax.axis_size("rep")
    _, sec_dev, half, width = left_env.shape
    entries = sec_count * sec_dev * rep_count * half * width
    split = sec_count * op_count <= 8
    params = pltpu.CompilerParams(vmem_limit_bytes=VMEM_BYTES)

    def with_others(array):
        arrays = [array]
        for step in range(1, rep_count):
            turn = [((i + step) % rep_count, i) for i in range(rep_count)]
            arrays.append(lax.ppermute(array, "rep", turn))
        return arrays

    pairing_t = pairing.T
    energy_t = energy.T
    psi_all = with_others(psi)
    packets = sigma_packets(
        True, split, pairing_t, block_rows, block_cols, left_env, right_env,
        psi_all, with_others(energy_t),
    )
    gathered = exchange(packets, split)
    count = len(gathered)
    vec_shape = (sec_dev, half, width)
    sum_scratch = [pltpu.VMEM(vec_shape, F32)]
    first_out, sigma_one, vector, norm = pl.pallas_call(
        functools.partial(first_kernel, split, count),
        out_shape=[
            jax.ShapeDtypeStruct(vec_shape, BF16),
            jax.ShapeDtypeStruct(vec_shape, F32),
            jax.ShapeDtypeStruct(vec_shape, BF16),
            jax.ShapeDtypeStruct((8, LANES), F32),
        ],
        in_specs=[whole(pltpu.SMEM)] * 2 + [whole(pltpu.VMEM)] * (count + 2),
        out_specs=[whole(pltpu.VMEM)] * 4,
        scratch_shapes=sum_scratch,
        compiler_params=params,
        name="combine_first",
    )(block_rows, block_cols, *gathered, psi, energy_t)

    packets = sigma_packets(
        False, split, pairing_t, block_rows, block_cols, left_env, right_env,
        psi_all, with_others(vector),
    )
    gathered = exchange(packets, split)
    (second_out,) = pl.pallas_call(
        functools.partial(second_kernel, split, count, entries),
        out_shape=[jax.ShapeDtypeStruct(vec_shape, BF16)],
        in_specs=[whole(pltpu.SMEM)] * 2 + [whole(pltpu.VMEM)] * (count + 4),
        out_specs=[whole(pltpu.VMEM)],
        scratch_shapes=sum_scratch,
        compiler_params=params,
        name="combine_second",
    )(block_rows, block_cols, *gathered, vector, energy_t, sigma_one, norm)
    return (first_out, second_out)


def solution(mesh):
    return jax.shard_map(
        body,
        mesh=mesh,
        in_specs=(
            P(("grp", "sec"), "rep", None),
            P(("grp", "op"), "sec", "rep", None),
            P(("grp", "op"), None, None),
            P(("grp", "op"), "sec"),
            P(("grp", "sec")),
            P(("grp", "sec")),
            P(("grp", "sec"), "rep"),
        ),
        out_specs=(P(("grp", "sec"), "rep", None), P(("grp", "sec"), "rep", None)),
        check_vma=False,
    )
```

```python
import functools

import jax
import jax.numpy as jnp
from jax import lax
from jax.experimental import pallas as pl
from jax.experimental.pallas import tpu as pltpu
from jax.sharding import PartitionSpec as P

EPSILON = 1e-06
HEAD = 16
PARTS = 3
LANES = 128
VMEM_BYTES = 24 * 1024 * 1024
F32 = jnp.float32
BF16 = jnp.bfloat16


def whole(space):
    return pl.BlockSpec(memory_space=space)


def live(limit_ref, s, first_row, shape):
    sec_dev = limit_ref.shape[0] // 2
    repeat = shape[1] // LANES
    rows = jnp.concatenate([limit_ref[s:s + 1, :]] * repeat, axis=1)
    cols = jnp.concatenate([limit_ref[sec_dev + s:sec_dev + s + 1, :]] * repeat, axis=1)
    row_ids = first_row + lax.broadcasted_iota(jnp.int32, shape, 0)
    col_ids = lax.broadcasted_iota(jnp.int32, shape, 1)
    return (row_ids < rows) & (col_ids < cols)


def energy_columns(level):
    missing = -level.shape[0] % 8
    if missing:
        level = jnp.concatenate([level, jnp.zeros((missing, level.shape[1]), F32)], axis=0)
    return level.T


def spread(array, width):
    return jnp.concatenate([array] * (width // LANES), axis=1)


def total(array):
    return jnp.sum(jnp.sum(array, axis=0, keepdims=True), axis=1, keepdims=True)


def header(slot, scalars):
    row_ids = lax.broadcasted_iota(jnp.int32, (HEAD, LANES), 0)
    head = jnp.where(row_ids == 0, slot.astype(F32), 0.0)
    row = 1
    for scalar in scalars:
        rest = jnp.broadcast_to(scalar, (HEAD, LANES))
        for _ in range(PARTS):
            piece = rest.astype(BF16).astype(F32)
            head = jnp.where(row_ids == row, piece, head)
            rest = rest - piece
            row += 1
    return head.astype(BF16)


def head_scalar(head_sum, index):
    first = 1 + PARTS * index
    return jnp.sum(head_sum[first:first + PARTS], axis=0, keepdims=True)


def load_kernel(
    psi_hbm, left_hbm, right_hbm, pairing_hbm, rows_hbm, cols_hbm, energy_hbm,
    start_ref, left_ref, right_ref, pairing_ref, limit_ref, energy_ref, scalar_ref,
    psi_ref, level_ref, rows_ref, cols_ref, sems,
):
    sec_dev, half, width = psi_ref.shape
    pairs = [
        (rows_hbm, rows_ref), (cols_hbm, cols_ref), (energy_hbm, level_ref), (psi_hbm, psi_ref),
        (pairing_hbm, pairing_ref), (left_hbm, left_ref), (right_hbm, right_ref),
    ]
    copies = [
        pltpu.make_async_copy(source, target, sems.at[i])
        for i, (source, target) in enumerate(pairs)
    ]
    for copy in copies:
        copy.start()
    for copy in copies[:3]:
        copy.wait()
    for s in range(sec_dev):
        limit_ref[s:s + 1, :] = jnp.full((1, LANES), rows_ref[s], jnp.int32)
        limit_ref[sec_dev + s:sec_dev + s + 1, :] = jnp.full((1, LANES), cols_ref[s], jnp.int32)
    columns = energy_columns(level_ref[...])
    for s in range(sec_dev):
        energy_ref[s] = jnp.broadcast_to(columns[:, s:s + 1], (half, LANES))
    copies[3].wait()
    first_row = lax.axis_index("rep") * half
    norm = jnp.zeros((1, 1), F32)
    level = jnp.zeros((1, 1), F32)
    for s in range(sec_dev):
        vector = jnp.where(
            live(limit_ref, s, first_row, (half, width)), psi_ref[s].astype(F32), 0.0
        )
        start_ref[s] = vector.astype(BF16)
        by_row = jnp.sum(vector * vector, axis=1, keepdims=True)
        norm += jnp.sum(by_row, axis=0, keepdims=True)
        level += jnp.sum(by_row * columns[:, s:s + 1], axis=0, keepdims=True)
    scalar_ref[0:1, :] = jnp.broadcast_to(norm, (1, LANES))
    scalar_ref[1:2, :] = jnp.broadcast_to(level, (1, LANES))
    for copy in copies[4:]:
        copy.wait()


def product_kernel(is_first, split, rep_count, sec_count, *refs):
    refs = list(refs)
    take = lambda count: [refs.pop(0) for _ in range(count)]
    pairing_ref, left_ref, right_ref, start_ref = take(4)
    psi_refs = take(rep_count - 1)
    if is_first:
        limit_ref, scalar_ref = take(2)
        level_refs = take(rep_count - 1)
    else:
        vector_refs = take(rep_count)
    out_refs = take(sec_count if split else 1)
    vec_ref, inner_ref, sum_ref, slot_ref = refs
    terms, sec_dev, half, width = left_ref.shape
    rep = lax.axis_index("rep")
    sec = lax.axis_index("sec")

    if is_first:
        scalar_a = scalar_ref[0:1, 0:1]
        scalar_b = scalar_ref[1:2, 0:1]
        rows = pl.ds(pl.multiple_of(rep * half, half), half)
        for s in range(sec_dev):
            vec_ref[s, rows, :] = start_ref[s]
        for step in range(1, rep_count):
            first_row = pl.multiple_of(lax.rem(rep + step, rep_count) * half, half)
            columns = energy_columns(level_refs[step - 1][...])
            for s in range(sec_dev):
                psi = psi_refs[step - 1][s].astype(F32)
                vector = jnp.where(live(limit_ref, s, first_row, (half, width)), psi, 0.0)
                by_row = jnp.sum(vector * vector, axis=1, keepdims=True)
                scalar_a += jnp.sum(by_row, axis=0, keepdims=True)
                scalar_b += jnp.sum(by_row * columns[:, s:s + 1], axis=0, keepdims=True)
                vec_ref[s, pl.ds(first_row, half), :] = vector.astype(BF16)
    else:
        scalar_a = jnp.zeros((1, 1), F32)
        scalar_b = jnp.zeros((1, 1), F32)
        for step in range(rep_count):
            first_row = pl.multiple_of(lax.rem(rep + step, rep_count) * half, half)
            for s in range(sec_dev):
                psi = (psi_refs[step - 1] if step else start_ref)[s].astype(F32)
                vector = vector_refs[step][s].astype(F32)
                scalar_a += total(psi * vector)
                scalar_b += total(vector * vector)
                vec_ref[s, pl.ds(first_row, half), :] = vector_refs[step][s]

    for d in range(sec_count):
        slot_ref[d] = 0
        sum_ref[d] = jnp.zeros((half, width), F32)
    for s in range(sec_dev):
        inner = jnp.dot(
            left_ref[:, s].reshape(terms * half, width), vec_ref[s], preferred_element_type=F32
        )
        inner_ref[s] = inner.astype(BF16).reshape(terms, half, width)
    for t in range(terms):
        outer = jnp.dot(
            inner_ref[:, t].reshape(sec_dev * half, width),
            right_ref[t],
            preferred_element_type=F32,
        )
        for s in range(sec_dev):
            target = pairing_ref[s, t]
            owner = lax.div(target, sec_dev)
            place = lax.rem(owner - sec + sec_count, sec_count) if split else owner
            slot_ref[place] = lax.rem(target, sec_dev)
            sum_ref[place] += outer[s * half:(s + 1) * half]
    for d in range(sec_count):
        out = out_refs[d] if split else out_refs[0].at[d]
        for column in range(width // LANES):
            out[column * half:(column + 1) * half, :] = sum_ref[
                d, :, column * LANES:(column + 1) * LANES
            ].astype(BF16)
        out[width // LANES * half:, :] = header(slot_ref[d], (scalar_a, scalar_b))


def sigma_packets(is_first, split, pairing, left_env, right_env, start, psi_others, more):
    terms, sec_dev, half, width = left_env.shape
    sec_count = lax.axis_size("sec")
    rep_count = len(psi_others) + 1
    packet = (width // LANES * half + HEAD, LANES)
    if split:
        outs = [jax.ShapeDtypeStruct(packet, BF16)] * sec_count
    else:
        outs = [jax.ShapeDtypeStruct((sec_count,) + packet, BF16)]
    pair_flops = 2 * half * width * width * 2
    operands = [left_env, right_env, start, *psi_others, *more]
    return pl.pallas_call(
        functools.partial(product_kernel, is_first, split, rep_count, sec_count),
        out_shape=outs,
        in_specs=[whole(pltpu.SMEM)] + [whole(pltpu.VMEM)] * len(operands),
        out_specs=[whole(pltpu.VMEM)] * len(outs),
        scratch_shapes=[
            pltpu.VMEM((sec_dev, rep_count * half, width), BF16),
            pltpu.VMEM((sec_dev, terms, half, width), BF16),
            pltpu.VMEM((sec_count, half, width), F32),
            pltpu.SMEM((sec_count,), jnp.int32),
        ],
        compiler_params=pltpu.CompilerParams(vmem_limit_bytes=VMEM_BYTES),
        cost_estimate=pl.CostEstimate(
            flops=terms * sec_dev * pair_flops,
            bytes_accessed=2 * (left_env.size + right_env.size),
            transcendentals=0,
        ),
        name="products_first" if is_first else "products_second",
    )(pairing, *operands)


def exchange(packets, split):
    sec_count = lax.axis_size("sec")
    op_count = lax.axis_size("op")
    if not split:
        arrived = lax.all_to_all(packets[0], "sec", split_axis=0, concat_axis=0, tiled=True)
        gathered = [arrived]
        for step in range(1, op_count):
            turn = [(i, (i + step) % op_count) for i in range(op_count)]
            gathered.append(lax.ppermute(arrived, "op", turn))
        return gathered
    arrived = [packets[0]]
    for step in range(1, sec_count):
        turn = [(i, (i + step) % sec_count) for i in range(sec_count)]
        arrived.append(lax.ppermute(packets[step], "sec", turn))
    gathered = list(arrived)
    for step in range(1, op_count):
        turn = [(i, (i + step) % op_count) for i in range(op_count)]
        gathered += [lax.ppermute(packet, "op", turn) for packet in arrived]
    return gathered


def add_packets(packet_refs, split, sec_dev, half, width, sum_ref):
    own = lax.axis_size("sec") if split else 1
    body_rows = width // LANES * half
    sum_ref[...] = jnp.zeros_like(sum_ref)
    if split:
        heads = [ref[body_rows:].astype(F32) for ref in packet_refs]
        for column in range(width // LANES):
            for s in range(sec_dev):
                part = jnp.zeros((half, LANES), F32)
                for ref, head in zip(packet_refs, heads):
                    body = ref[column * half:(column + 1) * half].astype(F32)
                    part += jnp.where(head[0:1] == s, body, 0.0)
                sum_ref[s, :, column * LANES:(column + 1) * LANES] = part
        return sum(heads[1:own], heads[0])

    head_sum = jnp.zeros((HEAD, LANES), F32)
    for index, ref in enumerate(packet_refs):
        def add_one(p, carry):
            head = ref[p, body_rows:, :].astype(F32)
            for column in range(width // LANES):
                body = ref[p, column * half:(column + 1) * half, :].astype(F32)
                lanes = slice(column * LANES, (column + 1) * LANES)
                for s in range(sec_dev):
                    sum_ref[s, :, lanes] += jnp.where(head[0:1] == s, body, 0.0)
            return carry + head
        result = lax.fori_loop(0, ref.shape[0], add_one, jnp.zeros((HEAD, LANES), F32))
        if index < own:
            head_sum = head_sum + result
    return head_sum


def first_kernel(split, count, *refs):
    limit_ref = refs[0]
    packet_refs = refs[1:1 + count]
    start_ref, energy_ref, first_ref, one_ref, vec_ref, norm_ref, sum_ref = refs[1 + count:]
    sec_dev, half, width = start_ref.shape
    head_sum = add_packets(packet_refs, split, sec_dev, half, width, sum_ref)
    norm = head_scalar(head_sum, 0)
    shift = spread(head_scalar(head_sum, 1) / norm, width)
    norm_ref[...] = jnp.broadcast_to(norm, norm_ref.shape)
    first_row = lax.axis_index("rep") * half
    for s in range(sec_dev):
        mask = live(limit_ref, s, first_row, (half, width))
        start = start_ref[s].astype(F32)
        one = jnp.where(mask, sum_ref[s] + spread(energy_ref[s], width) * start, 0.0)
        one_ref[s] = one
        first_ref[s] = one.astype(BF16)
        vec_ref[s] = (one - shift * start).astype(BF16)


def second_kernel(split, count, entries, *refs):
    limit_ref = refs[0]
    packet_refs = refs[1:1 + count]
    vec_ref, energy_ref, one_ref, norm_ref, second_ref, sum_ref = refs[1 + count:]
    sec_dev, half, width = vec_ref.shape
    head_sum = add_packets(packet_refs, split, sec_dev, half, width, sum_ref)
    cross = head_scalar(head_sum, 0)
    square = head_scalar(head_sum, 1)
    excess = cross / norm_ref[0:1]
    resid_sq = jnp.maximum(square - excess * cross, 0.0)
    scale = spread(lax.rsqrt(resid_sq / entries + EPSILON), width)
    excess = spread(excess, width)
    first_row = lax.axis_index("rep") * half
    for s in range(sec_dev):
        mask = live(limit_ref, s, first_row, (half, width))
        mapped = sum_ref[s] + spread(energy_ref[s], width) * vec_ref[s].astype(F32)
        value = jnp.where(mask, scale * (mapped - excess * one_ref[s]), 0.0)
        second_ref[s] = value.astype(BF16)


def body(psi, left_env, right_env, pairing, block_rows, block_cols, energy):
    sec_count = lax.axis_size("sec")
    op_count = lax.axis_size("op")
    rep_count = lax.axis_size("rep")
    terms, sec_dev, half, width = left_env.shape
    entries = sec_count * sec_dev * rep_count * half * width
    split = sec_count * op_count <= 8
    params = pltpu.CompilerParams(vmem_limit_bytes=VMEM_BYTES)
    vec_shape = (sec_dev, half, width)
    vec_bf16 = jax.ShapeDtypeStruct(vec_shape, BF16)
    sum_scratch = [pltpu.VMEM(vec_shape, F32)]

    def from_others(array):
        arrays = []
        for step in range(1, rep_count):
            turn = [((i + step) % rep_count, i) for i in range(rep_count)]
            arrays.append(lax.ppermute(array, "rep", turn))
        return arrays

    psi_others = from_others(psi)
    level_others = from_others(energy)
    start, left_env, right_env, pairing, limits, levels, scalars = pl.pallas_call(
        load_kernel,
        out_shape=[
            vec_bf16,
            jax.ShapeDtypeStruct(left_env.shape, BF16),
            jax.ShapeDtypeStruct(right_env.shape, BF16),
            jax.ShapeDtypeStruct((sec_dev, terms), jnp.int32),
            jax.ShapeDtypeStruct((2 * sec_dev, LANES), jnp.int32),
            jax.ShapeDtypeStruct((sec_dev, half, LANES), F32),
            jax.ShapeDtypeStruct((8, LANES), F32),
        ],
        in_specs=[whole(pltpu.HBM)] * 7,
        out_specs=[whole(pltpu.VMEM)] * 7,
        scratch_shapes=[
            pltpu.VMEM(vec_shape, BF16),
            pltpu.VMEM((sec_dev, half), F32),
            pltpu.SMEM((sec_dev,), jnp.int32),
            pltpu.SMEM((sec_dev,), jnp.int32),
            pltpu.SemaphoreType.DMA((7,)),
        ],
        compiler_params=params,
        name="load",
    )(*(
        pltpu.with_memory_space_constraint(array, pltpu.HBM)
        for array in (psi, left_env, right_env, pairing.T, block_rows, block_cols, energy)
    ))

    packets = sigma_packets(
        True, split, pairing, left_env, right_env, start, psi_others,
        [limits, scalars, *level_others],
    )
    gathered = exchange(packets, split)
    count = len(gathered)
    first_out, sigma_one, vector, norm = pl.pallas_call(
        functools.partial(first_kernel, split, count),
        out_shape=[
            vec_bf16,
            jax.ShapeDtypeStruct(vec_shape, F32),
            vec_bf16,
            jax.ShapeDtypeStruct((8, LANES), F32),
        ],
        in_specs=[whole(pltpu.VMEM)] * (count + 3),
        out_specs=[whole(pltpu.VMEM)] * 4,
        scratch_shapes=sum_scratch,
        compiler_params=params,
        name="combine_first",
    )(limits, *gathered, start, levels)

    packets = sigma_packets(
        False, split, pairing, left_env, right_env, start, psi_others,
        [vector, *from_others(vector)],
    )
    gathered = exchange(packets, split)
    (second_out,) = pl.pallas_call(
        functools.partial(second_kernel, split, count, entries),
        out_shape=[vec_bf16],
        in_specs=[whole(pltpu.VMEM)] * (count + 5),
        out_specs=[whole(pltpu.VMEM)],
        scratch_shapes=sum_scratch,
        compiler_params=params,
        name="combine_second",
    )(limits, *gathered, vector, levels, sigma_one, norm)
    return (first_out, second_out)


def solution(mesh):
    return jax.shard_map(
        body,
        mesh=mesh,
        in_specs=(
            P(("grp", "sec"), "rep", None),
            P(("grp", "op"), "sec", "rep", None),
            P(("grp", "op"), None, None),
            P(("grp", "op"), "sec"),
            P(("grp", "sec")),
            P(("grp", "sec")),
            P(("grp", "sec"), "rep"),
        ),
        out_specs=(P(("grp", "sec"), "rep", None), P(("grp", "sec"), "rep", None)),
        check_vma=False,
    )
```

```python
import functools

import jax
import jax.numpy as jnp
from jax import lax
from jax.experimental import pallas as pl
from jax.experimental.pallas import tpu as pltpu
from jax.sharding import PartitionSpec as P

EPSILON = 1e-06
HEAD = 16
PARTS = 3
LANES = 128
VMEM_BYTES = 24 * 1024 * 1024
F32 = jnp.float32
BF16 = jnp.bfloat16


def whole(space):
    return pl.BlockSpec(memory_space=space)


def live(limit_ref, s, first_row, shape):
    sec_dev = limit_ref.shape[0] // 2
    repeat = shape[1] // LANES
    rows = jnp.concatenate([limit_ref[s:s + 1, :]] * repeat, axis=1)
    cols = jnp.concatenate([limit_ref[sec_dev + s:sec_dev + s + 1, :]] * repeat, axis=1)
    row_ids = first_row + lax.broadcasted_iota(jnp.int32, shape, 0)
    col_ids = lax.broadcasted_iota(jnp.int32, shape, 1)
    return (row_ids < rows) & (col_ids < cols)


def energy_columns(level):
    missing = -level.shape[0] % 8
    if missing:
        level = jnp.concatenate([level, jnp.zeros((missing, level.shape[1]), F32)], axis=0)
    return level.T


def spread(array, width):
    return jnp.concatenate([array] * (width // LANES), axis=1)


def total(array):
    return jnp.sum(jnp.sum(array, axis=0, keepdims=True), axis=1, keepdims=True)


def header(slot, scalars):
    row_ids = lax.broadcasted_iota(jnp.int32, (HEAD, LANES), 0)
    head = jnp.where(row_ids == 0, slot.astype(F32), 0.0)
    row = 1
    for scalar in scalars:
        rest = jnp.broadcast_to(scalar, (HEAD, LANES))
        for _ in range(PARTS):
            piece = rest.astype(BF16).astype(F32)
            head = jnp.where(row_ids == row, piece, head)
            rest = rest - piece
            row += 1
    return head.astype(BF16)


def head_scalar(head_sum, index):
    first = 1 + PARTS * index
    return jnp.sum(head_sum[first:first + PARTS], axis=0, keepdims=True)


def load_kernel(
    psi_hbm, left_hbm, right_hbm, pairing_hbm, rows_hbm, cols_hbm, energy_hbm,
    start_ref, left_ref, right_ref, pairing_ref, limit_ref, energy_ref, scalar_ref,
    psi_ref, level_ref, rows_ref, cols_ref, sems,
):
    sec_dev, half, width = psi_ref.shape
    pairs = [
        (rows_hbm, rows_ref), (cols_hbm, cols_ref), (energy_hbm, level_ref), (psi_hbm, psi_ref),
        (pairing_hbm, pairing_ref), (left_hbm, left_ref), (right_hbm, right_ref),
    ]
    copies = [
        pltpu.make_async_copy(source, target, sems.at[i])
        for i, (source, target) in enumerate(pairs)
    ]
    for copy in copies:
        copy.start()
    for copy in copies[:3]:
        copy.wait()
    for s in range(sec_dev):
        limit_ref[s:s + 1, :] = jnp.full((1, LANES), rows_ref[s], jnp.int32)
        limit_ref[sec_dev + s:sec_dev + s + 1, :] = jnp.full((1, LANES), cols_ref[s], jnp.int32)
    columns = energy_columns(level_ref[...])
    for s in range(sec_dev):
        energy_ref[s] = jnp.broadcast_to(columns[:, s:s + 1], (half, LANES))
    copies[3].wait()
    first_row = lax.axis_index("rep") * half
    norm = jnp.zeros((1, 1), F32)
    level = jnp.zeros((1, 1), F32)
    for s in range(sec_dev):
        vector = jnp.where(
            live(limit_ref, s, first_row, (half, width)), psi_ref[s].astype(F32), 0.0
        )
        start_ref[s] = vector.astype(BF16)
        by_row = jnp.sum(vector * vector, axis=1, keepdims=True)
        norm += jnp.sum(by_row, axis=0, keepdims=True)
        level += jnp.sum(by_row * columns[:, s:s + 1], axis=0, keepdims=True)
    scalar_ref[0:1, :] = jnp.broadcast_to(norm, (1, LANES))
    scalar_ref[1:2, :] = jnp.broadcast_to(level, (1, LANES))
    for copy in copies[4:]:
        copy.wait()


def product_kernel(is_first, split, rep_count, sec_count, *refs):
    refs = list(refs)
    take = lambda count: [refs.pop(0) for _ in range(count)]
    pairing_ref, left_ref, right_ref, start_ref = take(4)
    psi_refs = take(rep_count - 1)
    if is_first:
        limit_ref, scalar_ref = take(2)
        level_refs = take(rep_count - 1)
    else:
        vector_refs = take(rep_count)
    out_refs = take(sec_count if split else 1)
    vec_ref, inner_ref, sum_ref, slot_ref, target_ref, sem = refs
    terms, sec_dev, half, width = left_ref.shape
    rep = lax.axis_index("rep")
    sec = lax.axis_index("sec")
    fetch = pltpu.make_async_copy(pairing_ref, target_ref, sem)
    fetch.start()

    if is_first:
        scalar_a = scalar_ref[0:1, 0:1]
        scalar_b = scalar_ref[1:2, 0:1]
        rows = pl.ds(pl.multiple_of(rep * half, half), half)
        for s in range(sec_dev):
            vec_ref[s, rows, :] = start_ref[s]
        for step in range(1, rep_count):
            first_row = pl.multiple_of(lax.rem(rep + step, rep_count) * half, half)
            columns = energy_columns(level_refs[step - 1][...])
            for s in range(sec_dev):
                psi = psi_refs[step - 1][s].astype(F32)
                vector = jnp.where(live(limit_ref, s, first_row, (half, width)), psi, 0.0)
                by_row = jnp.sum(vector * vector, axis=1, keepdims=True)
                scalar_a += jnp.sum(by_row, axis=0, keepdims=True)
                scalar_b += jnp.sum(by_row * columns[:, s:s + 1], axis=0, keepdims=True)
                vec_ref[s, pl.ds(first_row, half), :] = vector.astype(BF16)
    else:
        scalar_a = jnp.zeros((1, 1), F32)
        scalar_b = jnp.zeros((1, 1), F32)
        for step in range(rep_count):
            first_row = pl.multiple_of(lax.rem(rep + step, rep_count) * half, half)
            for s in range(sec_dev):
                psi = (psi_refs[step - 1] if step else start_ref)[s].astype(F32)
                vector = vector_refs[step][s].astype(F32)
                scalar_a += total(psi * vector)
                scalar_b += total(vector * vector)
                vec_ref[s, pl.ds(first_row, half), :] = vector_refs[step][s]

    for d in range(sec_count):
        slot_ref[d] = 0
        sum_ref[d] = jnp.zeros((half, width), F32)
    for s in range(sec_dev):
        inner = jnp.dot(
            left_ref[:, s].reshape(terms * half, width), vec_ref[s], preferred_element_type=F32
        )
        inner_ref[s] = inner.astype(BF16).reshape(terms, half, width)
    fetch.wait()
    for t in range(terms):
        outer = jnp.dot(
            inner_ref[:, t].reshape(sec_dev * half, width),
            right_ref[t],
            preferred_element_type=F32,
        )
        for s in range(sec_dev):
            target = target_ref[s, t]
            owner = lax.div(target, sec_dev)
            place = lax.rem(owner - sec + sec_count, sec_count) if split else owner
            slot_ref[place] = lax.rem(target, sec_dev)
            sum_ref[place] += outer[s * half:(s + 1) * half]
    for d in range(sec_count):
        out = out_refs[d] if split else out_refs[0].at[d]
        for column in range(width // LANES):
            out[column * half:(column + 1) * half, :] = sum_ref[
                d, :, column * LANES:(column + 1) * LANES
            ].astype(BF16)
        out[width // LANES * half:, :] = header(slot_ref[d], (scalar_a, scalar_b))


def sigma_packets(is_first, split, pairing, left_env, right_env, start, psi_others, more):
    terms, sec_dev, half, width = left_env.shape
    sec_count = lax.axis_size("sec")
    rep_count = len(psi_others) + 1
    packet = (width // LANES * half + HEAD, LANES)
    if split:
        outs = [jax.ShapeDtypeStruct(packet, BF16)] * sec_count
    else:
        outs = [jax.ShapeDtypeStruct((sec_count,) + packet, BF16)]
    pair_flops = 2 * half * width * width * 2
    operands = [pairing, left_env, right_env, start, *psi_others, *more]
    return pl.pallas_call(
        functools.partial(product_kernel, is_first, split, rep_count, sec_count),
        out_shape=outs,
        in_specs=[whole(pltpu.VMEM)] * len(operands),
        out_specs=[whole(pltpu.VMEM)] * len(outs),
        scratch_shapes=[
            pltpu.VMEM((sec_dev, rep_count * half, width), BF16),
            pltpu.VMEM((sec_dev, terms, half, width), BF16),
            pltpu.VMEM((sec_count, half, width), F32),
            pltpu.SMEM((sec_count,), jnp.int32),
            pltpu.SMEM(pairing.shape, jnp.int32),
            pltpu.SemaphoreType.DMA,
        ],
        compiler_params=pltpu.CompilerParams(vmem_limit_bytes=VMEM_BYTES),
        cost_estimate=pl.CostEstimate(
            flops=terms * sec_dev * pair_flops,
            bytes_accessed=2 * (left_env.size + right_env.size),
            transcendentals=0,
        ),
        name="products_first" if is_first else "products_second",
    )(*operands)


def exchange(packets, split):
    sec_count = lax.axis_size("sec")
    op_count = lax.axis_size("op")
    if not split:
        arrived = lax.all_to_all(packets[0], "sec", split_axis=0, concat_axis=0, tiled=True)
        gathered = [arrived]
        for step in range(1, op_count):
            turn = [(i, (i + step) % op_count) for i in range(op_count)]
            gathered.append(lax.ppermute(arrived, "op", turn))
        return gathered
    arrived = [packets[0]]
    for step in range(1, sec_count):
        turn = [(i, (i + step) % sec_count) for i in range(sec_count)]
        arrived.append(lax.ppermute(packets[step], "sec", turn))
    gathered = list(arrived)
    for step in range(1, op_count):
        turn = [(i, (i + step) % op_count) for i in range(op_count)]
        gathered += [lax.ppermute(packet, "op", turn) for packet in arrived]
    return gathered


def add_packets(packet_refs, split, sec_dev, half, width, sum_ref):
    own = lax.axis_size("sec") if split else 1
    body_rows = width // LANES * half
    sum_ref[...] = jnp.zeros_like(sum_ref)
    if split:
        heads = [ref[body_rows:].astype(F32) for ref in packet_refs]
        for column in range(width // LANES):
            for s in range(sec_dev):
                part = jnp.zeros((half, LANES), F32)
                for ref, head in zip(packet_refs, heads):
                    body = ref[column * half:(column + 1) * half].astype(F32)
                    part += jnp.where(head[0:1] == s, body, 0.0)
                sum_ref[s, :, column * LANES:(column + 1) * LANES] = part
        return sum(heads[1:own], heads[0])

    head_sum = jnp.zeros((HEAD, LANES), F32)
    for index, ref in enumerate(packet_refs):
        def add_one(p, carry):
            head = ref[p, body_rows:, :].astype(F32)
            for column in range(width // LANES):
                body = ref[p, column * half:(column + 1) * half, :].astype(F32)
                lanes = slice(column * LANES, (column + 1) * LANES)
                for s in range(sec_dev):
                    sum_ref[s, :, lanes] += jnp.where(head[0:1] == s, body, 0.0)
            return carry + head
        result = lax.fori_loop(0, ref.shape[0], add_one, jnp.zeros((HEAD, LANES), F32))
        if index < own:
            head_sum = head_sum + result
    return head_sum


def first_kernel(split, count, *refs):
    limit_ref = refs[0]
    packet_refs = refs[1:1 + count]
    start_ref, energy_ref, first_ref, one_ref, vec_ref, norm_ref, sum_ref = refs[1 + count:]
    sec_dev, half, width = start_ref.shape
    head_sum = add_packets(packet_refs, split, sec_dev, half, width, sum_ref)
    norm = head_scalar(head_sum, 0)
    shift = spread(head_scalar(head_sum, 1) / norm, width)
    norm_ref[...] = jnp.broadcast_to(norm, norm_ref.shape)
    first_row = lax.axis_index("rep") * half
    for s in range(sec_dev):
        mask = live(limit_ref, s, first_row, (half, width))
        start = start_ref[s].astype(F32)
        one = jnp.where(mask, sum_ref[s] + spread(energy_ref[s], width) * start, 0.0)
        one_ref[s] = one
        first_ref[s] = one.astype(BF16)
        vec_ref[s] = (one - shift * start).astype(BF16)


def second_kernel(split, count, entries, *refs):
    limit_ref = refs[0]
    packet_refs = refs[1:1 + count]
    vec_ref, energy_ref, one_ref, norm_ref, second_ref, sum_ref = refs[1 + count:]
    sec_dev, half, width = vec_ref.shape
    head_sum = add_packets(packet_refs, split, sec_dev, half, width, sum_ref)
    cross = head_scalar(head_sum, 0)
    square = head_scalar(head_sum, 1)
    excess = cross / norm_ref[0:1]
    resid_sq = jnp.maximum(square - excess * cross, 0.0)
    scale = spread(lax.rsqrt(resid_sq / entries + EPSILON), width)
    excess = spread(excess, width)
    first_row = lax.axis_index("rep") * half
    for s in range(sec_dev):
        mask = live(limit_ref, s, first_row, (half, width))
        mapped = sum_ref[s] + spread(energy_ref[s], width) * vec_ref[s].astype(F32)
        value = jnp.where(mask, scale * (mapped - excess * one_ref[s]), 0.0)
        second_ref[s] = value.astype(BF16)


def body(psi, left_env, right_env, pairing, block_rows, block_cols, energy):
    sec_count = lax.axis_size("sec")
    op_count = lax.axis_size("op")
    rep_count = lax.axis_size("rep")
    terms, sec_dev, half, width = left_env.shape
    entries = sec_count * sec_dev * rep_count * half * width
    split = sec_count * op_count <= 8
    params = pltpu.CompilerParams(vmem_limit_bytes=VMEM_BYTES)
    vec_shape = (sec_dev, half, width)
    vec_bf16 = jax.ShapeDtypeStruct(vec_shape, BF16)
    sum_scratch = [pltpu.VMEM(vec_shape, F32)]

    def from_others(array):
        arrays = []
        for step in range(1, rep_count):
            turn = [((i + step) % rep_count, i) for i in range(rep_count)]
            arrays.append(lax.ppermute(array, "rep", turn))
        return arrays

    psi_others = from_others(psi)
    level_others = from_others(energy)
    start, left_env, right_env, pairing, limits, levels, scalars = pl.pallas_call(
        load_kernel,
        out_shape=[
            vec_bf16,
            jax.ShapeDtypeStruct(left_env.shape, BF16),
            jax.ShapeDtypeStruct(right_env.shape, BF16),
            jax.ShapeDtypeStruct((sec_dev, terms), jnp.int32),
            jax.ShapeDtypeStruct((2 * sec_dev, LANES), jnp.int32),
            jax.ShapeDtypeStruct((sec_dev, half, LANES), F32),
            jax.ShapeDtypeStruct((8, LANES), F32),
        ],
        in_specs=[whole(pltpu.HBM)] * 7,
        out_specs=[whole(pltpu.VMEM)] * 7,
        scratch_shapes=[
            pltpu.VMEM(vec_shape, BF16),
            pltpu.VMEM((sec_dev, half), F32),
            pltpu.SMEM((sec_dev,), jnp.int32),
            pltpu.SMEM((sec_dev,), jnp.int32),
            pltpu.SemaphoreType.DMA((7,)),
        ],
        compiler_params=params,
        name="load",
    )(*(
        pltpu.with_memory_space_constraint(array, pltpu.HBM)
        for array in (psi, left_env, right_env, pairing.T, block_rows, block_cols, energy)
    ))

    packets = sigma_packets(
        True, split, pairing, left_env, right_env, start, psi_others,
        [limits, scalars, *level_others],
    )
    gathered = exchange(packets, split)
    count = len(gathered)
    first_out, sigma_one, vector, norm = pl.pallas_call(
        functools.partial(first_kernel, split, count),
        out_shape=[
            pltpu.VMEM(vec_shape, BF16),
            jax.ShapeDtypeStruct(vec_shape, F32),
            vec_bf16,
            jax.ShapeDtypeStruct((8, LANES), F32),
        ],
        in_specs=[whole(pltpu.VMEM)] * (count + 3),
        out_specs=[whole(pltpu.VMEM)] * 4,
        scratch_shapes=sum_scratch,
        compiler_params=params,
        name="combine_first",
    )(limits, *gathered, start, levels)

    packets = sigma_packets(
        False, split, pairing, left_env, right_env, start, psi_others,
        [vector, *from_others(vector)],
    )
    gathered = exchange(packets, split)
    (second_out,) = pl.pallas_call(
        functools.partial(second_kernel, split, count, entries),
        out_shape=[vec_bf16],
        in_specs=[whole(pltpu.VMEM)] * (count + 5),
        out_specs=[whole(pltpu.VMEM)],
        scratch_shapes=sum_scratch,
        compiler_params=params,
        name="combine_second",
    )(limits, *gathered, vector, levels, sigma_one, norm)
    return (first_out, second_out)


def solution(mesh):
    return jax.shard_map(
        body,
        mesh=mesh,
        in_specs=(
            P(("grp", "sec"), "rep", None),
            P(("grp", "op"), "sec", "rep", None),
            P(("grp", "op"), None, None),
            P(("grp", "op"), "sec"),
            P(("grp", "sec")),
            P(("grp", "sec")),
            P(("grp", "sec"), "rep"),
        ),
        out_specs=(P(("grp", "sec"), "rep", None), P(("grp", "sec"), "rep", None)),
        check_vma=False,
    )
```

```python
import functools

import jax
import jax.numpy as jnp
from jax import lax
from jax.experimental import pallas as pl
from jax.experimental.pallas import tpu as pltpu
from jax.sharding import PartitionSpec as P

EPSILON = 1e-06
HEAD = 16
PARTS = 3
LANES = 128
VMEM_BYTES = 24 * 1024 * 1024
F32 = jnp.float32
BF16 = jnp.bfloat16


def whole(space):
    return pl.BlockSpec(memory_space=space)


def live(limit_ref, s, first_row, shape):
    sec_dev = limit_ref.shape[0] // 2
    repeat = shape[1] // LANES
    rows = jnp.concatenate([limit_ref[s:s + 1, :]] * repeat, axis=1)
    cols = jnp.concatenate([limit_ref[sec_dev + s:sec_dev + s + 1, :]] * repeat, axis=1)
    row_ids = first_row + lax.broadcasted_iota(jnp.int32, shape, 0)
    col_ids = lax.broadcasted_iota(jnp.int32, shape, 1)
    return (row_ids < rows) & (col_ids < cols)


def energy_columns(level):
    missing = -level.shape[0] % 8
    if missing:
        level = jnp.concatenate([level, jnp.zeros((missing, level.shape[1]), F32)], axis=0)
    return level.T


def spread(array, width):
    return jnp.concatenate([array] * (width // LANES), axis=1)


def total(array):
    return jnp.sum(jnp.sum(array, axis=0, keepdims=True), axis=1, keepdims=True)


def header(slot, scalars):
    row_ids = lax.broadcasted_iota(jnp.int32, (HEAD, LANES), 0)
    head = jnp.where(row_ids == 0, slot.astype(F32), 0.0)
    row = 1
    for scalar in scalars:
        rest = jnp.broadcast_to(scalar, (HEAD, LANES))
        for _ in range(PARTS):
            piece = rest.astype(BF16).astype(F32)
            head = jnp.where(row_ids == row, piece, head)
            rest = rest - piece
            row += 1
    return head.astype(BF16)


def head_scalar(head_sum, index):
    first = 1 + PARTS * index
    return jnp.sum(head_sum[first:first + PARTS], axis=0, keepdims=True)


def load_kernel(
    psi_hbm, left_hbm, right_hbm, pairing_hbm, rows_hbm, cols_hbm, energy_hbm,
    start_ref, left_ref, right_ref, pairing_ref, limit_ref, energy_ref, scalar_ref,
    psi_ref, level_ref, rows_ref, cols_ref, sems,
):
    sec_dev, half, width = psi_ref.shape
    pairs = [
        (rows_hbm, rows_ref), (cols_hbm, cols_ref), (energy_hbm, level_ref), (psi_hbm, psi_ref),
        (pairing_hbm, pairing_ref), (left_hbm, left_ref), (right_hbm, right_ref),
    ]
    copies = [
        pltpu.make_async_copy(source, target, sems.at[i])
        for i, (source, target) in enumerate(pairs)
    ]
    for copy in copies:
        copy.start()
    for copy in copies[:3]:
        copy.wait()
    for s in range(sec_dev):
        limit_ref[s:s + 1, :] = jnp.full((1, LANES), rows_ref[s], jnp.int32)
        limit_ref[sec_dev + s:sec_dev + s + 1, :] = jnp.full((1, LANES), cols_ref[s], jnp.int32)
    columns = energy_columns(level_ref[...])
    for s in range(sec_dev):
        energy_ref[s] = jnp.broadcast_to(columns[:, s:s + 1], (half, LANES))
    copies[3].wait()
    first_row = lax.axis_index("rep") * half
    norm = jnp.zeros((1, 1), F32)
    level = jnp.zeros((1, 1), F32)
    for s in range(sec_dev):
        vector = jnp.where(
            live(limit_ref, s, first_row, (half, width)), psi_ref[s].astype(F32), 0.0
        )
        start_ref[s] = vector.astype(BF16)
        by_row = jnp.sum(vector * vector, axis=1, keepdims=True)
        norm += jnp.sum(by_row, axis=0, keepdims=True)
        level += jnp.sum(by_row * columns[:, s:s + 1], axis=0, keepdims=True)
    scalar_ref[0:1, :] = jnp.broadcast_to(norm, (1, LANES))
    scalar_ref[1:2, :] = jnp.broadcast_to(level, (1, LANES))
    for copy in copies[4:]:
        copy.wait()


def product_kernel(is_first, split, paired, rep_count, sec_count, *refs):
    refs = list(refs)
    take = lambda count: [refs.pop(0) for _ in range(count)]
    pairing_ref, left_ref, right_ref, start_ref = take(4)
    psi_refs = take(rep_count - 1)
    if is_first:
        limit_ref, scalar_ref = take(2)
        level_refs = take(rep_count - 1)
    else:
        vector_refs = take(rep_count)
    out_refs = take(sec_count if split else 1)
    vec_ref, inner_ref, sum_ref, slot_ref, target_ref, sem = refs
    terms, sec_dev, half, width = left_ref.shape
    rep = lax.axis_index("rep")
    sec = lax.axis_index("sec")
    fetch = pltpu.make_async_copy(pairing_ref, target_ref, sem)
    fetch.start()

    if is_first:
        scalar_a = scalar_ref[0:1, 0:1]
        scalar_b = scalar_ref[1:2, 0:1]
        rows = pl.ds(pl.multiple_of(rep * half, half), half)
        for s in range(sec_dev):
            vec_ref[s, rows, :] = start_ref[s]
        for step in range(1, rep_count):
            first_row = pl.multiple_of(lax.rem(rep + step, rep_count) * half, half)
            columns = energy_columns(level_refs[step - 1][...])
            for s in range(sec_dev):
                psi = psi_refs[step - 1][s].astype(F32)
                vector = jnp.where(live(limit_ref, s, first_row, (half, width)), psi, 0.0)
                by_row = jnp.sum(vector * vector, axis=1, keepdims=True)
                scalar_a += jnp.sum(by_row, axis=0, keepdims=True)
                scalar_b += jnp.sum(by_row * columns[:, s:s + 1], axis=0, keepdims=True)
                vec_ref[s, pl.ds(first_row, half), :] = vector.astype(BF16)
    else:
        scalar_a = jnp.zeros((1, 1), F32)
        scalar_b = jnp.zeros((1, 1), F32)
        for step in range(rep_count):
            first_row = pl.multiple_of(lax.rem(rep + step, rep_count) * half, half)
            for s in range(sec_dev):
                psi = (psi_refs[step - 1] if step else start_ref)[s].astype(F32)
                vector = vector_refs[step][s].astype(F32)
                scalar_a += total(psi * vector)
                scalar_b += total(vector * vector)
                vec_ref[s, pl.ds(first_row, half), :] = vector_refs[step][s]

    for d in range(sec_count):
        slot_ref[d] = 0
        sum_ref[d] = jnp.zeros((half, width), F32)
    for s in range(sec_dev):
        inner = jnp.dot(
            left_ref[:, s].reshape(terms * half, width), vec_ref[s], preferred_element_type=F32
        )
        inner_ref[s] = inner.astype(BF16).reshape(terms, half, width)
    fetch.wait()
    for t in range(terms):
        outer = jnp.dot(
            inner_ref[:, t].reshape(sec_dev * half, width),
            right_ref[t],
            preferred_element_type=F32,
        )
        for s in range(sec_dev):
            target = target_ref[s, t]
            owner = lax.div(target, sec_dev)
            if not split:
                place = owner
            elif paired:
                place = owner ^ sec
            else:
                place = lax.rem(owner - sec + sec_count, sec_count)
            slot_ref[place] = lax.rem(target, sec_dev)
            sum_ref[place] += outer[s * half:(s + 1) * half]
    for d in range(sec_count):
        out = out_refs[d] if split else out_refs[0].at[d]
        for column in range(width // LANES):
            out[column * half:(column + 1) * half, :] = sum_ref[
                d, :, column * LANES:(column + 1) * LANES
            ].astype(BF16)
        out[width // LANES * half:, :] = header(slot_ref[d], (scalar_a, scalar_b))


def sigma_packets(
    is_first, split, paired, pairing, left_env, right_env, start, psi_others, more
):
    terms, sec_dev, half, width = left_env.shape
    sec_count = lax.axis_size("sec")
    rep_count = len(psi_others) + 1
    packet = (width // LANES * half + HEAD, LANES)
    if split:
        outs = [jax.ShapeDtypeStruct(packet, BF16)] * sec_count
    else:
        outs = [jax.ShapeDtypeStruct((sec_count,) + packet, BF16)]
    pair_flops = 2 * half * width * width * 2
    operands = [pairing, left_env, right_env, start, *psi_others, *more]
    return pl.pallas_call(
        functools.partial(product_kernel, is_first, split, paired, rep_count, sec_count),
        out_shape=outs,
        in_specs=[whole(pltpu.VMEM)] * len(operands),
        out_specs=[whole(pltpu.VMEM)] * len(outs),
        scratch_shapes=[
            pltpu.VMEM((sec_dev, rep_count * half, width), BF16),
            pltpu.VMEM((sec_dev, terms, half, width), BF16),
            pltpu.VMEM((sec_count, half, width), F32),
            pltpu.SMEM((sec_count,), jnp.int32),
            pltpu.SMEM(pairing.shape, jnp.int32),
            pltpu.SemaphoreType.DMA,
        ],
        compiler_params=pltpu.CompilerParams(vmem_limit_bytes=VMEM_BYTES),
        cost_estimate=pl.CostEstimate(
            flops=terms * sec_dev * pair_flops,
            bytes_accessed=2 * (left_env.size + right_env.size),
            transcendentals=0,
        ),
        name="products_first" if is_first else "products_second",
    )(*operands)


def exchange(packets, split, paired, order, own_at):
    sec_count = lax.axis_size("sec")
    op_count = lax.axis_size("op")
    op_turns = [
        [(i, (i + step) % op_count) for i in range(op_count)] for step in range(1, op_count)
    ]
    over_op = lambda packet: [lax.ppermute(packet, "op", turn) for turn in op_turns]
    if not split:
        arrived = lax.all_to_all(packets[0], "sec", split_axis=0, concat_axis=0, tiled=True)
        return [arrived] + over_op(arrived)
    arrived = {0: packets[0]}
    crossed = {}
    for position, step in enumerate(order):
        if position == own_at:
            crossed[0] = over_op(packets[0])
        reach = (lambda i: i ^ step) if paired else (lambda i: (i + step) % sec_count)
        turn = [(i, reach(i)) for i in range(sec_count)]
        arrived[step] = lax.ppermute(packets[step], "sec", turn)
    if own_at >= len(order):
        crossed[0] = over_op(packets[0])
    for step in order:
        crossed[step] = over_op(arrived[step])
    steps = [0, *order]
    return [arrived[step] for step in steps] + sum([crossed[step] for step in steps], [])


def add_packets(packet_refs, split, sec_dev, half, width, sum_ref):
    own = lax.axis_size("sec") if split else 1
    body_rows = width // LANES * half
    sum_ref[...] = jnp.zeros_like(sum_ref)
    if split:
        heads = [ref[body_rows:].astype(F32) for ref in packet_refs]
        for column in range(width // LANES):
            for s in range(sec_dev):
                part = jnp.zeros((half, LANES), F32)
                for ref, head in zip(packet_refs, heads):
                    body = ref[column * half:(column + 1) * half].astype(F32)
                    part += jnp.where(head[0:1] == s, body, 0.0)
                sum_ref[s, :, column * LANES:(column + 1) * LANES] = part
        return sum(heads[1:own], heads[0])

    head_sum = jnp.zeros((HEAD, LANES), F32)
    for index, ref in enumerate(packet_refs):
        def add_one(p, carry):
            head = ref[p, body_rows:, :].astype(F32)
            for column in range(width // LANES):
                body = ref[p, column * half:(column + 1) * half, :].astype(F32)
                lanes = slice(column * LANES, (column + 1) * LANES)
                for s in range(sec_dev):
                    sum_ref[s, :, lanes] += jnp.where(head[0:1] == s, body, 0.0)
            return carry + head
        result = lax.fori_loop(0, ref.shape[0], add_one, jnp.zeros((HEAD, LANES), F32))
        if index < own:
            head_sum = head_sum + result
    return head_sum


def first_kernel(split, count, *refs):
    limit_ref = refs[0]
    packet_refs = refs[1:1 + count]
    start_ref, energy_ref, first_ref, one_ref, vec_ref, norm_ref, sum_ref = refs[1 + count:]
    sec_dev, half, width = start_ref.shape
    head_sum = add_packets(packet_refs, split, sec_dev, half, width, sum_ref)
    norm = head_scalar(head_sum, 0)
    shift = spread(head_scalar(head_sum, 1) / norm, width)
    norm_ref[...] = jnp.broadcast_to(norm, norm_ref.shape)
    first_row = lax.axis_index("rep") * half
    for s in range(sec_dev):
        mask = live(limit_ref, s, first_row, (half, width))
        start = start_ref[s].astype(F32)
        one = jnp.where(mask, sum_ref[s] + spread(energy_ref[s], width) * start, 0.0)
        one_ref[s] = one
        first_ref[s] = one.astype(BF16)
        vec_ref[s] = (one - shift * start).astype(BF16)


def second_kernel(split, count, entries, *refs):
    limit_ref = refs[0]
    packet_refs = refs[1:1 + count]
    vec_ref, energy_ref, one_ref, norm_ref, second_ref, sum_ref = refs[1 + count:]
    sec_dev, half, width = vec_ref.shape
    head_sum = add_packets(packet_refs, split, sec_dev, half, width, sum_ref)
    cross = head_scalar(head_sum, 0)
    square = head_scalar(head_sum, 1)
    excess = cross / norm_ref[0:1]
    resid_sq = jnp.maximum(square - excess * cross, 0.0)
    scale = spread(lax.rsqrt(resid_sq / entries + EPSILON), width)
    excess = spread(excess, width)
    first_row = lax.axis_index("rep") * half
    for s in range(sec_dev):
        mask = live(limit_ref, s, first_row, (half, width))
        mapped = sum_ref[s] + spread(energy_ref[s], width) * vec_ref[s].astype(F32)
        value = jnp.where(mask, scale * (mapped - excess * one_ref[s]), 0.0)
        second_ref[s] = value.astype(BF16)


def body(psi, left_env, right_env, pairing, block_rows, block_cols, energy):
    sec_count = lax.axis_size("sec")
    op_count = lax.axis_size("op")
    rep_count = lax.axis_size("rep")
    terms, sec_dev, half, width = left_env.shape
    entries = sec_count * sec_dev * rep_count * half * width
    split = sec_count * op_count <= 8
    can_pair = sec_count & (sec_count - 1) == 0
    steps = list(range(1, sec_count))
    first_plan = (False, steps, sec_count - 1)
    second_plan = (can_pair, steps[1:2] + steps[:1] + steps[2:], sec_count - 1)
    params = pltpu.CompilerParams(vmem_limit_bytes=VMEM_BYTES)
    vec_shape = (sec_dev, half, width)
    vec_bf16 = jax.ShapeDtypeStruct(vec_shape, BF16)
    sum_scratch = [pltpu.VMEM(vec_shape, F32)]

    def from_others(array):
        arrays = []
        for step in range(1, rep_count):
            turn = [((i + step) % rep_count, i) for i in range(rep_count)]
            arrays.append(lax.ppermute(array, "rep", turn))
        return arrays

    psi_others = from_others(psi)
    level_others = from_others(energy)
    start, left_env, right_env, pairing, limits, levels, scalars = pl.pallas_call(
        load_kernel,
        out_shape=[
            vec_bf16,
            jax.ShapeDtypeStruct(left_env.shape, BF16),
            jax.ShapeDtypeStruct(right_env.shape, BF16),
            jax.ShapeDtypeStruct((sec_dev, terms), jnp.int32),
            jax.ShapeDtypeStruct((2 * sec_dev, LANES), jnp.int32),
            jax.ShapeDtypeStruct((sec_dev, half, LANES), F32),
            jax.ShapeDtypeStruct((8, LANES), F32),
        ],
        in_specs=[whole(pltpu.HBM)] * 7,
        out_specs=[whole(pltpu.VMEM)] * 7,
        scratch_shapes=[
            pltpu.VMEM(vec_shape, BF16),
            pltpu.VMEM((sec_dev, half), F32),
            pltpu.SMEM((sec_dev,), jnp.int32),
            pltpu.SMEM((sec_dev,), jnp.int32),
            pltpu.SemaphoreType.DMA((7,)),
        ],
        compiler_params=params,
        name="load",
    )(*(
        pltpu.with_memory_space_constraint(array, pltpu.HBM)
        for array in (psi, left_env, right_env, pairing.T, block_rows, block_cols, energy)
    ))

    packets = sigma_packets(
        True, split, first_plan[0], pairing, left_env, right_env, start, psi_others,
        [limits, scalars, *level_others],
    )
    gathered = exchange(packets, split, *first_plan)
    count = len(gathered)
    first_out, sigma_one, vector, norm = pl.pallas_call(
        functools.partial(first_kernel, split, count),
        out_shape=[
            pltpu.VMEM(vec_shape, BF16),
            jax.ShapeDtypeStruct(vec_shape, F32),
            vec_bf16,
            jax.ShapeDtypeStruct((8, LANES), F32),
        ],
        in_specs=[whole(pltpu.VMEM)] * (count + 3),
        out_specs=[whole(pltpu.VMEM)] * 4,
        scratch_shapes=sum_scratch,
        compiler_params=params,
        name="combine_first",
    )(limits, *gathered, start, levels)

    packets = sigma_packets(
        False, split, second_plan[0], pairing, left_env, right_env, start, psi_others,
        [vector, *from_others(vector)],
    )
    gathered = exchange(packets, split, *second_plan)
    (second_out,) = pl.pallas_call(
        functools.partial(second_kernel, split, count, entries),
        out_shape=[vec_bf16],
        in_specs=[whole(pltpu.VMEM)] * (count + 5),
        out_specs=[whole(pltpu.VMEM)],
        scratch_shapes=sum_scratch,
        compiler_params=params,
        name="combine_second",
    )(limits, *gathered, vector, levels, sigma_one, norm)
    return (first_out, second_out)


def solution(mesh):
    return jax.shard_map(
        body,
        mesh=mesh,
        in_specs=(
            P(("grp", "sec"), "rep", None),
            P(("grp", "op"), "sec", "rep", None),
            P(("grp", "op"), None, None),
            P(("grp", "op"), "sec"),
            P(("grp", "sec")),
            P(("grp", "sec")),
            P(("grp", "sec"), "rep"),
        ),
        out_specs=(P(("grp", "sec"), "rep", None), P(("grp", "sec"), "rep", None)),
        check_vma=False,
    )
```

```python
import functools

import jax
import jax.numpy as jnp
from jax import lax
from jax.experimental import pallas as pl
from jax.experimental.pallas import tpu as pltpu
from jax.sharding import PartitionSpec as P

EPSILON = 1e-06
HEAD = 8
PARTS = 3
LANES = 128
VMEM_BYTES = 24 * 1024 * 1024
F32 = jnp.float32
BF16 = jnp.bfloat16


def whole(space):
    return pl.BlockSpec(memory_space=space)


def live(limit_ref, s, first_row, shape):
    sec_dev = limit_ref.shape[0] // 2
    repeat = shape[1] // LANES
    rows = jnp.concatenate([limit_ref[s:s + 1, :]] * repeat, axis=1)
    cols = jnp.concatenate([limit_ref[sec_dev + s:sec_dev + s + 1, :]] * repeat, axis=1)
    row_ids = first_row + lax.broadcasted_iota(jnp.int32, shape, 0)
    col_ids = lax.broadcasted_iota(jnp.int32, shape, 1)
    return (row_ids < rows) & (col_ids < cols)


def energy_columns(level):
    missing = -level.shape[0] % 8
    if missing:
        level = jnp.concatenate([level, jnp.zeros((missing, level.shape[1]), F32)], axis=0)
    return level.T


def spread(array, width):
    return jnp.concatenate([array] * (width // LANES), axis=1)


def quotient(value, count):
    return value >> (count.bit_length() - 1) if count & (count - 1) == 0 else lax.div(value, count)


def remainder(value, count):
    return value & (count - 1) if count & (count - 1) == 0 else lax.rem(value, count)


def total(array):
    return jnp.sum(jnp.sum(array, axis=0, keepdims=True), axis=1, keepdims=True)


def header(slot, scalars):
    row_ids = lax.broadcasted_iota(jnp.int32, (HEAD, LANES), 0)
    head = jnp.where(row_ids == 0, slot.astype(F32), 0.0)
    row = 1
    for scalar in scalars:
        rest = jnp.broadcast_to(scalar, (HEAD, LANES))
        for _ in range(PARTS):
            piece = rest.astype(BF16).astype(F32)
            head = jnp.where(row_ids == row, piece, head)
            rest = rest - piece
            row += 1
    return head.astype(BF16)


def head_scalar(head_sum, index):
    first = 1 + PARTS * index
    return jnp.sum(head_sum[first:first + PARTS], axis=0, keepdims=True)


def load_kernel(
    psi_hbm, left_hbm, right_hbm, pairing_hbm, rows_hbm, cols_hbm, energy_hbm,
    start_ref, left_ref, right_ref, pairing_ref, limit_ref, energy_ref, scalar_ref,
    psi_ref, level_ref, rows_ref, cols_ref, sems,
):
    sec_dev, half, width = psi_ref.shape
    pairs = [
        (rows_hbm, rows_ref), (cols_hbm, cols_ref), (energy_hbm, level_ref), (psi_hbm, psi_ref),
        (pairing_hbm, pairing_ref),
    ]
    for t in range(left_ref.shape[0]):
        pairs.append((left_hbm.at[t], left_ref.at[t]))
        pairs.append((right_hbm.at[t], right_ref.at[t]))
    copies = [
        pltpu.make_async_copy(source, target, sems.at[i])
        for i, (source, target) in enumerate(pairs)
    ]
    for copy in copies:
        copy.start()
    for copy in copies[:3]:
        copy.wait()
    for s in range(sec_dev):
        limit_ref[s:s + 1, :] = jnp.full((1, LANES), rows_ref[s], jnp.int32)
        limit_ref[sec_dev + s:sec_dev + s + 1, :] = jnp.full((1, LANES), cols_ref[s], jnp.int32)
    columns = energy_columns(level_ref[...])
    for s in range(sec_dev):
        energy_ref[s] = jnp.broadcast_to(columns[:, s:s + 1], (half, LANES))
    copies[3].wait()
    first_row = lax.axis_index("rep") * half
    norm = jnp.zeros((1, 1), F32)
    level = jnp.zeros((1, 1), F32)
    for s in range(sec_dev):
        vector = jnp.where(
            live(limit_ref, s, first_row, (half, width)), psi_ref[s].astype(F32), 0.0
        )
        start_ref[s] = vector.astype(BF16)
        by_row = jnp.sum(vector * vector, axis=1, keepdims=True)
        norm += jnp.sum(by_row, axis=0, keepdims=True)
        level += jnp.sum(by_row * columns[:, s:s + 1], axis=0, keepdims=True)
    scalar_ref[0:1, :] = jnp.broadcast_to(norm, (1, LANES))
    scalar_ref[1:2, :] = jnp.broadcast_to(level, (1, LANES))
    for copy in copies[4:]:
        copy.wait()


def product_kernel(is_first, split, paired, rep_count, sec_count, *refs):
    refs = list(refs)
    take = lambda count: [refs.pop(0) for _ in range(count)]
    pairing_ref, left_ref, right_ref, start_ref = take(4)
    psi_refs = take(rep_count - 1)
    if is_first:
        limit_ref, scalar_ref = take(2)
        level_refs = take(rep_count - 1)
    else:
        vector_refs = take(rep_count)
    out_refs = take(sec_count if split else 1)
    vec_ref, inner_ref, sum_ref, slot_ref, target_ref, sem = refs
    terms, sec_dev, half, width = left_ref.shape
    rep = lax.axis_index("rep")
    sec = lax.axis_index("sec")
    fetch = pltpu.make_async_copy(pairing_ref, target_ref, sem)
    fetch.start()

    if is_first:
        scalar_a = scalar_ref[0:1, 0:1]
        scalar_b = scalar_ref[1:2, 0:1]
        rows = pl.ds(pl.multiple_of(rep * half, half), half)
        for s in range(sec_dev):
            vec_ref[s, rows, :] = start_ref[s]
        for step in range(1, rep_count):
            first_row = pl.multiple_of(remainder(rep + step, rep_count) * half, half)
            columns = energy_columns(level_refs[step - 1][...])
            for s in range(sec_dev):
                psi = psi_refs[step - 1][s].astype(F32)
                vector = jnp.where(live(limit_ref, s, first_row, (half, width)), psi, 0.0)
                by_row = jnp.sum(vector * vector, axis=1, keepdims=True)
                scalar_a += jnp.sum(by_row, axis=0, keepdims=True)
                scalar_b += jnp.sum(by_row * columns[:, s:s + 1], axis=0, keepdims=True)
                vec_ref[s, pl.ds(first_row, half), :] = vector.astype(BF16)
    else:
        scalar_a = jnp.zeros((1, 1), F32)
        scalar_b = jnp.zeros((1, 1), F32)
        for step in range(rep_count):
            first_row = pl.multiple_of(remainder(rep + step, rep_count) * half, half)
            for s in range(sec_dev):
                psi = (psi_refs[step - 1] if step else start_ref)[s].astype(F32)
                vector = vector_refs[step][s].astype(F32)
                scalar_a += total(psi * vector)
                scalar_b += total(vector * vector)
                vec_ref[s, pl.ds(first_row, half), :] = vector_refs[step][s]

    for d in range(sec_count):
        slot_ref[d] = 0
        sum_ref[d] = jnp.zeros((half, width), F32)
    for s in range(sec_dev):
        inner = jnp.dot(
            left_ref[:, s].reshape(terms * half, width), vec_ref[s], preferred_element_type=F32
        )
        inner_ref[s] = inner.astype(BF16).reshape(terms, half, width)
    fetch.wait()
    for t in range(terms):
        outer = jnp.dot(
            inner_ref[:, t].reshape(sec_dev * half, width),
            right_ref[t],
            preferred_element_type=F32,
        )
        for s in range(sec_dev):
            target = target_ref[s, t]
            owner = quotient(target, sec_dev)
            if not split:
                place = owner
            elif paired:
                place = owner ^ sec
            else:
                place = remainder(owner - sec + sec_count, sec_count)
            slot_ref[place] = remainder(target, sec_dev)
            sum_ref[place] += outer[s * half:(s + 1) * half]
    for d in range(sec_count):
        out = out_refs[d] if split else out_refs[0].at[d]
        for column in range(width // LANES):
            out[column * half:(column + 1) * half, :] = sum_ref[
                d, :, column * LANES:(column + 1) * LANES
            ].astype(BF16)
        out[width // LANES * half:, :] = header(slot_ref[d], (scalar_a, scalar_b))


def sigma_packets(
    is_first, split, paired, pairing, left_env, right_env, start, psi_others, more
):
    terms, sec_dev, half, width = left_env.shape
    sec_count = lax.axis_size("sec")
    rep_count = len(psi_others) + 1
    packet = (width // LANES * half + HEAD, LANES)
    if split:
        outs = [jax.ShapeDtypeStruct(packet, BF16)] * sec_count
    else:
        outs = [jax.ShapeDtypeStruct((sec_count,) + packet, BF16)]
    pair_flops = 2 * half * width * width * 2
    operands = [pairing, left_env, right_env, start, *psi_others, *more]
    return pl.pallas_call(
        functools.partial(product_kernel, is_first, split, paired, rep_count, sec_count),
        out_shape=outs,
        in_specs=[whole(pltpu.VMEM)] * len(operands),
        out_specs=[whole(pltpu.VMEM)] * len(outs),
        scratch_shapes=[
            pltpu.VMEM((sec_dev, rep_count * half, width), BF16),
            pltpu.VMEM((sec_dev, terms, half, width), BF16),
            pltpu.VMEM((sec_count, half, width), F32),
            pltpu.SMEM((sec_count,), jnp.int32),
            pltpu.SMEM(pairing.shape, jnp.int32),
            pltpu.SemaphoreType.DMA,
        ],
        compiler_params=pltpu.CompilerParams(vmem_limit_bytes=VMEM_BYTES),
        cost_estimate=pl.CostEstimate(
            flops=terms * sec_dev * pair_flops,
            bytes_accessed=2 * (left_env.size + right_env.size),
            transcendentals=0,
        ),
        name="products_first" if is_first else "products_second",
    )(*operands)


def exchange(packets, split, paired, order, own_at):
    sec_count = lax.axis_size("sec")
    op_count = lax.axis_size("op")
    op_turns = [
        [(i, (i + step) % op_count) for i in range(op_count)] for step in range(1, op_count)
    ]
    over_op = lambda packet: [lax.ppermute(packet, "op", turn) for turn in op_turns]
    if not split:
        arrived = lax.all_to_all(packets[0], "sec", split_axis=0, concat_axis=0, tiled=True)
        return [arrived] + over_op(arrived)
    arrived = {0: packets[0]}
    crossed = {}
    for position, step in enumerate(order):
        if position == own_at:
            crossed[0] = over_op(packets[0])
        reach = (lambda i: i ^ step) if paired else (lambda i: (i + step) % sec_count)
        turn = [(i, reach(i)) for i in range(sec_count)]
        arrived[step] = lax.ppermute(packets[step], "sec", turn)
    if own_at >= len(order):
        crossed[0] = over_op(packets[0])
    for step in order:
        crossed[step] = over_op(arrived[step])
    steps = [0, *order]
    return [arrived[step] for step in steps] + sum([crossed[step] for step in steps], [])


def add_packets(packet_refs, split, sec_dev, half, width, sum_ref):
    own = lax.axis_size("sec") if split else 1
    body_rows = width // LANES * half
    sum_ref[...] = jnp.zeros_like(sum_ref)
    if split:
        heads = [ref[body_rows:].astype(F32) for ref in packet_refs]
        for column in range(width // LANES):
            for s in range(sec_dev):
                part = jnp.zeros((half, LANES), F32)
                for ref, head in zip(packet_refs, heads):
                    body = ref[column * half:(column + 1) * half].astype(F32)
                    part += jnp.where(head[0:1] == s, body, 0.0)
                sum_ref[s, :, column * LANES:(column + 1) * LANES] = part
        return sum(heads[1:own], heads[0])

    head_sum = jnp.zeros((HEAD, LANES), F32)
    for index, ref in enumerate(packet_refs):
        def add_one(p, carry):
            head = ref[p, body_rows:, :].astype(F32)
            for column in range(width // LANES):
                body = ref[p, column * half:(column + 1) * half, :].astype(F32)
                lanes = slice(column * LANES, (column + 1) * LANES)
                for s in range(sec_dev):
                    sum_ref[s, :, lanes] += jnp.where(head[0:1] == s, body, 0.0)
            return carry + head
        result = lax.fori_loop(0, ref.shape[0], add_one, jnp.zeros((HEAD, LANES), F32))
        if index < own:
            head_sum = head_sum + result
    return head_sum


def first_kernel(split, count, *refs):
    limit_ref = refs[0]
    packet_refs = refs[1:1 + count]
    start_ref, energy_ref, first_ref, one_ref, vec_ref, norm_ref, sum_ref = refs[1 + count:]
    sec_dev, half, width = start_ref.shape
    head_sum = add_packets(packet_refs, split, sec_dev, half, width, sum_ref)
    norm = head_scalar(head_sum, 0)
    shift = spread(head_scalar(head_sum, 1) / norm, width)
    norm_ref[...] = jnp.broadcast_to(norm, norm_ref.shape)
    first_row = lax.axis_index("rep") * half
    for s in range(sec_dev):
        mask = live(limit_ref, s, first_row, (half, width))
        start = start_ref[s].astype(F32)
        one = jnp.where(mask, sum_ref[s] + spread(energy_ref[s], width) * start, 0.0)
        one_ref[s] = one
        first_ref[s] = one.astype(BF16)
        vec_ref[s] = (one - shift * start).astype(BF16)


def second_kernel(split, count, entries, *refs):
    limit_ref = refs[0]
    packet_refs = refs[1:1 + count]
    vec_ref, energy_ref, one_ref, norm_ref, second_ref, sum_ref = refs[1 + count:]
    sec_dev, half, width = vec_ref.shape
    head_sum = add_packets(packet_refs, split, sec_dev, half, width, sum_ref)
    cross = head_scalar(head_sum, 0)
    square = head_scalar(head_sum, 1)
    excess = cross / norm_ref[0:1]
    resid_sq = jnp.maximum(square - excess * cross, 0.0)
    scale = spread(lax.rsqrt(resid_sq / entries + EPSILON), width)
    excess = spread(excess, width)
    first_row = lax.axis_index("rep") * half
    for s in range(sec_dev):
        mask = live(limit_ref, s, first_row, (half, width))
        mapped = sum_ref[s] + spread(energy_ref[s], width) * vec_ref[s].astype(F32)
        value = jnp.where(mask, scale * (mapped - excess * one_ref[s]), 0.0)
        second_ref[s] = value.astype(BF16)


def body(psi, left_env, right_env, pairing, block_rows, block_cols, energy):
    sec_count = lax.axis_size("sec")
    op_count = lax.axis_size("op")
    rep_count = lax.axis_size("rep")
    terms, sec_dev, half, width = left_env.shape
    entries = sec_count * sec_dev * rep_count * half * width
    split = sec_count * op_count <= 8
    can_pair = sec_count & (sec_count - 1) == 0
    steps = list(range(1, sec_count))
    first_plan = (False, steps, sec_count - 1)
    second_plan = (can_pair, steps[1:2] + steps[:1] + steps[2:], sec_count - 1)
    params = pltpu.CompilerParams(vmem_limit_bytes=VMEM_BYTES)
    vec_shape = (sec_dev, half, width)
    vec_bf16 = jax.ShapeDtypeStruct(vec_shape, BF16)
    sum_scratch = [pltpu.VMEM(vec_shape, F32)]

    def from_others(array):
        arrays = []
        for step in range(1, rep_count):
            turn = [((i + step) % rep_count, i) for i in range(rep_count)]
            arrays.append(lax.ppermute(array, "rep", turn))
        return arrays

    psi_others = from_others(psi)
    level_others = from_others(energy)
    start, left_env, right_env, pairing, limits, levels, scalars = pl.pallas_call(
        load_kernel,
        out_shape=[
            vec_bf16,
            jax.ShapeDtypeStruct(left_env.shape, BF16),
            jax.ShapeDtypeStruct(right_env.shape, BF16),
            jax.ShapeDtypeStruct((sec_dev, terms), jnp.int32),
            jax.ShapeDtypeStruct((2 * sec_dev, LANES), jnp.int32),
            jax.ShapeDtypeStruct((sec_dev, half, LANES), F32),
            jax.ShapeDtypeStruct((8, LANES), F32),
        ],
        in_specs=[whole(pltpu.HBM)] * 7,
        out_specs=[whole(pltpu.VMEM)] * 7,
        scratch_shapes=[
            pltpu.VMEM(vec_shape, BF16),
            pltpu.VMEM((sec_dev, half), F32),
            pltpu.SMEM((sec_dev,), jnp.int32),
            pltpu.SMEM((sec_dev,), jnp.int32),
            pltpu.SemaphoreType.DMA((5 + 2 * terms,)),
        ],
        compiler_params=params,
        name="load",
    )(*(
        pltpu.with_memory_space_constraint(array, pltpu.HBM)
        for array in (psi, left_env, right_env, pairing.T, block_rows, block_cols, energy)
    ))

    packets = sigma_packets(
        True, split, first_plan[0], pairing, left_env, right_env, start, psi_others,
        [limits, scalars, *level_others],
    )
    gathered = exchange(packets, split, *first_plan)
    count = len(gathered)
    first_out, sigma_one, vector, norm = pl.pallas_call(
        functools.partial(first_kernel, split, count),
        out_shape=[
            pltpu.VMEM(vec_shape, BF16),
            jax.ShapeDtypeStruct(vec_shape, F32),
            vec_bf16,
            jax.ShapeDtypeStruct((8, LANES), F32),
        ],
        in_specs=[whole(pltpu.VMEM)] * (count + 3),
        out_specs=[whole(pltpu.VMEM)] * 4,
        scratch_shapes=sum_scratch,
        compiler_params=params,
        name="combine_first",
    )(limits, *gathered, start, levels)

    packets = sigma_packets(
        False, split, second_plan[0], pairing, left_env, right_env, start, psi_others,
        [vector, *from_others(vector)],
    )
    gathered = exchange(packets, split, *second_plan)
    (second_out,) = pl.pallas_call(
        functools.partial(second_kernel, split, count, entries),
        out_shape=[vec_bf16],
        in_specs=[whole(pltpu.VMEM)] * (count + 5),
        out_specs=[whole(pltpu.VMEM)],
        scratch_shapes=sum_scratch,
        compiler_params=params,
        name="combine_second",
    )(limits, *gathered, vector, levels, sigma_one, norm)
    return (first_out, second_out)


def solution(mesh):
    return jax.shard_map(
        body,
        mesh=mesh,
        in_specs=(
            P(("grp", "sec"), "rep", None),
            P(("grp", "op"), "sec", "rep", None),
            P(("grp", "op"), None, None),
            P(("grp", "op"), "sec"),
            P(("grp", "sec")),
            P(("grp", "sec")),
            P(("grp", "sec"), "rep"),
        ),
        out_specs=(P(("grp", "sec"), "rep", None), P(("grp", "sec"), "rep", None)),
        check_vma=False,
    )
```

```python
import functools

import jax
import jax.numpy as jnp
from jax import lax
from jax.experimental import pallas as pl
from jax.experimental.pallas import tpu as pltpu
from jax.sharding import PartitionSpec as P

EPSILON = 1e-06
HEAD = 8
PARTS = 3
LANES = 128
VMEM_BYTES = 24 * 1024 * 1024
F32 = jnp.float32
BF16 = jnp.bfloat16


def whole(space):
    return pl.BlockSpec(memory_space=space)


def live(limit_ref, s, first_row, shape):
    sec_dev = limit_ref.shape[0] // 2
    repeat = shape[1] // LANES
    rows = jnp.concatenate([limit_ref[s:s + 1, :]] * repeat, axis=1)
    cols = jnp.concatenate([limit_ref[sec_dev + s:sec_dev + s + 1, :]] * repeat, axis=1)
    row_ids = first_row + lax.broadcasted_iota(jnp.int32, shape, 0)
    col_ids = lax.broadcasted_iota(jnp.int32, shape, 1)
    return (row_ids < rows) & (col_ids < cols)


def energy_columns(level):
    missing = -level.shape[0] % 8
    if missing:
        level = jnp.concatenate([level, jnp.zeros((missing, level.shape[1]), F32)], axis=0)
    return level.T


def spread(array, width):
    return jnp.concatenate([array] * (width // LANES), axis=1)


def quotient(value, count):
    return value >> (count.bit_length() - 1) if count & (count - 1) == 0 else lax.div(value, count)


def remainder(value, count):
    return value & (count - 1) if count & (count - 1) == 0 else lax.rem(value, count)


def total(array):
    return jnp.sum(jnp.sum(array, axis=0, keepdims=True), axis=1, keepdims=True)


def header(slot, scalars):
    row_ids = lax.broadcasted_iota(jnp.int32, (HEAD, LANES), 0)
    head = jnp.where(row_ids == 0, slot.astype(F32), 0.0)
    row = 1
    for scalar in scalars:
        rest = jnp.broadcast_to(scalar, (HEAD, LANES))
        for _ in range(PARTS):
            piece = rest.astype(BF16).astype(F32)
            head = jnp.where(row_ids == row, piece, head)
            rest = rest - piece
            row += 1
    return head.astype(BF16)


def head_scalar(head_sum, index):
    first = 1 + PARTS * index
    return jnp.sum(head_sum[first:first + PARTS], axis=0, keepdims=True)


def most_pairs(pairs, sec_count):
    return pairs // sec_count + 1


def load_kernel(
    psi_hbm, left_hbm, right_hbm, pairing_hbm, rows_hbm, cols_hbm, energy_hbm,
    start_ref, left_ref, right_ref, list_ref, limit_ref, energy_ref, scalar_ref,
    psi_ref, level_ref, rows_ref, cols_ref, pairing_ref, entry_ref, count_ref, sems,
):
    sec_dev, half, width = psi_ref.shape
    terms = left_ref.shape[0]
    sec_count = list_ref.shape[0]
    cap = most_pairs(terms * sec_dev, sec_count)
    pairs = [
        (rows_hbm, rows_ref), (cols_hbm, cols_ref), (energy_hbm, level_ref), (psi_hbm, psi_ref),
        (pairing_hbm, pairing_ref),
    ]
    for t in range(left_ref.shape[0]):
        pairs.append((left_hbm.at[t], left_ref.at[t]))
        pairs.append((right_hbm.at[t], right_ref.at[t]))
    copies = [
        pltpu.make_async_copy(source, target, sems.at[i])
        for i, (source, target) in enumerate(pairs)
    ]
    for copy in copies:
        copy.start()
    for owner in range(sec_count):
        count_ref[owner] = 0
        entry_ref[owner, cap] = 0
        for i in range(cap):
            entry_ref[owner, i] = terms * sec_dev
    for copy in copies[:3]:
        copy.wait()
    for s in range(sec_dev):
        limit_ref[s:s + 1, :] = jnp.full((1, LANES), rows_ref[s], jnp.int32)
        limit_ref[sec_dev + s:sec_dev + s + 1, :] = jnp.full((1, LANES), cols_ref[s], jnp.int32)
    columns = energy_columns(level_ref[...])
    for s in range(sec_dev):
        energy_ref[s] = jnp.broadcast_to(columns[:, s:s + 1], (half, LANES))
    copies[3].wait()
    first_row = lax.axis_index("rep") * half
    norm = jnp.zeros((1, 1), F32)
    level = jnp.zeros((1, 1), F32)
    for s in range(sec_dev):
        vector = jnp.where(
            live(limit_ref, s, first_row, (half, width)), psi_ref[s].astype(F32), 0.0
        )
        start_ref[s] = vector.astype(BF16)
        by_row = jnp.sum(vector * vector, axis=1, keepdims=True)
        norm += jnp.sum(by_row, axis=0, keepdims=True)
        level += jnp.sum(by_row * columns[:, s:s + 1], axis=0, keepdims=True)
    scalar_ref[0:1, :] = jnp.broadcast_to(norm, (1, LANES))
    scalar_ref[1:2, :] = jnp.broadcast_to(level, (1, LANES))
    copies[4].wait()
    for t in range(terms):
        for s in range(sec_dev):
            target = pairing_ref[s, t]
            owner = quotient(target, sec_dev)
            count = count_ref[owner]
            entry_ref[owner, count] = t * sec_dev + s
            entry_ref[owner, cap] = remainder(target, sec_dev)
            count_ref[owner] = count + 1
    entries = pltpu.make_async_copy(entry_ref, list_ref, sems.at[len(copies)])
    entries.start()
    for copy in copies[5:]:
        copy.wait()
    entries.wait()


def product_kernel(is_first, split, paired, rep_count, sec_count, *refs):
    refs = list(refs)
    take = lambda count: [refs.pop(0) for _ in range(count)]
    list_ref, left_ref, right_ref, start_ref = take(4)
    psi_refs = take(rep_count - 1)
    if is_first:
        limit_ref, scalar_ref = take(2)
        level_refs = take(rep_count - 1)
    else:
        vector_refs = take(rep_count)
    out_refs = take(sec_count if split else 1)
    vec_ref, inner_ref, entry_ref, sem = refs
    terms, sec_dev, half, width = left_ref.shape
    rep = lax.axis_index("rep")
    sec = lax.axis_index("sec")
    fetch = pltpu.make_async_copy(list_ref, entry_ref, sem)
    fetch.start()

    if is_first:
        scalar_a = scalar_ref[0:1, 0:1]
        scalar_b = scalar_ref[1:2, 0:1]
        rows = pl.ds(pl.multiple_of(rep * half, half), half)
        for s in range(sec_dev):
            vec_ref[s, rows, :] = start_ref[s]
        for step in range(1, rep_count):
            first_row = pl.multiple_of(remainder(rep + step, rep_count) * half, half)
            columns = energy_columns(level_refs[step - 1][...])
            for s in range(sec_dev):
                psi = psi_refs[step - 1][s].astype(F32)
                vector = jnp.where(live(limit_ref, s, first_row, (half, width)), psi, 0.0)
                by_row = jnp.sum(vector * vector, axis=1, keepdims=True)
                scalar_a += jnp.sum(by_row, axis=0, keepdims=True)
                scalar_b += jnp.sum(by_row * columns[:, s:s + 1], axis=0, keepdims=True)
                vec_ref[s, pl.ds(first_row, half), :] = vector.astype(BF16)
    else:
        scalar_a = jnp.zeros((1, 1), F32)
        scalar_b = jnp.zeros((1, 1), F32)
        for step in range(rep_count):
            first_row = pl.multiple_of(remainder(rep + step, rep_count) * half, half)
            for s in range(sec_dev):
                psi = (psi_refs[step - 1] if step else start_ref)[s].astype(F32)
                vector = vector_refs[step][s].astype(F32)
                scalar_a += total(psi * vector)
                scalar_b += total(vector * vector)
                vec_ref[s, pl.ds(first_row, half), :] = vector_refs[step][s]

    pairs = terms * sec_dev
    cap = most_pairs(pairs, sec_count)
    inner_ref[pairs] = jnp.zeros((half, width), BF16)
    for s in range(sec_dev):
        inner = jnp.dot(
            left_ref[:, s].reshape(terms * half, width), vec_ref[s], preferred_element_type=F32
        ).astype(BF16)
        for t in range(terms):
            inner_ref[t * sec_dev + s] = inner[t * half:(t + 1) * half]
    fetch.wait()
    for d in range(sec_count):
        if not split:
            owner = d
        elif paired:
            owner = sec ^ d
        else:
            owner = remainder(sec + d, sec_count)
        packet = jnp.zeros((half, width), F32)
        for i in range(cap):
            pair = entry_ref[owner, i]
            term = jnp.minimum(quotient(pair, sec_dev), terms - 1)
            packet += jnp.dot(inner_ref[pair], right_ref[term], preferred_element_type=F32)
        out = out_refs[d] if split else out_refs[0].at[d]
        for column in range(width // LANES):
            out[column * half:(column + 1) * half, :] = packet[
                :, column * LANES:(column + 1) * LANES
            ].astype(BF16)
        out[width // LANES * half:, :] = header(entry_ref[owner, cap], (scalar_a, scalar_b))


def sigma_packets(
    is_first, split, paired, lists, left_env, right_env, start, psi_others, more
):
    terms, sec_dev, half, width = left_env.shape
    sec_count = lax.axis_size("sec")
    rep_count = len(psi_others) + 1
    packet = (width // LANES * half + HEAD, LANES)
    if split:
        outs = [jax.ShapeDtypeStruct(packet, BF16)] * sec_count
    else:
        outs = [jax.ShapeDtypeStruct((sec_count,) + packet, BF16)]
    pair_flops = 2 * half * width * width * 2
    operands = [lists, left_env, right_env, start, *psi_others, *more]
    return pl.pallas_call(
        functools.partial(product_kernel, is_first, split, paired, rep_count, sec_count),
        out_shape=outs,
        in_specs=[whole(pltpu.VMEM)] * len(operands),
        out_specs=[whole(pltpu.VMEM)] * len(outs),
        scratch_shapes=[
            pltpu.VMEM((sec_dev, rep_count * half, width), BF16),
            pltpu.VMEM((terms * sec_dev + 1, half, width), BF16),
            pltpu.SMEM(lists.shape, jnp.int32),
            pltpu.SemaphoreType.DMA,
        ],
        compiler_params=pltpu.CompilerParams(vmem_limit_bytes=VMEM_BYTES),
        cost_estimate=pl.CostEstimate(
            flops=terms * sec_dev * pair_flops,
            bytes_accessed=2 * (left_env.size + right_env.size),
            transcendentals=0,
        ),
        name="products_first" if is_first else "products_second",
    )(*operands)


def exchange(packets, split, paired, order, own_at):
    sec_count = lax.axis_size("sec")
    op_count = lax.axis_size("op")
    op_turns = [
        [(i, (i + step) % op_count) for i in range(op_count)] for step in range(1, op_count)
    ]
    over_op = lambda packet: [lax.ppermute(packet, "op", turn) for turn in op_turns]
    if not split:
        arrived = lax.all_to_all(packets[0], "sec", split_axis=0, concat_axis=0, tiled=True)
        return [arrived] + over_op(arrived)
    arrived = {0: packets[0]}
    crossed = {}
    for position, step in enumerate(order):
        if position == own_at:
            crossed[0] = over_op(packets[0])
        reach = (lambda i: i ^ step) if paired else (lambda i: (i + step) % sec_count)
        turn = [(i, reach(i)) for i in range(sec_count)]
        arrived[step] = lax.ppermute(packets[step], "sec", turn)
    if own_at >= len(order):
        crossed[0] = over_op(packets[0])
    for step in order:
        crossed[step] = over_op(arrived[step])
    steps = [0, *order]
    return [arrived[step] for step in steps] + sum([crossed[step] for step in steps], [])


def add_packets(packet_refs, split, sec_dev, half, width, sum_ref):
    own = lax.axis_size("sec") if split else 1
    body_rows = width // LANES * half
    sum_ref[...] = jnp.zeros_like(sum_ref)
    if split:
        heads = [ref[body_rows:].astype(F32) for ref in packet_refs]
        for column in range(width // LANES):
            for s in range(sec_dev):
                part = jnp.zeros((half, LANES), F32)
                for ref, head in zip(packet_refs, heads):
                    body = ref[column * half:(column + 1) * half].astype(F32)
                    part += jnp.where(head[0:1] == s, body, 0.0)
                sum_ref[s, :, column * LANES:(column + 1) * LANES] = part
        return sum(heads[1:own], heads[0])

    head_sum = jnp.zeros((HEAD, LANES), F32)
    for index, ref in enumerate(packet_refs):
        def add_one(p, carry):
            head = ref[p, body_rows:, :].astype(F32)
            for column in range(width // LANES):
                body = ref[p, column * half:(column + 1) * half, :].astype(F32)
                lanes = slice(column * LANES, (column + 1) * LANES)
                for s in range(sec_dev):
                    sum_ref[s, :, lanes] += jnp.where(head[0:1] == s, body, 0.0)
            return carry + head
        result = lax.fori_loop(0, ref.shape[0], add_one, jnp.zeros((HEAD, LANES), F32))
        if index < own:
            head_sum = head_sum + result
    return head_sum


def first_kernel(split, count, *refs):
    limit_ref = refs[0]
    packet_refs = refs[1:1 + count]
    start_ref, energy_ref, first_ref, one_ref, vec_ref, norm_ref, sum_ref = refs[1 + count:]
    sec_dev, half, width = start_ref.shape
    head_sum = add_packets(packet_refs, split, sec_dev, half, width, sum_ref)
    norm = head_scalar(head_sum, 0)
    shift = spread(head_scalar(head_sum, 1) / norm, width)
    norm_ref[...] = jnp.broadcast_to(norm, norm_ref.shape)
    first_row = lax.axis_index("rep") * half
    for s in range(sec_dev):
        mask = live(limit_ref, s, first_row, (half, width))
        start = start_ref[s].astype(F32)
        one = jnp.where(mask, sum_ref[s] + spread(energy_ref[s], width) * start, 0.0)
        one_ref[s] = one
        first_ref[s] = one.astype(BF16)
        vec_ref[s] = (one - shift * start).astype(BF16)


def second_kernel(split, count, entries, *refs):
    limit_ref = refs[0]
    packet_refs = refs[1:1 + count]
    vec_ref, energy_ref, one_ref, norm_ref, second_ref, sum_ref = refs[1 + count:]
    sec_dev, half, width = vec_ref.shape
    head_sum = add_packets(packet_refs, split, sec_dev, half, width, sum_ref)
    cross = head_scalar(head_sum, 0)
    square = head_scalar(head_sum, 1)
    excess = cross / norm_ref[0:1]
    resid_sq = jnp.maximum(square - excess * cross, 0.0)
    scale = spread(lax.rsqrt(resid_sq / entries + EPSILON), width)
    excess = spread(excess, width)
    first_row = lax.axis_index("rep") * half
    for s in range(sec_dev):
        mask = live(limit_ref, s, first_row, (half, width))
        mapped = sum_ref[s] + spread(energy_ref[s], width) * vec_ref[s].astype(F32)
        value = jnp.where(mask, scale * (mapped - excess * one_ref[s]), 0.0)
        second_ref[s] = value.astype(BF16)


def body(psi, left_env, right_env, pairing, block_rows, block_cols, energy):
    sec_count = lax.axis_size("sec")
    op_count = lax.axis_size("op")
    rep_count = lax.axis_size("rep")
    terms, sec_dev, half, width = left_env.shape
    entries = sec_count * sec_dev * rep_count * half * width
    split = sec_count * op_count <= 8
    can_pair = sec_count & (sec_count - 1) == 0
    steps = list(range(1, sec_count))
    first_plan = (False, steps, sec_count - 1)
    second_plan = (can_pair, steps[1:2] + steps[:1] + steps[2:], sec_count - 1)
    params = pltpu.CompilerParams(vmem_limit_bytes=VMEM_BYTES)
    vec_shape = (sec_dev, half, width)
    vec_bf16 = jax.ShapeDtypeStruct(vec_shape, BF16)
    sum_scratch = [pltpu.VMEM(vec_shape, F32)]

    def from_others(array):
        arrays = []
        for step in range(1, rep_count):
            turn = [((i + step) % rep_count, i) for i in range(rep_count)]
            arrays.append(lax.ppermute(array, "rep", turn))
        return arrays

    psi_others = from_others(psi)
    level_others = from_others(energy)
    start, left_env, right_env, lists, limits, levels, scalars = pl.pallas_call(
        load_kernel,
        out_shape=[
            vec_bf16,
            jax.ShapeDtypeStruct(left_env.shape, BF16),
            jax.ShapeDtypeStruct(right_env.shape, BF16),
            jax.ShapeDtypeStruct((sec_count, LANES), jnp.int32),
            jax.ShapeDtypeStruct((2 * sec_dev, LANES), jnp.int32),
            jax.ShapeDtypeStruct((sec_dev, half, LANES), F32),
            jax.ShapeDtypeStruct((8, LANES), F32),
        ],
        in_specs=[whole(pltpu.HBM)] * 7,
        out_specs=[whole(pltpu.VMEM)] * 7,
        scratch_shapes=[
            pltpu.VMEM(vec_shape, BF16),
            pltpu.VMEM((sec_dev, half), F32),
            pltpu.SMEM((sec_dev,), jnp.int32),
            pltpu.SMEM((sec_dev,), jnp.int32),
            pltpu.SMEM((sec_dev, terms), jnp.int32),
            pltpu.SMEM((sec_count, LANES), jnp.int32),
            pltpu.SMEM((sec_count,), jnp.int32),
            pltpu.SemaphoreType.DMA((6 + 2 * terms,)),
        ],
        compiler_params=params,
        name="load",
    )(*(
        pltpu.with_memory_space_constraint(array, pltpu.HBM)
        for array in (psi, left_env, right_env, pairing.T, block_rows, block_cols, energy)
    ))

    packets = sigma_packets(
        True, split, first_plan[0], lists, left_env, right_env, start, psi_others,
        [limits, scalars, *level_others],
    )
    gathered = exchange(packets, split, *first_plan)
    count = len(gathered)
    first_out, sigma_one, vector, norm = pl.pallas_call(
        functools.partial(first_kernel, split, count),
        out_shape=[
            pltpu.VMEM(vec_shape, BF16),
            jax.ShapeDtypeStruct(vec_shape, F32),
            vec_bf16,
            jax.ShapeDtypeStruct((8, LANES), F32),
        ],
        in_specs=[whole(pltpu.VMEM)] * (count + 3),
        out_specs=[whole(pltpu.VMEM)] * 4,
        scratch_shapes=sum_scratch,
        compiler_params=params,
        name="combine_first",
    )(limits, *gathered, start, levels)

    packets = sigma_packets(
        False, split, second_plan[0], lists, left_env, right_env, start, psi_others,
        [vector, *from_others(vector)],
    )
    gathered = exchange(packets, split, *second_plan)
    (second_out,) = pl.pallas_call(
        functools.partial(second_kernel, split, count, entries),
        out_shape=[vec_bf16],
        in_specs=[whole(pltpu.VMEM)] * (count + 5),
        out_specs=[whole(pltpu.VMEM)],
        scratch_shapes=sum_scratch,
        compiler_params=params,
        name="combine_second",
    )(limits, *gathered, vector, levels, sigma_one, norm)
    return (first_out, second_out)


def solution(mesh):
    return jax.shard_map(
        body,
        mesh=mesh,
        in_specs=(
            P(("grp", "sec"), "rep", None),
            P(("grp", "op"), "sec", "rep", None),
            P(("grp", "op"), None, None),
            P(("grp", "op"), "sec"),
            P(("grp", "sec")),
            P(("grp", "sec")),
            P(("grp", "sec"), "rep"),
        ),
        out_specs=(P(("grp", "sec"), "rep", None), P(("grp", "sec"), "rep", None)),
        check_vma=False,
    )
```

```python
import functools

import jax
import jax.numpy as jnp
from jax import lax
from jax.experimental import pallas as pl
from jax.experimental.pallas import tpu as pltpu
from jax.sharding import PartitionSpec as P

EPSILON = 1e-06
HEAD = 8
PARTS = 3
LANES = 128
VMEM_BYTES = 24 * 1024 * 1024
F32 = jnp.float32
BF16 = jnp.bfloat16


def whole(space):
    return pl.BlockSpec(memory_space=space)


def live(limit_ref, s, first_row, shape):
    sec_dev = limit_ref.shape[0] // 2
    repeat = shape[1] // LANES
    rows = jnp.concatenate([limit_ref[s:s + 1, :]] * repeat, axis=1)
    cols = jnp.concatenate([limit_ref[sec_dev + s:sec_dev + s + 1, :]] * repeat, axis=1)
    row_ids = first_row + lax.broadcasted_iota(jnp.int32, shape, 0)
    col_ids = lax.broadcasted_iota(jnp.int32, shape, 1)
    return (row_ids < rows) & (col_ids < cols)


def energy_columns(level):
    missing = -level.shape[0] % 8
    if missing:
        level = jnp.concatenate([level, jnp.zeros((missing, level.shape[1]), F32)], axis=0)
    return level.T


def spread(array, width):
    return jnp.concatenate([array] * (width // LANES), axis=1)


def quotient(value, count):
    return value >> (count.bit_length() - 1) if count & (count - 1) == 0 else lax.div(value, count)


def remainder(value, count):
    return value & (count - 1) if count & (count - 1) == 0 else lax.rem(value, count)


def fold(array):
    rows, width = array.shape
    return jnp.sum(array.reshape(rows // 8, 8, width), axis=0)


def total(array):
    return jnp.sum(jnp.sum(array, axis=0, keepdims=True), axis=1, keepdims=True)


def header(slot, scalars):
    row_ids = lax.broadcasted_iota(jnp.int32, (HEAD, LANES), 0)
    head = jnp.where(row_ids == 0, slot.astype(F32), 0.0)
    row = 1
    for scalar in scalars:
        rest = jnp.broadcast_to(scalar, (HEAD, LANES))
        for _ in range(PARTS):
            piece = rest.astype(BF16).astype(F32)
            head = jnp.where(row_ids == row, piece, head)
            rest = rest - piece
            row += 1
    return head.astype(BF16)


def head_scalar(head_sum, index):
    first = 1 + PARTS * index
    return jnp.sum(head_sum[first:first + PARTS], axis=0, keepdims=True)


def most_pairs(pairs, sec_count):
    return pairs // sec_count + 1


def load_kernel(
    psi_hbm, left_hbm, right_hbm, pairing_hbm, rows_hbm, cols_hbm, energy_hbm,
    start_ref, left_ref, right_ref, list_ref, limit_ref, energy_ref, scalar_ref,
    psi_ref, level_ref, rows_ref, cols_ref, pairing_ref, entry_ref, count_ref, sems,
):
    sec_dev, half, width = psi_ref.shape
    terms = left_ref.shape[0]
    sec_count = list_ref.shape[0]
    cap = most_pairs(terms * sec_dev, sec_count)
    pairs = [
        (rows_hbm, rows_ref), (cols_hbm, cols_ref), (energy_hbm, level_ref),
        (pairing_hbm, pairing_ref), (psi_hbm, psi_ref),
    ]
    for t in range(left_ref.shape[0]):
        pairs.append((left_hbm.at[t], left_ref.at[t]))
        pairs.append((right_hbm.at[t], right_ref.at[t]))
    copies = [
        pltpu.make_async_copy(source, target, sems.at[i])
        for i, (source, target) in enumerate(pairs)
    ]
    for copy in copies:
        copy.start()
    for owner in range(sec_count):
        count_ref[owner] = 0
        entry_ref[owner, cap] = 0
        for i in range(cap):
            entry_ref[owner, i] = terms * sec_dev
    for copy in copies[:3]:
        copy.wait()
    for s in range(sec_dev):
        limit_ref[s:s + 1, :] = jnp.full((1, LANES), rows_ref[s], jnp.int32)
        limit_ref[sec_dev + s:sec_dev + s + 1, :] = jnp.full((1, LANES), cols_ref[s], jnp.int32)
    columns = energy_columns(level_ref[...])
    for s in range(sec_dev):
        energy_ref[s] = jnp.broadcast_to(columns[:, s:s + 1], (half, LANES))
    copies[3].wait()
    for t in range(terms):
        for s in range(sec_dev):
            target = pairing_ref[s, t]
            owner = quotient(target, sec_dev)
            count = count_ref[owner]
            entry_ref[owner, count] = t * sec_dev + s
            entry_ref[owner, cap] = remainder(target, sec_dev)
            count_ref[owner] = count + 1
    entries = pltpu.make_async_copy(entry_ref, list_ref, sems.at[len(copies)])
    entries.start()
    copies[4].wait()
    first_row = lax.axis_index("rep") * half
    norm = jnp.zeros((8, width), F32)
    level = jnp.zeros((8, width), F32)
    for s in range(sec_dev):
        vector = jnp.where(
            live(limit_ref, s, first_row, (half, width)), psi_ref[s].astype(F32), 0.0
        )
        start_ref[s] = vector.astype(BF16)
        square = vector * vector
        norm += fold(square)
        level += fold(square * spread(energy_ref[s], width))
    scalar_ref[0:8, :] = norm
    scalar_ref[8:16, :] = level
    for copy in copies[5:]:
        copy.wait()
    entries.wait()


def product_kernel(is_first, split, paired, rep_count, sec_count, *refs):
    refs = list(refs)
    take = lambda count: [refs.pop(0) for _ in range(count)]
    list_ref, left_ref, right_ref, start_ref = take(4)
    psi_refs = take(rep_count - 1)
    if is_first:
        limit_ref, scalar_ref = take(2)
        level_refs = take(rep_count - 1)
    else:
        vector_refs = take(rep_count)
    out_refs = take(sec_count if split else 1)
    inner_ref, entry_ref, sem = refs
    terms, sec_dev, half, width = left_ref.shape
    pairs = terms * sec_dev
    cap = most_pairs(pairs, sec_count)
    rep = lax.axis_index("rep")
    sec = lax.axis_index("sec")
    fetch = pltpu.make_async_copy(list_ref, entry_ref, sem)
    fetch.start()
    inner_ref[pairs] = jnp.zeros((half, width), BF16)

    def first_row(step):
        return remainder(rep + step, rep_count) * half

    if is_first:
        folded = [scalar_ref[0:8, :], scalar_ref[8:16, :]]
        columns = [energy_columns(ref[...]) for ref in level_refs]
    else:
        folded = [jnp.zeros((8, width), F32)] * 2
    for s in range(sec_dev):
        blocks = [start_ref[s] if is_first else vector_refs[0][s]]
        for step in range(1, rep_count):
            if is_first:
                psi = psi_refs[step - 1][s]
                mask = live(limit_ref, s, first_row(step), (half, width))
                blocks.append(jnp.where(mask, psi.astype(F32), 0.0).astype(BF16))
            else:
                blocks.append(vector_refs[step][s])
        vector = jnp.concatenate(blocks, axis=0)
        for turn in range(1, rep_count):
            turned = blocks[rep_count - turn:] + blocks[:rep_count - turn]
            vector = jnp.where(rep == turn, jnp.concatenate(turned, axis=0), vector)
        inner = jnp.dot(
            left_ref[:, s].reshape(terms * half, width), vector, preferred_element_type=F32
        ).astype(BF16)
        for t in range(terms):
            inner_ref[t * sec_dev + s] = inner[t * half:(t + 1) * half]
        for step in range(1 if is_first else 0, rep_count):
            block = blocks[step].astype(F32)
            square = block * block
            if is_first:
                energy = jnp.broadcast_to(columns[step - 1][:, s:s + 1], (half, width))
                folded = [folded[0] + fold(square), folded[1] + fold(square * energy)]
            else:
                psi = (psi_refs[step - 1] if step else start_ref)[s].astype(F32)
                folded = [folded[0] + fold(psi * block), folded[1] + fold(square)]
    scalars = [total(array) for array in folded]
    fetch.wait()
    for d in range(sec_count):
        if not split:
            owner = d
        elif paired:
            owner = sec ^ d
        else:
            owner = remainder(sec + d, sec_count)
        packet = jnp.zeros((half, width), F32)
        for i in range(cap):
            pair = entry_ref[owner, i]
            term = jnp.minimum(quotient(pair, sec_dev), terms - 1)
            packet += jnp.dot(inner_ref[pair], right_ref[term], preferred_element_type=F32)
        out = out_refs[d] if split else out_refs[0].at[d]
        for column in range(width // LANES):
            out[column * half:(column + 1) * half, :] = packet[
                :, column * LANES:(column + 1) * LANES
            ].astype(BF16)
        out[width // LANES * half:, :] = header(entry_ref[owner, cap], scalars)


def sigma_packets(
    is_first, split, paired, lists, left_env, right_env, start, psi_others, more
):
    terms, sec_dev, half, width = left_env.shape
    sec_count = lax.axis_size("sec")
    rep_count = len(psi_others) + 1
    packet = (width // LANES * half + HEAD, LANES)
    if split:
        outs = [jax.ShapeDtypeStruct(packet, BF16)] * sec_count
    else:
        outs = [jax.ShapeDtypeStruct((sec_count,) + packet, BF16)]
    pair_flops = 2 * half * width * width * 2
    operands = [lists, left_env, right_env, start, *psi_others, *more]
    return pl.pallas_call(
        functools.partial(product_kernel, is_first, split, paired, rep_count, sec_count),
        out_shape=outs,
        in_specs=[whole(pltpu.VMEM)] * len(operands),
        out_specs=[whole(pltpu.VMEM)] * len(outs),
        scratch_shapes=[
            pltpu.VMEM((terms * sec_dev + 1, half, width), BF16),
            pltpu.SMEM(lists.shape, jnp.int32),
            pltpu.SemaphoreType.DMA,
        ],
        compiler_params=pltpu.CompilerParams(vmem_limit_bytes=VMEM_BYTES),
        cost_estimate=pl.CostEstimate(
            flops=terms * sec_dev * pair_flops,
            bytes_accessed=2 * (left_env.size + right_env.size),
            transcendentals=0,
        ),
        name="products_first" if is_first else "products_second",
    )(*operands)


def exchange(packets, split, paired, order, own_at):
    sec_count = lax.axis_size("sec")
    op_count = lax.axis_size("op")
    op_turns = [
        [(i, (i + step) % op_count) for i in range(op_count)] for step in range(1, op_count)
    ]
    over_op = lambda packet: [lax.ppermute(packet, "op", turn) for turn in op_turns]
    if not split:
        arrived = lax.all_to_all(packets[0], "sec", split_axis=0, concat_axis=0, tiled=True)
        return [arrived] + over_op(arrived)
    arrived = {0: packets[0]}
    crossed = {}
    for position, step in enumerate(order):
        if position == own_at:
            crossed[0] = over_op(packets[0])
        reach = (lambda i: i ^ step) if paired else (lambda i: (i + step) % sec_count)
        turn = [(i, reach(i)) for i in range(sec_count)]
        arrived[step] = lax.ppermute(packets[step], "sec", turn)
    if own_at >= len(order):
        crossed[0] = over_op(packets[0])
    for step in order:
        crossed[step] = over_op(arrived[step])
    steps = [0, *order]
    return [arrived[step] for step in steps] + sum([crossed[step] for step in steps], [])


def add_packets(packet_refs, split, sec_dev, half, width, sum_ref):
    own = lax.axis_size("sec") if split else 1
    body_rows = width // LANES * half
    sum_ref[...] = jnp.zeros_like(sum_ref)
    if split:
        heads = [ref[body_rows:].astype(F32) for ref in packet_refs]
        for column in range(width // LANES):
            for s in range(sec_dev):
                part = jnp.zeros((half, LANES), F32)
                for ref, head in zip(packet_refs, heads):
                    body = ref[column * half:(column + 1) * half].astype(F32)
                    part += jnp.where(head[0:1] == s, body, 0.0)
                sum_ref[s, :, column * LANES:(column + 1) * LANES] = part
        return sum(heads[1:own], heads[0])

    head_sum = jnp.zeros((HEAD, LANES), F32)
    for index, ref in enumerate(packet_refs):
        def add_one(p, carry):
            head = ref[p, body_rows:, :].astype(F32)
            for column in range(width // LANES):
                body = ref[p, column * half:(column + 1) * half, :].astype(F32)
                lanes = slice(column * LANES, (column + 1) * LANES)
                for s in range(sec_dev):
                    sum_ref[s, :, lanes] += jnp.where(head[0:1] == s, body, 0.0)
            return carry + head
        result = lax.fori_loop(0, ref.shape[0], add_one, jnp.zeros((HEAD, LANES), F32))
        if index < own:
            head_sum = head_sum + result
    return head_sum


def first_kernel(split, count, *refs):
    limit_ref = refs[0]
    packet_refs = refs[1:1 + count]
    start_ref, energy_ref, first_ref, one_ref, vec_ref, norm_ref, sum_ref = refs[1 + count:]
    sec_dev, half, width = start_ref.shape
    head_sum = add_packets(packet_refs, split, sec_dev, half, width, sum_ref)
    norm = head_scalar(head_sum, 0)
    shift = spread(head_scalar(head_sum, 1) / norm, width)
    norm_ref[...] = jnp.broadcast_to(norm, norm_ref.shape)
    first_row = lax.axis_index("rep") * half
    for s in range(sec_dev):
        mask = live(limit_ref, s, first_row, (half, width))
        start = start_ref[s].astype(F32)
        one = jnp.where(mask, sum_ref[s] + spread(energy_ref[s], width) * start, 0.0)
        one_ref[s] = one
        first_ref[s] = one.astype(BF16)
        vec_ref[s] = (one - shift * start).astype(BF16)


def second_kernel(split, count, entries, *refs):
    limit_ref = refs[0]
    packet_refs = refs[1:1 + count]
    vec_ref, energy_ref, one_ref, norm_ref, second_ref, sum_ref = refs[1 + count:]
    sec_dev, half, width = vec_ref.shape
    head_sum = add_packets(packet_refs, split, sec_dev, half, width, sum_ref)
    cross = head_scalar(head_sum, 0)
    square = head_scalar(head_sum, 1)
    excess = cross / norm_ref[0:1]
    resid_sq = jnp.maximum(square - excess * cross, 0.0)
    scale = spread(lax.rsqrt(resid_sq / entries + EPSILON), width)
    excess = spread(excess, width)
    first_row = lax.axis_index("rep") * half
    for s in range(sec_dev):
        mask = live(limit_ref, s, first_row, (half, width))
        mapped = sum_ref[s] + spread(energy_ref[s], width) * vec_ref[s].astype(F32)
        value = jnp.where(mask, scale * (mapped - excess * one_ref[s]), 0.0)
        second_ref[s] = value.astype(BF16)


def body(psi, left_env, right_env, pairing, block_rows, block_cols, energy):
    sec_count = lax.axis_size("sec")
    op_count = lax.axis_size("op")
    rep_count = lax.axis_size("rep")
    terms, sec_dev, half, width = left_env.shape
    entries = sec_count * sec_dev * rep_count * half * width
    split = sec_count * op_count <= 8
    can_pair = sec_count & (sec_count - 1) == 0
    steps = list(range(1, sec_count))
    first_plan = (False, steps, sec_count - 1)
    second_plan = (can_pair, steps[1:2] + steps[:1] + steps[2:], sec_count - 1)
    params = pltpu.CompilerParams(vmem_limit_bytes=VMEM_BYTES)
    vec_shape = (sec_dev, half, width)
    vec_bf16 = jax.ShapeDtypeStruct(vec_shape, BF16)
    sum_scratch = [pltpu.VMEM(vec_shape, F32)]

    def from_others(array):
        arrays = []
        for step in range(1, rep_count):
            turn = [((i + step) % rep_count, i) for i in range(rep_count)]
            arrays.append(lax.ppermute(array, "rep", turn))
        return arrays

    psi_others = from_others(psi)
    level_others = from_others(energy)
    start, left_env, right_env, lists, limits, levels, scalars = pl.pallas_call(
        load_kernel,
        out_shape=[
            vec_bf16,
            jax.ShapeDtypeStruct(left_env.shape, BF16),
            jax.ShapeDtypeStruct(right_env.shape, BF16),
            jax.ShapeDtypeStruct((sec_count, LANES), jnp.int32),
            jax.ShapeDtypeStruct((2 * sec_dev, LANES), jnp.int32),
            jax.ShapeDtypeStruct((sec_dev, half, LANES), F32),
            jax.ShapeDtypeStruct((16, width), F32),
        ],
        in_specs=[whole(pltpu.HBM)] * 7,
        out_specs=[whole(pltpu.VMEM)] * 7,
        scratch_shapes=[
            pltpu.VMEM(vec_shape, BF16),
            pltpu.VMEM((sec_dev, half), F32),
            pltpu.SMEM((sec_dev,), jnp.int32),
            pltpu.SMEM((sec_dev,), jnp.int32),
            pltpu.SMEM((sec_dev, terms), jnp.int32),
            pltpu.SMEM((sec_count, LANES), jnp.int32),
            pltpu.SMEM((sec_count,), jnp.int32),
            pltpu.SemaphoreType.DMA((6 + 2 * terms,)),
        ],
        compiler_params=params,
        name="load",
    )(*(
        pltpu.with_memory_space_constraint(array, pltpu.HBM)
        for array in (psi, left_env, right_env, pairing.T, block_rows, block_cols, energy)
    ))

    packets = sigma_packets(
        True, split, first_plan[0], lists, left_env, right_env, start, psi_others,
        [limits, scalars, *level_others],
    )
    gathered = exchange(packets, split, *first_plan)
    count = len(gathered)
    first_out, sigma_one, vector, norm = pl.pallas_call(
        functools.partial(first_kernel, split, count),
        out_shape=[
            pltpu.VMEM(vec_shape, BF16),
            jax.ShapeDtypeStruct(vec_shape, F32),
            vec_bf16,
            jax.ShapeDtypeStruct((8, LANES), F32),
        ],
        in_specs=[whole(pltpu.VMEM)] * (count + 3),
        out_specs=[whole(pltpu.VMEM)] * 4,
        scratch_shapes=sum_scratch,
        compiler_params=params,
        name="combine_first",
    )(limits, *gathered, start, levels)

    packets = sigma_packets(
        False, split, second_plan[0], lists, left_env, right_env, start, psi_others,
        [vector, *from_others(vector)],
    )
    gathered = exchange(packets, split, *second_plan)
    (second_out,) = pl.pallas_call(
        functools.partial(second_kernel, split, count, entries),
        out_shape=[vec_bf16],
        in_specs=[whole(pltpu.VMEM)] * (count + 5),
        out_specs=[whole(pltpu.VMEM)],
        scratch_shapes=sum_scratch,
        compiler_params=params,
        name="combine_second",
    )(limits, *gathered, vector, levels, sigma_one, norm)
    return (first_out, second_out)


def solution(mesh):
    return jax.shard_map(
        body,
        mesh=mesh,
        in_specs=(
            P(("grp", "sec"), "rep", None),
            P(("grp", "op"), "sec", "rep", None),
            P(("grp", "op"), None, None),
            P(("grp", "op"), "sec"),
            P(("grp", "sec")),
            P(("grp", "sec")),
            P(("grp", "sec"), "rep"),
        ),
        out_specs=(P(("grp", "sec"), "rep", None), P(("grp", "sec"), "rep", None)),
        check_vma=False,
    )
```

```python
import functools

import jax
import jax.numpy as jnp
from jax import lax
from jax.experimental import pallas as pl
from jax.experimental.pallas import tpu as pltpu
from jax.sharding import PartitionSpec as P

EPSILON = 1e-06
HEAD = 8
PARTS = 3
MORE_ROWS = 16
LANES = 128
VMEM_BYTES = 24 * 1024 * 1024
F32 = jnp.float32
BF16 = jnp.bfloat16


def whole(space):
    return pl.BlockSpec(memory_space=space)


def live(limit_ref, s, first_row, shape):
    sec_dev = limit_ref.shape[0] // 2
    repeat = shape[1] // LANES
    rows = jnp.concatenate([limit_ref[s:s + 1, :]] * repeat, axis=1)
    cols = jnp.concatenate([limit_ref[sec_dev + s:sec_dev + s + 1, :]] * repeat, axis=1)
    row_ids = first_row + lax.broadcasted_iota(jnp.int32, shape, 0)
    col_ids = lax.broadcasted_iota(jnp.int32, shape, 1)
    return (row_ids < rows) & (col_ids < cols)


def energy_columns(level):
    missing = -level.shape[0] % 8
    if missing:
        level = jnp.concatenate([level, jnp.zeros((missing, level.shape[1]), F32)], axis=0)
    return level.T


def spread(array, width):
    return jnp.concatenate([array] * (width // LANES), axis=1)


def quotient(value, count):
    return value >> (count.bit_length() - 1) if count & (count - 1) == 0 else lax.div(value, count)


def remainder(value, count):
    return value & (count - 1) if count & (count - 1) == 0 else lax.rem(value, count)


def fold(array):
    rows, width = array.shape
    return jnp.sum(array.reshape(rows // 8, 8, width), axis=0)


def total(array):
    return jnp.sum(jnp.sum(array, axis=0, keepdims=True), axis=1, keepdims=True)


def header(slot, scalars, shape=(HEAD, LANES)):
    row_ids = lax.broadcasted_iota(jnp.int32, shape, 0)
    head = jnp.where(row_ids == 0, slot.astype(F32), 0.0)
    row = 1
    for scalar in scalars:
        rest = jnp.broadcast_to(scalar, shape)
        for _ in range(PARTS):
            piece = rest.astype(BF16).astype(F32)
            head = jnp.where(row_ids == row, piece, head)
            rest = rest - piece
            row += 1
    return head.astype(BF16)


def head_scalar(head_sum, index):
    first = 1 + PARTS * index
    return jnp.sum(head_sum[first:first + PARTS], axis=0, keepdims=True)


def most_pairs(pairs, sec_count):
    return pairs // sec_count + 1


def load_kernel(
    psi_hbm, left_hbm, right_hbm, pairing_hbm, rows_hbm, cols_hbm, energy_hbm,
    start_ref, left_ref, right_ref, list_ref, limit_ref, energy_ref, scalar_ref,
    psi_ref, level_ref, rows_ref, cols_ref, pairing_ref, entry_ref, count_ref, sems,
):
    sec_dev, half, width = psi_ref.shape
    terms = left_ref.shape[0]
    sec_count = list_ref.shape[0]
    cap = most_pairs(terms * sec_dev, sec_count)
    pairs = [
        (rows_hbm, rows_ref), (cols_hbm, cols_ref), (energy_hbm, level_ref),
        (pairing_hbm, pairing_ref), (psi_hbm, psi_ref),
    ]
    for t in range(left_ref.shape[0]):
        pairs.append((left_hbm.at[t], left_ref.at[t]))
        pairs.append((right_hbm.at[t], right_ref.at[t]))
    copies = [
        pltpu.make_async_copy(source, target, sems.at[i])
        for i, (source, target) in enumerate(pairs)
    ]
    for copy in copies:
        copy.start()
    for owner in range(sec_count):
        count_ref[owner] = 0
        entry_ref[owner, cap] = 0
        for i in range(cap):
            entry_ref[owner, i] = terms * sec_dev
    for copy in copies[:3]:
        copy.wait()
    for s in range(sec_dev):
        limit_ref[s:s + 1, :] = jnp.full((1, LANES), rows_ref[s], jnp.int32)
        limit_ref[sec_dev + s:sec_dev + s + 1, :] = jnp.full((1, LANES), cols_ref[s], jnp.int32)
    columns = energy_columns(level_ref[...])
    for s in range(sec_dev):
        energy_ref[s] = jnp.broadcast_to(columns[:, s:s + 1], (half, LANES))
    copies[3].wait()
    for t in range(terms):
        for s in range(sec_dev):
            target = pairing_ref[s, t]
            owner = quotient(target, sec_dev)
            count = count_ref[owner]
            entry_ref[owner, count] = t * sec_dev + s
            entry_ref[owner, cap] = remainder(target, sec_dev)
            count_ref[owner] = count + 1
    entries = pltpu.make_async_copy(entry_ref, list_ref, sems.at[len(copies)])
    entries.start()
    copies[4].wait()
    first_row = lax.axis_index("rep") * half
    norm = jnp.zeros((8, width), F32)
    level = jnp.zeros((8, width), F32)
    for s in range(sec_dev):
        vector = jnp.where(
            live(limit_ref, s, first_row, (half, width)), psi_ref[s].astype(F32), 0.0
        )
        start_ref[s] = vector.astype(BF16)
        square = vector * vector
        norm += fold(square)
        level += fold(square * spread(energy_ref[s], width))
    scalar_ref[0:8, :] = norm
    scalar_ref[8:16, :] = level
    for copy in copies[5:]:
        copy.wait()
    entries.wait()


def product_kernel(is_first, split, paired, rep_count, sec_count, *refs):
    refs = list(refs)
    take = lambda count: [refs.pop(0) for _ in range(count)]
    list_ref, left_ref, right_ref = take(3)
    if is_first:
        start_ref, limit_ref, scalar_ref = take(3)
        psi_refs = take(rep_count - 1)
        level_refs = take(rep_count - 1)
    else:
        vector_refs = take(rep_count)
    out_refs = take(sec_count if split else 1)
    inner_ref, entry_ref, sem = refs
    terms, sec_dev, half, width = left_ref.shape
    pairs = terms * sec_dev
    cap = most_pairs(pairs, sec_count)
    rep = lax.axis_index("rep")
    sec = lax.axis_index("sec")
    fetch = pltpu.make_async_copy(list_ref, entry_ref, sem)
    fetch.start()
    inner_ref[pairs] = jnp.zeros((half, width), BF16)

    def first_row(step):
        return remainder(rep + step, rep_count) * half

    if is_first:
        folded = [scalar_ref[0:8, :], scalar_ref[8:16, :]]
        columns = [energy_columns(ref[...]) for ref in level_refs]
    for s in range(sec_dev):
        if is_first:
            blocks = [start_ref[s]]
            for step in range(1, rep_count):
                psi = psi_refs[step - 1][s]
                mask = live(limit_ref, s, first_row(step), (half, width))
                blocks.append(jnp.where(mask, psi.astype(F32), 0.0).astype(BF16))
        else:
            blocks = [ref[s * half:(s + 1) * half] for ref in vector_refs]
        vector = jnp.concatenate(blocks, axis=0)
        for turn in range(1, rep_count):
            turned = blocks[rep_count - turn:] + blocks[:rep_count - turn]
            vector = jnp.where(rep == turn, jnp.concatenate(turned, axis=0), vector)
        inner = jnp.dot(
            left_ref[:, s].reshape(terms * half, width), vector, preferred_element_type=F32
        ).astype(BF16)
        for t in range(terms):
            inner_ref[t * sec_dev + s] = inner[t * half:(t + 1) * half]
        if is_first:
            for step in range(1, rep_count):
                block = blocks[step].astype(F32)
                square = block * block
                energy = jnp.broadcast_to(columns[step - 1][:, s:s + 1], (half, width))
                folded = [folded[0] + fold(square), folded[1] + fold(square * energy)]
    if is_first:
        scalars = [total(array) for array in folded]
    else:
        head = sum(ref[sec_dev * half:].astype(F32) for ref in vector_refs)
        scalars = [head_scalar(head, i)[:, :LANES] for i in range(2)]
    fetch.wait()
    for d in range(sec_count):
        if not split:
            owner = d
        elif paired:
            owner = sec ^ d
        else:
            owner = remainder(sec + d, sec_count)
        packet = jnp.zeros((half, width), F32)
        for i in range(cap):
            pair = entry_ref[owner, i]
            term = jnp.minimum(quotient(pair, sec_dev), terms - 1)
            packet += jnp.dot(inner_ref[pair], right_ref[term], preferred_element_type=F32)
        out = out_refs[d] if split else out_refs[0].at[d]
        for column in range(width // LANES):
            out[column * half:(column + 1) * half, :] = packet[
                :, column * LANES:(column + 1) * LANES
            ].astype(BF16)
        out[width // LANES * half:, :] = header(entry_ref[owner, cap], scalars)


def sigma_packets(is_first, split, paired, rep_count, lists, left_env, right_env, more):
    terms, sec_dev, half, width = left_env.shape
    sec_count = lax.axis_size("sec")
    packet = (width // LANES * half + HEAD, LANES)
    if split:
        outs = [jax.ShapeDtypeStruct(packet, BF16)] * sec_count
    else:
        outs = [jax.ShapeDtypeStruct((sec_count,) + packet, BF16)]
    pair_flops = 2 * half * width * width * 2
    operands = [lists, left_env, right_env, *more]
    return pl.pallas_call(
        functools.partial(product_kernel, is_first, split, paired, rep_count, sec_count),
        out_shape=outs,
        in_specs=[whole(pltpu.VMEM)] * len(operands),
        out_specs=[whole(pltpu.VMEM)] * len(outs),
        scratch_shapes=[
            pltpu.VMEM((terms * sec_dev + 1, half, width), BF16),
            pltpu.SMEM(lists.shape, jnp.int32),
            pltpu.SemaphoreType.DMA,
        ],
        compiler_params=pltpu.CompilerParams(vmem_limit_bytes=VMEM_BYTES),
        cost_estimate=pl.CostEstimate(
            flops=terms * sec_dev * pair_flops,
            bytes_accessed=2 * (left_env.size + right_env.size),
            transcendentals=0,
        ),
        name="products_first" if is_first else "products_second",
    )(*operands)


def exchange(packets, split, paired, order, own_at):
    sec_count = lax.axis_size("sec")
    op_count = lax.axis_size("op")
    op_turns = [
        [(i, (i + step) % op_count) for i in range(op_count)] for step in range(1, op_count)
    ]
    over_op = lambda packet: [lax.ppermute(packet, "op", turn) for turn in op_turns]
    if not split:
        arrived = lax.all_to_all(packets[0], "sec", split_axis=0, concat_axis=0, tiled=True)
        return [arrived] + over_op(arrived), []
    arrived = {0: packets[0]}
    crossed = {}
    for position, step in enumerate(order):
        if position == own_at:
            crossed[0] = over_op(packets[0])
        reach = (lambda i: i ^ step) if paired else (lambda i: (i + step) % sec_count)
        turn = [(i, reach(i)) for i in range(sec_count)]
        arrived[step] = lax.ppermute(packets[step], "sec", turn)
    if own_at >= len(order):
        crossed[0] = over_op(packets[0])
    for step in order:
        crossed[step] = over_op(arrived[step])
    steps = [0, *order]
    gathered = [arrived[step] for step in steps] + sum([crossed[step] for step in steps], [])
    return gathered[:-1], gathered[-1:]


def add_packets(packet_refs, split, half, base_ref):
    sec_dev, _, width = base_ref.shape
    own = lax.axis_size("sec") if split else 1
    body_rows = width // LANES * half
    if split:
        heads = [ref[body_rows:].astype(F32) for ref in packet_refs]
        for column in range(width // LANES):
            lanes = slice(column * LANES, (column + 1) * LANES)
            for s in range(sec_dev):
                part = base_ref[s, :, lanes]
                for ref, head in zip(packet_refs, heads):
                    body = ref[column * half:(column + 1) * half].astype(F32)
                    part += jnp.where(head[0:1] == s, body, 0.0)
                base_ref[s, :, lanes] = part
        return sum(heads[1:own], heads[0])

    head_sum = jnp.zeros((HEAD, LANES), F32)
    for index, ref in enumerate(packet_refs):
        def add_one(p, carry):
            head = ref[p, body_rows:, :].astype(F32)
            for column in range(width // LANES):
                body = ref[p, column * half:(column + 1) * half, :].astype(F32)
                lanes = slice(column * LANES, (column + 1) * LANES)
                for s in range(sec_dev):
                    base_ref[s, :, lanes] += jnp.where(head[0:1] == s, body, 0.0)
            return carry + head
        result = lax.fori_loop(0, ref.shape[0], add_one, jnp.zeros((HEAD, LANES), F32))
        if index < own:
            head_sum = head_sum + result
    return head_sum


def late_sum(packet_refs, s, half, width):
    body_rows = width // LANES * half
    value = jnp.zeros((half, width), F32)
    for ref in packet_refs:
        body = jnp.concatenate(
            [ref[c * half:(c + 1) * half].astype(F32) for c in range(width // LANES)], axis=1
        )
        slot = spread(ref[body_rows:].astype(F32)[0:1], width)
        value += jnp.where(slot == s, body, 0.0)
    return value


def first_early_kernel(split, count, *refs):
    packet_refs = refs[:count]
    start_ref, energy_ref, base_ref, scalar_ref = refs[count:]
    sec_dev, half, width = start_ref.shape
    for s in range(sec_dev):
        base_ref[s] = spread(energy_ref[s], width) * start_ref[s].astype(F32)
    head_sum = add_packets(packet_refs, split, half, base_ref)
    norm = head_scalar(head_sum, 0)
    scalar_ref[0:1] = norm
    scalar_ref[1:2] = head_scalar(head_sum, 1) / norm


def first_kernel(count, *refs):
    packet_refs = refs[:count]
    limit_ref, start_ref, base_ref, scalar_ref, first_ref, one_ref, vec_ref = refs[count:]
    sec_dev, half, width = start_ref.shape
    shift = spread(scalar_ref[1:2], width)
    first_row = lax.axis_index("rep") * half
    cross = jnp.zeros((8, width), F32)
    square = jnp.zeros((8, width), F32)
    for s in range(sec_dev):
        mask = live(limit_ref, s, first_row, (half, width))
        start = start_ref[s].astype(F32)
        one = jnp.where(mask, base_ref[s] + late_sum(packet_refs, s, half, width), 0.0)
        one_ref[s] = one
        first_ref[s] = one.astype(BF16)
        vector = one - shift * start
        vec_ref[s * half:(s + 1) * half] = vector.astype(BF16)
        cross += fold(start * vector)
        square += fold(vector * vector)
    scalars = (total(cross), total(square))
    vec_ref[sec_dev * half:] = header(jnp.int32(0), scalars, (MORE_ROWS, width))


def second_early_kernel(split, count, entries, *refs):
    packet_refs = refs[:count]
    vec_ref, energy_ref, one_ref, scalar_ref, base_ref, scale_ref = refs[count:]
    sec_dev, half, width = one_ref.shape
    for s in range(sec_dev):
        vector = vec_ref[s * half:(s + 1) * half].astype(F32)
        base_ref[s] = spread(energy_ref[s], width) * vector
    head_sum = add_packets(packet_refs, split, half, base_ref)
    cross = head_scalar(head_sum, 0)
    square = head_scalar(head_sum, 1)
    excess = cross / scalar_ref[0:1]
    resid_sq = jnp.maximum(square - excess * cross, 0.0)
    scale = lax.rsqrt(resid_sq / entries + EPSILON)
    scale_ref[...] = jnp.broadcast_to(scale, scale_ref.shape)
    for s in range(sec_dev):
        base_ref[s] = base_ref[s] - spread(excess, width) * one_ref[s]


def second_kernel(count, *refs):
    packet_refs = refs[:count]
    limit_ref, base_ref, scale_ref, second_ref = refs[count:]
    sec_dev, half, width = base_ref.shape
    scale = spread(scale_ref[0:1], width)
    first_row = lax.axis_index("rep") * half
    for s in range(sec_dev):
        mask = live(limit_ref, s, first_row, (half, width))
        value = scale * (base_ref[s] + late_sum(packet_refs, s, half, width))
        second_ref[s] = jnp.where(mask, value, 0.0).astype(BF16)


def call(kernel, name, outs, *operands):
    return pl.pallas_call(
        kernel,
        out_shape=outs,
        in_specs=[whole(pltpu.VMEM)] * len(operands),
        out_specs=[whole(pltpu.VMEM)] * len(outs),
        compiler_params=pltpu.CompilerParams(vmem_limit_bytes=VMEM_BYTES),
        name=name,
    )(*operands)


def body(psi, left_env, right_env, pairing, block_rows, block_cols, energy):
    sec_count = lax.axis_size("sec")
    op_count = lax.axis_size("op")
    rep_count = lax.axis_size("rep")
    terms, sec_dev, half, width = left_env.shape
    entries = sec_count * sec_dev * rep_count * half * width
    split = sec_count * op_count <= 8
    can_pair = sec_count & (sec_count - 1) == 0
    steps = list(range(1, sec_count))
    first_plan = (False, steps, sec_count - 1)
    second_plan = (can_pair, steps[1:2] + steps[:1] + steps[2:], sec_count - 1)
    params = pltpu.CompilerParams(vmem_limit_bytes=VMEM_BYTES)
    vec_shape = (sec_dev, half, width)
    vec_bf16 = jax.ShapeDtypeStruct(vec_shape, BF16)

    def from_others(array):
        arrays = []
        for step in range(1, rep_count):
            turn = [((i + step) % rep_count, i) for i in range(rep_count)]
            arrays.append(lax.ppermute(array, "rep", turn))
        return arrays

    psi_others = from_others(psi)
    level_others = from_others(energy)
    start, left_env, right_env, lists, limits, levels, scalars = pl.pallas_call(
        load_kernel,
        out_shape=[
            vec_bf16,
            jax.ShapeDtypeStruct(left_env.shape, BF16),
            jax.ShapeDtypeStruct(right_env.shape, BF16),
            jax.ShapeDtypeStruct((sec_count, LANES), jnp.int32),
            jax.ShapeDtypeStruct((2 * sec_dev, LANES), jnp.int32),
            jax.ShapeDtypeStruct((sec_dev, half, LANES), F32),
            jax.ShapeDtypeStruct((16, width), F32),
        ],
        in_specs=[whole(pltpu.HBM)] * 7,
        out_specs=[whole(pltpu.VMEM)] * 7,
        scratch_shapes=[
            pltpu.VMEM(vec_shape, BF16),
            pltpu.VMEM((sec_dev, half), F32),
            pltpu.SMEM((sec_dev,), jnp.int32),
            pltpu.SMEM((sec_dev,), jnp.int32),
            pltpu.SMEM((sec_dev, terms), jnp.int32),
            pltpu.SMEM((sec_count, LANES), jnp.int32),
            pltpu.SMEM((sec_count,), jnp.int32),
            pltpu.SemaphoreType.DMA((6 + 2 * terms,)),
        ],
        compiler_params=params,
        name="load",
    )(*(
        pltpu.with_memory_space_constraint(array, pltpu.HBM)
        for array in (psi, left_env, right_env, pairing.T, block_rows, block_cols, energy)
    ))

    block_f32 = jax.ShapeDtypeStruct(vec_shape, F32)
    row_f32 = jax.ShapeDtypeStruct((8, LANES), F32)

    packets = sigma_packets(
        True, split, first_plan[0], rep_count, lists, left_env, right_env,
        [start, limits, scalars, *psi_others, *level_others],
    )
    early, late = exchange(packets, split, *first_plan)
    base, scalars = call(
        functools.partial(first_early_kernel, split, len(early)), "combine_first_early",
        [block_f32, row_f32], *early, start, levels,
    )
    first_out, sigma_one, vector = call(
        functools.partial(first_kernel, len(late)), "combine_first",
        [
            pltpu.VMEM(vec_shape, BF16),
            block_f32,
            jax.ShapeDtypeStruct((sec_dev * half + MORE_ROWS, width), BF16),
        ],
        *late, limits, start, base, scalars,
    )

    packets = sigma_packets(
        False, split, second_plan[0], rep_count, lists, left_env, right_env,
        [vector, *from_others(vector)],
    )
    early, late = exchange(packets, split, *second_plan)
    base, scale = call(
        functools.partial(second_early_kernel, split, len(early), entries),
        "combine_second_early", [block_f32, row_f32], *early, vector, levels, sigma_one, scalars,
    )
    (second_out,) = call(
        functools.partial(second_kernel, len(late)), "combine_second", [vec_bf16],
        *late, limits, base, scale,
    )
    return (first_out, second_out)


def solution(mesh):
    return jax.shard_map(
        body,
        mesh=mesh,
        in_specs=(
            P(("grp", "sec"), "rep", None),
            P(("grp", "op"), "sec", "rep", None),
            P(("grp", "op"), None, None),
            P(("grp", "op"), "sec"),
            P(("grp", "sec")),
            P(("grp", "sec")),
            P(("grp", "sec"), "rep"),
        ),
        out_specs=(P(("grp", "sec"), "rep", None), P(("grp", "sec"), "rep", None)),
        check_vma=False,
    )
```

```python
import functools

import jax
import jax.numpy as jnp
from jax import lax
from jax.experimental import pallas as pl
from jax.experimental.pallas import tpu as pltpu
from jax.sharding import PartitionSpec as P

EPSILON = 1e-06
HEAD = 8
PARTS = 3
MORE_ROWS = 16
LANES = 128
VMEM_BYTES = 24 * 1024 * 1024
F32 = jnp.float32
BF16 = jnp.bfloat16


def whole(space):
    return pl.BlockSpec(memory_space=space)


def live(limit_ref, s, first_row, shape):
    sec_dev = limit_ref.shape[0] // 2
    repeat = shape[1] // LANES
    rows = jnp.concatenate([limit_ref[s:s + 1, :]] * repeat, axis=1)
    cols = jnp.concatenate([limit_ref[sec_dev + s:sec_dev + s + 1, :]] * repeat, axis=1)
    row_ids = first_row + lax.broadcasted_iota(jnp.int32, shape, 0)
    col_ids = lax.broadcasted_iota(jnp.int32, shape, 1)
    return (row_ids < rows) & (col_ids < cols)


def energy_columns(level):
    missing = -level.shape[0] % 8
    if missing:
        level = jnp.concatenate([level, jnp.zeros((missing, level.shape[1]), F32)], axis=0)
    return level.T


def spread(array, width):
    return jnp.concatenate([array] * (width // LANES), axis=1)


def quotient(value, count):
    return value >> (count.bit_length() - 1) if count & (count - 1) == 0 else lax.div(value, count)


def remainder(value, count):
    return value & (count - 1) if count & (count - 1) == 0 else lax.rem(value, count)


def fold(array):
    rows, width = array.shape
    return jnp.sum(array.reshape(rows // 8, 8, width), axis=0)


def total(array):
    return jnp.sum(jnp.sum(array, axis=0, keepdims=True), axis=1, keepdims=True)


def header(slot, scalars, shape=(HEAD, LANES)):
    row_ids = lax.broadcasted_iota(jnp.int32, shape, 0)
    head = jnp.where(row_ids == 0, slot.astype(F32), 0.0)
    row = 1
    for scalar in scalars:
        rest = jnp.broadcast_to(scalar, shape)
        for _ in range(PARTS):
            piece = rest.astype(BF16).astype(F32)
            head = jnp.where(row_ids == row, piece, head)
            rest = rest - piece
            row += 1
    return head.astype(BF16)


def head_scalar(head_sum, index):
    first = 1 + PARTS * index
    return jnp.sum(head_sum[first:first + PARTS], axis=0, keepdims=True)


def most_pairs(pairs, sec_count):
    return pairs // sec_count + 1


def load_kernel(
    psi_hbm, left_hbm, pairing_hbm, rows_hbm, cols_hbm, energy_hbm,
    start_ref, left_ref, list_ref, limit_ref, energy_ref, scalar_ref,
    psi_ref, level_ref, rows_ref, cols_ref, pairing_ref, entry_ref, count_ref, sems,
):
    sec_dev, half, width = psi_ref.shape
    terms = left_ref.shape[0]
    sec_count = list_ref.shape[0]
    cap = most_pairs(terms * sec_dev, sec_count)
    pairs = [
        (rows_hbm, rows_ref), (cols_hbm, cols_ref), (energy_hbm, level_ref),
        (pairing_hbm, pairing_ref), (psi_hbm, psi_ref),
    ]
    for t in range(left_ref.shape[0]):
        pairs.append((left_hbm.at[t], left_ref.at[t]))
    copies = [
        pltpu.make_async_copy(source, target, sems.at[i])
        for i, (source, target) in enumerate(pairs)
    ]
    for copy in copies:
        copy.start()
    for owner in range(sec_count):
        count_ref[owner] = 0
        entry_ref[owner, cap] = 0
        for i in range(cap):
            entry_ref[owner, i] = terms * sec_dev
    for copy in copies[:3]:
        copy.wait()
    for s in range(sec_dev):
        limit_ref[s:s + 1, :] = jnp.full((1, LANES), rows_ref[s], jnp.int32)
        limit_ref[sec_dev + s:sec_dev + s + 1, :] = jnp.full((1, LANES), cols_ref[s], jnp.int32)
    columns = energy_columns(level_ref[...])
    for s in range(sec_dev):
        energy_ref[s] = jnp.broadcast_to(columns[:, s:s + 1], (half, LANES))
    copies[3].wait()
    for t in range(terms):
        for s in range(sec_dev):
            target = pairing_ref[s, t]
            owner = quotient(target, sec_dev)
            count = count_ref[owner]
            entry_ref[owner, count] = t * sec_dev + s
            entry_ref[owner, cap] = remainder(target, sec_dev)
            count_ref[owner] = count + 1
    entries = pltpu.make_async_copy(entry_ref, list_ref, sems.at[len(copies)])
    entries.start()
    copies[4].wait()
    first_row = lax.axis_index("rep") * half
    norm = jnp.zeros((8, width), F32)
    level = jnp.zeros((8, width), F32)
    for s in range(sec_dev):
        vector = jnp.where(
            live(limit_ref, s, first_row, (half, width)), psi_ref[s].astype(F32), 0.0
        )
        start_ref[s] = vector.astype(BF16)
        square = vector * vector
        norm += fold(square)
        level += fold(square * spread(energy_ref[s], width))
    scalar_ref[0:8, :] = norm
    scalar_ref[8:16, :] = level
    for copy in copies[5:]:
        copy.wait()
    entries.wait()


def product_kernel(is_first, split, paired, rep_count, sec_count, *refs):
    refs = list(refs)
    take = lambda count: [refs.pop(0) for _ in range(count)]
    list_ref, left_ref, right_ref = take(3)
    if is_first:
        start_ref, limit_ref, scalar_ref = take(3)
        psi_refs = take(rep_count - 1)
        level_refs = take(rep_count - 1)
    else:
        vector_refs = take(rep_count)
    out_refs = take(sec_count if split else 1)
    inner_ref, entry_ref, sem = refs
    terms, sec_dev, half, width = left_ref.shape
    pairs = terms * sec_dev
    cap = most_pairs(pairs, sec_count)
    rep = lax.axis_index("rep")
    sec = lax.axis_index("sec")
    fetch = pltpu.make_async_copy(list_ref, entry_ref, sem)
    fetch.start()
    inner_ref[pairs] = jnp.zeros((half, width), BF16)

    def first_row(step):
        return remainder(rep + step, rep_count) * half

    if is_first:
        folded = [scalar_ref[0:8, :], scalar_ref[8:16, :]]
        columns = [energy_columns(ref[...]) for ref in level_refs]
    for s in range(sec_dev):
        if is_first:
            blocks = [start_ref[s]]
            for step in range(1, rep_count):
                psi = psi_refs[step - 1][s]
                mask = live(limit_ref, s, first_row(step), (half, width))
                blocks.append(jnp.where(mask, psi.astype(F32), 0.0).astype(BF16))
        else:
            blocks = [ref[s * half:(s + 1) * half] for ref in vector_refs]
        vector = jnp.concatenate(blocks, axis=0)
        for turn in range(1, rep_count):
            turned = blocks[rep_count - turn:] + blocks[:rep_count - turn]
            vector = jnp.where(rep == turn, jnp.concatenate(turned, axis=0), vector)
        inner = jnp.dot(
            left_ref[:, s].reshape(terms * half, width), vector, preferred_element_type=F32
        ).astype(BF16)
        for t in range(terms):
            inner_ref[t * sec_dev + s] = inner[t * half:(t + 1) * half]
        if is_first:
            for step in range(1, rep_count):
                block = blocks[step].astype(F32)
                square = block * block
                energy = jnp.broadcast_to(columns[step - 1][:, s:s + 1], (half, width))
                folded = [folded[0] + fold(square), folded[1] + fold(square * energy)]
    if is_first:
        scalars = [total(array) for array in folded]
    else:
        head = sum(ref[sec_dev * half:].astype(F32) for ref in vector_refs)
        scalars = [head_scalar(head, i)[:, :LANES] for i in range(2)]
    fetch.wait()
    for d in range(sec_count):
        if not split:
            owner = d
        elif paired:
            owner = sec ^ d
        else:
            owner = remainder(sec + d, sec_count)
        packet = jnp.zeros((half, width), F32)
        for i in range(cap):
            pair = entry_ref[owner, i]
            term = jnp.minimum(quotient(pair, sec_dev), terms - 1)
            packet += jnp.dot(inner_ref[pair], right_ref[term], preferred_element_type=F32)
        out = out_refs[d] if split else out_refs[0].at[d]
        for column in range(width // LANES):
            out[column * half:(column + 1) * half, :] = packet[
                :, column * LANES:(column + 1) * LANES
            ].astype(BF16)
        out[width // LANES * half:, :] = header(entry_ref[owner, cap], scalars)


def sigma_packets(is_first, split, paired, rep_count, lists, left_env, right_env, more):
    terms, sec_dev, half, width = left_env.shape
    sec_count = lax.axis_size("sec")
    packet = (width // LANES * half + HEAD, LANES)
    if split:
        outs = [jax.ShapeDtypeStruct(packet, BF16)] * sec_count
    else:
        outs = [jax.ShapeDtypeStruct((sec_count,) + packet, BF16)]
    pair_flops = 2 * half * width * width * 2
    operands = [lists, left_env, right_env, *more]
    return pl.pallas_call(
        functools.partial(product_kernel, is_first, split, paired, rep_count, sec_count),
        out_shape=outs,
        in_specs=[whole(pltpu.VMEM)] * len(operands),
        out_specs=[whole(pltpu.VMEM)] * len(outs),
        scratch_shapes=[
            pltpu.VMEM((terms * sec_dev + 1, half, width), BF16),
            pltpu.SMEM(lists.shape, jnp.int32),
            pltpu.SemaphoreType.DMA,
        ],
        compiler_params=pltpu.CompilerParams(vmem_limit_bytes=VMEM_BYTES),
        cost_estimate=pl.CostEstimate(
            flops=terms * sec_dev * pair_flops,
            bytes_accessed=2 * (left_env.size + right_env.size),
            transcendentals=0,
        ),
        name="products_first" if is_first else "products_second",
    )(*operands)


def exchange(packets, split, paired, order, own_at):
    sec_count = lax.axis_size("sec")
    op_count = lax.axis_size("op")
    op_turns = [
        [(i, (i + step) % op_count) for i in range(op_count)] for step in range(1, op_count)
    ]
    over_op = lambda packet: [lax.ppermute(packet, "op", turn) for turn in op_turns]
    if not split:
        arrived = lax.all_to_all(packets[0], "sec", split_axis=0, concat_axis=0, tiled=True)
        return [arrived] + over_op(arrived), []
    arrived = {0: packets[0]}
    crossed = {}
    for position, step in enumerate(order):
        if position == own_at:
            crossed[0] = over_op(packets[0])
        reach = (lambda i: i ^ step) if paired else (lambda i: (i + step) % sec_count)
        turn = [(i, reach(i)) for i in range(sec_count)]
        arrived[step] = lax.ppermute(packets[step], "sec", turn)
    if own_at >= len(order):
        crossed[0] = over_op(packets[0])
    for step in order:
        crossed[step] = over_op(arrived[step])
    steps = [0, *order]
    gathered = [arrived[step] for step in steps] + sum([crossed[step] for step in steps], [])
    return gathered[:-1], gathered[-1:]


def add_packets(packet_refs, split, half, base_ref):
    sec_dev, _, width = base_ref.shape
    own = lax.axis_size("sec") if split else 1
    body_rows = width // LANES * half
    if split:
        heads = [ref[body_rows:].astype(F32) for ref in packet_refs]
        for column in range(width // LANES):
            lanes = slice(column * LANES, (column + 1) * LANES)
            for s in range(sec_dev):
                part = base_ref[s, :, lanes]
                for ref, head in zip(packet_refs, heads):
                    body = ref[column * half:(column + 1) * half].astype(F32)
                    part += jnp.where(head[0:1] == s, body, 0.0)
                base_ref[s, :, lanes] = part
        return sum(heads[1:own], heads[0])

    head_sum = jnp.zeros((HEAD, LANES), F32)
    for index, ref in enumerate(packet_refs):
        def add_one(p, carry):
            head = ref[p, body_rows:, :].astype(F32)
            for column in range(width // LANES):
                body = ref[p, column * half:(column + 1) * half, :].astype(F32)
                lanes = slice(column * LANES, (column + 1) * LANES)
                for s in range(sec_dev):
                    base_ref[s, :, lanes] += jnp.where(head[0:1] == s, body, 0.0)
            return carry + head
        result = lax.fori_loop(0, ref.shape[0], add_one, jnp.zeros((HEAD, LANES), F32))
        if index < own:
            head_sum = head_sum + result
    return head_sum


def late_sum(packet_refs, s, half, width):
    body_rows = width // LANES * half
    value = jnp.zeros((half, width), F32)
    for ref in packet_refs:
        body = jnp.concatenate(
            [ref[c * half:(c + 1) * half].astype(F32) for c in range(width // LANES)], axis=1
        )
        slot = spread(ref[body_rows:].astype(F32)[0:1], width)
        value += jnp.where(slot == s, body, 0.0)
    return value


def first_early_kernel(split, count, *refs):
    packet_refs = refs[:count]
    start_ref, energy_ref, base_ref, scalar_ref = refs[count:]
    sec_dev, half, width = start_ref.shape
    for s in range(sec_dev):
        base_ref[s] = spread(energy_ref[s], width) * start_ref[s].astype(F32)
    head_sum = add_packets(packet_refs, split, half, base_ref)
    norm = head_scalar(head_sum, 0)
    scalar_ref[0:1] = norm
    scalar_ref[1:2] = head_scalar(head_sum, 1) / norm


def first_kernel(count, *refs):
    packet_refs = refs[:count]
    limit_ref, start_ref, base_ref, scalar_ref, first_ref, one_ref, vec_ref = refs[count:]
    sec_dev, half, width = start_ref.shape
    shift = spread(scalar_ref[1:2], width)
    first_row = lax.axis_index("rep") * half
    cross = jnp.zeros((8, width), F32)
    square = jnp.zeros((8, width), F32)
    for s in range(sec_dev):
        mask = live(limit_ref, s, first_row, (half, width))
        start = start_ref[s].astype(F32)
        one = jnp.where(mask, base_ref[s] + late_sum(packet_refs, s, half, width), 0.0)
        one_ref[s] = one
        first_ref[s] = one.astype(BF16)
        vector = one - shift * start
        vec_ref[s * half:(s + 1) * half] = vector.astype(BF16)
        cross += fold(start * vector)
        square += fold(vector * vector)
    scalars = (total(cross), total(square))
    vec_ref[sec_dev * half:] = header(jnp.int32(0), scalars, (MORE_ROWS, width))


def second_early_kernel(split, count, entries, *refs):
    packet_refs = refs[:count]
    vec_ref, energy_ref, one_ref, scalar_ref, base_ref, scale_ref = refs[count:]
    sec_dev, half, width = one_ref.shape
    for s in range(sec_dev):
        vector = vec_ref[s * half:(s + 1) * half].astype(F32)
        base_ref[s] = spread(energy_ref[s], width) * vector
    head_sum = add_packets(packet_refs, split, half, base_ref)
    cross = head_scalar(head_sum, 0)
    square = head_scalar(head_sum, 1)
    excess = cross / scalar_ref[0:1]
    resid_sq = jnp.maximum(square - excess * cross, 0.0)
    scale = lax.rsqrt(resid_sq / entries + EPSILON)
    scale_ref[...] = jnp.broadcast_to(scale, scale_ref.shape)
    for s in range(sec_dev):
        base_ref[s] = base_ref[s] - spread(excess, width) * one_ref[s]


def second_kernel(count, *refs):
    packet_refs = refs[:count]
    limit_ref, base_ref, scale_ref, second_ref = refs[count:]
    sec_dev, half, width = base_ref.shape
    scale = spread(scale_ref[0:1], width)
    first_row = lax.axis_index("rep") * half
    for s in range(sec_dev):
        mask = live(limit_ref, s, first_row, (half, width))
        value = scale * (base_ref[s] + late_sum(packet_refs, s, half, width))
        second_ref[s] = jnp.where(mask, value, 0.0).astype(BF16)


def call(kernel, name, outs, *operands):
    return pl.pallas_call(
        kernel,
        out_shape=outs,
        in_specs=[whole(pltpu.VMEM)] * len(operands),
        out_specs=[whole(pltpu.VMEM)] * len(outs),
        compiler_params=pltpu.CompilerParams(vmem_limit_bytes=VMEM_BYTES),
        name=name,
    )(*operands)


def body(psi, left_env, right_env, pairing, block_rows, block_cols, energy):
    sec_count = lax.axis_size("sec")
    op_count = lax.axis_size("op")
    rep_count = lax.axis_size("rep")
    terms, sec_dev, half, width = left_env.shape
    entries = sec_count * sec_dev * rep_count * half * width
    split = sec_count * op_count <= 8
    can_pair = sec_count & (sec_count - 1) == 0
    steps = list(range(1, sec_count))
    first_plan = (False, steps, sec_count - 1)
    second_plan = (can_pair, steps[1:2] + steps[:1] + steps[2:], sec_count - 1)
    params = pltpu.CompilerParams(vmem_limit_bytes=VMEM_BYTES)
    vec_shape = (sec_dev, half, width)
    vec_bf16 = jax.ShapeDtypeStruct(vec_shape, BF16)

    def from_others(array):
        arrays = []
        for step in range(1, rep_count):
            turn = [((i + step) % rep_count, i) for i in range(rep_count)]
            arrays.append(lax.ppermute(array, "rep", turn))
        return arrays

    psi_others = from_others(psi)
    level_others = from_others(energy)
    start, left_env, lists, limits, levels, scalars = pl.pallas_call(
        load_kernel,
        out_shape=[
            vec_bf16,
            jax.ShapeDtypeStruct(left_env.shape, BF16),
            jax.ShapeDtypeStruct((sec_count, LANES), jnp.int32),
            jax.ShapeDtypeStruct((2 * sec_dev, LANES), jnp.int32),
            jax.ShapeDtypeStruct((sec_dev, half, LANES), F32),
            jax.ShapeDtypeStruct((16, width), F32),
        ],
        in_specs=[whole(pltpu.HBM)] * 6,
        out_specs=[whole(pltpu.VMEM)] * 6,
        scratch_shapes=[
            pltpu.VMEM(vec_shape, BF16),
            pltpu.VMEM((sec_dev, half), F32),
            pltpu.SMEM((sec_dev,), jnp.int32),
            pltpu.SMEM((sec_dev,), jnp.int32),
            pltpu.SMEM((sec_dev, terms), jnp.int32),
            pltpu.SMEM((sec_count, LANES), jnp.int32),
            pltpu.SMEM((sec_count,), jnp.int32),
            pltpu.SemaphoreType.DMA((6 + terms,)),
        ],
        compiler_params=params,
        name="load",
    )(*(
        pltpu.with_memory_space_constraint(array, pltpu.HBM)
        for array in (psi, left_env, pairing.T, block_rows, block_cols, energy)
    ))

    block_f32 = jax.ShapeDtypeStruct(vec_shape, F32)
    row_f32 = jax.ShapeDtypeStruct((8, LANES), F32)

    packets = sigma_packets(
        True, split, first_plan[0], rep_count, lists, left_env, right_env,
        [start, limits, scalars, *psi_others, *level_others],
    )
    early, late = exchange(packets, split, *first_plan)
    base, scalars = call(
        functools.partial(first_early_kernel, split, len(early)), "combine_first_early",
        [block_f32, row_f32], *early, start, levels,
    )
    first_out, sigma_one, vector = call(
        functools.partial(first_kernel, len(late)), "combine_first",
        [
            pltpu.VMEM(vec_shape, BF16),
            block_f32,
            jax.ShapeDtypeStruct((sec_dev * half + MORE_ROWS, width), BF16),
        ],
        *late, limits, start, base, scalars,
    )

    packets = sigma_packets(
        False, split, second_plan[0], rep_count, lists, left_env, right_env,
        [vector, *from_others(vector)],
    )
    early, late = exchange(packets, split, *second_plan)
    base, scale = call(
        functools.partial(second_early_kernel, split, len(early), entries),
        "combine_second_early", [block_f32, row_f32], *early, vector, levels, sigma_one, scalars,
    )
    (second_out,) = call(
        functools.partial(second_kernel, len(late)), "combine_second", [vec_bf16],
        *late, limits, base, scale,
    )
    return (first_out, second_out)


def solution(mesh):
    return jax.shard_map(
        body,
        mesh=mesh,
        in_specs=(
            P(("grp", "sec"), "rep", None),
            P(("grp", "op"), "sec", "rep", None),
            P(("grp", "op"), None, None),
            P(("grp", "op"), "sec"),
            P(("grp", "sec")),
            P(("grp", "sec")),
            P(("grp", "sec"), "rep"),
        ),
        out_specs=(P(("grp", "sec"), "rep", None), P(("grp", "sec"), "rep", None)),
        check_vma=False,
    )
```

```python
import functools

import jax
import jax.numpy as jnp
from jax import lax
from jax.experimental import pallas as pl
from jax.experimental.pallas import tpu as pltpu
from jax.sharding import PartitionSpec as P

EPSILON = 1e-06
HEAD = 8
PARTS = 3
MORE_ROWS = 16
LANES = 128
VMEM_BYTES = 24 * 1024 * 1024
F32 = jnp.float32
BF16 = jnp.bfloat16


def whole(space):
    return pl.BlockSpec(memory_space=space)


def live(limit_ref, s, first_row, shape):
    sec_dev = limit_ref.shape[0] // 2
    repeat = shape[1] // LANES
    rows = jnp.concatenate([limit_ref[s:s + 1, :]] * repeat, axis=1)
    cols = jnp.concatenate([limit_ref[sec_dev + s:sec_dev + s + 1, :]] * repeat, axis=1)
    row_ids = first_row + lax.broadcasted_iota(jnp.int32, shape, 0)
    col_ids = lax.broadcasted_iota(jnp.int32, shape, 1)
    return (row_ids < rows) & (col_ids < cols)


def energy_columns(level):
    missing = -level.shape[0] % 8
    if missing:
        level = jnp.concatenate([level, jnp.zeros((missing, level.shape[1]), F32)], axis=0)
    return level.T


def spread(array, width):
    return jnp.concatenate([array] * (width // LANES), axis=1)


def quotient(value, count):
    return value >> (count.bit_length() - 1) if count & (count - 1) == 0 else lax.div(value, count)


def remainder(value, count):
    return value & (count - 1) if count & (count - 1) == 0 else lax.rem(value, count)


def fold(array):
    rows, width = array.shape
    return jnp.sum(array.reshape(rows // 8, 8, width), axis=0)


def total(array):
    return jnp.sum(jnp.sum(array, axis=0, keepdims=True), axis=1, keepdims=True)


def header(slot, scalars, shape=(HEAD, LANES)):
    row_ids = lax.broadcasted_iota(jnp.int32, shape, 0)
    head = jnp.where(row_ids == 0, slot.astype(F32), 0.0)
    row = 1
    for scalar in scalars:
        rest = jnp.broadcast_to(scalar, shape)
        for _ in range(PARTS):
            piece = rest.astype(BF16).astype(F32)
            head = jnp.where(row_ids == row, piece, head)
            rest = rest - piece
            row += 1
    return head.astype(BF16)


def head_scalar(head_sum, index):
    first = 1 + PARTS * index
    return jnp.sum(head_sum[first:first + PARTS], axis=0, keepdims=True)


def most_pairs(pairs, sec_count):
    return pairs // sec_count + 1


def load_kernel(
    psi_hbm, left_hbm, pairing_hbm, rows_hbm, cols_hbm, energy_hbm,
    start_ref, left_ref, list_ref, limit_ref, energy_ref, scalar_ref,
    psi_ref, level_ref, rows_ref, cols_ref, pairing_ref, entry_ref, count_ref, sems,
):
    sec_dev, half, width = psi_ref.shape
    terms = left_ref.shape[0]
    sec_count = list_ref.shape[0]
    cap = most_pairs(terms * sec_dev, sec_count)
    pairs = [
        (rows_hbm, rows_ref), (cols_hbm, cols_ref), (energy_hbm, level_ref),
        (pairing_hbm, pairing_ref), (psi_hbm, psi_ref),
    ]
    for t in range(left_ref.shape[0]):
        pairs.append((left_hbm.at[t], left_ref.at[t]))
    copies = [
        pltpu.make_async_copy(source, target, sems.at[i])
        for i, (source, target) in enumerate(pairs)
    ]
    for copy in copies:
        copy.start()
    for owner in range(sec_count):
        count_ref[owner] = 0
        entry_ref[owner, cap] = 0
        for i in range(cap):
            entry_ref[owner, i] = terms * sec_dev
    for copy in copies[:3]:
        copy.wait()
    for s in range(sec_dev):
        limit_ref[s:s + 1, :] = jnp.full((1, LANES), rows_ref[s], jnp.int32)
        limit_ref[sec_dev + s:sec_dev + s + 1, :] = jnp.full((1, LANES), cols_ref[s], jnp.int32)
    columns = energy_columns(level_ref[...])
    for s in range(sec_dev):
        energy_ref[s] = jnp.broadcast_to(columns[:, s:s + 1], (half, LANES))
    copies[3].wait()
    for t in range(terms):
        for s in range(sec_dev):
            target = pairing_ref[s, t]
            owner = quotient(target, sec_dev)
            count = count_ref[owner]
            entry_ref[owner, count] = t * sec_dev + s
            entry_ref[owner, cap] = remainder(target, sec_dev)
            count_ref[owner] = count + 1
    entries = pltpu.make_async_copy(entry_ref, list_ref, sems.at[len(copies)])
    entries.start()
    copies[4].wait()
    first_row = lax.axis_index("rep") * half
    norm = jnp.zeros((8, width), F32)
    level = jnp.zeros((8, width), F32)
    for s in range(sec_dev):
        vector = jnp.where(
            live(limit_ref, s, first_row, (half, width)), psi_ref[s].astype(F32), 0.0
        )
        start_ref[s] = vector.astype(BF16)
        square = vector * vector
        norm += fold(square)
        level += fold(square * spread(energy_ref[s], width))
    scalar_ref[0:8, :] = norm
    scalar_ref[8:16, :] = level
    for copy in copies[5:]:
        copy.wait()
    entries.wait()


def product_kernel(is_first, split, paired, rep_count, sec_count, *refs):
    refs = list(refs)
    take = lambda count: [refs.pop(0) for _ in range(count)]
    list_ref, left_ref, right_ref = take(3)
    if is_first:
        start_ref, limit_ref, scalar_ref = take(3)
        psi_refs = take(rep_count - 1)
        level_refs = take(rep_count - 1)
    else:
        vector_refs = take(rep_count)
    out_refs = take(sec_count if split else 1)
    inner_ref, entry_ref, sem = refs
    terms, sec_dev, half, width = left_ref.shape
    pairs = terms * sec_dev
    cap = most_pairs(pairs, sec_count)
    rep = lax.axis_index("rep")
    sec = lax.axis_index("sec")
    fetch = pltpu.make_async_copy(list_ref, entry_ref, sem)
    fetch.start()
    inner_ref[pairs] = jnp.zeros((half, width), BF16)

    def first_row(step):
        return remainder(rep + step, rep_count) * half

    if is_first:
        folded = [scalar_ref[0:8, :], scalar_ref[8:16, :]]
        columns = [energy_columns(ref[...]) for ref in level_refs]
    for s in range(sec_dev):
        if is_first:
            blocks = [start_ref[s]]
            for step in range(1, rep_count):
                psi = psi_refs[step - 1][s]
                mask = live(limit_ref, s, first_row(step), (half, width))
                blocks.append(jnp.where(mask, psi.astype(F32), 0.0).astype(BF16))
        else:
            blocks = [ref[s * half:(s + 1) * half] for ref in vector_refs]
        vector = jnp.concatenate(blocks, axis=0)
        for turn in range(1, rep_count):
            turned = blocks[rep_count - turn:] + blocks[:rep_count - turn]
            vector = jnp.where(rep == turn, jnp.concatenate(turned, axis=0), vector)
        inner = jnp.dot(
            left_ref[:, s].reshape(terms * half, width), vector, preferred_element_type=F32
        ).astype(BF16)
        for t in range(terms):
            inner_ref[t * sec_dev + s] = inner[t * half:(t + 1) * half]
        if is_first:
            for step in range(1, rep_count):
                block = blocks[step].astype(F32)
                square = block * block
                energy = jnp.broadcast_to(columns[step - 1][:, s:s + 1], (half, width))
                folded = [folded[0] + fold(square), folded[1] + fold(square * energy)]
    if is_first:
        scalars = [total(array) for array in folded]
    else:
        head = sum(ref[sec_dev * half:].astype(F32) for ref in vector_refs)
        scalars = [head_scalar(head, i)[:, :LANES] for i in range(2)]
    for t in range(terms):
        block = pl.ds(t * sec_dev, sec_dev)
        outer = jnp.dot(
            inner_ref[block].reshape(sec_dev * half, width),
            right_ref[t],
            preferred_element_type=F32,
        )
        inner_ref[block] = outer.astype(BF16).reshape(sec_dev, half, width)
    fetch.wait()
    for d in range(sec_count):
        if not split:
            owner = d
        elif paired:
            owner = sec ^ d
        else:
            owner = remainder(sec + d, sec_count)
        packet = jnp.zeros((half, width), F32)
        for i in range(cap):
            packet += inner_ref[entry_ref[owner, i]].astype(F32)
        out = out_refs[d] if split else out_refs[0].at[d]
        for column in range(width // LANES):
            out[column * half:(column + 1) * half, :] = packet[
                :, column * LANES:(column + 1) * LANES
            ].astype(BF16)
        out[width // LANES * half:, :] = header(entry_ref[owner, cap], scalars)


def sigma_packets(is_first, split, paired, rep_count, lists, left_env, right_env, more):
    terms, sec_dev, half, width = left_env.shape
    sec_count = lax.axis_size("sec")
    packet = (width // LANES * half + HEAD, LANES)
    if split:
        outs = [jax.ShapeDtypeStruct(packet, BF16)] * sec_count
    else:
        outs = [jax.ShapeDtypeStruct((sec_count,) + packet, BF16)]
    pair_flops = 2 * half * width * width * 2
    operands = [lists, left_env, right_env, *more]
    return pl.pallas_call(
        functools.partial(product_kernel, is_first, split, paired, rep_count, sec_count),
        out_shape=outs,
        in_specs=[whole(pltpu.VMEM)] * len(operands),
        out_specs=[whole(pltpu.VMEM)] * len(outs),
        scratch_shapes=[
            pltpu.VMEM((terms * sec_dev + 1, half, width), BF16),
            pltpu.SMEM(lists.shape, jnp.int32),
            pltpu.SemaphoreType.DMA,
        ],
        compiler_params=pltpu.CompilerParams(vmem_limit_bytes=VMEM_BYTES),
        cost_estimate=pl.CostEstimate(
            flops=terms * sec_dev * pair_flops,
            bytes_accessed=2 * (left_env.size + right_env.size),
            transcendentals=0,
        ),
        name="products_first" if is_first else "products_second",
    )(*operands)


def exchange(packets, split, paired, order, own_at):
    sec_count = lax.axis_size("sec")
    op_count = lax.axis_size("op")
    op_turns = [
        [(i, (i + step) % op_count) for i in range(op_count)] for step in range(1, op_count)
    ]
    over_op = lambda packet: [lax.ppermute(packet, "op", turn) for turn in op_turns]
    if not split:
        arrived = lax.all_to_all(packets[0], "sec", split_axis=0, concat_axis=0, tiled=True)
        return [arrived] + over_op(arrived), []
    arrived = {0: packets[0]}
    crossed = {}
    for position, step in enumerate(order):
        if position == own_at:
            crossed[0] = over_op(packets[0])
        reach = (lambda i: i ^ step) if paired else (lambda i: (i + step) % sec_count)
        turn = [(i, reach(i)) for i in range(sec_count)]
        arrived[step] = lax.ppermute(packets[step], "sec", turn)
    if own_at >= len(order):
        crossed[0] = over_op(packets[0])
    for step in order:
        crossed[step] = over_op(arrived[step])
    steps = [0, *order]
    gathered = [arrived[step] for step in steps] + sum([crossed[step] for step in steps], [])
    return gathered[:-1], gathered[-1:]


def add_packets(packet_refs, split, half, base_ref):
    sec_dev, _, width = base_ref.shape
    own = lax.axis_size("sec") if split else 1
    body_rows = width // LANES * half
    if split:
        heads = [ref[body_rows:].astype(F32) for ref in packet_refs]
        for column in range(width // LANES):
            lanes = slice(column * LANES, (column + 1) * LANES)
            for s in range(sec_dev):
                part = base_ref[s, :, lanes]
                for ref, head in zip(packet_refs, heads):
                    body = ref[column * half:(column + 1) * half].astype(F32)
                    part += jnp.where(head[0:1] == s, body, 0.0)
                base_ref[s, :, lanes] = part
        return sum(heads[1:own], heads[0])

    head_sum = jnp.zeros((HEAD, LANES), F32)
    for index, ref in enumerate(packet_refs):
        def add_one(p, carry):
            head = ref[p, body_rows:, :].astype(F32)
            for column in range(width // LANES):
                body = ref[p, column * half:(column + 1) * half, :].astype(F32)
                lanes = slice(column * LANES, (column + 1) * LANES)
                for s in range(sec_dev):
                    base_ref[s, :, lanes] += jnp.where(head[0:1] == s, body, 0.0)
            return carry + head
        result = lax.fori_loop(0, ref.shape[0], add_one, jnp.zeros((HEAD, LANES), F32))
        if index < own:
            head_sum = head_sum + result
    return head_sum


def late_sum(packet_refs, s, half, width):
    body_rows = width // LANES * half
    value = jnp.zeros((half, width), F32)
    for ref in packet_refs:
        body = jnp.concatenate(
            [ref[c * half:(c + 1) * half].astype(F32) for c in range(width // LANES)], axis=1
        )
        slot = spread(ref[body_rows:].astype(F32)[0:1], width)
        value += jnp.where(slot == s, body, 0.0)
    return value


def first_early_kernel(split, count, *refs):
    packet_refs = refs[:count]
    start_ref, energy_ref, base_ref, scalar_ref = refs[count:]
    sec_dev, half, width = start_ref.shape
    for s in range(sec_dev):
        base_ref[s] = spread(energy_ref[s], width) * start_ref[s].astype(F32)
    head_sum = add_packets(packet_refs, split, half, base_ref)
    norm = head_scalar(head_sum, 0)
    scalar_ref[0:1] = norm
    scalar_ref[1:2] = head_scalar(head_sum, 1) / norm


def first_kernel(count, *refs):
    packet_refs = refs[:count]
    limit_ref, start_ref, base_ref, scalar_ref, first_ref, one_ref, vec_ref = refs[count:]
    sec_dev, half, width = start_ref.shape
    shift = spread(scalar_ref[1:2], width)
    first_row = lax.axis_index("rep") * half
    cross = jnp.zeros((8, width), F32)
    square = jnp.zeros((8, width), F32)
    for s in range(sec_dev):
        mask = live(limit_ref, s, first_row, (half, width))
        start = start_ref[s].astype(F32)
        one = jnp.where(mask, base_ref[s] + late_sum(packet_refs, s, half, width), 0.0)
        one_ref[s] = one
        first_ref[s] = one.astype(BF16)
        vector = one - shift * start
        vec_ref[s * half:(s + 1) * half] = vector.astype(BF16)
        cross += fold(start * vector)
        square += fold(vector * vector)
    scalars = (total(cross), total(square))
    vec_ref[sec_dev * half:] = header(jnp.int32(0), scalars, (MORE_ROWS, width))


def second_early_kernel(split, count, entries, *refs):
    packet_refs = refs[:count]
    vec_ref, energy_ref, one_ref, scalar_ref, base_ref, scale_ref = refs[count:]
    sec_dev, half, width = one_ref.shape
    for s in range(sec_dev):
        vector = vec_ref[s * half:(s + 1) * half].astype(F32)
        base_ref[s] = spread(energy_ref[s], width) * vector
    head_sum = add_packets(packet_refs, split, half, base_ref)
    cross = head_scalar(head_sum, 0)
    square = head_scalar(head_sum, 1)
    excess = cross / scalar_ref[0:1]
    resid_sq = jnp.maximum(square - excess * cross, 0.0)
    scale = lax.rsqrt(resid_sq / entries + EPSILON)
    scale_ref[...] = jnp.broadcast_to(scale, scale_ref.shape)
    for s in range(sec_dev):
        base_ref[s] = base_ref[s] - spread(excess, width) * one_ref[s]


def second_kernel(count, *refs):
    packet_refs = refs[:count]
    limit_ref, base_ref, scale_ref, second_ref = refs[count:]
    sec_dev, half, width = base_ref.shape
    scale = spread(scale_ref[0:1], width)
    first_row = lax.axis_index("rep") * half
    for s in range(sec_dev):
        mask = live(limit_ref, s, first_row, (half, width))
        value = scale * (base_ref[s] + late_sum(packet_refs, s, half, width))
        second_ref[s] = jnp.where(mask, value, 0.0).astype(BF16)


def call(kernel, name, outs, *operands):
    return pl.pallas_call(
        kernel,
        out_shape=outs,
        in_specs=[whole(pltpu.VMEM)] * len(operands),
        out_specs=[whole(pltpu.VMEM)] * len(outs),
        compiler_params=pltpu.CompilerParams(vmem_limit_bytes=VMEM_BYTES),
        name=name,
    )(*operands)


def body(psi, left_env, right_env, pairing, block_rows, block_cols, energy):
    sec_count = lax.axis_size("sec")
    op_count = lax.axis_size("op")
    rep_count = lax.axis_size("rep")
    terms, sec_dev, half, width = left_env.shape
    entries = sec_count * sec_dev * rep_count * half * width
    split = sec_count * op_count <= 8
    can_pair = sec_count & (sec_count - 1) == 0
    steps = list(range(1, sec_count))
    first_plan = (False, steps, sec_count - 1)
    second_plan = (can_pair, steps[1:2] + steps[:1] + steps[2:], sec_count - 1)
    params = pltpu.CompilerParams(vmem_limit_bytes=VMEM_BYTES)
    vec_shape = (sec_dev, half, width)
    vec_bf16 = jax.ShapeDtypeStruct(vec_shape, BF16)

    def from_others(array):
        arrays = []
        for step in range(1, rep_count):
            turn = [((i + step) % rep_count, i) for i in range(rep_count)]
            arrays.append(lax.ppermute(array, "rep", turn))
        return arrays

    psi_others = from_others(psi)
    level_others = from_others(energy)
    start, left_env, lists, limits, levels, scalars = pl.pallas_call(
        load_kernel,
        out_shape=[
            vec_bf16,
            jax.ShapeDtypeStruct(left_env.shape, BF16),
            jax.ShapeDtypeStruct((sec_count, LANES), jnp.int32),
            jax.ShapeDtypeStruct((2 * sec_dev, LANES), jnp.int32),
            jax.ShapeDtypeStruct((sec_dev, half, LANES), F32),
            jax.ShapeDtypeStruct((16, width), F32),
        ],
        in_specs=[whole(pltpu.HBM)] * 6,
        out_specs=[whole(pltpu.VMEM)] * 6,
        scratch_shapes=[
            pltpu.VMEM(vec_shape, BF16),
            pltpu.VMEM((sec_dev, half), F32),
            pltpu.SMEM((sec_dev,), jnp.int32),
            pltpu.SMEM((sec_dev,), jnp.int32),
            pltpu.SMEM((sec_dev, terms), jnp.int32),
            pltpu.SMEM((sec_count, LANES), jnp.int32),
            pltpu.SMEM((sec_count,), jnp.int32),
            pltpu.SemaphoreType.DMA((6 + terms,)),
        ],
        compiler_params=params,
        name="load",
    )(*(
        pltpu.with_memory_space_constraint(array, pltpu.HBM)
        for array in (psi, left_env, pairing.T, block_rows, block_cols, energy)
    ))

    block_f32 = jax.ShapeDtypeStruct(vec_shape, F32)
    row_f32 = jax.ShapeDtypeStruct((8, LANES), F32)

    packets = sigma_packets(
        True, split, first_plan[0], rep_count, lists, left_env, right_env,
        [start, limits, scalars, *psi_others, *level_others],
    )
    early, late = exchange(packets, split, *first_plan)
    base, scalars = call(
        functools.partial(first_early_kernel, split, len(early)), "combine_first_early",
        [block_f32, row_f32], *early, start, levels,
    )
    first_out, sigma_one, vector = call(
        functools.partial(first_kernel, len(late)), "combine_first",
        [
            pltpu.VMEM(vec_shape, BF16),
            block_f32,
            jax.ShapeDtypeStruct((sec_dev * half + MORE_ROWS, width), BF16),
        ],
        *late, limits, start, base, scalars,
    )

    packets = sigma_packets(
        False, split, second_plan[0], rep_count, lists, left_env, right_env,
        [vector, *from_others(vector)],
    )
    early, late = exchange(packets, split, *second_plan)
    base, scale = call(
        functools.partial(second_early_kernel, split, len(early), entries),
        "combine_second_early", [block_f32, row_f32], *early, vector, levels, sigma_one, scalars,
    )
    (second_out,) = call(
        functools.partial(second_kernel, len(late)), "combine_second", [vec_bf16],
        *late, limits, base, scale,
    )
    return (first_out, second_out)


def solution(mesh):
    return jax.shard_map(
        body,
        mesh=mesh,
        in_specs=(
            P(("grp", "sec"), "rep", None),
            P(("grp", "op"), "sec", "rep", None),
            P(("grp", "op"), None, None),
            P(("grp", "op"), "sec"),
            P(("grp", "sec")),
            P(("grp", "sec")),
            P(("grp", "sec"), "rep"),
        ),
        out_specs=(P(("grp", "sec"), "rep", None), P(("grp", "sec"), "rep", None)),
        check_vma=False,
    )
```

```python
import functools

import jax
import jax.numpy as jnp
from jax import lax
from jax.experimental import pallas as pl
from jax.experimental.pallas import tpu as pltpu
from jax.sharding import PartitionSpec as P

EPSILON = 1e-06
HEAD = 8
PARTS = 3
MORE_ROWS = 16
LANES = 128
VMEM_BYTES = 24 * 1024 * 1024
F32 = jnp.float32
BF16 = jnp.bfloat16


def whole(space):
    return pl.BlockSpec(memory_space=space)


def live(limit_ref, s, first_row, shape):
    sec_dev = limit_ref.shape[0] // 2
    repeat = shape[1] // LANES
    rows = jnp.concatenate([limit_ref[s:s + 1, :]] * repeat, axis=1)
    cols = jnp.concatenate([limit_ref[sec_dev + s:sec_dev + s + 1, :]] * repeat, axis=1)
    row_ids = first_row + lax.broadcasted_iota(jnp.int32, shape, 0)
    col_ids = lax.broadcasted_iota(jnp.int32, shape, 1)
    return (row_ids < rows) & (col_ids < cols)


def energy_columns(level):
    missing = -level.shape[0] % 8
    if missing:
        level = jnp.concatenate([level, jnp.zeros((missing, level.shape[1]), F32)], axis=0)
    return level.T


def spread(array, width):
    return jnp.concatenate([array] * (width // LANES), axis=1)


def quotient(value, count):
    return value >> (count.bit_length() - 1) if count & (count - 1) == 0 else lax.div(value, count)


def remainder(value, count):
    return value & (count - 1) if count & (count - 1) == 0 else lax.rem(value, count)


def fold(array):
    rows, width = array.shape
    return jnp.sum(array.reshape(rows // 8, 8, width), axis=0)


def total(array):
    return jnp.sum(jnp.sum(array, axis=0, keepdims=True), axis=1, keepdims=True)


def header(slot, scalars, shape=(HEAD, LANES)):
    row_ids = lax.broadcasted_iota(jnp.int32, shape, 0)
    head = jnp.where(row_ids == 0, slot.astype(F32), 0.0)
    row = 1
    for scalar in scalars:
        rest = jnp.broadcast_to(scalar, shape)
        for _ in range(PARTS):
            piece = rest.astype(BF16).astype(F32)
            head = jnp.where(row_ids == row, piece, head)
            rest = rest - piece
            row += 1
    return head.astype(BF16)


def head_scalar(head_sum, index):
    first = 1 + PARTS * index
    return jnp.sum(head_sum[first:first + PARTS], axis=0, keepdims=True)


def most_pairs(pairs, sec_count):
    return pairs // sec_count + 1


def load_kernel(
    psi_hbm, left_hbm, pairing_hbm, rows_hbm, cols_hbm, energy_hbm,
    start_ref, left_ref, list_ref, limit_ref, energy_ref, scalar_ref,
    psi_ref, level_ref, rows_ref, cols_ref, pairing_ref, entry_ref, count_ref, sems,
):
    sec_dev, half, width = psi_ref.shape
    terms = left_ref.shape[0]
    sec_count = list_ref.shape[0]
    cap = most_pairs(terms * sec_dev, sec_count)
    pairs = [
        (rows_hbm, rows_ref), (cols_hbm, cols_ref), (energy_hbm, level_ref),
        (pairing_hbm, pairing_ref), (psi_hbm, psi_ref),
    ]
    for t in range(left_ref.shape[0]):
        pairs.append((left_hbm.at[t], left_ref.at[t]))
    copies = [
        pltpu.make_async_copy(source, target, sems.at[i])
        for i, (source, target) in enumerate(pairs)
    ]
    for copy in copies:
        copy.start()
    for owner in range(sec_count):
        count_ref[owner] = 0
        entry_ref[owner, cap] = 0
        for i in range(cap):
            entry_ref[owner, i] = terms * sec_dev
    for copy in copies[:3]:
        copy.wait()
    for s in range(sec_dev):
        limit_ref[s:s + 1, :] = jnp.full((1, LANES), rows_ref[s], jnp.int32)
        limit_ref[sec_dev + s:sec_dev + s + 1, :] = jnp.full((1, LANES), cols_ref[s], jnp.int32)
    columns = energy_columns(level_ref[...])
    for s in range(sec_dev):
        energy_ref[s] = jnp.broadcast_to(columns[:, s:s + 1], (half, LANES))
    copies[3].wait()
    for t in range(terms):
        for s in range(sec_dev):
            target = pairing_ref[s, t]
            owner = quotient(target, sec_dev)
            count = count_ref[owner]
            entry_ref[owner, count] = t * sec_dev + s
            entry_ref[owner, cap] = remainder(target, sec_dev)
            count_ref[owner] = count + 1
    entries = pltpu.make_async_copy(entry_ref, list_ref, sems.at[len(copies)])
    entries.start()
    copies[4].wait()
    first_row = lax.axis_index("rep") * half
    norm = jnp.zeros((8, width), F32)
    level = jnp.zeros((8, width), F32)
    for s in range(sec_dev):
        vector = jnp.where(
            live(limit_ref, s, first_row, (half, width)), psi_ref[s].astype(F32), 0.0
        )
        start_ref[s] = vector.astype(BF16)
        square = vector * vector
        norm += fold(square)
        level += fold(square * spread(energy_ref[s], width))
    scalar_ref[0:8, :] = norm
    scalar_ref[8:16, :] = level
    for copy in copies[5:]:
        copy.wait()
    entries.wait()


def product_kernel(is_first, split, paired, rep_count, sec_count, *refs):
    refs = list(refs)
    take = lambda count: [refs.pop(0) for _ in range(count)]
    list_ref, left_ref, right_ref = take(3)
    if is_first:
        start_ref, limit_ref, scalar_ref = take(3)
        psi_refs = take(rep_count - 1)
        level_refs = take(rep_count - 1)
    else:
        vector_refs = take(rep_count)
    out_refs = take(sec_count if split else 1)
    inner_ref, entry_ref, sem = refs
    terms, sec_dev, half, width = left_ref.shape
    pairs = terms * sec_dev
    cap = most_pairs(pairs, sec_count)
    rep = lax.axis_index("rep")
    sec = lax.axis_index("sec")
    fetch = pltpu.make_async_copy(list_ref, entry_ref, sem)
    fetch.start()
    inner_ref[pairs] = jnp.zeros((half, width), BF16)

    def first_row(step):
        return remainder(rep + step, rep_count) * half

    if is_first:
        folded = [scalar_ref[0:8, :], scalar_ref[8:16, :]]
        columns = [energy_columns(ref[...]) for ref in level_refs]
    for s in range(sec_dev):
        if is_first:
            blocks = [start_ref[s]]
            for step in range(1, rep_count):
                psi = psi_refs[step - 1][s]
                mask = live(limit_ref, s, first_row(step), (half, width))
                blocks.append(jnp.where(mask, psi.astype(F32), 0.0).astype(BF16))
        else:
            blocks = [ref[s * half:(s + 1) * half] for ref in vector_refs]
        vector = jnp.concatenate(blocks, axis=0)
        for turn in range(1, rep_count):
            turned = blocks[rep_count - turn:] + blocks[:rep_count - turn]
            vector = jnp.where(rep == turn, jnp.concatenate(turned, axis=0), vector)
        inner = jnp.dot(
            left_ref[:, s].reshape(terms * half, width), vector, preferred_element_type=F32
        ).astype(BF16)
        for t in range(terms):
            inner_ref[t * sec_dev + s] = inner[t * half:(t + 1) * half]
        if is_first:
            for step in range(1, rep_count):
                block = blocks[step].astype(F32)
                square = block * block
                energy = jnp.broadcast_to(columns[step - 1][:, s:s + 1], (half, width))
                folded = [folded[0] + fold(square), folded[1] + fold(square * energy)]
    if is_first:
        scalars = [total(array) for array in folded]
    else:
        head = sum(ref[sec_dev * half:].astype(F32) for ref in vector_refs)
        scalars = [head_scalar(head, i)[:, :LANES] for i in range(2)]
    fetch.wait()
    for d in range(sec_count):
        if not split:
            owner = d
        elif paired:
            owner = sec ^ d
        else:
            owner = remainder(sec + d, sec_count)
        packet = jnp.zeros((half, width), F32)
        for i in range(cap):
            pair = entry_ref[owner, i]
            term = jnp.minimum(quotient(pair, sec_dev), terms - 1)
            packet += jnp.dot(inner_ref[pair], right_ref[term], preferred_element_type=F32)
        out = out_refs[d] if split else out_refs[0].at[d]
        for column in range(width // LANES):
            out[column * half:(column + 1) * half, :] = packet[
                :, column * LANES:(column + 1) * LANES
            ].astype(BF16)
        out[width // LANES * half:, :] = header(entry_ref[owner, cap], scalars)


def sigma_packets(is_first, split, paired, rep_count, lists, left_env, right_env, more):
    terms, sec_dev, half, width = left_env.shape
    sec_count = lax.axis_size("sec")
    packet = (width // LANES * half + HEAD, LANES)
    if split:
        outs = [jax.ShapeDtypeStruct(packet, BF16)] * sec_count
    else:
        outs = [jax.ShapeDtypeStruct((sec_count,) + packet, BF16)]
    pair_flops = 2 * half * width * width * 2
    operands = [lists, left_env, right_env, *more]
    return pl.pallas_call(
        functools.partial(product_kernel, is_first, split, paired, rep_count, sec_count),
        out_shape=outs,
        in_specs=[whole(pltpu.VMEM)] * len(operands),
        out_specs=[whole(pltpu.VMEM)] * len(outs),
        scratch_shapes=[
            pltpu.VMEM((terms * sec_dev + 1, half, width), BF16),
            pltpu.SMEM(lists.shape, jnp.int32),
            pltpu.SemaphoreType.DMA,
        ],
        compiler_params=pltpu.CompilerParams(vmem_limit_bytes=VMEM_BYTES),
        cost_estimate=pl.CostEstimate(
            flops=terms * sec_dev * pair_flops,
            bytes_accessed=2 * (left_env.size + right_env.size),
            transcendentals=0,
        ),
        name="products_first" if is_first else "products_second",
    )(*operands)


def exchange(packets, split, paired, order, own_at):
    sec_count = lax.axis_size("sec")
    op_count = lax.axis_size("op")
    op_turns = [
        [(i, (i + step) % op_count) for i in range(op_count)] for step in range(1, op_count)
    ]
    over_op = lambda packet: [lax.ppermute(packet, "op", turn) for turn in op_turns]
    if not split:
        arrived = lax.all_to_all(packets[0], "sec", split_axis=0, concat_axis=0, tiled=True)
        return [arrived] + over_op(arrived), []
    arrived = {0: packets[0]}
    crossed = {}
    for position, step in enumerate(order):
        if position == own_at:
            crossed[0] = over_op(packets[0])
        reach = (lambda i: i ^ step) if paired else (lambda i: (i + step) % sec_count)
        turn = [(i, reach(i)) for i in range(sec_count)]
        arrived[step] = lax.ppermute(packets[step], "sec", turn)
    if own_at >= len(order):
        crossed[0] = over_op(packets[0])
    for step in order:
        crossed[step] = over_op(arrived[step])
    steps = [0, *order]
    gathered = [arrived[step] for step in steps] + sum([crossed[step] for step in steps], [])
    return gathered[:-1], gathered[-1:]


def add_packets(packet_refs, split, half, base_ref):
    sec_dev, _, width = base_ref.shape
    own = lax.axis_size("sec") if split else 1
    body_rows = width // LANES * half
    if split:
        heads = [ref[body_rows:].astype(F32) for ref in packet_refs]
        for column in range(width // LANES):
            lanes = slice(column * LANES, (column + 1) * LANES)
            for s in range(sec_dev):
                part = base_ref[s, :, lanes]
                for ref, head in zip(packet_refs, heads):
                    body = ref[column * half:(column + 1) * half].astype(F32)
                    part += jnp.where(head[0:1] == s, body, 0.0)
                base_ref[s, :, lanes] = part
        return sum(heads[1:own], heads[0])

    head_sum = jnp.zeros((HEAD, LANES), F32)
    for index, ref in enumerate(packet_refs):
        def add_one(p, carry):
            head = ref[p, body_rows:, :].astype(F32)
            for column in range(width // LANES):
                body = ref[p, column * half:(column + 1) * half, :].astype(F32)
                lanes = slice(column * LANES, (column + 1) * LANES)
                for s in range(sec_dev):
                    base_ref[s, :, lanes] += jnp.where(head[0:1] == s, body, 0.0)
            return carry + head
        result = lax.fori_loop(0, ref.shape[0], add_one, jnp.zeros((HEAD, LANES), F32))
        if index < own:
            head_sum = head_sum + result
    return head_sum


def late_sum(packet_refs, s, half, width):
    body_rows = width // LANES * half
    value = jnp.zeros((half, width), F32)
    for ref in packet_refs:
        body = jnp.concatenate(
            [ref[c * half:(c + 1) * half].astype(F32) for c in range(width // LANES)], axis=1
        )
        slot = spread(ref[body_rows:].astype(F32)[0:1], width)
        value += jnp.where(slot == s, body, 0.0)
    return value


def first_early_kernel(split, count, *refs):
    packet_refs = refs[:count]
    start_ref, energy_ref, base_ref, scalar_ref = refs[count:]
    sec_dev, half, width = start_ref.shape
    for s in range(sec_dev):
        base_ref[s] = spread(energy_ref[s], width) * start_ref[s].astype(F32)
    head_sum = add_packets(packet_refs, split, half, base_ref)
    norm = head_scalar(head_sum, 0)
    scalar_ref[0:1] = norm
    scalar_ref[1:2] = head_scalar(head_sum, 1) / norm


def first_kernel(count, *refs):
    packet_refs = refs[:count]
    limit_ref, start_ref, base_ref, scalar_ref, first_ref, one_ref, vec_ref = refs[count:]
    sec_dev, half, width = start_ref.shape
    shift = spread(scalar_ref[1:2], width)
    first_row = lax.axis_index("rep") * half
    cross = jnp.zeros((8, width), F32)
    square = jnp.zeros((8, width), F32)
    for s in range(sec_dev):
        mask = live(limit_ref, s, first_row, (half, width))
        start = start_ref[s].astype(F32)
        one = jnp.where(mask, base_ref[s] + late_sum(packet_refs, s, half, width), 0.0)
        one_ref[s] = one
        first_ref[s] = one.astype(BF16)
        vector = one - shift * start
        vec_ref[s * half:(s + 1) * half] = vector.astype(BF16)
        cross += fold(start * vector)
        square += fold(vector * vector)
    scalars = (total(cross), total(square))
    vec_ref[sec_dev * half:] = header(jnp.int32(0), scalars, (MORE_ROWS, width))


def second_early_kernel(split, count, entries, *refs):
    packet_refs = refs[:count]
    vec_ref, energy_ref, one_ref, scalar_ref, base_ref, scale_ref = refs[count:]
    sec_dev, half, width = one_ref.shape
    for s in range(sec_dev):
        vector = vec_ref[s * half:(s + 1) * half].astype(F32)
        base_ref[s] = spread(energy_ref[s], width) * vector
    head_sum = add_packets(packet_refs, split, half, base_ref)
    cross = head_scalar(head_sum, 0)
    square = head_scalar(head_sum, 1)
    excess = cross / scalar_ref[0:1]
    resid_sq = jnp.maximum(square - excess * cross, 0.0)
    scale = lax.rsqrt(resid_sq / entries + EPSILON)
    scale_ref[...] = jnp.broadcast_to(scale, scale_ref.shape)
    for s in range(sec_dev):
        base_ref[s] = base_ref[s] - spread(excess, width) * one_ref[s]


def second_kernel(count, *refs):
    packet_refs = refs[:count]
    limit_ref, base_ref, scale_ref, second_ref = refs[count:]
    sec_dev, half, width = base_ref.shape
    scale = spread(scale_ref[0:1], width)
    first_row = lax.axis_index("rep") * half
    for s in range(sec_dev):
        mask = live(limit_ref, s, first_row, (half, width))
        value = scale * (base_ref[s] + late_sum(packet_refs, s, half, width))
        second_ref[s] = jnp.where(mask, value, 0.0).astype(BF16)


def call(kernel, name, outs, *operands):
    return pl.pallas_call(
        kernel,
        out_shape=outs,
        in_specs=[whole(pltpu.VMEM)] * len(operands),
        out_specs=[whole(pltpu.VMEM)] * len(outs),
        compiler_params=pltpu.CompilerParams(vmem_limit_bytes=VMEM_BYTES),
        name=name,
    )(*operands)


def body(psi, left_env, right_env, pairing, block_rows, block_cols, energy):
    sec_count = lax.axis_size("sec")
    op_count = lax.axis_size("op")
    rep_count = lax.axis_size("rep")
    terms, sec_dev, half, width = left_env.shape
    entries = sec_count * sec_dev * rep_count * half * width
    split = sec_count * op_count <= 8
    can_pair = sec_count & (sec_count - 1) == 0
    steps = list(range(1, sec_count))
    first_plan = (can_pair, steps[1:2] + steps[:1] + steps[2:], sec_count - 1)
    second_plan = (can_pair, steps[1:2] + steps[:1] + steps[2:], sec_count - 1)
    params = pltpu.CompilerParams(vmem_limit_bytes=VMEM_BYTES)
    vec_shape = (sec_dev, half, width)
    vec_bf16 = jax.ShapeDtypeStruct(vec_shape, BF16)

    def from_others(array):
        arrays = []
        for step in range(1, rep_count):
            turn = [((i + step) % rep_count, i) for i in range(rep_count)]
            arrays.append(lax.ppermute(array, "rep", turn))
        return arrays

    psi_others = from_others(psi)
    level_others = from_others(energy)
    start, left_env, lists, limits, levels, scalars = pl.pallas_call(
        load_kernel,
        out_shape=[
            vec_bf16,
            jax.ShapeDtypeStruct(left_env.shape, BF16),
            jax.ShapeDtypeStruct((sec_count, LANES), jnp.int32),
            jax.ShapeDtypeStruct((2 * sec_dev, LANES), jnp.int32),
            jax.ShapeDtypeStruct((sec_dev, half, LANES), F32),
            jax.ShapeDtypeStruct((16, width), F32),
        ],
        in_specs=[whole(pltpu.HBM)] * 6,
        out_specs=[whole(pltpu.VMEM)] * 6,
        scratch_shapes=[
            pltpu.VMEM(vec_shape, BF16),
            pltpu.VMEM((sec_dev, half), F32),
            pltpu.SMEM((sec_dev,), jnp.int32),
            pltpu.SMEM((sec_dev,), jnp.int32),
            pltpu.SMEM((sec_dev, terms), jnp.int32),
            pltpu.SMEM((sec_count, LANES), jnp.int32),
            pltpu.SMEM((sec_count,), jnp.int32),
            pltpu.SemaphoreType.DMA((6 + terms,)),
        ],
        compiler_params=params,
        name="load",
    )(*(
        pltpu.with_memory_space_constraint(array, pltpu.HBM)
        for array in (psi, left_env, pairing.T, block_rows, block_cols, energy)
    ))

    block_f32 = jax.ShapeDtypeStruct(vec_shape, F32)
    row_f32 = jax.ShapeDtypeStruct((8, LANES), F32)

    packets = sigma_packets(
        True, split, first_plan[0], rep_count, lists, left_env, right_env,
        [start, limits, scalars, *psi_others, *level_others],
    )
    early, late = exchange(packets, split, *first_plan)
    base, scalars = call(
        functools.partial(first_early_kernel, split, len(early)), "combine_first_early",
        [block_f32, row_f32], *early, start, levels,
    )
    first_out, sigma_one, vector = call(
        functools.partial(first_kernel, len(late)), "combine_first",
        [
            pltpu.VMEM(vec_shape, BF16),
            block_f32,
            jax.ShapeDtypeStruct((sec_dev * half + MORE_ROWS, width), BF16),
        ],
        *late, limits, start, base, scalars,
    )

    packets = sigma_packets(
        False, split, second_plan[0], rep_count, lists, left_env, right_env,
        [vector, *from_others(vector)],
    )
    early, late = exchange(packets, split, *second_plan)
    base, scale = call(
        functools.partial(second_early_kernel, split, len(early), entries),
        "combine_second_early", [block_f32, row_f32], *early, vector, levels, sigma_one, scalars,
    )
    (second_out,) = call(
        functools.partial(second_kernel, len(late)), "combine_second", [vec_bf16],
        *late, limits, base, scale,
    )
    return (first_out, second_out)


def solution(mesh):
    return jax.shard_map(
        body,
        mesh=mesh,
        in_specs=(
            P(("grp", "sec"), "rep", None),
            P(("grp", "op"), "sec", "rep", None),
            P(("grp", "op"), None, None),
            P(("grp", "op"), "sec"),
            P(("grp", "sec")),
            P(("grp", "sec")),
            P(("grp", "sec"), "rep"),
        ),
        out_specs=(P(("grp", "sec"), "rep", None), P(("grp", "sec"), "rep", None)),
        check_vma=False,
    )
```

```python
import functools

import jax
import jax.numpy as jnp
from jax import lax
from jax.experimental import pallas as pl
from jax.experimental.pallas import tpu as pltpu
from jax.sharding import PartitionSpec as P

EPSILON = 1e-06
HEAD = 8
PARTS = 3
MORE_ROWS = 16
LANES = 128
VMEM_BYTES = 24 * 1024 * 1024
F32 = jnp.float32
BF16 = jnp.bfloat16


def whole(space):
    return pl.BlockSpec(memory_space=space)


def live(limit_ref, s, first_row, shape):
    sec_dev = limit_ref.shape[0] // 2
    repeat = shape[1] // LANES
    rows = jnp.concatenate([limit_ref[s:s + 1, :]] * repeat, axis=1)
    cols = jnp.concatenate([limit_ref[sec_dev + s:sec_dev + s + 1, :]] * repeat, axis=1)
    row_ids = first_row + lax.broadcasted_iota(jnp.int32, shape, 0)
    col_ids = lax.broadcasted_iota(jnp.int32, shape, 1)
    return (row_ids < rows) & (col_ids < cols)


def energy_columns(level):
    missing = -level.shape[0] % 8
    if missing:
        level = jnp.concatenate([level, jnp.zeros((missing, level.shape[1]), F32)], axis=0)
    return level.T


def spread(array, width):
    return jnp.concatenate([array] * (width // LANES), axis=1)


def quotient(value, count):
    return value >> (count.bit_length() - 1) if count & (count - 1) == 0 else lax.div(value, count)


def remainder(value, count):
    return value & (count - 1) if count & (count - 1) == 0 else lax.rem(value, count)


def fold(array):
    rows, width = array.shape
    return jnp.sum(array.reshape(rows // 8, 8, width), axis=0)


def total(array):
    return jnp.sum(jnp.sum(array, axis=0, keepdims=True), axis=1, keepdims=True)


def header(slot, scalars, shape=(HEAD, LANES)):
    row_ids = lax.broadcasted_iota(jnp.int32, shape, 0)
    head = jnp.where(row_ids == 0, slot.astype(F32), 0.0)
    row = 1
    for scalar in scalars:
        rest = jnp.broadcast_to(scalar, shape)
        for _ in range(PARTS):
            piece = rest.astype(BF16).astype(F32)
            head = jnp.where(row_ids == row, piece, head)
            rest = rest - piece
            row += 1
    return head.astype(BF16)


def head_scalar(head_sum, index):
    first = 1 + PARTS * index
    return jnp.sum(head_sum[first:first + PARTS], axis=0, keepdims=True)


def most_pairs(pairs, sec_count):
    return pairs // sec_count + 1


def load_kernel(
    psi_hbm, left_hbm, pairing_hbm, rows_hbm, cols_hbm, energy_hbm,
    start_ref, left_ref, list_ref, limit_ref, energy_ref, scalar_ref,
    psi_ref, level_ref, rows_ref, cols_ref, pairing_ref, entry_ref, count_ref, sems,
):
    sec_dev, half, width = psi_ref.shape
    terms = left_ref.shape[0]
    sec_count = list_ref.shape[0]
    cap = most_pairs(terms * sec_dev, sec_count)
    pairs = [
        (rows_hbm, rows_ref), (cols_hbm, cols_ref), (energy_hbm, level_ref),
        (pairing_hbm, pairing_ref), (psi_hbm, psi_ref),
    ]
    for t in range(left_ref.shape[0]):
        pairs.append((left_hbm.at[t], left_ref.at[t]))
    copies = [
        pltpu.make_async_copy(source, target, sems.at[i])
        for i, (source, target) in enumerate(pairs)
    ]
    for copy in copies:
        copy.start()
    for owner in range(sec_count):
        count_ref[owner] = 0
        entry_ref[owner, cap] = 0
        for i in range(cap):
            entry_ref[owner, i] = terms * sec_dev
    for copy in copies[:3]:
        copy.wait()
    for s in range(sec_dev):
        limit_ref[s:s + 1, :] = jnp.full((1, LANES), rows_ref[s], jnp.int32)
        limit_ref[sec_dev + s:sec_dev + s + 1, :] = jnp.full((1, LANES), cols_ref[s], jnp.int32)
    columns = energy_columns(level_ref[...])
    for s in range(sec_dev):
        energy_ref[s] = jnp.broadcast_to(columns[:, s:s + 1], (half, LANES))
    copies[3].wait()
    for t in range(terms):
        for s in range(sec_dev):
            target = pairing_ref[s, t]
            owner = quotient(target, sec_dev)
            count = count_ref[owner]
            entry_ref[owner, count] = t * sec_dev + s
            entry_ref[owner, cap] = remainder(target, sec_dev)
            count_ref[owner] = count + 1
    entries = pltpu.make_async_copy(entry_ref, list_ref, sems.at[len(copies)])
    entries.start()
    copies[4].wait()
    first_row = lax.axis_index("rep") * half
    norm = jnp.zeros((8, width), F32)
    level = jnp.zeros((8, width), F32)
    for s in range(sec_dev):
        vector = jnp.where(
            live(limit_ref, s, first_row, (half, width)), psi_ref[s].astype(F32), 0.0
        )
        start_ref[s] = vector.astype(BF16)
        square = vector * vector
        norm += fold(square)
        level += fold(square * spread(energy_ref[s], width))
    scalar_ref[0:8, :] = norm
    scalar_ref[8:16, :] = level
    for copy in copies[5:]:
        copy.wait()
    entries.wait()


def product_kernel(is_first, split, paired, rep_count, sec_count, *refs):
    refs = list(refs)
    take = lambda count: [refs.pop(0) for _ in range(count)]
    list_ref, left_ref, right_ref = take(3)
    if is_first:
        start_ref, limit_ref, scalar_ref = take(3)
        psi_refs = take(rep_count - 1)
        level_refs = take(rep_count - 1)
    else:
        vector_refs = take(rep_count)
    out_refs = take(sec_count if split else 1)
    inner_ref, entry_ref, sem = refs
    terms, sec_dev, half, width = left_ref.shape
    pairs = terms * sec_dev
    cap = most_pairs(pairs, sec_count)
    rep = lax.axis_index("rep")
    sec = lax.axis_index("sec")
    fetch = pltpu.make_async_copy(list_ref, entry_ref, sem)
    fetch.start()
    inner_ref[pairs] = jnp.zeros((half, width), BF16)

    def first_row(step):
        return remainder(rep + step, rep_count) * half

    if is_first:
        folded = [scalar_ref[0:8, :], scalar_ref[8:16, :]]
        columns = [energy_columns(ref[...]) for ref in level_refs]
    for s in range(sec_dev):
        if is_first:
            blocks = [start_ref[s]]
            for step in range(1, rep_count):
                psi = psi_refs[step - 1][s]
                mask = live(limit_ref, s, first_row(step), (half, width))
                blocks.append(jnp.where(mask, psi.astype(F32), 0.0).astype(BF16))
        else:
            blocks = [ref[s * half:(s + 1) * half] for ref in vector_refs]
        vector = jnp.concatenate(blocks, axis=0)
        for turn in range(1, rep_count):
            turned = blocks[rep_count - turn:] + blocks[:rep_count - turn]
            vector = jnp.where(rep == turn, jnp.concatenate(turned, axis=0), vector)
        inner = jnp.dot(
            left_ref[:, s].reshape(terms * half, width), vector, preferred_element_type=F32
        ).astype(BF16)
        for t in range(terms):
            inner_ref[t * sec_dev + s] = inner[t * half:(t + 1) * half]
        if is_first:
            for step in range(1, rep_count):
                block = blocks[step].astype(F32)
                square = block * block
                energy = jnp.broadcast_to(columns[step - 1][:, s:s + 1], (half, width))
                folded = [folded[0] + fold(square), folded[1] + fold(square * energy)]
    if is_first:
        scalars = [total(array) for array in folded]
    else:
        head = sum(ref[sec_dev * half:].astype(F32) for ref in vector_refs)
        scalars = [head_scalar(head, i)[:, :LANES] for i in range(2)]
    fetch.wait()
    for d in range(sec_count):
        if not split:
            owner = d
        elif paired:
            owner = sec ^ d
        else:
            owner = remainder(sec + d, sec_count)
        packet = jnp.zeros((half, width), F32)
        for i in range(cap):
            pair = entry_ref[owner, i]
            term = jnp.minimum(quotient(pair, sec_dev), terms - 1)
            packet += jnp.dot(inner_ref[pair], right_ref[term], preferred_element_type=F32)
        out = out_refs[d] if split else out_refs[0].at[d]
        for column in range(width // LANES):
            out[column * half:(column + 1) * half, :] = packet[
                :, column * LANES:(column + 1) * LANES
            ].astype(BF16)
        out[width // LANES * half:, :] = header(entry_ref[owner, cap], scalars)


def sigma_packets(is_first, split, paired, rep_count, lists, left_env, right_env, more):
    terms, sec_dev, half, width = left_env.shape
    sec_count = lax.axis_size("sec")
    packet = (width // LANES * half + HEAD, LANES)
    if split:
        outs = [jax.ShapeDtypeStruct(packet, BF16)] * sec_count
    else:
        outs = [jax.ShapeDtypeStruct((sec_count,) + packet, BF16)]
    pair_flops = 2 * half * width * width * 2
    operands = [lists, left_env, right_env, *more]
    return pl.pallas_call(
        functools.partial(product_kernel, is_first, split, paired, rep_count, sec_count),
        out_shape=outs,
        in_specs=[whole(pltpu.VMEM)] * len(operands),
        out_specs=[whole(pltpu.VMEM)] * len(outs),
        scratch_shapes=[
            pltpu.VMEM((terms * sec_dev + 1, half, width), BF16),
            pltpu.SMEM(lists.shape, jnp.int32),
            pltpu.SemaphoreType.DMA,
        ],
        compiler_params=pltpu.CompilerParams(vmem_limit_bytes=VMEM_BYTES),
        cost_estimate=pl.CostEstimate(
            flops=terms * sec_dev * pair_flops,
            bytes_accessed=2 * (left_env.size + right_env.size),
            transcendentals=0,
        ),
        name="products_first" if is_first else "products_second",
    )(*operands)


def exchange(packets, split, paired, order, together):
    sec_count = lax.axis_size("sec")
    op_count = lax.axis_size("op")
    op_turns = [
        [(i, (i + step) % op_count) for i in range(op_count)] for step in range(1, op_count)
    ]
    over_op = lambda packet: [lax.ppermute(packet, "op", turn) for turn in op_turns]
    if not split:
        arrived = lax.all_to_all(packets[0], "sec", split_axis=0, concat_axis=0, tiled=True)
        return [arrived] + over_op(arrived), []
    arrived = {0: packets[0]}
    for step in order:
        reach = (lambda i: i ^ step) if paired else (lambda i: (i + step) % sec_count)
        turn = [(i, reach(i)) for i in range(sec_count)]
        arrived[step] = lax.ppermute(packets[step], "sec", turn)
    steps = [0, *order]
    alone = steps[:len(steps) - together]
    crossed = sum([over_op(arrived[step]) for step in alone], [])
    waiting = [arrived[step] for step in steps[len(alone):]]
    if together > 1:
        waiting = lax.optimization_barrier((waiting, crossed))[0]
    last = jnp.stack(waiting)
    return [arrived[step] for step in steps] + crossed, over_op(last)


def add_packets(packet_refs, split, half, base_ref):
    sec_dev, _, width = base_ref.shape
    own = lax.axis_size("sec") if split else 1
    body_rows = width // LANES * half
    if split:
        heads = [ref[body_rows:].astype(F32) for ref in packet_refs]
        for column in range(width // LANES):
            lanes = slice(column * LANES, (column + 1) * LANES)
            for s in range(sec_dev):
                part = base_ref[s, :, lanes]
                for ref, head in zip(packet_refs, heads):
                    body = ref[column * half:(column + 1) * half].astype(F32)
                    part += jnp.where(head[0:1] == s, body, 0.0)
                base_ref[s, :, lanes] = part
        return sum(heads[1:own], heads[0])

    head_sum = jnp.zeros((HEAD, LANES), F32)
    for index, ref in enumerate(packet_refs):
        def add_one(p, carry):
            head = ref[p, body_rows:, :].astype(F32)
            for column in range(width // LANES):
                body = ref[p, column * half:(column + 1) * half, :].astype(F32)
                lanes = slice(column * LANES, (column + 1) * LANES)
                for s in range(sec_dev):
                    base_ref[s, :, lanes] += jnp.where(head[0:1] == s, body, 0.0)
            return carry + head
        result = lax.fori_loop(0, ref.shape[0], add_one, jnp.zeros((HEAD, LANES), F32))
        if index < own:
            head_sum = head_sum + result
    return head_sum


def late_sum(packet_refs, s, half, width):
    body_rows = width // LANES * half
    value = jnp.zeros((half, width), F32)
    for ref in packet_refs:
        for i in range(ref.shape[0]):
            body = jnp.concatenate(
                [ref[i, c * half:(c + 1) * half].astype(F32) for c in range(width // LANES)],
                axis=1,
            )
            slot = spread(ref[i, body_rows:].astype(F32)[0:1], width)
            value += jnp.where(slot == s, body, 0.0)
    return value


def first_early_kernel(split, count, *refs):
    packet_refs = refs[:count]
    start_ref, energy_ref, base_ref, scalar_ref = refs[count:]
    sec_dev, half, width = start_ref.shape
    for s in range(sec_dev):
        base_ref[s] = spread(energy_ref[s], width) * start_ref[s].astype(F32)
    head_sum = add_packets(packet_refs, split, half, base_ref)
    norm = head_scalar(head_sum, 0)
    scalar_ref[0:1] = norm
    scalar_ref[1:2] = head_scalar(head_sum, 1) / norm


def first_kernel(count, *refs):
    packet_refs = refs[:count]
    limit_ref, start_ref, base_ref, scalar_ref, first_ref, one_ref, vec_ref = refs[count:]
    sec_dev, half, width = start_ref.shape
    shift = spread(scalar_ref[1:2], width)
    first_row = lax.axis_index("rep") * half
    cross = jnp.zeros((8, width), F32)
    square = jnp.zeros((8, width), F32)
    for s in range(sec_dev):
        mask = live(limit_ref, s, first_row, (half, width))
        start = start_ref[s].astype(F32)
        one = jnp.where(mask, base_ref[s] + late_sum(packet_refs, s, half, width), 0.0)
        one_ref[s] = one
        first_ref[s] = one.astype(BF16)
        vector = one - shift * start
        vec_ref[s * half:(s + 1) * half] = vector.astype(BF16)
        cross += fold(start * vector)
        square += fold(vector * vector)
    scalars = (total(cross), total(square))
    vec_ref[sec_dev * half:] = header(jnp.int32(0), scalars, (MORE_ROWS, width))


def second_early_kernel(split, count, entries, *refs):
    packet_refs = refs[:count]
    vec_ref, energy_ref, one_ref, scalar_ref, base_ref, scale_ref = refs[count:]
    sec_dev, half, width = one_ref.shape
    for s in range(sec_dev):
        vector = vec_ref[s * half:(s + 1) * half].astype(F32)
        base_ref[s] = spread(energy_ref[s], width) * vector
    head_sum = add_packets(packet_refs, split, half, base_ref)
    cross = head_scalar(head_sum, 0)
    square = head_scalar(head_sum, 1)
    excess = cross / scalar_ref[0:1]
    resid_sq = jnp.maximum(square - excess * cross, 0.0)
    scale = lax.rsqrt(resid_sq / entries + EPSILON)
    scale_ref[...] = jnp.broadcast_to(scale, scale_ref.shape)
    for s in range(sec_dev):
        base_ref[s] = base_ref[s] - spread(excess, width) * one_ref[s]


def second_kernel(count, *refs):
    packet_refs = refs[:count]
    limit_ref, base_ref, scale_ref, second_ref = refs[count:]
    sec_dev, half, width = base_ref.shape
    scale = spread(scale_ref[0:1], width)
    first_row = lax.axis_index("rep") * half
    for s in range(sec_dev):
        mask = live(limit_ref, s, first_row, (half, width))
        value = scale * (base_ref[s] + late_sum(packet_refs, s, half, width))
        second_ref[s] = jnp.where(mask, value, 0.0).astype(BF16)


def call(kernel, name, outs, *operands):
    return pl.pallas_call(
        kernel,
        out_shape=outs,
        in_specs=[whole(pltpu.VMEM)] * len(operands),
        out_specs=[whole(pltpu.VMEM)] * len(outs),
        compiler_params=pltpu.CompilerParams(vmem_limit_bytes=VMEM_BYTES),
        name=name,
    )(*operands)


def body(psi, left_env, right_env, pairing, block_rows, block_cols, energy):
    sec_count = lax.axis_size("sec")
    op_count = lax.axis_size("op")
    rep_count = lax.axis_size("rep")
    terms, sec_dev, half, width = left_env.shape
    entries = sec_count * sec_dev * rep_count * half * width
    split = sec_count * op_count <= 8
    can_pair = sec_count & (sec_count - 1) == 0
    steps = list(range(1, sec_count))
    first_plan = (False, steps, 2)
    second_plan = (can_pair, steps[1:2] + steps[:1] + steps[2:], 1)
    params = pltpu.CompilerParams(vmem_limit_bytes=VMEM_BYTES)
    vec_shape = (sec_dev, half, width)
    vec_bf16 = jax.ShapeDtypeStruct(vec_shape, BF16)

    def from_others(array):
        arrays = []
        for step in range(1, rep_count):
            turn = [((i + step) % rep_count, i) for i in range(rep_count)]
            arrays.append(lax.ppermute(array, "rep", turn))
        return arrays

    psi_others = from_others(psi)
    level_others = from_others(energy)
    start, left_env, lists, limits, levels, scalars = pl.pallas_call(
        load_kernel,
        out_shape=[
            vec_bf16,
            jax.ShapeDtypeStruct(left_env.shape, BF16),
            jax.ShapeDtypeStruct((sec_count, LANES), jnp.int32),
            jax.ShapeDtypeStruct((2 * sec_dev, LANES), jnp.int32),
            jax.ShapeDtypeStruct((sec_dev, half, LANES), F32),
            jax.ShapeDtypeStruct((16, width), F32),
        ],
        in_specs=[whole(pltpu.HBM)] * 6,
        out_specs=[whole(pltpu.VMEM)] * 6,
        scratch_shapes=[
            pltpu.VMEM(vec_shape, BF16),
            pltpu.VMEM((sec_dev, half), F32),
            pltpu.SMEM((sec_dev,), jnp.int32),
            pltpu.SMEM((sec_dev,), jnp.int32),
            pltpu.SMEM((sec_dev, terms), jnp.int32),
            pltpu.SMEM((sec_count, LANES), jnp.int32),
            pltpu.SMEM((sec_count,), jnp.int32),
            pltpu.SemaphoreType.DMA((6 + terms,)),
        ],
        compiler_params=params,
        name="load",
    )(*(
        pltpu.with_memory_space_constraint(array, pltpu.HBM)
        for array in (psi, left_env, pairing.T, block_rows, block_cols, energy)
    ))

    block_f32 = jax.ShapeDtypeStruct(vec_shape, F32)
    row_f32 = jax.ShapeDtypeStruct((8, LANES), F32)

    packets = sigma_packets(
        True, split, first_plan[0], rep_count, lists, left_env, right_env,
        [start, limits, scalars, *psi_others, *level_others],
    )
    early, late = exchange(packets, split, *first_plan)
    base, scalars = call(
        functools.partial(first_early_kernel, split, len(early)), "combine_first_early",
        [block_f32, row_f32], *early, start, levels,
    )
    first_out, sigma_one, vector = call(
        functools.partial(first_kernel, len(late)), "combine_first",
        [
            pltpu.VMEM(vec_shape, BF16),
            block_f32,
            jax.ShapeDtypeStruct((sec_dev * half + MORE_ROWS, width), BF16),
        ],
        *late, limits, start, base, scalars,
    )

    packets = sigma_packets(
        False, split, second_plan[0], rep_count, lists, left_env, right_env,
        [vector, *from_others(vector)],
    )
    early, late = exchange(packets, split, *second_plan)
    base, scale = call(
        functools.partial(second_early_kernel, split, len(early), entries),
        "combine_second_early", [block_f32, row_f32], *early, vector, levels, sigma_one, scalars,
    )
    (second_out,) = call(
        functools.partial(second_kernel, len(late)), "combine_second", [vec_bf16],
        *late, limits, base, scale,
    )
    return (first_out, second_out)


def solution(mesh):
    return jax.shard_map(
        body,
        mesh=mesh,
        in_specs=(
            P(("grp", "sec"), "rep", None),
            P(("grp", "op"), "sec", "rep", None),
            P(("grp", "op"), None, None),
            P(("grp", "op"), "sec"),
            P(("grp", "sec")),
            P(("grp", "sec")),
            P(("grp", "sec"), "rep"),
        ),
        out_specs=(P(("grp", "sec"), "rep", None), P(("grp", "sec"), "rep", None)),
        check_vma=False,
    )
```

```python
import functools

import jax
import jax.numpy as jnp
from jax import lax
from jax.experimental import pallas as pl
from jax.experimental.pallas import tpu as pltpu
from jax.sharding import PartitionSpec as P

EPSILON = 1e-06
HEAD = 8
PARTS = 3
EARLY_FLOPS = 10**9
MORE_ROWS = 16
LANES = 128
VMEM_BYTES = 24 * 1024 * 1024
F32 = jnp.float32
BF16 = jnp.bfloat16


def whole(space):
    return pl.BlockSpec(memory_space=space)


def live(limit_ref, s, first_row, shape):
    sec_dev = limit_ref.shape[0] // 2
    repeat = shape[1] // LANES
    rows = jnp.concatenate([limit_ref[s:s + 1, :]] * repeat, axis=1)
    cols = jnp.concatenate([limit_ref[sec_dev + s:sec_dev + s + 1, :]] * repeat, axis=1)
    row_ids = first_row + lax.broadcasted_iota(jnp.int32, shape, 0)
    col_ids = lax.broadcasted_iota(jnp.int32, shape, 1)
    return (row_ids < rows) & (col_ids < cols)


def energy_columns(level):
    missing = -level.shape[0] % 8
    if missing:
        level = jnp.concatenate([level, jnp.zeros((missing, level.shape[1]), F32)], axis=0)
    return level.T


def spread(array, width):
    return jnp.concatenate([array] * (width // LANES), axis=1)


def quotient(value, count):
    return value >> (count.bit_length() - 1) if count & (count - 1) == 0 else lax.div(value, count)


def remainder(value, count):
    return value & (count - 1) if count & (count - 1) == 0 else lax.rem(value, count)


def fold(array):
    rows, width = array.shape
    return jnp.sum(array.reshape(rows // 8, 8, width), axis=0)


def total(array):
    return jnp.sum(jnp.sum(array, axis=0, keepdims=True), axis=1, keepdims=True)


def header(slot, scalars, shape=(HEAD, LANES)):
    row_ids = lax.broadcasted_iota(jnp.int32, shape, 0)
    head = jnp.where(row_ids == 0, slot.astype(F32), 0.0)
    row = 1
    for scalar in scalars:
        rest = jnp.broadcast_to(scalar, shape)
        for _ in range(PARTS):
            piece = rest.astype(BF16).astype(F32)
            head = jnp.where(row_ids == row, piece, head)
            rest = rest - piece
            row += 1
    return head.astype(BF16)


def head_scalar(head_sum, index):
    first = 1 + PARTS * index
    return jnp.sum(head_sum[first:first + PARTS], axis=0, keepdims=True)


def most_pairs(pairs, sec_count):
    return pairs // sec_count + 1


def load_kernel(
    psi_hbm, left_hbm, pairing_hbm, rows_hbm, cols_hbm, energy_hbm,
    start_ref, left_ref, list_ref, limit_ref, energy_ref, scalar_ref,
    psi_ref, level_ref, rows_ref, cols_ref, pairing_ref, entry_ref, count_ref, sems,
):
    sec_dev, half, width = psi_ref.shape
    terms = left_ref.shape[0]
    sec_count = list_ref.shape[0]
    cap = most_pairs(terms * sec_dev, sec_count)
    pairs = [
        (rows_hbm, rows_ref), (cols_hbm, cols_ref), (energy_hbm, level_ref),
        (pairing_hbm, pairing_ref), (psi_hbm, psi_ref),
    ]
    for t in range(left_ref.shape[0]):
        pairs.append((left_hbm.at[t], left_ref.at[t]))
    copies = [
        pltpu.make_async_copy(source, target, sems.at[i])
        for i, (source, target) in enumerate(pairs)
    ]
    for copy in copies:
        copy.start()
    for owner in range(sec_count):
        count_ref[owner] = 0
        entry_ref[owner, cap] = 0
        for i in range(cap):
            entry_ref[owner, i] = terms * sec_dev
    for copy in copies[:3]:
        copy.wait()
    for s in range(sec_dev):
        limit_ref[s:s + 1, :] = jnp.full((1, LANES), rows_ref[s], jnp.int32)
        limit_ref[sec_dev + s:sec_dev + s + 1, :] = jnp.full((1, LANES), cols_ref[s], jnp.int32)
    columns = energy_columns(level_ref[...])
    for s in range(sec_dev):
        energy_ref[s] = jnp.broadcast_to(columns[:, s:s + 1], (half, LANES))
    copies[3].wait()
    for t in range(terms):
        for s in range(sec_dev):
            target = pairing_ref[s, t]
            owner = quotient(target, sec_dev)
            count = count_ref[owner]
            entry_ref[owner, count] = t * sec_dev + s
            entry_ref[owner, cap] = remainder(target, sec_dev)
            count_ref[owner] = count + 1
    entries = pltpu.make_async_copy(entry_ref, list_ref, sems.at[len(copies)])
    entries.start()
    copies[4].wait()
    first_row = lax.axis_index("rep") * half
    norm = jnp.zeros((8, width), F32)
    level = jnp.zeros((8, width), F32)
    for s in range(sec_dev):
        vector = jnp.where(
            live(limit_ref, s, first_row, (half, width)), psi_ref[s].astype(F32), 0.0
        )
        start_ref[s] = vector.astype(BF16)
        square = vector * vector
        norm += fold(square)
        level += fold(square * spread(energy_ref[s], width))
    scalar_ref[0:8, :] = norm
    scalar_ref[8:16, :] = level
    for copy in copies[5:]:
        copy.wait()
    entries.wait()


def product_kernel(is_first, split, paired, rep_count, sec_count, *refs):
    refs = list(refs)
    take = lambda count: [refs.pop(0) for _ in range(count)]
    list_ref, left_ref, right_ref = take(3)
    if is_first:
        start_ref, limit_ref, scalar_ref = take(3)
        psi_refs = take(rep_count - 1)
        level_refs = take(rep_count - 1)
    else:
        vector_refs = take(rep_count)
    out_refs = take(sec_count if split else 1)
    inner_ref, entry_ref, sem = refs
    terms, sec_dev, half, width = left_ref.shape
    pairs = terms * sec_dev
    cap = most_pairs(pairs, sec_count)
    rep = lax.axis_index("rep")
    sec = lax.axis_index("sec")
    fetch = pltpu.make_async_copy(list_ref, entry_ref, sem)
    fetch.start()
    inner_ref[pairs] = jnp.zeros((half, width), BF16)

    def first_row(step):
        return remainder(rep + step, rep_count) * half

    if is_first:
        folded = [scalar_ref[0:8, :], scalar_ref[8:16, :]]
        columns = [energy_columns(ref[...]) for ref in level_refs]
    for s in range(sec_dev):
        if is_first:
            blocks = [start_ref[s]]
            for step in range(1, rep_count):
                psi = psi_refs[step - 1][s]
                mask = live(limit_ref, s, first_row(step), (half, width))
                blocks.append(jnp.where(mask, psi.astype(F32), 0.0).astype(BF16))
        else:
            blocks = [ref[s * half:(s + 1) * half] for ref in vector_refs]
        vector = jnp.concatenate(blocks, axis=0)
        for turn in range(1, rep_count):
            turned = blocks[rep_count - turn:] + blocks[:rep_count - turn]
            vector = jnp.where(rep == turn, jnp.concatenate(turned, axis=0), vector)
        inner = jnp.dot(
            left_ref[:, s].reshape(terms * half, width), vector, preferred_element_type=F32
        ).astype(BF16)
        for t in range(terms):
            inner_ref[t * sec_dev + s] = inner[t * half:(t + 1) * half]
        if is_first:
            for step in range(1, rep_count):
                block = blocks[step].astype(F32)
                square = block * block
                energy = jnp.broadcast_to(columns[step - 1][:, s:s + 1], (half, width))
                folded = [folded[0] + fold(square), folded[1] + fold(square * energy)]
    if is_first:
        scalars = [total(array) for array in folded]
    else:
        head = sum(ref[sec_dev * half:].astype(F32) for ref in vector_refs)
        scalars = [head_scalar(head, i)[:, :LANES] for i in range(2)]
    fetch.wait()
    for d in range(sec_count):
        if not split:
            owner = d
        elif paired:
            owner = sec ^ d
        else:
            owner = remainder(sec + d, sec_count)
        packet = jnp.zeros((half, width), F32)
        for i in range(cap):
            pair = entry_ref[owner, i]
            term = jnp.minimum(quotient(pair, sec_dev), terms - 1)
            packet += jnp.dot(inner_ref[pair], right_ref[term], preferred_element_type=F32)
        out = out_refs[d] if split else out_refs[0].at[d]
        for column in range(width // LANES):
            out[column * half:(column + 1) * half, :] = packet[
                :, column * LANES:(column + 1) * LANES
            ].astype(BF16)
        out[width // LANES * half:, :] = header(entry_ref[owner, cap], scalars)


def sigma_packets(is_first, split, paired, rep_count, lists, left_env, right_env, more):
    terms, sec_dev, half, width = left_env.shape
    sec_count = lax.axis_size("sec")
    packet = (width // LANES * half + HEAD, LANES)
    if split:
        outs = [jax.ShapeDtypeStruct(packet, BF16)] * sec_count
    else:
        outs = [jax.ShapeDtypeStruct((sec_count,) + packet, BF16)]
    pair_flops = 2 * half * width * width * 2
    operands = [lists, left_env, right_env, *more]
    return pl.pallas_call(
        functools.partial(product_kernel, is_first, split, paired, rep_count, sec_count),
        out_shape=outs,
        in_specs=[whole(pltpu.VMEM)] * len(operands),
        out_specs=[whole(pltpu.VMEM)] * len(outs),
        scratch_shapes=[
            pltpu.VMEM((terms * sec_dev + 1, half, width), BF16),
            pltpu.SMEM(lists.shape, jnp.int32),
            pltpu.SemaphoreType.DMA,
        ],
        compiler_params=pltpu.CompilerParams(vmem_limit_bytes=VMEM_BYTES),
        cost_estimate=pl.CostEstimate(
            flops=terms * sec_dev * pair_flops,
            bytes_accessed=2 * (left_env.size + right_env.size),
            transcendentals=0,
        ),
        name="products_first" if is_first else "products_second",
    )(*operands)


def exchange(packets, split, paired, order, together):
    sec_count = lax.axis_size("sec")
    op_count = lax.axis_size("op")
    op_turns = [
        [(i, (i + step) % op_count) for i in range(op_count)] for step in range(1, op_count)
    ]
    over_op = lambda packet: [lax.ppermute(packet, "op", turn) for turn in op_turns]
    if not split:
        arrived = lax.all_to_all(packets[0], "sec", split_axis=0, concat_axis=0, tiled=True)
        return [arrived] + over_op(arrived), []
    arrived = {0: packets[0]}
    for step in order:
        reach = (lambda i: i ^ step) if paired else (lambda i: (i + step) % sec_count)
        turn = [(i, reach(i)) for i in range(sec_count)]
        arrived[step] = lax.ppermute(packets[step], "sec", turn)
    steps = [0, *order]
    alone = steps[:len(steps) - together]
    crossed = sum([over_op(arrived[step]) for step in alone], [])
    waiting = [arrived[step] for step in steps[len(alone):]]
    last = jnp.stack(waiting)
    return [arrived[step] for step in steps] + crossed, over_op(last)


def add_packets(packet_refs, split, half, base_ref):
    sec_dev, _, width = base_ref.shape
    own = lax.axis_size("sec") if split else 1
    body_rows = width // LANES * half
    if split:
        heads = [ref[body_rows:].astype(F32) for ref in packet_refs]
        for column in range(width // LANES):
            lanes = slice(column * LANES, (column + 1) * LANES)
            for s in range(sec_dev):
                part = base_ref[s, :, lanes]
                for ref, head in zip(packet_refs, heads):
                    body = ref[column * half:(column + 1) * half].astype(F32)
                    part += jnp.where(head[0:1] == s, body, 0.0)
                base_ref[s, :, lanes] = part
        return sum(heads[1:own], heads[0])

    head_sum = jnp.zeros((HEAD, LANES), F32)
    for index, ref in enumerate(packet_refs):
        def add_one(p, carry):
            head = ref[p, body_rows:, :].astype(F32)
            for column in range(width // LANES):
                body = ref[p, column * half:(column + 1) * half, :].astype(F32)
                lanes = slice(column * LANES, (column + 1) * LANES)
                for s in range(sec_dev):
                    base_ref[s, :, lanes] += jnp.where(head[0:1] == s, body, 0.0)
            return carry + head
        result = lax.fori_loop(0, ref.shape[0], add_one, jnp.zeros((HEAD, LANES), F32))
        if index < own:
            head_sum = head_sum + result
    return head_sum


def late_sum(packet_refs, s, half, width):
    body_rows = width // LANES * half
    value = jnp.zeros((half, width), F32)
    for ref in packet_refs:
        for i in range(ref.shape[0]):
            body = jnp.concatenate(
                [ref[i, c * half:(c + 1) * half].astype(F32) for c in range(width // LANES)],
                axis=1,
            )
            slot = spread(ref[i, body_rows:].astype(F32)[0:1], width)
            value += jnp.where(slot == s, body, 0.0)
    return value


def first_early_kernel(split, count, *refs):
    packet_refs = refs[:count]
    start_ref, energy_ref, base_ref, scalar_ref = refs[count:]
    sec_dev, half, width = start_ref.shape
    for s in range(sec_dev):
        base_ref[s] = spread(energy_ref[s], width) * start_ref[s].astype(F32)
    head_sum = add_packets(packet_refs, split, half, base_ref)
    norm = head_scalar(head_sum, 0)
    scalar_ref[0:1] = norm
    scalar_ref[1:2] = head_scalar(head_sum, 1) / norm


def first_kernel(count, *refs):
    packet_refs = refs[:count]
    limit_ref, start_ref, base_ref, scalar_ref, first_ref, one_ref, vec_ref = refs[count:]
    sec_dev, half, width = start_ref.shape
    shift = spread(scalar_ref[1:2], width)
    first_row = lax.axis_index("rep") * half
    cross = jnp.zeros((8, width), F32)
    square = jnp.zeros((8, width), F32)
    for s in range(sec_dev):
        mask = live(limit_ref, s, first_row, (half, width))
        start = start_ref[s].astype(F32)
        one = jnp.where(mask, base_ref[s] + late_sum(packet_refs, s, half, width), 0.0)
        one_ref[s] = one
        first_ref[s] = one.astype(BF16)
        vector = one - shift * start
        vec_ref[s * half:(s + 1) * half] = vector.astype(BF16)
        cross += fold(start * vector)
        square += fold(vector * vector)
    scalars = (total(cross), total(square))
    vec_ref[sec_dev * half:] = header(jnp.int32(0), scalars, (MORE_ROWS, width))


def second_early_kernel(split, count, entries, *refs):
    packet_refs = refs[:count]
    vec_ref, energy_ref, one_ref, scalar_ref, base_ref, scale_ref = refs[count:]
    sec_dev, half, width = one_ref.shape
    for s in range(sec_dev):
        vector = vec_ref[s * half:(s + 1) * half].astype(F32)
        base_ref[s] = spread(energy_ref[s], width) * vector
    head_sum = add_packets(packet_refs, split, half, base_ref)
    cross = head_scalar(head_sum, 0)
    square = head_scalar(head_sum, 1)
    excess = cross / scalar_ref[0:1]
    resid_sq = jnp.maximum(square - excess * cross, 0.0)
    scale = lax.rsqrt(resid_sq / entries + EPSILON)
    scale_ref[...] = jnp.broadcast_to(scale, scale_ref.shape)
    for s in range(sec_dev):
        base_ref[s] = base_ref[s] - spread(excess, width) * one_ref[s]


def second_kernel(count, *refs):
    packet_refs = refs[:count]
    limit_ref, base_ref, scale_ref, second_ref = refs[count:]
    sec_dev, half, width = base_ref.shape
    scale = spread(scale_ref[0:1], width)
    first_row = lax.axis_index("rep") * half
    for s in range(sec_dev):
        mask = live(limit_ref, s, first_row, (half, width))
        value = scale * (base_ref[s] + late_sum(packet_refs, s, half, width))
        second_ref[s] = jnp.where(mask, value, 0.0).astype(BF16)


def call(kernel, name, outs, *operands, flops=0):
    return pl.pallas_call(
        kernel,
        out_shape=outs,
        in_specs=[whole(pltpu.VMEM)] * len(operands),
        out_specs=[whole(pltpu.VMEM)] * len(outs),
        compiler_params=pltpu.CompilerParams(vmem_limit_bytes=VMEM_BYTES),
        cost_estimate=pl.CostEstimate(flops=flops, bytes_accessed=0, transcendentals=0),
        name=name,
    )(*operands)


def body(psi, left_env, right_env, pairing, block_rows, block_cols, energy):
    sec_count = lax.axis_size("sec")
    op_count = lax.axis_size("op")
    rep_count = lax.axis_size("rep")
    terms, sec_dev, half, width = left_env.shape
    entries = sec_count * sec_dev * rep_count * half * width
    split = sec_count * op_count <= 8
    can_pair = sec_count & (sec_count - 1) == 0
    steps = list(range(1, sec_count))
    first_plan = (False, steps, 2)
    second_plan = (can_pair, steps[1:2] + steps[:1] + steps[2:], 1)
    params = pltpu.CompilerParams(vmem_limit_bytes=VMEM_BYTES)
    vec_shape = (sec_dev, half, width)
    vec_bf16 = jax.ShapeDtypeStruct(vec_shape, BF16)

    def from_others(array):
        arrays = []
        for step in range(1, rep_count):
            turn = [((i + step) % rep_count, i) for i in range(rep_count)]
            arrays.append(lax.ppermute(array, "rep", turn))
        return arrays

    psi_others = from_others(psi)
    level_others = from_others(energy)
    start, left_env, lists, limits, levels, scalars = pl.pallas_call(
        load_kernel,
        out_shape=[
            vec_bf16,
            jax.ShapeDtypeStruct(left_env.shape, BF16),
            jax.ShapeDtypeStruct((sec_count, LANES), jnp.int32),
            jax.ShapeDtypeStruct((2 * sec_dev, LANES), jnp.int32),
            jax.ShapeDtypeStruct((sec_dev, half, LANES), F32),
            jax.ShapeDtypeStruct((16, width), F32),
        ],
        in_specs=[whole(pltpu.HBM)] * 6,
        out_specs=[whole(pltpu.VMEM)] * 6,
        scratch_shapes=[
            pltpu.VMEM(vec_shape, BF16),
            pltpu.VMEM((sec_dev, half), F32),
            pltpu.SMEM((sec_dev,), jnp.int32),
            pltpu.SMEM((sec_dev,), jnp.int32),
            pltpu.SMEM((sec_dev, terms), jnp.int32),
            pltpu.SMEM((sec_count, LANES), jnp.int32),
            pltpu.SMEM((sec_count,), jnp.int32),
            pltpu.SemaphoreType.DMA((6 + terms,)),
        ],
        compiler_params=params,
        name="load",
    )(*(
        pltpu.with_memory_space_constraint(array, pltpu.HBM)
        for array in (psi, left_env, pairing.T, block_rows, block_cols, energy)
    ))

    block_f32 = jax.ShapeDtypeStruct(vec_shape, F32)
    row_f32 = jax.ShapeDtypeStruct((8, LANES), F32)

    packets = sigma_packets(
        True, split, first_plan[0], rep_count, lists, left_env, right_env,
        [start, limits, scalars, *psi_others, *level_others],
    )
    early, late = exchange(packets, split, *first_plan)
    base, scalars = call(
        functools.partial(first_early_kernel, split, len(early)), "combine_first_early",
        [block_f32, row_f32], *early, start, levels, flops=EARLY_FLOPS,
    )
    first_out, sigma_one, vector = call(
        functools.partial(first_kernel, len(late)), "combine_first",
        [
            pltpu.VMEM(vec_shape, BF16),
            block_f32,
            jax.ShapeDtypeStruct((sec_dev * half + MORE_ROWS, width), BF16),
        ],
        *late, limits, start, base, scalars,
    )

    packets = sigma_packets(
        False, split, second_plan[0], rep_count, lists, left_env, right_env,
        [vector, *from_others(vector)],
    )
    early, late = exchange(packets, split, *second_plan)
    base, scale = call(
        functools.partial(second_early_kernel, split, len(early), entries),
        "combine_second_early", [block_f32, row_f32], *early, vector, levels, sigma_one, scalars,
    )
    (second_out,) = call(
        functools.partial(second_kernel, len(late)), "combine_second", [vec_bf16],
        *late, limits, base, scale,
    )
    return (first_out, second_out)


def solution(mesh):
    return jax.shard_map(
        body,
        mesh=mesh,
        in_specs=(
            P(("grp", "sec"), "rep", None),
            P(("grp", "op"), "sec", "rep", None),
            P(("grp", "op"), None, None),
            P(("grp", "op"), "sec"),
            P(("grp", "sec")),
            P(("grp", "sec")),
            P(("grp", "sec"), "rep"),
        ),
        out_specs=(P(("grp", "sec"), "rep", None), P(("grp", "sec"), "rep", None)),
        check_vma=False,
    )
```

```python
import functools

import jax
import jax.numpy as jnp
from jax import lax
from jax.experimental import pallas as pl
from jax.experimental.pallas import tpu as pltpu
from jax.sharding import PartitionSpec as P

EPSILON = 1e-06
HEAD = 8
PARTS = 3
EARLY_FLOPS = 10**9
MORE_ROWS = 16
LANES = 128
VMEM_BYTES = 24 * 1024 * 1024
F32 = jnp.float32
BF16 = jnp.bfloat16


def whole(space):
    return pl.BlockSpec(memory_space=space)


def live(limit_ref, s, first_row, shape):
    sec_dev = limit_ref.shape[0] // 2
    repeat = shape[1] // LANES
    rows = jnp.concatenate([limit_ref[s:s + 1, :]] * repeat, axis=1)
    cols = jnp.concatenate([limit_ref[sec_dev + s:sec_dev + s + 1, :]] * repeat, axis=1)
    row_ids = first_row + lax.broadcasted_iota(jnp.int32, shape, 0)
    col_ids = lax.broadcasted_iota(jnp.int32, shape, 1)
    return (row_ids < rows) & (col_ids < cols)


def energy_columns(level):
    missing = -level.shape[0] % 8
    if missing:
        level = jnp.concatenate([level, jnp.zeros((missing, level.shape[1]), F32)], axis=0)
    return level.T


def spread(array, width):
    return jnp.concatenate([array] * (width // LANES), axis=1)


def quotient(value, count):
    return value >> (count.bit_length() - 1) if count & (count - 1) == 0 else lax.div(value, count)


def remainder(value, count):
    return value & (count - 1) if count & (count - 1) == 0 else lax.rem(value, count)


def fold(array):
    rows, width = array.shape
    return jnp.sum(array.reshape(rows // 8, 8, width), axis=0)


def total(array):
    return jnp.sum(jnp.sum(array, axis=0, keepdims=True), axis=1, keepdims=True)


def header(slot, scalars, shape=(HEAD, LANES)):
    row_ids = lax.broadcasted_iota(jnp.int32, shape, 0)
    head = jnp.where(row_ids == 0, slot.astype(F32), 0.0)
    row = 1
    for scalar in scalars:
        rest = jnp.broadcast_to(scalar, shape)
        for _ in range(PARTS):
            piece = rest.astype(BF16).astype(F32)
            head = jnp.where(row_ids == row, piece, head)
            rest = rest - piece
            row += 1
    return head.astype(BF16)


def head_scalar(head_sum, index):
    first = 1 + PARTS * index
    return jnp.sum(head_sum[first:first + PARTS], axis=0, keepdims=True)


def most_pairs(pairs, sec_count):
    return pairs // sec_count + 1


def load_kernel(
    psi_hbm, left_hbm, pairing_hbm, rows_hbm, cols_hbm, energy_hbm,
    start_ref, left_ref, list_ref, limit_ref, energy_ref, scalar_ref,
    psi_ref, level_ref, rows_ref, cols_ref, pairing_ref, entry_ref, count_ref, sems,
):
    sec_dev, half, width = psi_ref.shape
    terms = left_ref.shape[0]
    sec_count = list_ref.shape[0]
    cap = most_pairs(terms * sec_dev, sec_count)
    pairs = [
        (rows_hbm, rows_ref), (cols_hbm, cols_ref), (energy_hbm, level_ref),
        (pairing_hbm, pairing_ref), (psi_hbm, psi_ref),
    ]
    for t in range(left_ref.shape[0]):
        pairs.append((left_hbm.at[t], left_ref.at[t]))
    copies = [
        pltpu.make_async_copy(source, target, sems.at[i])
        for i, (source, target) in enumerate(pairs)
    ]
    for copy in copies:
        copy.start()
    for owner in range(sec_count):
        count_ref[owner] = 0
        entry_ref[owner, cap] = 0
        for i in range(cap):
            entry_ref[owner, i] = terms * sec_dev
    for copy in copies[:3]:
        copy.wait()
    for s in range(sec_dev):
        limit_ref[s:s + 1, :] = jnp.full((1, LANES), rows_ref[s], jnp.int32)
        limit_ref[sec_dev + s:sec_dev + s + 1, :] = jnp.full((1, LANES), cols_ref[s], jnp.int32)
    columns = energy_columns(level_ref[...])
    for s in range(sec_dev):
        energy_ref[s] = jnp.broadcast_to(columns[:, s:s + 1], (half, LANES))
    copies[3].wait()
    for t in range(terms):
        for s in range(sec_dev):
            target = pairing_ref[s, t]
            owner = quotient(target, sec_dev)
            count = count_ref[owner]
            entry_ref[owner, count] = t * sec_dev + s
            entry_ref[owner, cap] = remainder(target, sec_dev)
            count_ref[owner] = count + 1
    entries = pltpu.make_async_copy(entry_ref, list_ref, sems.at[len(copies)])
    entries.start()
    copies[4].wait()
    first_row = lax.axis_index("rep") * half
    norm = jnp.zeros((8, width), F32)
    level = jnp.zeros((8, width), F32)
    for s in range(sec_dev):
        vector = jnp.where(
            live(limit_ref, s, first_row, (half, width)), psi_ref[s].astype(F32), 0.0
        )
        start_ref[s] = vector.astype(BF16)
        square = vector * vector
        norm += fold(square)
        level += fold(square * spread(energy_ref[s], width))
    scalar_ref[0:8, :] = norm
    scalar_ref[8:16, :] = level
    for copy in copies[5:]:
        copy.wait()
    entries.wait()


def product_kernel(is_first, split, paired, rep_count, sec_count, *refs):
    refs = list(refs)
    take = lambda count: [refs.pop(0) for _ in range(count)]
    list_ref, left_ref, right_ref = take(3)
    if is_first:
        start_ref, limit_ref, scalar_ref = take(3)
        psi_refs = take(rep_count - 1)
        level_refs = take(rep_count - 1)
    else:
        (first_ref,) = take(1)
        vector_refs = take(rep_count)
    out_refs = take(sec_count if split else 1)
    if not is_first:
        (first_hbm,) = take(1)
    inner_ref, entry_ref, sems = refs
    terms, sec_dev, half, width = left_ref.shape
    pairs = terms * sec_dev
    cap = most_pairs(pairs, sec_count)
    rep = lax.axis_index("rep")
    sec = lax.axis_index("sec")
    fetch = pltpu.make_async_copy(list_ref, entry_ref, sems.at[0])
    fetch.start()
    if not is_first:
        put = pltpu.make_async_copy(first_ref, first_hbm, sems.at[1])
        put.start()
    inner_ref[pairs] = jnp.zeros((half, width), BF16)

    def first_row(step):
        return remainder(rep + step, rep_count) * half

    if is_first:
        folded = [scalar_ref[0:8, :], scalar_ref[8:16, :]]
        columns = [energy_columns(ref[...]) for ref in level_refs]
    for s in range(sec_dev):
        if is_first:
            blocks = [start_ref[s]]
            for step in range(1, rep_count):
                psi = psi_refs[step - 1][s]
                mask = live(limit_ref, s, first_row(step), (half, width))
                blocks.append(jnp.where(mask, psi.astype(F32), 0.0).astype(BF16))
        else:
            blocks = [ref[s * half:(s + 1) * half] for ref in vector_refs]
        vector = jnp.concatenate(blocks, axis=0)
        for turn in range(1, rep_count):
            turned = blocks[rep_count - turn:] + blocks[:rep_count - turn]
            vector = jnp.where(rep == turn, jnp.concatenate(turned, axis=0), vector)
        inner = jnp.dot(
            left_ref[:, s].reshape(terms * half, width), vector, preferred_element_type=F32
        ).astype(BF16)
        for t in range(terms):
            inner_ref[t * sec_dev + s] = inner[t * half:(t + 1) * half]
        if is_first:
            for step in range(1, rep_count):
                block = blocks[step].astype(F32)
                square = block * block
                energy = jnp.broadcast_to(columns[step - 1][:, s:s + 1], (half, width))
                folded = [folded[0] + fold(square), folded[1] + fold(square * energy)]
    if is_first:
        scalars = [total(array) for array in folded]
    else:
        head = sum(ref[sec_dev * half:].astype(F32) for ref in vector_refs)
        scalars = [head_scalar(head, i)[:, :LANES] for i in range(2)]
    fetch.wait()
    for d in range(sec_count):
        if not split:
            owner = d
        elif paired:
            owner = sec ^ d
        else:
            owner = remainder(sec + d, sec_count)
        packet = jnp.zeros((half, width), F32)
        for i in range(cap):
            pair = entry_ref[owner, i]
            term = jnp.minimum(quotient(pair, sec_dev), terms - 1)
            packet += jnp.dot(inner_ref[pair], right_ref[term], preferred_element_type=F32)
        out = out_refs[d] if split else out_refs[0].at[d]
        for column in range(width // LANES):
            out[column * half:(column + 1) * half, :] = packet[
                :, column * LANES:(column + 1) * LANES
            ].astype(BF16)
        out[width // LANES * half:, :] = header(entry_ref[owner, cap], scalars)
    if not is_first:
        put.wait()


def sigma_packets(is_first, split, paired, rep_count, lists, left_env, right_env, more):
    terms, sec_dev, half, width = left_env.shape
    sec_count = lax.axis_size("sec")
    packet = (width // LANES * half + HEAD, LANES)
    if split:
        outs = [jax.ShapeDtypeStruct(packet, BF16)] * sec_count
    else:
        outs = [jax.ShapeDtypeStruct((sec_count,) + packet, BF16)]
    out_specs = [whole(pltpu.VMEM)] * len(outs)
    if not is_first:
        outs.append(jax.ShapeDtypeStruct((sec_dev, half, width), BF16))
        out_specs.append(whole(pltpu.HBM))
    pair_flops = 2 * half * width * width * 2
    operands = [lists, left_env, right_env, *more]
    return pl.pallas_call(
        functools.partial(product_kernel, is_first, split, paired, rep_count, sec_count),
        out_shape=outs,
        in_specs=[whole(pltpu.VMEM)] * len(operands),
        out_specs=out_specs,
        scratch_shapes=[
            pltpu.VMEM((terms * sec_dev + 1, half, width), BF16),
            pltpu.SMEM(lists.shape, jnp.int32),
            pltpu.SemaphoreType.DMA((2,)),
        ],
        compiler_params=pltpu.CompilerParams(vmem_limit_bytes=VMEM_BYTES),
        cost_estimate=pl.CostEstimate(
            flops=terms * sec_dev * pair_flops,
            bytes_accessed=2 * (left_env.size + right_env.size),
            transcendentals=0,
        ),
        name="products_first" if is_first else "products_second",
    )(*operands)


def exchange(packets, split, paired, order, groups):
    sec_count = lax.axis_size("sec")
    op_count = lax.axis_size("op")
    op_turns = [
        [(i, (i + step) % op_count) for i in range(op_count)] for step in range(1, op_count)
    ]
    over_op = lambda packet: [lax.ppermute(packet, "op", turn) for turn in op_turns]
    if not split:
        arrived = lax.all_to_all(packets[0], "sec", split_axis=0, concat_axis=0, tiled=True)
        return [arrived] + over_op(arrived), []
    arrived = {0: packets[0]}
    for step in order:
        reach = (lambda i: i ^ step) if paired else (lambda i: (i + step) % sec_count)
        turn = [(i, reach(i)) for i in range(sec_count)]
        arrived[step] = lax.ppermute(packets[step], "sec", turn)
    crossed = [over_op(jnp.stack([arrived[step] for step in group])) for group in groups]
    return [arrived[step] for step in [0, *order]] + sum(crossed[:-1], []), crossed[-1]


def views(refs):
    return [
        view
        for ref in refs
        for view in ([ref] if len(ref.shape) == 2 else [ref.at[i] for i in range(ref.shape[0])])
    ]


def add_packets(packet_refs, split, half, base_ref):
    sec_dev, _, width = base_ref.shape
    own = lax.axis_size("sec") if split else 1
    body_rows = width // LANES * half
    if split:
        packet_refs = views(packet_refs)
        heads = [ref[body_rows:].astype(F32) for ref in packet_refs]
        for column in range(width // LANES):
            lanes = slice(column * LANES, (column + 1) * LANES)
            for s in range(sec_dev):
                part = base_ref[s, :, lanes]
                for ref, head in zip(packet_refs, heads):
                    body = ref[column * half:(column + 1) * half].astype(F32)
                    part += jnp.where(head[0:1] == s, body, 0.0)
                base_ref[s, :, lanes] = part
        return sum(heads[1:own], heads[0])

    head_sum = jnp.zeros((HEAD, LANES), F32)
    for index, ref in enumerate(packet_refs):
        def add_one(p, carry):
            head = ref[p, body_rows:, :].astype(F32)
            for column in range(width // LANES):
                body = ref[p, column * half:(column + 1) * half, :].astype(F32)
                lanes = slice(column * LANES, (column + 1) * LANES)
                for s in range(sec_dev):
                    base_ref[s, :, lanes] += jnp.where(head[0:1] == s, body, 0.0)
            return carry + head
        result = lax.fori_loop(0, ref.shape[0], add_one, jnp.zeros((HEAD, LANES), F32))
        if index < own:
            head_sum = head_sum + result
    return head_sum


def late_sum(packet_refs, s, half, width):
    body_rows = width // LANES * half
    value = jnp.zeros((half, width), F32)
    for ref in views(packet_refs):
        body = jnp.concatenate(
            [ref[c * half:(c + 1) * half].astype(F32) for c in range(width // LANES)], axis=1
        )
        slot = spread(ref[body_rows:].astype(F32)[0:1], width)
        value += jnp.where(slot == s, body, 0.0)
    return value


def first_early_kernel(split, count, *refs):
    packet_refs = refs[:count]
    start_ref, energy_ref, base_ref, scalar_ref = refs[count:]
    sec_dev, half, width = start_ref.shape
    for s in range(sec_dev):
        base_ref[s] = spread(energy_ref[s], width) * start_ref[s].astype(F32)
    head_sum = add_packets(packet_refs, split, half, base_ref)
    norm = head_scalar(head_sum, 0)
    scalar_ref[0:1] = norm
    scalar_ref[1:2] = head_scalar(head_sum, 1) / norm


def first_kernel(count, *refs):
    packet_refs = refs[:count]
    limit_ref, start_ref, base_ref, scalar_ref, first_ref, one_ref, vec_ref = refs[count:]
    sec_dev, half, width = start_ref.shape
    shift = spread(scalar_ref[1:2], width)
    first_row = lax.axis_index("rep") * half
    cross = jnp.zeros((8, width), F32)
    square = jnp.zeros((8, width), F32)
    for s in range(sec_dev):
        mask = live(limit_ref, s, first_row, (half, width))
        start = start_ref[s].astype(F32)
        one = jnp.where(mask, base_ref[s] + late_sum(packet_refs, s, half, width), 0.0)
        one_ref[s] = one
        first_ref[s] = one.astype(BF16)
        vector = one - shift * start
        vec_ref[s * half:(s + 1) * half] = vector.astype(BF16)
        cross += fold(start * vector)
        square += fold(vector * vector)
    scalars = (total(cross), total(square))
    vec_ref[sec_dev * half:] = header(jnp.int32(0), scalars, (MORE_ROWS, width))


def second_early_kernel(split, count, entries, *refs):
    packet_refs = refs[:count]
    vec_ref, energy_ref, one_ref, scalar_ref, base_ref, scale_ref = refs[count:]
    sec_dev, half, width = one_ref.shape
    for s in range(sec_dev):
        vector = vec_ref[s * half:(s + 1) * half].astype(F32)
        base_ref[s] = spread(energy_ref[s], width) * vector
    head_sum = add_packets(packet_refs, split, half, base_ref)
    cross = head_scalar(head_sum, 0)
    square = head_scalar(head_sum, 1)
    excess = cross / scalar_ref[0:1]
    resid_sq = jnp.maximum(square - excess * cross, 0.0)
    scale = lax.rsqrt(resid_sq / entries + EPSILON)
    scale_ref[...] = jnp.broadcast_to(scale, scale_ref.shape)
    for s in range(sec_dev):
        base_ref[s] = base_ref[s] - spread(excess, width) * one_ref[s]


def second_kernel(count, *refs):
    packet_refs = refs[:count]
    limit_ref, base_ref, scale_ref, second_ref = refs[count:]
    sec_dev, half, width = base_ref.shape
    scale = spread(scale_ref[0:1], width)
    first_row = lax.axis_index("rep") * half
    for s in range(sec_dev):
        mask = live(limit_ref, s, first_row, (half, width))
        value = scale * (base_ref[s] + late_sum(packet_refs, s, half, width))
        second_ref[s] = jnp.where(mask, value, 0.0).astype(BF16)


def call(kernel, name, outs, *operands, flops=0):
    return pl.pallas_call(
        kernel,
        out_shape=outs,
        in_specs=[whole(pltpu.VMEM)] * len(operands),
        out_specs=[whole(pltpu.VMEM)] * len(outs),
        compiler_params=pltpu.CompilerParams(vmem_limit_bytes=VMEM_BYTES),
        cost_estimate=pl.CostEstimate(flops=flops, bytes_accessed=0, transcendentals=0),
        name=name,
    )(*operands)


def body(psi, left_env, right_env, pairing, block_rows, block_cols, energy):
    sec_count = lax.axis_size("sec")
    op_count = lax.axis_size("op")
    rep_count = lax.axis_size("rep")
    terms, sec_dev, half, width = left_env.shape
    entries = sec_count * sec_dev * rep_count * half * width
    split = sec_count * op_count <= 8
    can_pair = sec_count & (sec_count - 1) == 0
    steps = list(range(1, sec_count))
    first_plan = (False, steps, [[0]] + [[k] for k in steps[:-2]] + [steps[-2:]])
    second_plan = (can_pair, steps[::-1], [[0]] + [[k] for k in steps[::-1]])
    params = pltpu.CompilerParams(vmem_limit_bytes=VMEM_BYTES)
    vec_shape = (sec_dev, half, width)
    vec_bf16 = jax.ShapeDtypeStruct(vec_shape, BF16)

    def from_others(array):
        arrays = []
        for step in range(1, rep_count):
            turn = [((i + step) % rep_count, i) for i in range(rep_count)]
            arrays.append(lax.ppermute(array, "rep", turn))
        return arrays

    psi_others = from_others(psi)
    level_others = from_others(energy)
    start, left_env, lists, limits, levels, scalars = pl.pallas_call(
        load_kernel,
        out_shape=[
            vec_bf16,
            jax.ShapeDtypeStruct(left_env.shape, BF16),
            jax.ShapeDtypeStruct((sec_count, LANES), jnp.int32),
            jax.ShapeDtypeStruct((2 * sec_dev, LANES), jnp.int32),
            jax.ShapeDtypeStruct((sec_dev, half, LANES), F32),
            jax.ShapeDtypeStruct((16, width), F32),
        ],
        in_specs=[whole(pltpu.HBM)] * 6,
        out_specs=[whole(pltpu.VMEM)] * 6,
        scratch_shapes=[
            pltpu.VMEM(vec_shape, BF16),
            pltpu.VMEM((sec_dev, half), F32),
            pltpu.SMEM((sec_dev,), jnp.int32),
            pltpu.SMEM((sec_dev,), jnp.int32),
            pltpu.SMEM((sec_dev, terms), jnp.int32),
            pltpu.SMEM((sec_count, LANES), jnp.int32),
            pltpu.SMEM((sec_count,), jnp.int32),
            pltpu.SemaphoreType.DMA((6 + terms,)),
        ],
        compiler_params=params,
        name="load",
    )(*(
        pltpu.with_memory_space_constraint(array, pltpu.HBM)
        for array in (psi, left_env, pairing.T, block_rows, block_cols, energy)
    ))

    block_f32 = jax.ShapeDtypeStruct(vec_shape, F32)
    row_f32 = jax.ShapeDtypeStruct((8, LANES), F32)

    packets = sigma_packets(
        True, split, first_plan[0], rep_count, lists, left_env, right_env,
        [start, limits, scalars, *psi_others, *level_others],
    )
    early, late = exchange(packets, split, *first_plan)
    base, scalars = call(
        functools.partial(first_early_kernel, split, len(early)), "combine_first_early",
        [block_f32, row_f32], *early, start, levels, flops=EARLY_FLOPS,
    )
    first, sigma_one, vector = call(
        functools.partial(first_kernel, len(late)), "combine_first",
        [
            pltpu.VMEM(vec_shape, BF16),
            block_f32,
            jax.ShapeDtypeStruct((sec_dev * half + MORE_ROWS, width), BF16),
        ],
        *late, limits, start, base, scalars,
    )

    *packets, first_out = sigma_packets(
        False, split, second_plan[0], rep_count, lists, left_env, right_env,
        [first, vector, *from_others(vector)],
    )
    early, late = exchange(packets, split, *second_plan)
    base, scale = call(
        functools.partial(second_early_kernel, split, len(early), entries),
        "combine_second_early", [block_f32, row_f32], *early, vector, levels, sigma_one, scalars,
        flops=EARLY_FLOPS,
    )
    (second_out,) = call(
        functools.partial(second_kernel, len(late)), "combine_second", [vec_bf16],
        *late, limits, base, scale,
    )
    return (first_out, second_out)


def solution(mesh):
    return jax.shard_map(
        body,
        mesh=mesh,
        in_specs=(
            P(("grp", "sec"), "rep", None),
            P(("grp", "op"), "sec", "rep", None),
            P(("grp", "op"), None, None),
            P(("grp", "op"), "sec"),
            P(("grp", "sec")),
            P(("grp", "sec")),
            P(("grp", "sec"), "rep"),
        ),
        out_specs=(P(("grp", "sec"), "rep", None), P(("grp", "sec"), "rep", None)),
        check_vma=False,
    )
```

```python
import functools

import jax
import jax.numpy as jnp
from jax import lax
from jax.experimental import pallas as pl
from jax.experimental.pallas import tpu as pltpu
from jax.sharding import PartitionSpec as P

EPSILON = 1e-06
HEAD = 8
PARTS = 3
EARLY_FLOPS = 10**9
MORE_ROWS = 16
LANES = 128
VMEM_BYTES = 24 * 1024 * 1024
F32 = jnp.float32
BF16 = jnp.bfloat16


def whole(space):
    return pl.BlockSpec(memory_space=space)


def live(limit_ref, s, first_row, shape):
    sec_dev = limit_ref.shape[0] // 2
    repeat = shape[1] // LANES
    rows = jnp.concatenate([limit_ref[s:s + 1, :]] * repeat, axis=1)
    cols = jnp.concatenate([limit_ref[sec_dev + s:sec_dev + s + 1, :]] * repeat, axis=1)
    row_ids = first_row + lax.broadcasted_iota(jnp.int32, shape, 0)
    col_ids = lax.broadcasted_iota(jnp.int32, shape, 1)
    return (row_ids < rows) & (col_ids < cols)


def energy_columns(level):
    missing = -level.shape[0] % 8
    if missing:
        level = jnp.concatenate([level, jnp.zeros((missing, level.shape[1]), F32)], axis=0)
    return level.T


def spread(array, width):
    return jnp.concatenate([array] * (width // LANES), axis=1)


def quotient(value, count):
    return value >> (count.bit_length() - 1) if count & (count - 1) == 0 else lax.div(value, count)


def remainder(value, count):
    return value & (count - 1) if count & (count - 1) == 0 else lax.rem(value, count)


def fold(array):
    rows, width = array.shape
    return jnp.sum(array.reshape(rows // 8, 8, width), axis=0)


def total(array):
    return jnp.sum(jnp.sum(array, axis=0, keepdims=True), axis=1, keepdims=True)


def header(slot, scalars, shape=(HEAD, LANES)):
    row_ids = lax.broadcasted_iota(jnp.int32, shape, 0)
    head = jnp.where(row_ids == 0, slot.astype(F32), 0.0)
    row = 1
    for scalar in scalars:
        rest = jnp.broadcast_to(scalar, shape)
        for _ in range(PARTS):
            piece = rest.astype(BF16).astype(F32)
            head = jnp.where(row_ids == row, piece, head)
            rest = rest - piece
            row += 1
    return head.astype(BF16)


def head_scalar(head_sum, index):
    first = 1 + PARTS * index
    return jnp.sum(head_sum[first:first + PARTS], axis=0, keepdims=True)


def most_pairs(pairs, sec_count):
    return pairs // sec_count + 1


def load_kernel(
    psi_hbm, left_hbm, pairing_hbm, rows_hbm, cols_hbm, energy_hbm,
    start_ref, left_ref, list_ref, limit_ref, energy_ref, scalar_ref,
    psi_ref, level_ref, rows_ref, cols_ref, pairing_ref, entry_ref, count_ref, sems,
):
    sec_dev, half, width = psi_ref.shape
    terms = left_ref.shape[0]
    sec_count = list_ref.shape[0]
    cap = most_pairs(terms * sec_dev, sec_count)
    pairs = [
        (rows_hbm, rows_ref), (cols_hbm, cols_ref), (energy_hbm, level_ref),
        (pairing_hbm, pairing_ref), (psi_hbm, psi_ref),
    ]
    for t in range(left_ref.shape[0]):
        pairs.append((left_hbm.at[t], left_ref.at[t]))
    copies = [
        pltpu.make_async_copy(source, target, sems.at[i])
        for i, (source, target) in enumerate(pairs)
    ]
    for copy in copies:
        copy.start()
    for owner in range(sec_count):
        count_ref[owner] = 0
        entry_ref[owner, cap] = 0
        for i in range(cap):
            entry_ref[owner, i] = terms * sec_dev
    for copy in copies[:3]:
        copy.wait()
    for s in range(sec_dev):
        limit_ref[s:s + 1, :] = jnp.full((1, LANES), rows_ref[s], jnp.int32)
        limit_ref[sec_dev + s:sec_dev + s + 1, :] = jnp.full((1, LANES), cols_ref[s], jnp.int32)
    columns = energy_columns(level_ref[...])
    for s in range(sec_dev):
        energy_ref[s] = jnp.broadcast_to(columns[:, s:s + 1], (half, LANES))
    copies[3].wait()
    for t in range(terms):
        for s in range(sec_dev):
            target = pairing_ref[s, t]
            owner = quotient(target, sec_dev)
            count = count_ref[owner]
            entry_ref[owner, count] = t * sec_dev + s
            entry_ref[owner, cap] = remainder(target, sec_dev)
            count_ref[owner] = count + 1
    entries = pltpu.make_async_copy(entry_ref, list_ref, sems.at[len(copies)])
    entries.start()
    copies[4].wait()
    first_row = lax.axis_index("rep") * half
    norm = jnp.zeros((8, width), F32)
    level = jnp.zeros((8, width), F32)
    for s in range(sec_dev):
        vector = jnp.where(
            live(limit_ref, s, first_row, (half, width)), psi_ref[s].astype(F32), 0.0
        )
        start_ref[s] = vector.astype(BF16)
        square = vector * vector
        norm += fold(square)
        level += fold(square * spread(energy_ref[s], width))
    scalar_ref[0:8, :] = norm
    scalar_ref[8:16, :] = level
    for copy in copies[5:]:
        copy.wait()
    entries.wait()


def product_kernel(is_first, split, paired, rep_count, sec_count, *refs):
    refs = list(refs)
    take = lambda count: [refs.pop(0) for _ in range(count)]
    list_ref, left_ref, right_ref = take(3)
    if is_first:
        start_ref, limit_ref, scalar_ref = take(3)
        psi_refs = take(rep_count - 1)
        level_refs = take(rep_count - 1)
    else:
        (first_ref,) = take(1)
        vector_refs = take(rep_count)
    out_refs = take(sec_count if split else 1)
    if not is_first:
        (first_hbm,) = take(1)
    inner_ref, entry_ref, sems = refs
    terms, sec_dev, half, width = left_ref.shape
    pairs = terms * sec_dev
    cap = most_pairs(pairs, sec_count)
    rep = lax.axis_index("rep")
    sec = lax.axis_index("sec")
    fetch = pltpu.make_async_copy(list_ref, entry_ref, sems.at[0])
    fetch.start()
    if not is_first:
        put = pltpu.make_async_copy(first_ref, first_hbm, sems.at[1])
        put.start()
    inner_ref[pairs] = jnp.zeros((half, width), BF16)

    def first_row(step):
        return remainder(rep + step, rep_count) * half

    if is_first:
        folded = [scalar_ref[0:8, :], scalar_ref[8:16, :]]
        columns = [energy_columns(ref[...]) for ref in level_refs]
    for s in range(sec_dev):
        if is_first:
            blocks = [start_ref[s]]
            for step in range(1, rep_count):
                psi = psi_refs[step - 1][s]
                mask = live(limit_ref, s, first_row(step), (half, width))
                blocks.append(jnp.where(mask, psi.astype(F32), 0.0).astype(BF16))
        else:
            blocks = [ref[s * half:(s + 1) * half] for ref in vector_refs]
        vector = jnp.concatenate(blocks, axis=0)
        for turn in range(1, rep_count):
            turned = blocks[rep_count - turn:] + blocks[:rep_count - turn]
            vector = jnp.where(rep == turn, jnp.concatenate(turned, axis=0), vector)
        inner = jnp.dot(
            left_ref[:, s].reshape(terms * half, width), vector, preferred_element_type=F32
        ).astype(BF16)
        for t in range(terms):
            inner_ref[t * sec_dev + s] = inner[t * half:(t + 1) * half]
        if is_first:
            for step in range(1, rep_count):
                block = blocks[step].astype(F32)
                square = block * block
                energy = jnp.broadcast_to(columns[step - 1][:, s:s + 1], (half, width))
                folded = [folded[0] + fold(square), folded[1] + fold(square * energy)]
    if is_first:
        scalars = [total(array) for array in folded]
    else:
        head = sum(ref[sec_dev * half:].astype(F32) for ref in vector_refs)
        scalars = [head_scalar(head, i)[:, :LANES] for i in range(2)]
    fetch.wait()
    for d in range(sec_count):
        if not split:
            owner = d
        elif paired:
            owner = sec ^ d
        else:
            owner = remainder(sec + d, sec_count)
        packet = jnp.zeros((half, width), F32)
        for i in range(cap):
            pair = entry_ref[owner, i]
            term = jnp.minimum(quotient(pair, sec_dev), terms - 1)
            packet += jnp.dot(inner_ref[pair], right_ref[term], preferred_element_type=F32)
        out = out_refs[d] if split else out_refs[0].at[d]
        for column in range(width // LANES):
            out[column * half:(column + 1) * half, :] = packet[
                :, column * LANES:(column + 1) * LANES
            ].astype(BF16)
        out[width // LANES * half:, :] = header(entry_ref[owner, cap], scalars)
    if not is_first:
        put.wait()


def sigma_packets(is_first, split, paired, rep_count, lists, left_env, right_env, more):
    terms, sec_dev, half, width = left_env.shape
    sec_count = lax.axis_size("sec")
    packet = (width // LANES * half + HEAD, LANES)
    if split:
        outs = [jax.ShapeDtypeStruct(packet, BF16)] * sec_count
    else:
        outs = [jax.ShapeDtypeStruct((sec_count,) + packet, BF16)]
    out_specs = [whole(pltpu.VMEM)] * len(outs)
    if not is_first:
        outs.append(jax.ShapeDtypeStruct((sec_dev, half, width), BF16))
        out_specs.append(whole(pltpu.HBM))
    pair_flops = 2 * half * width * width * 2
    operands = [lists, left_env, right_env, *more]
    return pl.pallas_call(
        functools.partial(product_kernel, is_first, split, paired, rep_count, sec_count),
        out_shape=outs,
        in_specs=[whole(pltpu.VMEM)] * len(operands),
        out_specs=out_specs,
        scratch_shapes=[
            pltpu.VMEM((terms * sec_dev + 1, half, width), BF16),
            pltpu.SMEM(lists.shape, jnp.int32),
            pltpu.SemaphoreType.DMA((2,)),
        ],
        compiler_params=pltpu.CompilerParams(vmem_limit_bytes=VMEM_BYTES),
        cost_estimate=pl.CostEstimate(
            flops=terms * sec_dev * pair_flops,
            bytes_accessed=2 * (left_env.size + right_env.size),
            transcendentals=0,
        ),
        name="products_first" if is_first else "products_second",
    )(*operands)


def exchange(packets, split, paired, order, groups, apart=False):
    sec_count = lax.axis_size("sec")
    op_count = lax.axis_size("op")
    op_turns = [
        [(i, (i + step) % op_count) for i in range(op_count)] for step in range(1, op_count)
    ]
    over_op = lambda packet: [lax.ppermute(packet, "op", turn) for turn in op_turns]
    rep_count = lax.axis_size("rep")

    def over_op_of(packet, core):
        return [
            lax.ppermute(
                packet,
                ("op", "rep"),
                [(i * rep_count + core, j * rep_count + core) for i, j in turn],
            )
            for turn in op_turns
        ]

    if not split:
        arrived = lax.all_to_all(packets[0], "sec", split_axis=0, concat_axis=0, tiled=True)
        return [arrived] + over_op(arrived), []
    crossed = []
    packets = list(packets)
    if apart:
        for core in range(rep_count - 1, 0, -1):
            crossed.append(over_op_of(packets[0], core))
        last = order[-1]
        packets[last] = lax.optimization_barrier((packets[last], crossed))[0]
    arrived = {0: packets[0]}
    for step in order:
        reach = (lambda i: i ^ step) if paired else (lambda i: (i + step) % sec_count)
        turn = [(i, reach(i)) for i in range(sec_count)]
        arrived[step] = lax.ppermute(packets[step], "sec", turn)
    for group in groups:
        if apart and group == [0]:
            crossed.append(over_op_of(packets[0], 0))
        else:
            crossed.append(over_op(jnp.stack([arrived[step] for step in group])))
    return [arrived[step] for step in [0, *order]] + sum(crossed[:-1], []), crossed[-1]


def views(refs):
    return [
        view
        for ref in refs
        for view in ([ref] if len(ref.shape) == 2 else [ref.at[i] for i in range(ref.shape[0])])
    ]


def add_packets(packet_refs, split, half, base_ref):
    sec_dev, _, width = base_ref.shape
    own = lax.axis_size("sec") if split else 1
    body_rows = width // LANES * half
    if split:
        packet_refs = views(packet_refs)
        heads = [ref[body_rows:].astype(F32) for ref in packet_refs]
        for column in range(width // LANES):
            lanes = slice(column * LANES, (column + 1) * LANES)
            for s in range(sec_dev):
                part = base_ref[s, :, lanes]
                for ref, head in zip(packet_refs, heads):
                    body = ref[column * half:(column + 1) * half].astype(F32)
                    part += jnp.where(head[0:1] == s, body, 0.0)
                base_ref[s, :, lanes] = part
        return sum(heads[1:own], heads[0])

    head_sum = jnp.zeros((HEAD, LANES), F32)
    for index, ref in enumerate(packet_refs):
        def add_one(p, carry):
            head = ref[p, body_rows:, :].astype(F32)
            for column in range(width // LANES):
                body = ref[p, column * half:(column + 1) * half, :].astype(F32)
                lanes = slice(column * LANES, (column + 1) * LANES)
                for s in range(sec_dev):
                    base_ref[s, :, lanes] += jnp.where(head[0:1] == s, body, 0.0)
            return carry + head
        result = lax.fori_loop(0, ref.shape[0], add_one, jnp.zeros((HEAD, LANES), F32))
        if index < own:
            head_sum = head_sum + result
    return head_sum


def late_sum(packet_refs, s, half, width):
    body_rows = width // LANES * half
    value = jnp.zeros((half, width), F32)
    for ref in views(packet_refs):
        body = jnp.concatenate(
            [ref[c * half:(c + 1) * half].astype(F32) for c in range(width // LANES)], axis=1
        )
        slot = spread(ref[body_rows:].astype(F32)[0:1], width)
        value += jnp.where(slot == s, body, 0.0)
    return value


def first_early_kernel(split, count, *refs):
    packet_refs = refs[:count]
    start_ref, energy_ref, base_ref, scalar_ref = refs[count:]
    sec_dev, half, width = start_ref.shape
    for s in range(sec_dev):
        base_ref[s] = spread(energy_ref[s], width) * start_ref[s].astype(F32)
    head_sum = add_packets(packet_refs, split, half, base_ref)
    norm = head_scalar(head_sum, 0)
    scalar_ref[0:1] = norm
    scalar_ref[1:2] = head_scalar(head_sum, 1) / norm


def first_kernel(count, *refs):
    packet_refs = refs[:count]
    limit_ref, start_ref, base_ref, scalar_ref, first_ref, one_ref, vec_ref = refs[count:]
    sec_dev, half, width = start_ref.shape
    shift = spread(scalar_ref[1:2], width)
    first_row = lax.axis_index("rep") * half
    cross = jnp.zeros((8, width), F32)
    square = jnp.zeros((8, width), F32)
    for s in range(sec_dev):
        mask = live(limit_ref, s, first_row, (half, width))
        start = start_ref[s].astype(F32)
        one = jnp.where(mask, base_ref[s] + late_sum(packet_refs, s, half, width), 0.0)
        one_ref[s] = one
        first_ref[s] = one.astype(BF16)
        vector = one - shift * start
        vec_ref[s * half:(s + 1) * half] = vector.astype(BF16)
        cross += fold(start * vector)
        square += fold(vector * vector)
    scalars = (total(cross), total(square))
    vec_ref[sec_dev * half:] = header(jnp.int32(0), scalars, (MORE_ROWS, width))


def second_early_kernel(split, count, entries, *refs):
    packet_refs = refs[:count]
    vec_ref, energy_ref, one_ref, scalar_ref, base_ref, scale_ref = refs[count:]
    sec_dev, half, width = one_ref.shape
    for s in range(sec_dev):
        vector = vec_ref[s * half:(s + 1) * half].astype(F32)
        base_ref[s] = spread(energy_ref[s], width) * vector
    head_sum = add_packets(packet_refs, split, half, base_ref)
    cross = head_scalar(head_sum, 0)
    square = head_scalar(head_sum, 1)
    excess = cross / scalar_ref[0:1]
    resid_sq = jnp.maximum(square - excess * cross, 0.0)
    scale = lax.rsqrt(resid_sq / entries + EPSILON)
    scale_ref[...] = jnp.broadcast_to(scale, scale_ref.shape)
    for s in range(sec_dev):
        base_ref[s] = base_ref[s] - spread(excess, width) * one_ref[s]


def second_kernel(count, *refs):
    packet_refs = refs[:count]
    limit_ref, base_ref, scale_ref, second_ref = refs[count:]
    sec_dev, half, width = base_ref.shape
    scale = spread(scale_ref[0:1], width)
    first_row = lax.axis_index("rep") * half
    for s in range(sec_dev):
        mask = live(limit_ref, s, first_row, (half, width))
        value = scale * (base_ref[s] + late_sum(packet_refs, s, half, width))
        second_ref[s] = jnp.where(mask, value, 0.0).astype(BF16)


def call(kernel, name, outs, *operands, flops=0):
    return pl.pallas_call(
        kernel,
        out_shape=outs,
        in_specs=[whole(pltpu.VMEM)] * len(operands),
        out_specs=[whole(pltpu.VMEM)] * len(outs),
        compiler_params=pltpu.CompilerParams(vmem_limit_bytes=VMEM_BYTES),
        cost_estimate=pl.CostEstimate(flops=flops, bytes_accessed=0, transcendentals=0),
        name=name,
    )(*operands)


def body(psi, left_env, right_env, pairing, block_rows, block_cols, energy):
    sec_count = lax.axis_size("sec")
    op_count = lax.axis_size("op")
    rep_count = lax.axis_size("rep")
    terms, sec_dev, half, width = left_env.shape
    entries = sec_count * sec_dev * rep_count * half * width
    split = sec_count * op_count <= 8
    can_pair = sec_count & (sec_count - 1) == 0
    steps = list(range(1, sec_count))
    first_plan = (False, steps, [[0], [1], [2, 3]], True)
    second_groups = [[0]] + [[k] for k in steps[1:2] + steps[:1] + steps[2:]]
    second_plan = (can_pair, steps[1:2] + steps[:1] + steps[2:], second_groups, True)
    params = pltpu.CompilerParams(vmem_limit_bytes=VMEM_BYTES)
    vec_shape = (sec_dev, half, width)
    vec_bf16 = jax.ShapeDtypeStruct(vec_shape, BF16)

    def from_others(array):
        arrays = []
        for step in range(1, rep_count):
            turn = [((i + step) % rep_count, i) for i in range(rep_count)]
            arrays.append(lax.ppermute(array, "rep", turn))
        return arrays

    psi_others = from_others(psi)
    level_others = from_others(energy)
    start, left_env, lists, limits, levels, scalars = pl.pallas_call(
        load_kernel,
        out_shape=[
            vec_bf16,
            jax.ShapeDtypeStruct(left_env.shape, BF16),
            jax.ShapeDtypeStruct((sec_count, LANES), jnp.int32),
            jax.ShapeDtypeStruct((2 * sec_dev, LANES), jnp.int32),
            jax.ShapeDtypeStruct((sec_dev, half, LANES), F32),
            jax.ShapeDtypeStruct((16, width), F32),
        ],
        in_specs=[whole(pltpu.HBM)] * 6,
        out_specs=[whole(pltpu.VMEM)] * 6,
        scratch_shapes=[
            pltpu.VMEM(vec_shape, BF16),
            pltpu.VMEM((sec_dev, half), F32),
            pltpu.SMEM((sec_dev,), jnp.int32),
            pltpu.SMEM((sec_dev,), jnp.int32),
            pltpu.SMEM((sec_dev, terms), jnp.int32),
            pltpu.SMEM((sec_count, LANES), jnp.int32),
            pltpu.SMEM((sec_count,), jnp.int32),
            pltpu.SemaphoreType.DMA((6 + terms,)),
        ],
        compiler_params=params,
        name="load",
    )(*(
        pltpu.with_memory_space_constraint(array, pltpu.HBM)
        for array in (psi, left_env, pairing.T, block_rows, block_cols, energy)
    ))

    block_f32 = jax.ShapeDtypeStruct(vec_shape, F32)
    row_f32 = jax.ShapeDtypeStruct((8, LANES), F32)

    packets = sigma_packets(
        True, split, first_plan[0], rep_count, lists, left_env, right_env,
        [start, limits, scalars, *psi_others, *level_others],
    )
    early, late = exchange(packets, split, *first_plan)
    base, scalars = call(
        functools.partial(first_early_kernel, split, len(early)), "combine_first_early",
        [block_f32, row_f32], *early, start, levels, flops=EARLY_FLOPS,
    )
    first, sigma_one, vector = call(
        functools.partial(first_kernel, len(late)), "combine_first",
        [
            pltpu.VMEM(vec_shape, BF16),
            block_f32,
            jax.ShapeDtypeStruct((sec_dev * half + MORE_ROWS, width), BF16),
        ],
        *late, limits, start, base, scalars,
    )

    *packets, first_out = sigma_packets(
        False, split, second_plan[0], rep_count, lists, left_env, right_env,
        [first, vector, *from_others(vector)],
    )
    early, late = exchange(packets, split, *second_plan)
    base, scale = call(
        functools.partial(second_early_kernel, split, len(early), entries),
        "combine_second_early", [block_f32, row_f32], *early, vector, levels, sigma_one, scalars,
        flops=10**8,
    )
    (second_out,) = call(
        functools.partial(second_kernel, len(late)), "combine_second", [vec_bf16],
        *late, limits, base, scale,
    )
    return (first_out, second_out)


def solution(mesh):
    return jax.shard_map(
        body,
        mesh=mesh,
        in_specs=(
            P(("grp", "sec"), "rep", None),
            P(("grp", "op"), "sec", "rep", None),
            P(("grp", "op"), None, None),
            P(("grp", "op"), "sec"),
            P(("grp", "sec")),
            P(("grp", "sec")),
            P(("grp", "sec"), "rep"),
        ),
        out_specs=(P(("grp", "sec"), "rep", None), P(("grp", "sec"), "rep", None)),
        check_vma=False,
    )
```

```python
import functools

import jax
import jax.numpy as jnp
from jax import lax
from jax.experimental import pallas as pl
from jax.experimental.pallas import tpu as pltpu
from jax.sharding import PartitionSpec as P

EPSILON = 1e-06
HEAD = 8
PARTS = 3
EARLY_FLOPS = 10**9
MORE_ROWS = 16
LANES = 128
VMEM_BYTES = 24 * 1024 * 1024
F32 = jnp.float32
BF16 = jnp.bfloat16


def whole(space):
    return pl.BlockSpec(memory_space=space)


def live(limit_ref, s, first_row, shape):
    sec_dev = limit_ref.shape[0] // 2
    repeat = shape[1] // LANES
    rows = jnp.concatenate([limit_ref[s:s + 1, :]] * repeat, axis=1)
    cols = jnp.concatenate([limit_ref[sec_dev + s:sec_dev + s + 1, :]] * repeat, axis=1)
    row_ids = first_row + lax.broadcasted_iota(jnp.int32, shape, 0)
    col_ids = lax.broadcasted_iota(jnp.int32, shape, 1)
    return (row_ids < rows) & (col_ids < cols)


def energy_columns(level):
    missing = -level.shape[0] % 8
    if missing:
        level = jnp.concatenate([level, jnp.zeros((missing, level.shape[1]), F32)], axis=0)
    return level.T


def spread(array, width):
    return jnp.concatenate([array] * (width // LANES), axis=1)


def quotient(value, count):
    return value >> (count.bit_length() - 1) if count & (count - 1) == 0 else lax.div(value, count)


def remainder(value, count):
    return value & (count - 1) if count & (count - 1) == 0 else lax.rem(value, count)


def fold(array):
    rows, width = array.shape
    return jnp.sum(array.reshape(rows // 8, 8, width), axis=0)


def total(array):
    return jnp.sum(jnp.sum(array, axis=0, keepdims=True), axis=1, keepdims=True)


def header(slot, scalars, shape=(HEAD, LANES)):
    row_ids = lax.broadcasted_iota(jnp.int32, shape, 0)
    head = jnp.where(row_ids == 0, slot.astype(F32), 0.0)
    row = 1
    for scalar in scalars:
        rest = jnp.broadcast_to(scalar, shape)
        for _ in range(PARTS):
            piece = rest.astype(BF16).astype(F32)
            head = jnp.where(row_ids == row, piece, head)
            rest = rest - piece
            row += 1
    return head.astype(BF16)


def head_scalar(head_sum, index):
    first = 1 + PARTS * index
    return jnp.sum(head_sum[first:first + PARTS], axis=0, keepdims=True)


def most_pairs(pairs, sec_count):
    return pairs // sec_count + 1


def load_kernel(
    psi_hbm, left_hbm, pairing_hbm, rows_hbm, cols_hbm, energy_hbm,
    start_ref, left_ref, list_ref, limit_ref, energy_ref, scalar_ref,
    psi_ref, level_ref, rows_ref, cols_ref, pairing_ref, entry_ref, count_ref, sems,
):
    sec_dev, half, width = psi_ref.shape
    terms = left_ref.shape[0]
    sec_count = list_ref.shape[0]
    cap = most_pairs(terms * sec_dev, sec_count)
    pairs = [
        (rows_hbm, rows_ref), (cols_hbm, cols_ref), (energy_hbm, level_ref),
        (pairing_hbm, pairing_ref), (psi_hbm, psi_ref),
    ]
    for t in range(left_ref.shape[0]):
        pairs.append((left_hbm.at[t], left_ref.at[t]))
    copies = [
        pltpu.make_async_copy(source, target, sems.at[i])
        for i, (source, target) in enumerate(pairs)
    ]
    for copy in copies:
        copy.start()
    for owner in range(sec_count):
        count_ref[owner] = 0
        entry_ref[owner, cap] = 0
        for i in range(cap):
            entry_ref[owner, i] = terms * sec_dev
    for copy in copies[:3]:
        copy.wait()
    for s in range(sec_dev):
        limit_ref[s:s + 1, :] = jnp.full((1, LANES), rows_ref[s], jnp.int32)
        limit_ref[sec_dev + s:sec_dev + s + 1, :] = jnp.full((1, LANES), cols_ref[s], jnp.int32)
    columns = energy_columns(level_ref[...])
    for s in range(sec_dev):
        energy_ref[s] = jnp.broadcast_to(columns[:, s:s + 1], (half, LANES))
    copies[3].wait()
    for t in range(terms):
        for s in range(sec_dev):
            target = pairing_ref[s, t]
            owner = quotient(target, sec_dev)
            count = count_ref[owner]
            entry_ref[owner, count] = t * sec_dev + s
            entry_ref[owner, cap] = remainder(target, sec_dev)
            count_ref[owner] = count + 1
    entries = pltpu.make_async_copy(entry_ref, list_ref, sems.at[len(copies)])
    entries.start()
    copies[4].wait()
    first_row = lax.axis_index("rep") * half
    norm = jnp.zeros((8, width), F32)
    level = jnp.zeros((8, width), F32)
    for s in range(sec_dev):
        vector = jnp.where(
            live(limit_ref, s, first_row, (half, width)), psi_ref[s].astype(F32), 0.0
        )
        start_ref[s] = vector.astype(BF16)
        square = vector * vector
        norm += fold(square)
        level += fold(square * spread(energy_ref[s], width))
    scalar_ref[0:8, :] = norm
    scalar_ref[8:16, :] = level
    for copy in copies[5:]:
        copy.wait()
    entries.wait()


def product_kernel(is_first, split, paired, rep_count, sec_count, *refs):
    refs = list(refs)
    take = lambda count: [refs.pop(0) for _ in range(count)]
    list_ref, left_ref, right_ref = take(3)
    if is_first:
        start_ref, limit_ref, scalar_ref = take(3)
        psi_refs = take(rep_count - 1)
        level_refs = take(rep_count - 1)
    else:
        (first_ref,) = take(1)
        vector_refs = take(rep_count)
    out_refs = take(sec_count if split else 1)
    if not is_first:
        (first_hbm,) = take(1)
    inner_ref, entry_ref, sems = refs
    terms, sec_dev, half, width = left_ref.shape
    pairs = terms * sec_dev
    cap = most_pairs(pairs, sec_count)
    rep = lax.axis_index("rep")
    sec = lax.axis_index("sec")
    fetch = pltpu.make_async_copy(list_ref, entry_ref, sems.at[0])
    fetch.start()
    if not is_first:
        put = pltpu.make_async_copy(first_ref, first_hbm, sems.at[1])
        put.start()
    inner_ref[pairs] = jnp.zeros((half, width), BF16)

    def first_row(step):
        return remainder(rep + step, rep_count) * half

    if is_first:
        folded = [scalar_ref[0:8, :], scalar_ref[8:16, :]]
        columns = [energy_columns(ref[...]) for ref in level_refs]
    for s in range(sec_dev):
        if is_first:
            blocks = [start_ref[s]]
            for step in range(1, rep_count):
                psi = psi_refs[step - 1][s]
                mask = live(limit_ref, s, first_row(step), (half, width))
                blocks.append(jnp.where(mask, psi.astype(F32), 0.0).astype(BF16))
        else:
            blocks = [ref[s * half:(s + 1) * half] for ref in vector_refs]
        vector = jnp.concatenate(blocks, axis=0)
        for turn in range(1, rep_count):
            turned = blocks[rep_count - turn:] + blocks[:rep_count - turn]
            vector = jnp.where(rep == turn, jnp.concatenate(turned, axis=0), vector)
        inner = jnp.dot(
            left_ref[:, s].reshape(terms * half, width), vector, preferred_element_type=F32
        ).astype(BF16)
        for t in range(terms):
            inner_ref[t * sec_dev + s] = inner[t * half:(t + 1) * half]
        if is_first:
            for step in range(1, rep_count):
                block = blocks[step].astype(F32)
                square = block * block
                energy = jnp.broadcast_to(columns[step - 1][:, s:s + 1], (half, width))
                folded = [folded[0] + fold(square), folded[1] + fold(square * energy)]
    if is_first:
        scalars = [total(array) for array in folded]
    else:
        head = sum(ref[sec_dev * half:].astype(F32) for ref in vector_refs)
        scalars = [head_scalar(head, i)[:, :LANES] for i in range(2)]
    fetch.wait()
    for d in range(sec_count):
        if not split:
            owner = d
        elif paired:
            owner = sec ^ d
        else:
            owner = remainder(sec + d, sec_count)
        packet = jnp.zeros((half, width), F32)
        for i in range(cap):
            pair = entry_ref[owner, i]
            term = jnp.minimum(quotient(pair, sec_dev), terms - 1)
            packet += jnp.dot(inner_ref[pair], right_ref[term], preferred_element_type=F32)
        out = out_refs[d] if split else out_refs[0].at[d]
        for column in range(width // LANES):
            out[column * half:(column + 1) * half, :] = packet[
                :, column * LANES:(column + 1) * LANES
            ].astype(BF16)
        out[width // LANES * half:, :] = header(entry_ref[owner, cap], scalars)
    if not is_first:
        put.wait()


def sigma_packets(is_first, split, paired, rep_count, lists, left_env, right_env, more):
    terms, sec_dev, half, width = left_env.shape
    sec_count = lax.axis_size("sec")
    packet = (width // LANES * half + HEAD, LANES)
    if split:
        outs = [jax.ShapeDtypeStruct(packet, BF16)] * sec_count
    else:
        outs = [jax.ShapeDtypeStruct((sec_count,) + packet, BF16)]
    out_specs = [whole(pltpu.VMEM)] * len(outs)
    if not is_first:
        outs.append(jax.ShapeDtypeStruct((sec_dev, half, width), BF16))
        out_specs.append(whole(pltpu.HBM))
    pair_flops = 2 * half * width * width * 2
    operands = [lists, left_env, right_env, *more]
    return pl.pallas_call(
        functools.partial(product_kernel, is_first, split, paired, rep_count, sec_count),
        out_shape=outs,
        in_specs=[whole(pltpu.VMEM)] * len(operands),
        out_specs=out_specs,
        scratch_shapes=[
            pltpu.VMEM((terms * sec_dev + 1, half, width), BF16),
            pltpu.SMEM(lists.shape, jnp.int32),
            pltpu.SemaphoreType.DMA((2,)),
        ],
        compiler_params=pltpu.CompilerParams(vmem_limit_bytes=VMEM_BYTES),
        cost_estimate=pl.CostEstimate(
            flops=terms * sec_dev * pair_flops,
            bytes_accessed=2 * (left_env.size + right_env.size),
            transcendentals=0,
        ),
        name="products_first" if is_first else "products_second",
    )(*operands)


def exchange(packets, split, paired, order, groups):
    sec_count = lax.axis_size("sec")
    op_count = lax.axis_size("op")
    op_turns = [
        [(i, (i + step) % op_count) for i in range(op_count)] for step in range(1, op_count)
    ]
    over_op = lambda packet: [lax.ppermute(packet, "op", turn) for turn in op_turns]
    if not split:
        arrived = lax.all_to_all(packets[0], "sec", split_axis=0, concat_axis=0, tiled=True)
        return [arrived] + over_op(arrived), []
    arrived = {0: packets[0]}
    for step in order:
        reach = (lambda i: i ^ step) if paired else (lambda i: (i + step) % sec_count)
        turn = [(i, reach(i)) for i in range(sec_count)]
        arrived[step] = lax.ppermute(packets[step], "sec", turn)
    crossed = [over_op(jnp.stack([arrived[step] for step in group])) for group in groups]
    return [arrived[step] for step in [0, *order]] + sum(crossed[:-1], []), crossed[-1]


def views(refs):
    return [
        view
        for ref in refs
        for view in ([ref] if len(ref.shape) == 2 else [ref.at[i] for i in range(ref.shape[0])])
    ]


def add_packets(packet_refs, split, half, base_ref):
    sec_dev, _, width = base_ref.shape
    own = lax.axis_size("sec") if split else 1
    body_rows = width // LANES * half
    if split:
        packet_refs = views(packet_refs)
        heads = [ref[body_rows:].astype(F32) for ref in packet_refs]
        for column in range(width // LANES):
            lanes = slice(column * LANES, (column + 1) * LANES)
            for s in range(sec_dev):
                part = base_ref[s, :, lanes]
                for ref, head in zip(packet_refs, heads):
                    body = ref[column * half:(column + 1) * half].astype(F32)
                    part += jnp.where(head[0:1] == s, body, 0.0)
                base_ref[s, :, lanes] = part
        return sum(heads[1:own], heads[0])

    head_sum = jnp.zeros((HEAD, LANES), F32)
    for index, ref in enumerate(packet_refs):
        def add_one(p, carry):
            head = ref[p, body_rows:, :].astype(F32)
            for column in range(width // LANES):
                body = ref[p, column * half:(column + 1) * half, :].astype(F32)
                lanes = slice(column * LANES, (column + 1) * LANES)
                for s in range(sec_dev):
                    base_ref[s, :, lanes] += jnp.where(head[0:1] == s, body, 0.0)
            return carry + head
        result = lax.fori_loop(0, ref.shape[0], add_one, jnp.zeros((HEAD, LANES), F32))
        if index < own:
            head_sum = head_sum + result
    return head_sum


def late_sum(packet_refs, s, half, width):
    body_rows = width // LANES * half
    value = jnp.zeros((half, width), F32)
    for ref in views(packet_refs):
        body = jnp.concatenate(
            [ref[c * half:(c + 1) * half].astype(F32) for c in range(width // LANES)], axis=1
        )
        slot = spread(ref[body_rows:].astype(F32)[0:1], width)
        value += jnp.where(slot == s, body, 0.0)
    return value


def first_early_kernel(split, count, *refs):
    packet_refs = refs[:count]
    start_ref, energy_ref, base_ref, scalar_ref = refs[count:]
    sec_dev, half, width = start_ref.shape
    for s in range(sec_dev):
        base_ref[s] = spread(energy_ref[s], width) * start_ref[s].astype(F32)
    head_sum = add_packets(packet_refs, split, half, base_ref)
    norm = head_scalar(head_sum, 0)
    scalar_ref[0:1] = norm
    scalar_ref[1:2] = head_scalar(head_sum, 1) / norm


def first_kernel(count, *refs):
    packet_refs = refs[:count]
    limit_ref, start_ref, base_ref, scalar_ref, first_ref, one_ref, vec_ref = refs[count:]
    sec_dev, half, width = start_ref.shape
    shift = spread(scalar_ref[1:2], width)
    first_row = lax.axis_index("rep") * half
    cross = jnp.zeros((8, width), F32)
    square = jnp.zeros((8, width), F32)
    for s in range(sec_dev):
        mask = live(limit_ref, s, first_row, (half, width))
        start = start_ref[s].astype(F32)
        one = jnp.where(mask, base_ref[s] + late_sum(packet_refs, s, half, width), 0.0)
        one_ref[s] = one
        first_ref[s] = one.astype(BF16)
        vector = one - shift * start
        vec_ref[s * half:(s + 1) * half] = vector.astype(BF16)
        cross += fold(start * vector)
        square += fold(vector * vector)
    scalars = (total(cross), total(square))
    vec_ref[sec_dev * half:] = header(jnp.int32(0), scalars, (MORE_ROWS, width))


def second_early_kernel(split, count, entries, *refs):
    packet_refs = refs[:count]
    vec_ref, energy_ref, one_ref, scalar_ref, base_ref, scale_ref = refs[count:]
    sec_dev, half, width = one_ref.shape
    for s in range(sec_dev):
        vector = vec_ref[s * half:(s + 1) * half].astype(F32)
        base_ref[s] = spread(energy_ref[s], width) * vector
    head_sum = add_packets(packet_refs, split, half, base_ref)
    cross = head_scalar(head_sum, 0)
    square = head_scalar(head_sum, 1)
    excess = cross / scalar_ref[0:1]
    resid_sq = jnp.maximum(square - excess * cross, 0.0)
    scale = lax.rsqrt(resid_sq / entries + EPSILON)
    scale_ref[...] = jnp.broadcast_to(scale, scale_ref.shape)
    for s in range(sec_dev):
        base_ref[s] = base_ref[s] - spread(excess, width) * one_ref[s]


def second_kernel(count, *refs):
    packet_refs = refs[:count]
    limit_ref, base_ref, scale_ref, second_ref = refs[count:]
    sec_dev, half, width = base_ref.shape
    scale = spread(scale_ref[0:1], width)
    first_row = lax.axis_index("rep") * half
    for s in range(sec_dev):
        mask = live(limit_ref, s, first_row, (half, width))
        value = scale * (base_ref[s] + late_sum(packet_refs, s, half, width))
        second_ref[s] = jnp.where(mask, value, 0.0).astype(BF16)


def call(kernel, name, outs, *operands, flops=0):
    return pl.pallas_call(
        kernel,
        out_shape=outs,
        in_specs=[whole(pltpu.VMEM)] * len(operands),
        out_specs=[whole(pltpu.VMEM)] * len(outs),
        compiler_params=pltpu.CompilerParams(vmem_limit_bytes=VMEM_BYTES),
        cost_estimate=pl.CostEstimate(flops=flops, bytes_accessed=0, transcendentals=0),
        name=name,
    )(*operands)


def body(psi, left_env, right_env, pairing, block_rows, block_cols, energy):
    sec_count = lax.axis_size("sec")
    op_count = lax.axis_size("op")
    rep_count = lax.axis_size("rep")
    terms, sec_dev, half, width = left_env.shape
    entries = sec_count * sec_dev * rep_count * half * width
    split = sec_count * op_count <= 8
    can_pair = sec_count & (sec_count - 1) == 0
    steps = list(range(1, sec_count))
    first_plan = (False, steps, [[0]] + [[k] for k in steps[:-2]] + [steps[-2:]])
    second_groups = [[0]] + [[k] for k in steps[1:2] + steps[:1] + steps[2:]]
    second_plan = (can_pair, steps[1:2] + steps[:1] + steps[2:], second_groups)
    params = pltpu.CompilerParams(vmem_limit_bytes=VMEM_BYTES)
    vec_shape = (sec_dev, half, width)
    vec_bf16 = jax.ShapeDtypeStruct(vec_shape, BF16)

    def from_others(array):
        arrays = []
        for step in range(1, rep_count):
            turn = [((i + step) % rep_count, i) for i in range(rep_count)]
            arrays.append(lax.ppermute(array, "rep", turn))
        return arrays

    psi_others = from_others(psi)
    level_others = from_others(energy)
    start, left_env, lists, limits, levels, scalars = pl.pallas_call(
        load_kernel,
        out_shape=[
            vec_bf16,
            jax.ShapeDtypeStruct(left_env.shape, BF16),
            jax.ShapeDtypeStruct((sec_count, LANES), jnp.int32),
            jax.ShapeDtypeStruct((2 * sec_dev, LANES), jnp.int32),
            jax.ShapeDtypeStruct((sec_dev, half, LANES), F32),
            jax.ShapeDtypeStruct((16, width), F32),
        ],
        in_specs=[whole(pltpu.HBM)] * 6,
        out_specs=[whole(pltpu.VMEM)] * 6,
        scratch_shapes=[
            pltpu.VMEM(vec_shape, BF16),
            pltpu.VMEM((sec_dev, half), F32),
            pltpu.SMEM((sec_dev,), jnp.int32),
            pltpu.SMEM((sec_dev,), jnp.int32),
            pltpu.SMEM((sec_dev, terms), jnp.int32),
            pltpu.SMEM((sec_count, LANES), jnp.int32),
            pltpu.SMEM((sec_count,), jnp.int32),
            pltpu.SemaphoreType.DMA((6 + terms,)),
        ],
        compiler_params=params,
        name="load",
    )(*(
        pltpu.with_memory_space_constraint(array, pltpu.HBM)
        for array in (psi, left_env, pairing.T, block_rows, block_cols, energy)
    ))

    block_f32 = jax.ShapeDtypeStruct(vec_shape, F32)
    row_f32 = jax.ShapeDtypeStruct((8, LANES), F32)

    packets = sigma_packets(
        True, split, first_plan[0], rep_count, lists, left_env, right_env,
        [start, limits, scalars, *psi_others, *level_others],
    )
    early, late = exchange(packets, split, *first_plan)
    base, scalars = call(
        functools.partial(first_early_kernel, split, len(early)), "combine_first_early",
        [block_f32, row_f32], *early, start, levels, flops=EARLY_FLOPS,
    )
    first, sigma_one, vector = call(
        functools.partial(first_kernel, len(late)), "combine_first",
        [
            pltpu.VMEM(vec_shape, BF16),
            block_f32,
            jax.ShapeDtypeStruct((sec_dev * half + MORE_ROWS, width), BF16),
        ],
        *late, limits, start, base, scalars,
    )

    *packets, first_out = sigma_packets(
        False, split, second_plan[0], rep_count, lists, left_env, right_env,
        [first, vector, *from_others(vector)],
    )
    early, late = exchange(packets, split, *second_plan)
    base, scale = call(
        functools.partial(second_early_kernel, split, len(early), entries),
        "combine_second_early", [block_f32, row_f32], *early, vector, levels, sigma_one, scalars,
        flops=10**8,
    )
    (second_out,) = call(
        functools.partial(second_kernel, len(late)), "combine_second", [vec_bf16],
        *late, limits, base, scale,
    )
    return (first_out, second_out)


def solution(mesh):
    return jax.shard_map(
        body,
        mesh=mesh,
        in_specs=(
            P(("grp", "sec"), "rep", None),
            P(("grp", "op"), "sec", "rep", None),
            P(("grp", "op"), None, None),
            P(("grp", "op"), "sec"),
            P(("grp", "sec")),
            P(("grp", "sec")),
            P(("grp", "sec"), "rep"),
        ),
        out_specs=(P(("grp", "sec"), "rep", None), P(("grp", "sec"), "rep", None)),
        check_vma=False,
    )
```

```python
import functools

import jax
import jax.numpy as jnp
from jax import lax
from jax.experimental import pallas as pl
from jax.experimental.pallas import tpu as pltpu
from jax.sharding import PartitionSpec as P

EPSILON = 1e-06
HEAD = 8
PARTS = 3
EARLY_FLOPS = 10**9
MORE_ROWS = 16
LANES = 128
VMEM_BYTES = 24 * 1024 * 1024
F32 = jnp.float32
BF16 = jnp.bfloat16


def whole(space):
    return pl.BlockSpec(memory_space=space)


def live(limit_ref, s, first_row, shape):
    sec_dev = limit_ref.shape[0] // 2
    repeat = shape[1] // LANES
    rows = jnp.concatenate([limit_ref[s:s + 1, :]] * repeat, axis=1)
    cols = jnp.concatenate([limit_ref[sec_dev + s:sec_dev + s + 1, :]] * repeat, axis=1)
    row_ids = first_row + lax.broadcasted_iota(jnp.int32, shape, 0)
    col_ids = lax.broadcasted_iota(jnp.int32, shape, 1)
    return (row_ids < rows) & (col_ids < cols)


def energy_columns(level):
    missing = -level.shape[0] % 8
    if missing:
        level = jnp.concatenate([level, jnp.zeros((missing, level.shape[1]), F32)], axis=0)
    return level.T


def spread(array, width):
    return jnp.concatenate([array] * (width // LANES), axis=1)


def quotient(value, count):
    return value >> (count.bit_length() - 1) if count & (count - 1) == 0 else lax.div(value, count)


def remainder(value, count):
    return value & (count - 1) if count & (count - 1) == 0 else lax.rem(value, count)


def fold(array):
    rows, width = array.shape
    return jnp.sum(array.reshape(rows // 8, 8, width), axis=0)


def total(array):
    return jnp.sum(jnp.sum(array, axis=0, keepdims=True), axis=1, keepdims=True)


def header(slot, scalars, shape=(HEAD, LANES)):
    row_ids = lax.broadcasted_iota(jnp.int32, shape, 0)
    head = jnp.where(row_ids == 0, slot.astype(F32), 0.0)
    row = 1
    for scalar in scalars:
        rest = jnp.broadcast_to(scalar, shape)
        for _ in range(PARTS):
            piece = rest.astype(BF16).astype(F32)
            head = jnp.where(row_ids == row, piece, head)
            rest = rest - piece
            row += 1
    return head.astype(BF16)


def head_scalar(head_sum, index):
    first = 1 + PARTS * index
    return jnp.sum(head_sum[first:first + PARTS], axis=0, keepdims=True)


def most_pairs(pairs, sec_count):
    return pairs // sec_count + 1


def load_kernel(
    psi_hbm, left_hbm, pairing_hbm, rows_hbm, cols_hbm, energy_hbm,
    start_ref, left_ref, list_ref, limit_ref, energy_ref, scalar_ref,
    psi_ref, level_ref, rows_ref, cols_ref, pairing_ref, entry_ref, count_ref, sems,
):
    sec_dev, half, width = psi_ref.shape
    terms = left_ref.shape[0]
    sec_count = list_ref.shape[0]
    cap = most_pairs(terms * sec_dev, sec_count)
    pairs = [
        (rows_hbm, rows_ref), (cols_hbm, cols_ref), (energy_hbm, level_ref),
        (pairing_hbm, pairing_ref), (psi_hbm, psi_ref),
    ]
    for t in range(left_ref.shape[0]):
        pairs.append((left_hbm.at[t], left_ref.at[t]))
    copies = [
        pltpu.make_async_copy(source, target, sems.at[i])
        for i, (source, target) in enumerate(pairs)
    ]
    for copy in copies:
        copy.start()
    for owner in range(sec_count):
        count_ref[owner] = 0
        entry_ref[owner, cap] = 0
        for i in range(cap):
            entry_ref[owner, i] = terms * sec_dev
    for copy in copies[:3]:
        copy.wait()
    for s in range(sec_dev):
        limit_ref[s:s + 1, :] = jnp.full((1, LANES), rows_ref[s], jnp.int32)
        limit_ref[sec_dev + s:sec_dev + s + 1, :] = jnp.full((1, LANES), cols_ref[s], jnp.int32)
    columns = energy_columns(level_ref[...])
    for s in range(sec_dev):
        energy_ref[s] = jnp.broadcast_to(columns[:, s:s + 1], (half, LANES))
    copies[3].wait()
    for t in range(terms):
        for s in range(sec_dev):
            target = pairing_ref[s, t]
            owner = quotient(target, sec_dev)
            count = count_ref[owner]
            entry_ref[owner, count] = t * sec_dev + s
            entry_ref[owner, cap] = remainder(target, sec_dev)
            count_ref[owner] = count + 1
    entries = pltpu.make_async_copy(entry_ref, list_ref, sems.at[len(copies)])
    entries.start()
    copies[4].wait()
    first_row = lax.axis_index("rep") * half
    norm = jnp.zeros((8, width), F32)
    level = jnp.zeros((8, width), F32)
    for s in range(sec_dev):
        vector = jnp.where(
            live(limit_ref, s, first_row, (half, width)), psi_ref[s].astype(F32), 0.0
        )
        start_ref[s] = vector.astype(BF16)
        square = vector * vector
        norm += fold(square)
        level += fold(square * spread(energy_ref[s], width))
    scalar_ref[0:8, :] = norm
    scalar_ref[8:16, :] = level
    for copy in copies[5:]:
        copy.wait()
    entries.wait()


def product_kernel(is_first, split, paired, rep_count, sec_count, *refs):
    refs = list(refs)
    take = lambda count: [refs.pop(0) for _ in range(count)]
    list_ref, left_ref, right_ref = take(3)
    if is_first:
        start_ref, limit_ref, scalar_ref = take(3)
        psi_refs = take(rep_count - 1)
        level_refs = take(rep_count - 1)
    else:
        (first_ref,) = take(1)
        vector_refs = take(rep_count)
    out_refs = take(sec_count if split else 1)
    if not is_first:
        (first_hbm,) = take(1)
    inner_ref, entry_ref, sems = refs
    terms, sec_dev, half, width = left_ref.shape
    pairs = terms * sec_dev
    cap = most_pairs(pairs, sec_count)
    rep = lax.axis_index("rep")
    sec = lax.axis_index("sec")
    fetch = pltpu.make_async_copy(list_ref, entry_ref, sems.at[0])
    fetch.start()
    if not is_first:
        put = pltpu.make_async_copy(first_ref, first_hbm, sems.at[1])
        put.start()
    inner_ref[pairs] = jnp.zeros((half, width), BF16)

    def first_row(step):
        return remainder(rep + step, rep_count) * half

    if is_first:
        folded = [scalar_ref[0:8, :], scalar_ref[8:16, :]]
        columns = [energy_columns(ref[...]) for ref in level_refs]
    for s in range(sec_dev):
        if is_first:
            blocks = [start_ref[s]]
            for step in range(1, rep_count):
                psi = psi_refs[step - 1][s]
                mask = live(limit_ref, s, first_row(step), (half, width))
                blocks.append(jnp.where(mask, psi.astype(F32), 0.0).astype(BF16))
        else:
            blocks = [ref[s * half:(s + 1) * half] for ref in vector_refs]
        vector = jnp.concatenate(blocks, axis=0)
        for turn in range(1, rep_count):
            turned = blocks[rep_count - turn:] + blocks[:rep_count - turn]
            vector = jnp.where(rep == turn, jnp.concatenate(turned, axis=0), vector)
        inner = jnp.dot(
            left_ref[:, s].reshape(terms * half, width), vector, preferred_element_type=F32
        ).astype(BF16)
        for t in range(terms):
            inner_ref[t * sec_dev + s] = inner[t * half:(t + 1) * half]
        if is_first:
            for step in range(1, rep_count):
                block = blocks[step].astype(F32)
                square = block * block
                energy = jnp.broadcast_to(columns[step - 1][:, s:s + 1], (half, width))
                folded = [folded[0] + fold(square), folded[1] + fold(square * energy)]
    if is_first:
        scalars = [total(array) for array in folded]
    else:
        head = sum(ref[sec_dev * half:].astype(F32) for ref in vector_refs)
        scalars = [head_scalar(head, i)[:, :LANES] for i in range(2)]
    fetch.wait()
    for d in range(sec_count):
        if not split:
            owner = d
        elif paired:
            owner = sec ^ d
        else:
            owner = remainder(sec + d, sec_count)
        packet = jnp.zeros((half, width), F32)
        for i in range(cap):
            pair = entry_ref[owner, i]
            term = jnp.minimum(quotient(pair, sec_dev), terms - 1)
            packet += jnp.dot(inner_ref[pair], right_ref[term], preferred_element_type=F32)
        out = out_refs[d] if split else out_refs[0].at[d]
        for column in range(width // LANES):
            out[column * half:(column + 1) * half, :] = packet[
                :, column * LANES:(column + 1) * LANES
            ].astype(BF16)
        out[width // LANES * half:, :] = header(entry_ref[owner, cap], scalars)
    if not is_first:
        put.wait()


def sigma_packets(is_first, split, paired, rep_count, lists, left_env, right_env, more):
    terms, sec_dev, half, width = left_env.shape
    sec_count = lax.axis_size("sec")
    packet = (width // LANES * half + HEAD, LANES)
    if split:
        outs = [jax.ShapeDtypeStruct(packet, BF16)] * sec_count
    else:
        outs = [jax.ShapeDtypeStruct((sec_count,) + packet, BF16)]
    out_specs = [whole(pltpu.VMEM)] * len(outs)
    if not is_first:
        outs.append(jax.ShapeDtypeStruct((sec_dev, half, width), BF16))
        out_specs.append(whole(pltpu.HBM))
    pair_flops = 2 * half * width * width * 2
    operands = [lists, left_env, right_env, *more]
    return pl.pallas_call(
        functools.partial(product_kernel, is_first, split, paired, rep_count, sec_count),
        out_shape=outs,
        in_specs=[whole(pltpu.VMEM)] * len(operands),
        out_specs=out_specs,
        scratch_shapes=[
            pltpu.VMEM((terms * sec_dev + 1, half, width), BF16),
            pltpu.SMEM(lists.shape, jnp.int32),
            pltpu.SemaphoreType.DMA((2,)),
        ],
        compiler_params=pltpu.CompilerParams(vmem_limit_bytes=VMEM_BYTES),
        cost_estimate=pl.CostEstimate(
            flops=terms * sec_dev * pair_flops,
            bytes_accessed=2 * (left_env.size + right_env.size),
            transcendentals=0,
        ),
        name="products_first" if is_first else "products_second",
    )(*operands)


def exchange(packets, split, paired, order, groups):
    sec_count = lax.axis_size("sec")
    op_count = lax.axis_size("op")
    op_turns = [
        [(i, (i + step) % op_count) for i in range(op_count)] for step in range(1, op_count)
    ]
    over_op = lambda packet: [lax.ppermute(packet, "op", turn) for turn in op_turns]
    if not split:
        arrived = lax.all_to_all(packets[0], "sec", split_axis=0, concat_axis=0, tiled=True)
        return [arrived] + over_op(arrived), []
    arrived = {0: packets[0]}
    for step in order:
        reach = (lambda i: i ^ step) if paired else (lambda i: (i + step) % sec_count)
        turn = [(i, reach(i)) for i in range(sec_count)]
        arrived[step] = lax.ppermute(packets[step], "sec", turn)
    crossed = [over_op(jnp.stack([arrived[step] for step in group])) for group in groups]
    return [arrived[step] for step in [0, *order]] + sum(crossed[:-1], []), crossed[-1]


def views(refs):
    return [
        view
        for ref in refs
        for view in ([ref] if len(ref.shape) == 2 else [ref.at[i] for i in range(ref.shape[0])])
    ]


def add_packets(packet_refs, split, half, base_ref):
    sec_dev, _, width = base_ref.shape
    own = lax.axis_size("sec") if split else 1
    body_rows = width // LANES * half
    if split:
        packet_refs = views(packet_refs)
        heads = [ref[body_rows:].astype(F32) for ref in packet_refs]
        for column in range(width // LANES):
            lanes = slice(column * LANES, (column + 1) * LANES)
            for s in range(sec_dev):
                part = base_ref[s, :, lanes]
                for ref, head in zip(packet_refs, heads):
                    body = ref[column * half:(column + 1) * half].astype(F32)
                    part += jnp.where(head[0:1] == s, body, 0.0)
                base_ref[s, :, lanes] = part
        return sum(heads[1:own], heads[0])

    head_sum = jnp.zeros((HEAD, LANES), F32)
    for index, ref in enumerate(packet_refs):
        def add_one(p, carry):
            head = ref[p, body_rows:, :].astype(F32)
            for column in range(width // LANES):
                body = ref[p, column * half:(column + 1) * half, :].astype(F32)
                lanes = slice(column * LANES, (column + 1) * LANES)
                for s in range(sec_dev):
                    base_ref[s, :, lanes] += jnp.where(head[0:1] == s, body, 0.0)
            return carry + head
        result = lax.fori_loop(0, ref.shape[0], add_one, jnp.zeros((HEAD, LANES), F32))
        if index < own:
            head_sum = head_sum + result
    return head_sum


def late_sum(packet_refs, s, half, width):
    body_rows = width // LANES * half
    value = jnp.zeros((half, width), F32)
    for ref in views(packet_refs):
        body = jnp.concatenate(
            [ref[c * half:(c + 1) * half].astype(F32) for c in range(width // LANES)], axis=1
        )
        slot = spread(ref[body_rows:].astype(F32)[0:1], width)
        value += jnp.where(slot == s, body, 0.0)
    return value


def first_early_kernel(split, count, *refs):
    packet_refs = refs[:count]
    start_ref, energy_ref, base_ref, scalar_ref = refs[count:]
    sec_dev, half, width = start_ref.shape
    for s in range(sec_dev):
        base_ref[s] = spread(energy_ref[s], width) * start_ref[s].astype(F32)
    head_sum = add_packets(packet_refs, split, half, base_ref)
    norm = head_scalar(head_sum, 0)
    scalar_ref[0:1] = norm
    scalar_ref[1:2] = head_scalar(head_sum, 1) / norm


def first_kernel(count, *refs):
    packet_refs = refs[:count]
    limit_ref, start_ref, base_ref, scalar_ref, first_ref, one_ref, vec_ref = refs[count:]
    sec_dev, half, width = start_ref.shape
    shift = spread(scalar_ref[1:2], width)
    first_row = lax.axis_index("rep") * half
    cross = jnp.zeros((8, width), F32)
    square = jnp.zeros((8, width), F32)
    for s in range(sec_dev):
        mask = live(limit_ref, s, first_row, (half, width))
        start = start_ref[s].astype(F32)
        one = jnp.where(mask, base_ref[s] + late_sum(packet_refs, s, half, width), 0.0)
        one_ref[s] = one
        first_ref[s] = one.astype(BF16)
        vector = one - shift * start
        vec_ref[s * half:(s + 1) * half] = vector.astype(BF16)
        cross += fold(start * vector)
        square += fold(vector * vector)
    scalars = (total(cross), total(square))
    vec_ref[sec_dev * half:] = header(jnp.int32(0), scalars, (MORE_ROWS, width))


def second_early_kernel(split, count, entries, *refs):
    packet_refs = refs[:count]
    vec_ref, energy_ref, one_ref, scalar_ref, base_ref, scale_ref = refs[count:]
    sec_dev, half, width = one_ref.shape
    for s in range(sec_dev):
        vector = vec_ref[s * half:(s + 1) * half].astype(F32)
        base_ref[s] = spread(energy_ref[s], width) * vector
    head_sum = add_packets(packet_refs, split, half, base_ref)
    cross = head_scalar(head_sum, 0)
    square = head_scalar(head_sum, 1)
    excess = cross / scalar_ref[0:1]
    resid_sq = jnp.maximum(square - excess * cross, 0.0)
    scale = lax.rsqrt(resid_sq / entries + EPSILON)
    scale_ref[...] = jnp.broadcast_to(scale, scale_ref.shape)
    for s in range(sec_dev):
        base_ref[s] = base_ref[s] - spread(excess, width) * one_ref[s]


def second_kernel(count, *refs):
    packet_refs = refs[:count]
    limit_ref, base_ref, scale_ref, second_ref = refs[count:]
    sec_dev, half, width = base_ref.shape
    scale = spread(scale_ref[0:1], width)
    first_row = lax.axis_index("rep") * half
    for s in range(sec_dev):
        mask = live(limit_ref, s, first_row, (half, width))
        value = scale * (base_ref[s] + late_sum(packet_refs, s, half, width))
        second_ref[s] = jnp.where(mask, value, 0.0).astype(BF16)


def call(kernel, name, outs, *operands, flops=0):
    return pl.pallas_call(
        kernel,
        out_shape=outs,
        in_specs=[whole(pltpu.VMEM)] * len(operands),
        out_specs=[whole(pltpu.VMEM)] * len(outs),
        compiler_params=pltpu.CompilerParams(vmem_limit_bytes=VMEM_BYTES),
        cost_estimate=pl.CostEstimate(flops=flops, bytes_accessed=0, transcendentals=0),
        name=name,
    )(*operands)


def body(psi, left_env, right_env, pairing, block_rows, block_cols, energy):
    sec_count = lax.axis_size("sec")
    op_count = lax.axis_size("op")
    rep_count = lax.axis_size("rep")
    terms, sec_dev, half, width = left_env.shape
    entries = sec_count * sec_dev * rep_count * half * width
    split = sec_count * op_count <= 8
    can_pair = sec_count & (sec_count - 1) == 0
    steps = list(range(1, sec_count))
    first_plan = (False, steps, [[0]] + [[k] for k in steps[:-2]] + [steps[-2:]])
    second_groups = [[0]] + [[k] for k in steps[1:2] + steps[:1] + steps[2:]]
    second_plan = (can_pair, steps[1:2] + steps[:1] + steps[2:], [[0], steps[1:2], steps[:1] + steps[2:]])
    params = pltpu.CompilerParams(vmem_limit_bytes=VMEM_BYTES)
    vec_shape = (sec_dev, half, width)
    vec_bf16 = jax.ShapeDtypeStruct(vec_shape, BF16)

    def from_others(array):
        arrays = []
        for step in range(1, rep_count):
            turn = [((i + step) % rep_count, i) for i in range(rep_count)]
            arrays.append(lax.ppermute(array, "rep", turn))
        return arrays

    psi_others = from_others(psi)
    level_others = from_others(energy)
    start, left_env, lists, limits, levels, scalars = pl.pallas_call(
        load_kernel,
        out_shape=[
            vec_bf16,
            jax.ShapeDtypeStruct(left_env.shape, BF16),
            jax.ShapeDtypeStruct((sec_count, LANES), jnp.int32),
            jax.ShapeDtypeStruct((2 * sec_dev, LANES), jnp.int32),
            jax.ShapeDtypeStruct((sec_dev, half, LANES), F32),
            jax.ShapeDtypeStruct((16, width), F32),
        ],
        in_specs=[whole(pltpu.HBM)] * 6,
        out_specs=[whole(pltpu.VMEM)] * 6,
        scratch_shapes=[
            pltpu.VMEM(vec_shape, BF16),
            pltpu.VMEM((sec_dev, half), F32),
            pltpu.SMEM((sec_dev,), jnp.int32),
            pltpu.SMEM((sec_dev,), jnp.int32),
            pltpu.SMEM((sec_dev, terms), jnp.int32),
            pltpu.SMEM((sec_count, LANES), jnp.int32),
            pltpu.SMEM((sec_count,), jnp.int32),
            pltpu.SemaphoreType.DMA((6 + terms,)),
        ],
        compiler_params=params,
        name="load",
    )(*(
        pltpu.with_memory_space_constraint(array, pltpu.HBM)
        for array in (psi, left_env, pairing.T, block_rows, block_cols, energy)
    ))

    block_f32 = jax.ShapeDtypeStruct(vec_shape, F32)
    row_f32 = jax.ShapeDtypeStruct((8, LANES), F32)

    packets = sigma_packets(
        True, split, first_plan[0], rep_count, lists, left_env, right_env,
        [start, limits, scalars, *psi_others, *level_others],
    )
    early, late = exchange(packets, split, *first_plan)
    base, scalars = call(
        functools.partial(first_early_kernel, split, len(early)), "combine_first_early",
        [block_f32, row_f32], *early, start, levels, flops=EARLY_FLOPS,
    )
    first, sigma_one, vector = call(
        functools.partial(first_kernel, len(late)), "combine_first",
        [
            pltpu.VMEM(vec_shape, BF16),
            block_f32,
            jax.ShapeDtypeStruct((sec_dev * half + MORE_ROWS, width), BF16),
        ],
        *late, limits, start, base, scalars,
    )

    *packets, first_out = sigma_packets(
        False, split, second_plan[0], rep_count, lists, left_env, right_env,
        [first, vector, *from_others(vector)],
    )
    early, late = exchange(packets, split, *second_plan)
    base, scale = call(
        functools.partial(second_early_kernel, split, len(early), entries),
        "combine_second_early", [block_f32, row_f32], *early, vector, levels, sigma_one, scalars,
        flops=10**8,
    )
    (second_out,) = call(
        functools.partial(second_kernel, len(late)), "combine_second", [vec_bf16],
        *late, limits, base, scale,
    )
    return (first_out, second_out)


def solution(mesh):
    return jax.shard_map(
        body,
        mesh=mesh,
        in_specs=(
            P(("grp", "sec"), "rep", None),
            P(("grp", "op"), "sec", "rep", None),
            P(("grp", "op"), None, None),
            P(("grp", "op"), "sec"),
            P(("grp", "sec")),
            P(("grp", "sec")),
            P(("grp", "sec"), "rep"),
        ),
        out_specs=(P(("grp", "sec"), "rep", None), P(("grp", "sec"), "rep", None)),
        check_vma=False,
    )
```

```python
import functools

import jax
import jax.numpy as jnp
from jax import lax
from jax.experimental import pallas as pl
from jax.experimental.pallas import tpu as pltpu
from jax.sharding import PartitionSpec as P

EPSILON = 1e-06
HEAD = 8
PARTS = 3
EARLY_FLOPS = 10**9
MORE_ROWS = 16
LANES = 128
VMEM_BYTES = 24 * 1024 * 1024
F32 = jnp.float32
BF16 = jnp.bfloat16


def whole(space):
    return pl.BlockSpec(memory_space=space)


def live(limit_ref, s, first_row, shape):
    sec_dev = limit_ref.shape[0] // 2
    repeat = shape[1] // LANES
    rows = jnp.concatenate([limit_ref[s:s + 1, :]] * repeat, axis=1)
    cols = jnp.concatenate([limit_ref[sec_dev + s:sec_dev + s + 1, :]] * repeat, axis=1)
    row_ids = first_row + lax.broadcasted_iota(jnp.int32, shape, 0)
    col_ids = lax.broadcasted_iota(jnp.int32, shape, 1)
    return (row_ids < rows) & (col_ids < cols)


def energy_columns(level):
    missing = -level.shape[0] % 8
    if missing:
        level = jnp.concatenate([level, jnp.zeros((missing, level.shape[1]), F32)], axis=0)
    return level.T


def spread(array, width):
    return jnp.concatenate([array] * (width // LANES), axis=1)


def quotient(value, count):
    return value >> (count.bit_length() - 1) if count & (count - 1) == 0 else lax.div(value, count)


def remainder(value, count):
    return value & (count - 1) if count & (count - 1) == 0 else lax.rem(value, count)


def fold(array):
    rows, width = array.shape
    return jnp.sum(array.reshape(rows // 8, 8, width), axis=0)


def total(array):
    return jnp.sum(jnp.sum(array, axis=0, keepdims=True), axis=1, keepdims=True)


def header(slot, scalars, shape=(HEAD, LANES)):
    row_ids = lax.broadcasted_iota(jnp.int32, shape, 0)
    head = jnp.where(row_ids == 0, slot.astype(F32), 0.0)
    row = 1
    for scalar in scalars:
        rest = jnp.broadcast_to(scalar, shape)
        for _ in range(PARTS):
            piece = rest.astype(BF16).astype(F32)
            head = jnp.where(row_ids == row, piece, head)
            rest = rest - piece
            row += 1
    return head.astype(BF16)


def head_scalar(head_sum, index):
    first = 1 + PARTS * index
    return jnp.sum(head_sum[first:first + PARTS], axis=0, keepdims=True)


def most_pairs(pairs, sec_count):
    return pairs // sec_count + 1


def load_kernel(
    psi_hbm, left_hbm, pairing_hbm, rows_hbm, cols_hbm, energy_hbm,
    start_ref, left_ref, list_ref, limit_ref, energy_ref, scalar_ref,
    psi_ref, level_ref, rows_ref, cols_ref, pairing_ref, entry_ref, count_ref, sems,
):
    sec_dev, half, width = psi_ref.shape
    terms = left_ref.shape[0]
    sec_count = list_ref.shape[0]
    cap = most_pairs(terms * sec_dev, sec_count)
    pairs = [
        (rows_hbm, rows_ref), (cols_hbm, cols_ref), (energy_hbm, level_ref),
        (pairing_hbm, pairing_ref), (psi_hbm, psi_ref),
    ]
    for t in range(left_ref.shape[0]):
        pairs.append((left_hbm.at[t], left_ref.at[t]))
    copies = [
        pltpu.make_async_copy(source, target, sems.at[i])
        for i, (source, target) in enumerate(pairs)
    ]
    for copy in copies:
        copy.start()
    for owner in range(sec_count):
        count_ref[owner] = 0
        entry_ref[owner, cap] = 0
        for i in range(cap):
            entry_ref[owner, i] = terms * sec_dev
    for copy in copies[:3]:
        copy.wait()
    for s in range(sec_dev):
        limit_ref[s:s + 1, :] = jnp.full((1, LANES), rows_ref[s], jnp.int32)
        limit_ref[sec_dev + s:sec_dev + s + 1, :] = jnp.full((1, LANES), cols_ref[s], jnp.int32)
    columns = energy_columns(level_ref[...])
    for s in range(sec_dev):
        energy_ref[s] = jnp.broadcast_to(columns[:, s:s + 1], (half, LANES))
    copies[3].wait()
    for t in range(terms):
        for s in range(sec_dev):
            target = pairing_ref[s, t]
            owner = quotient(target, sec_dev)
            count = count_ref[owner]
            entry_ref[owner, count] = t * sec_dev + s
            entry_ref[owner, cap] = remainder(target, sec_dev)
            count_ref[owner] = count + 1
    entries = pltpu.make_async_copy(entry_ref, list_ref, sems.at[len(copies)])
    entries.start()
    copies[4].wait()
    first_row = lax.axis_index("rep") * half
    norm = jnp.zeros((8, width), F32)
    level = jnp.zeros((8, width), F32)
    for s in range(sec_dev):
        vector = jnp.where(
            live(limit_ref, s, first_row, (half, width)), psi_ref[s].astype(F32), 0.0
        )
        start_ref[s] = vector.astype(BF16)
        square = vector * vector
        norm += fold(square)
        level += fold(square * spread(energy_ref[s], width))
    scalar_ref[0:8, :] = norm
    scalar_ref[8:16, :] = level
    for copy in copies[5:]:
        copy.wait()
    entries.wait()


def product_kernel(is_first, split, paired, rep_count, sec_count, *refs):
    refs = list(refs)
    take = lambda count: [refs.pop(0) for _ in range(count)]
    list_ref, left_ref, right_ref = take(3)
    if is_first:
        start_ref, limit_ref, scalar_ref = take(3)
        psi_refs = take(rep_count - 1)
        level_refs = take(rep_count - 1)
    else:
        (first_ref,) = take(1)
        vector_refs = take(rep_count)
    out_refs = take(sec_count if split else 1)
    if not is_first:
        (first_hbm,) = take(1)
    inner_ref, entry_ref, sems = refs
    terms, sec_dev, half, width = left_ref.shape
    pairs = terms * sec_dev
    cap = most_pairs(pairs, sec_count)
    rep = lax.axis_index("rep")
    sec = lax.axis_index("sec")
    fetch = pltpu.make_async_copy(list_ref, entry_ref, sems.at[0])
    fetch.start()
    if not is_first:
        put = pltpu.make_async_copy(first_ref, first_hbm, sems.at[1])
        put.start()
    inner_ref[pairs] = jnp.zeros((half, width), BF16)

    def first_row(step):
        return remainder(rep + step, rep_count) * half

    if is_first:
        folded = [scalar_ref[0:8, :], scalar_ref[8:16, :]]
        columns = [energy_columns(ref[...]) for ref in level_refs]
    for s in range(sec_dev):
        if is_first:
            blocks = [start_ref[s]]
            for step in range(1, rep_count):
                psi = psi_refs[step - 1][s]
                mask = live(limit_ref, s, first_row(step), (half, width))
                blocks.append(jnp.where(mask, psi.astype(F32), 0.0).astype(BF16))
        else:
            blocks = [ref[s * half:(s + 1) * half] for ref in vector_refs]
        vector = jnp.concatenate(blocks, axis=0)
        for turn in range(1, rep_count):
            turned = blocks[rep_count - turn:] + blocks[:rep_count - turn]
            vector = jnp.where(rep == turn, jnp.concatenate(turned, axis=0), vector)
        inner = jnp.dot(
            left_ref[:, s].reshape(terms * half, width), vector, preferred_element_type=F32
        ).astype(BF16)
        for t in range(terms):
            inner_ref[t * sec_dev + s] = inner[t * half:(t + 1) * half]
        if is_first:
            for step in range(1, rep_count):
                block = blocks[step].astype(F32)
                square = block * block
                energy = jnp.broadcast_to(columns[step - 1][:, s:s + 1], (half, width))
                folded = [folded[0] + fold(square), folded[1] + fold(square * energy)]
    if is_first:
        scalars = [total(array) for array in folded]
    else:
        head = sum(ref[sec_dev * half:].astype(F32) for ref in vector_refs)
        scalars = [head_scalar(head, i)[:, :LANES] for i in range(2)]
    fetch.wait()
    for d in range(sec_count):
        if not split:
            owner = d
        elif paired:
            owner = sec ^ d
        else:
            owner = remainder(sec + d, sec_count)
        packet = jnp.zeros((half, width), F32)
        for i in range(cap):
            pair = entry_ref[owner, i]
            term = jnp.minimum(quotient(pair, sec_dev), terms - 1)
            packet += jnp.dot(inner_ref[pair], right_ref[term], preferred_element_type=F32)
        out = out_refs[d] if split else out_refs[0].at[d]
        for column in range(width // LANES):
            out[column * half:(column + 1) * half, :] = packet[
                :, column * LANES:(column + 1) * LANES
            ].astype(BF16)
        out[width // LANES * half:, :] = header(entry_ref[owner, cap], scalars)
    if not is_first:
        put.wait()


def sigma_packets(is_first, split, paired, rep_count, lists, left_env, right_env, more):
    terms, sec_dev, half, width = left_env.shape
    sec_count = lax.axis_size("sec")
    packet = (width // LANES * half + HEAD, LANES)
    if split:
        outs = [jax.ShapeDtypeStruct(packet, BF16)] * sec_count
    else:
        outs = [jax.ShapeDtypeStruct((sec_count,) + packet, BF16)]
    out_specs = [whole(pltpu.VMEM)] * len(outs)
    if not is_first:
        outs.append(jax.ShapeDtypeStruct((sec_dev, half, width), BF16))
        out_specs.append(whole(pltpu.HBM))
    pair_flops = 2 * half * width * width * 2
    operands = [lists, left_env, right_env, *more]
    return pl.pallas_call(
        functools.partial(product_kernel, is_first, split, paired, rep_count, sec_count),
        out_shape=outs,
        in_specs=[whole(pltpu.VMEM)] * len(operands),
        out_specs=out_specs,
        scratch_shapes=[
            pltpu.VMEM((terms * sec_dev + 1, half, width), BF16),
            pltpu.SMEM(lists.shape, jnp.int32),
            pltpu.SemaphoreType.DMA((2,)),
        ],
        compiler_params=pltpu.CompilerParams(vmem_limit_bytes=VMEM_BYTES),
        cost_estimate=pl.CostEstimate(
            flops=terms * sec_dev * pair_flops,
            bytes_accessed=2 * (left_env.size + right_env.size),
            transcendentals=0,
        ),
        name="products_first" if is_first else "products_second",
    )(*operands)


def exchange(packets, split, paired, order, groups):
    sec_count = lax.axis_size("sec")
    op_count = lax.axis_size("op")
    op_turns = [
        [(i, (i + step) % op_count) for i in range(op_count)] for step in range(1, op_count)
    ]
    over_op = lambda packet: [lax.ppermute(packet, "op", turn) for turn in op_turns]
    if not split:
        arrived = lax.all_to_all(packets[0], "sec", split_axis=0, concat_axis=0, tiled=True)
        return [arrived] + over_op(arrived), []
    arrived = {0: packets[0]}
    for step in order:
        reach = (lambda i: i ^ step) if paired else (lambda i: (i + step) % sec_count)
        turn = [(i, reach(i)) for i in range(sec_count)]
        arrived[step] = lax.ppermute(packets[step], "sec", turn)
    crossed = [over_op(jnp.stack([arrived[step] for step in group])) for group in groups]
    return [arrived[step] for step in [0, *order]] + sum(crossed[:-1], []), crossed[-1]


def views(refs):
    return [
        view
        for ref in refs
        for view in ([ref] if len(ref.shape) == 2 else [ref.at[i] for i in range(ref.shape[0])])
    ]


def add_packets(packet_refs, split, half, base_ref):
    sec_dev, _, width = base_ref.shape
    own = lax.axis_size("sec") if split else 1
    body_rows = width // LANES * half
    if split:
        packet_refs = views(packet_refs)
        heads = [ref[body_rows:].astype(F32) for ref in packet_refs]
        for column in range(width // LANES):
            lanes = slice(column * LANES, (column + 1) * LANES)
            for s in range(sec_dev):
                part = base_ref[s, :, lanes]
                for ref, head in zip(packet_refs, heads):
                    body = ref[column * half:(column + 1) * half].astype(F32)
                    part += jnp.where(head[0:1] == s, body, 0.0)
                base_ref[s, :, lanes] = part
        return sum(heads[1:own], heads[0])

    head_sum = jnp.zeros((HEAD, LANES), F32)
    for index, ref in enumerate(packet_refs):
        def add_one(p, carry):
            head = ref[p, body_rows:, :].astype(F32)
            for column in range(width // LANES):
                body = ref[p, column * half:(column + 1) * half, :].astype(F32)
                lanes = slice(column * LANES, (column + 1) * LANES)
                for s in range(sec_dev):
                    base_ref[s, :, lanes] += jnp.where(head[0:1] == s, body, 0.0)
            return carry + head
        result = lax.fori_loop(0, ref.shape[0], add_one, jnp.zeros((HEAD, LANES), F32))
        if index < own:
            head_sum = head_sum + result
    return head_sum


def late_sum(packet_refs, s, half, width):
    body_rows = width // LANES * half
    value = jnp.zeros((half, width), F32)
    for ref in views(packet_refs):
        body = jnp.concatenate(
            [ref[c * half:(c + 1) * half].astype(F32) for c in range(width // LANES)], axis=1
        )
        slot = spread(ref[body_rows:].astype(F32)[0:1], width)
        value += jnp.where(slot == s, body, 0.0)
    return value


def first_early_kernel(split, count, *refs):
    packet_refs = refs[:count]
    start_ref, energy_ref, base_ref, scalar_ref = refs[count:]
    sec_dev, half, width = start_ref.shape
    for s in range(sec_dev):
        base_ref[s] = spread(energy_ref[s], width) * start_ref[s].astype(F32)
    head_sum = add_packets(packet_refs, split, half, base_ref)
    norm = head_scalar(head_sum, 0)
    scalar_ref[0:1] = norm
    scalar_ref[1:2] = head_scalar(head_sum, 1) / norm


def first_kernel(count, *refs):
    packet_refs = refs[:count]
    limit_ref, start_ref, base_ref, scalar_ref, first_ref, one_ref, vec_ref = refs[count:]
    sec_dev, half, width = start_ref.shape
    shift = spread(scalar_ref[1:2], width)
    first_row = lax.axis_index("rep") * half
    cross = jnp.zeros((8, width), F32)
    square = jnp.zeros((8, width), F32)
    for s in range(sec_dev):
        mask = live(limit_ref, s, first_row, (half, width))
        start = start_ref[s].astype(F32)
        one = jnp.where(mask, base_ref[s] + late_sum(packet_refs, s, half, width), 0.0)
        one_ref[s] = one
        first_ref[s] = one.astype(BF16)
        vector = one - shift * start
        vec_ref[s * half:(s + 1) * half] = vector.astype(BF16)
        cross += fold(start * vector)
        square += fold(vector * vector)
    scalars = (total(cross), total(square))
    vec_ref[sec_dev * half:] = header(jnp.int32(0), scalars, (MORE_ROWS, width))


def second_early_kernel(split, count, entries, *refs):
    packet_refs = refs[:count]
    vec_ref, energy_ref, one_ref, scalar_ref, base_ref, scale_ref = refs[count:]
    sec_dev, half, width = one_ref.shape
    for s in range(sec_dev):
        vector = vec_ref[s * half:(s + 1) * half].astype(F32)
        base_ref[s] = spread(energy_ref[s], width) * vector
    head_sum = add_packets(packet_refs, split, half, base_ref)
    cross = head_scalar(head_sum, 0)
    square = head_scalar(head_sum, 1)
    excess = cross / scalar_ref[0:1]
    resid_sq = jnp.maximum(square - excess * cross, 0.0)
    scale = lax.rsqrt(resid_sq / entries + EPSILON)
    scale_ref[...] = jnp.broadcast_to(scale, scale_ref.shape)
    for s in range(sec_dev):
        base_ref[s] = base_ref[s] - spread(excess, width) * one_ref[s]


def second_kernel(count, *refs):
    packet_refs = refs[:count]
    limit_ref, base_ref, scale_ref, second_ref = refs[count:]
    sec_dev, half, width = base_ref.shape
    scale = spread(scale_ref[0:1], width)
    first_row = lax.axis_index("rep") * half
    for s in range(sec_dev):
        mask = live(limit_ref, s, first_row, (half, width))
        value = scale * (base_ref[s] + late_sum(packet_refs, s, half, width))
        second_ref[s] = jnp.where(mask, value, 0.0).astype(BF16)


def call(kernel, name, outs, *operands, flops=0):
    return pl.pallas_call(
        kernel,
        out_shape=outs,
        in_specs=[whole(pltpu.VMEM)] * len(operands),
        out_specs=[whole(pltpu.VMEM)] * len(outs),
        compiler_params=pltpu.CompilerParams(vmem_limit_bytes=VMEM_BYTES),
        cost_estimate=pl.CostEstimate(flops=flops, bytes_accessed=0, transcendentals=0),
        name=name,
    )(*operands)


def body(psi, left_env, right_env, pairing, block_rows, block_cols, energy):
    sec_count = lax.axis_size("sec")
    op_count = lax.axis_size("op")
    rep_count = lax.axis_size("rep")
    terms, sec_dev, half, width = left_env.shape
    entries = sec_count * sec_dev * rep_count * half * width
    split = sec_count * op_count <= 8
    can_pair = sec_count & (sec_count - 1) == 0
    steps = list(range(1, sec_count))
    first_plan = (False, steps, [[0]] + [[k] for k in steps[:-2]] + [steps[-2:]])
    second_groups = [[0]] + [[k] for k in steps[1:2] + steps[:1] + steps[2:]]
    second_plan = (can_pair, steps[1:] + steps[:1], [[0], steps[1:2], steps[2:] + steps[:1]])
    params = pltpu.CompilerParams(vmem_limit_bytes=VMEM_BYTES)
    vec_shape = (sec_dev, half, width)
    vec_bf16 = jax.ShapeDtypeStruct(vec_shape, BF16)

    def from_others(array):
        arrays = []
        for step in range(1, rep_count):
            turn = [((i + step) % rep_count, i) for i in range(rep_count)]
            arrays.append(lax.ppermute(array, "rep", turn))
        return arrays

    psi_others = from_others(psi)
    level_others = from_others(energy)
    start, left_env, lists, limits, levels, scalars = pl.pallas_call(
        load_kernel,
        out_shape=[
            vec_bf16,
            jax.ShapeDtypeStruct(left_env.shape, BF16),
            jax.ShapeDtypeStruct((sec_count, LANES), jnp.int32),
            jax.ShapeDtypeStruct((2 * sec_dev, LANES), jnp.int32),
            jax.ShapeDtypeStruct((sec_dev, half, LANES), F32),
            jax.ShapeDtypeStruct((16, width), F32),
        ],
        in_specs=[whole(pltpu.HBM)] * 6,
        out_specs=[whole(pltpu.VMEM)] * 6,
        scratch_shapes=[
            pltpu.VMEM(vec_shape, BF16),
            pltpu.VMEM((sec_dev, half), F32),
            pltpu.SMEM((sec_dev,), jnp.int32),
            pltpu.SMEM((sec_dev,), jnp.int32),
            pltpu.SMEM((sec_dev, terms), jnp.int32),
            pltpu.SMEM((sec_count, LANES), jnp.int32),
            pltpu.SMEM((sec_count,), jnp.int32),
            pltpu.SemaphoreType.DMA((6 + terms,)),
        ],
        compiler_params=params,
        name="load",
    )(*(
        pltpu.with_memory_space_constraint(array, pltpu.HBM)
        for array in (psi, left_env, pairing.T, block_rows, block_cols, energy)
    ))

    block_f32 = jax.ShapeDtypeStruct(vec_shape, F32)
    row_f32 = jax.ShapeDtypeStruct((8, LANES), F32)

    packets = sigma_packets(
        True, split, first_plan[0], rep_count, lists, left_env, right_env,
        [start, limits, scalars, *psi_others, *level_others],
    )
    early, late = exchange(packets, split, *first_plan)
    base, scalars = call(
        functools.partial(first_early_kernel, split, len(early)), "combine_first_early",
        [block_f32, row_f32], *early, start, levels, flops=EARLY_FLOPS,
    )
    first, sigma_one, vector = call(
        functools.partial(first_kernel, len(late)), "combine_first",
        [
            pltpu.VMEM(vec_shape, BF16),
            block_f32,
            jax.ShapeDtypeStruct((sec_dev * half + MORE_ROWS, width), BF16),
        ],
        *late, limits, start, base, scalars,
    )

    *packets, first_out = sigma_packets(
        False, split, second_plan[0], rep_count, lists, left_env, right_env,
        [first, vector, *from_others(vector)],
    )
    early, late = exchange(packets, split, *second_plan)
    base, scale = call(
        functools.partial(second_early_kernel, split, len(early), entries),
        "combine_second_early", [block_f32, row_f32], *early, vector, levels, sigma_one, scalars,
        flops=EARLY_FLOPS,
    )
    (second_out,) = call(
        functools.partial(second_kernel, len(late)), "combine_second", [vec_bf16],
        *late, limits, base, scale,
    )
    return (first_out, second_out)


def solution(mesh):
    return jax.shard_map(
        body,
        mesh=mesh,
        in_specs=(
            P(("grp", "sec"), "rep", None),
            P(("grp", "op"), "sec", "rep", None),
            P(("grp", "op"), None, None),
            P(("grp", "op"), "sec"),
            P(("grp", "sec")),
            P(("grp", "sec")),
            P(("grp", "sec"), "rep"),
        ),
        out_specs=(P(("grp", "sec"), "rep", None), P(("grp", "sec"), "rep", None)),
        check_vma=False,
    )
```

```python
import functools

import jax
import jax.numpy as jnp
from jax import lax
from jax.experimental import pallas as pl
from jax.experimental.pallas import tpu as pltpu
from jax.sharding import PartitionSpec as P

EPSILON = 1e-06
HEAD = 8
PARTS = 3
EARLY_FLOPS = 10**9
VEC_PARTS = 2
MORE_ROWS = 16
LANES = 128
VMEM_BYTES = 24 * 1024 * 1024
F32 = jnp.float32
BF16 = jnp.bfloat16


def whole(space):
    return pl.BlockSpec(memory_space=space)


def live(limit_ref, s, first_row, shape):
    sec_dev = limit_ref.shape[0] // 2
    repeat = shape[1] // LANES
    rows = jnp.concatenate([limit_ref[s:s + 1, :]] * repeat, axis=1)
    cols = jnp.concatenate([limit_ref[sec_dev + s:sec_dev + s + 1, :]] * repeat, axis=1)
    row_ids = first_row + lax.broadcasted_iota(jnp.int32, shape, 0)
    col_ids = lax.broadcasted_iota(jnp.int32, shape, 1)
    return (row_ids < rows) & (col_ids < cols)


def energy_columns(level):
    missing = -level.shape[0] % 8
    if missing:
        level = jnp.concatenate([level, jnp.zeros((missing, level.shape[1]), F32)], axis=0)
    return level.T


def spread(array, width):
    return jnp.concatenate([array] * (width // LANES), axis=1)


def quotient(value, count):
    return value >> (count.bit_length() - 1) if count & (count - 1) == 0 else lax.div(value, count)


def remainder(value, count):
    return value & (count - 1) if count & (count - 1) == 0 else lax.rem(value, count)


def fold(array):
    rows, width = array.shape
    return jnp.sum(array.reshape(rows // 8, 8, width), axis=0)


def total(array):
    return jnp.sum(jnp.sum(array, axis=0, keepdims=True), axis=1, keepdims=True)


def header(slot, scalars, shape=(HEAD, LANES)):
    row_ids = lax.broadcasted_iota(jnp.int32, shape, 0)
    head = jnp.where(row_ids == 0, slot.astype(F32), 0.0)
    row = 1
    for scalar in scalars:
        rest = jnp.broadcast_to(scalar, shape)
        for _ in range(PARTS):
            piece = rest.astype(BF16).astype(F32)
            head = jnp.where(row_ids == row, piece, head)
            rest = rest - piece
            row += 1
    return head.astype(BF16)


def head_scalar(head_sum, index):
    first = 1 + PARTS * index
    return jnp.sum(head_sum[first:first + PARTS], axis=0, keepdims=True)


def vec_place(s, sec_dev, half):
    in_part = sec_dev // VEC_PARTS
    return s // in_part, s % in_part * half


def most_pairs(pairs, sec_count):
    return pairs // sec_count + 1


def load_kernel(
    psi_hbm, left_hbm, pairing_hbm, rows_hbm, cols_hbm, energy_hbm,
    start_ref, left_ref, list_ref, limit_ref, energy_ref, scalar_ref,
    psi_ref, level_ref, rows_ref, cols_ref, pairing_ref, entry_ref, count_ref, sems,
):
    sec_dev, half, width = psi_ref.shape
    terms = left_ref.shape[0]
    sec_count = list_ref.shape[0]
    cap = most_pairs(terms * sec_dev, sec_count)
    pairs = [
        (rows_hbm, rows_ref), (cols_hbm, cols_ref), (energy_hbm, level_ref),
        (pairing_hbm, pairing_ref), (psi_hbm, psi_ref),
    ]
    for t in range(left_ref.shape[0]):
        pairs.append((left_hbm.at[t], left_ref.at[t]))
    copies = [
        pltpu.make_async_copy(source, target, sems.at[i])
        for i, (source, target) in enumerate(pairs)
    ]
    for copy in copies:
        copy.start()
    for owner in range(sec_count):
        count_ref[owner] = 0
        entry_ref[owner, cap] = 0
        for i in range(cap):
            entry_ref[owner, i] = terms * sec_dev
    for copy in copies[:3]:
        copy.wait()
    for s in range(sec_dev):
        limit_ref[s:s + 1, :] = jnp.full((1, LANES), rows_ref[s], jnp.int32)
        limit_ref[sec_dev + s:sec_dev + s + 1, :] = jnp.full((1, LANES), cols_ref[s], jnp.int32)
    columns = energy_columns(level_ref[...])
    for s in range(sec_dev):
        energy_ref[s] = jnp.broadcast_to(columns[:, s:s + 1], (half, LANES))
    copies[3].wait()
    for t in range(terms):
        for s in range(sec_dev):
            target = pairing_ref[s, t]
            owner = quotient(target, sec_dev)
            count = count_ref[owner]
            entry_ref[owner, count] = t * sec_dev + s
            entry_ref[owner, cap] = remainder(target, sec_dev)
            count_ref[owner] = count + 1
    entries = pltpu.make_async_copy(entry_ref, list_ref, sems.at[len(copies)])
    entries.start()
    copies[4].wait()
    first_row = lax.axis_index("rep") * half
    norm = jnp.zeros((8, width), F32)
    level = jnp.zeros((8, width), F32)
    for s in range(sec_dev):
        vector = jnp.where(
            live(limit_ref, s, first_row, (half, width)), psi_ref[s].astype(F32), 0.0
        )
        start_ref[s] = vector.astype(BF16)
        square = vector * vector
        norm += fold(square)
        level += fold(square * spread(energy_ref[s], width))
    scalar_ref[0:8, :] = norm
    scalar_ref[8:16, :] = level
    for copy in copies[5:]:
        copy.wait()
    entries.wait()


def product_kernel(is_first, split, paired, rep_count, sec_count, *refs):
    refs = list(refs)
    take = lambda count: [refs.pop(0) for _ in range(count)]
    list_ref, left_ref, right_ref = take(3)
    if is_first:
        start_ref, limit_ref, scalar_ref = take(3)
        psi_refs = take(rep_count - 1)
        level_refs = take(rep_count - 1)
    else:
        (first_ref,) = take(1)
        vector_refs = [take(VEC_PARTS) for _ in range(rep_count)]
    out_refs = take(sec_count if split else 1)
    if not is_first:
        (first_hbm,) = take(1)
    inner_ref, entry_ref, sems = refs
    terms, sec_dev, half, width = left_ref.shape
    pairs = terms * sec_dev
    cap = most_pairs(pairs, sec_count)
    rep = lax.axis_index("rep")
    sec = lax.axis_index("sec")
    fetch = pltpu.make_async_copy(list_ref, entry_ref, sems.at[0])
    fetch.start()
    if not is_first:
        put = pltpu.make_async_copy(first_ref, first_hbm, sems.at[1])
        put.start()
    inner_ref[pairs] = jnp.zeros((half, width), BF16)

    def first_row(step):
        return remainder(rep + step, rep_count) * half

    if is_first:
        folded = [scalar_ref[0:8, :], scalar_ref[8:16, :]]
        columns = [energy_columns(ref[...]) for ref in level_refs]
    for s in range(sec_dev):
        if is_first:
            blocks = [start_ref[s]]
            for step in range(1, rep_count):
                psi = psi_refs[step - 1][s]
                mask = live(limit_ref, s, first_row(step), (half, width))
                blocks.append(jnp.where(mask, psi.astype(F32), 0.0).astype(BF16))
        else:
            part, row = vec_place(s, sec_dev, half)
            blocks = [parts[part][row:row + half] for parts in vector_refs]
        vector = jnp.concatenate(blocks, axis=0)
        for turn in range(1, rep_count):
            turned = blocks[rep_count - turn:] + blocks[:rep_count - turn]
            vector = jnp.where(rep == turn, jnp.concatenate(turned, axis=0), vector)
        inner = jnp.dot(
            left_ref[:, s].reshape(terms * half, width), vector, preferred_element_type=F32
        ).astype(BF16)
        for t in range(terms):
            inner_ref[t * sec_dev + s] = inner[t * half:(t + 1) * half]
        if is_first:
            for step in range(1, rep_count):
                block = blocks[step].astype(F32)
                square = block * block
                energy = jnp.broadcast_to(columns[step - 1][:, s:s + 1], (half, width))
                folded = [folded[0] + fold(square), folded[1] + fold(square * energy)]
    if is_first:
        scalars = [total(array) for array in folded]
    else:
        head = sum(parts[-1][sec_dev // VEC_PARTS * half:].astype(F32) for parts in vector_refs)
        scalars = [head_scalar(head, i)[:, :LANES] for i in range(2)]
    fetch.wait()
    for d in range(sec_count):
        if not split:
            owner = d
        elif paired:
            owner = sec ^ d
        else:
            owner = remainder(sec + d, sec_count)
        packet = jnp.zeros((half, width), F32)
        for i in range(cap):
            pair = entry_ref[owner, i]
            term = jnp.minimum(quotient(pair, sec_dev), terms - 1)
            packet += jnp.dot(inner_ref[pair], right_ref[term], preferred_element_type=F32)
        out = out_refs[d] if split else out_refs[0].at[d]
        for column in range(width // LANES):
            out[column * half:(column + 1) * half, :] = packet[
                :, column * LANES:(column + 1) * LANES
            ].astype(BF16)
        out[width // LANES * half:, :] = header(entry_ref[owner, cap], scalars)
    if not is_first:
        put.wait()


def sigma_packets(is_first, split, paired, rep_count, lists, left_env, right_env, more):
    terms, sec_dev, half, width = left_env.shape
    sec_count = lax.axis_size("sec")
    packet = (width // LANES * half + HEAD, LANES)
    if split:
        outs = [jax.ShapeDtypeStruct(packet, BF16)] * sec_count
    else:
        outs = [jax.ShapeDtypeStruct((sec_count,) + packet, BF16)]
    out_specs = [whole(pltpu.VMEM)] * len(outs)
    if not is_first:
        outs.append(jax.ShapeDtypeStruct((sec_dev, half, width), BF16))
        out_specs.append(whole(pltpu.HBM))
    pair_flops = 2 * half * width * width * 2
    operands = [lists, left_env, right_env, *more]
    return pl.pallas_call(
        functools.partial(product_kernel, is_first, split, paired, rep_count, sec_count),
        out_shape=outs,
        in_specs=[whole(pltpu.VMEM)] * len(operands),
        out_specs=out_specs,
        scratch_shapes=[
            pltpu.VMEM((terms * sec_dev + 1, half, width), BF16),
            pltpu.SMEM(lists.shape, jnp.int32),
            pltpu.SemaphoreType.DMA((2,)),
        ],
        compiler_params=pltpu.CompilerParams(vmem_limit_bytes=VMEM_BYTES),
        cost_estimate=pl.CostEstimate(
            flops=terms * sec_dev * pair_flops,
            bytes_accessed=2 * (left_env.size + right_env.size),
            transcendentals=0,
        ),
        name="products_first" if is_first else "products_second",
    )(*operands)


def exchange(packets, split, paired, order, groups):
    sec_count = lax.axis_size("sec")
    op_count = lax.axis_size("op")
    op_turns = [
        [(i, (i + step) % op_count) for i in range(op_count)] for step in range(1, op_count)
    ]
    over_op = lambda packet: [lax.ppermute(packet, "op", turn) for turn in op_turns]
    if not split:
        arrived = lax.all_to_all(packets[0], "sec", split_axis=0, concat_axis=0, tiled=True)
        return [arrived] + over_op(arrived), []
    arrived = {0: packets[0]}
    for step in order:
        reach = (lambda i: i ^ step) if paired else (lambda i: (i + step) % sec_count)
        turn = [(i, reach(i)) for i in range(sec_count)]
        arrived[step] = lax.ppermute(packets[step], "sec", turn)
    crossed = [over_op(jnp.stack([arrived[step] for step in group])) for group in groups]
    return [arrived[step] for step in [0, *order]] + sum(crossed[:-1], []), crossed[-1]


def views(refs):
    return [
        view
        for ref in refs
        for view in ([ref] if len(ref.shape) == 2 else [ref.at[i] for i in range(ref.shape[0])])
    ]


def add_packets(packet_refs, split, half, base_ref):
    sec_dev, _, width = base_ref.shape
    own = lax.axis_size("sec") if split else 1
    body_rows = width // LANES * half
    if split:
        packet_refs = views(packet_refs)
        heads = [ref[body_rows:].astype(F32) for ref in packet_refs]
        for column in range(width // LANES):
            lanes = slice(column * LANES, (column + 1) * LANES)
            for s in range(sec_dev):
                part = base_ref[s, :, lanes]
                for ref, head in zip(packet_refs, heads):
                    body = ref[column * half:(column + 1) * half].astype(F32)
                    part += jnp.where(head[0:1] == s, body, 0.0)
                base_ref[s, :, lanes] = part
        return sum(heads[1:own], heads[0])

    head_sum = jnp.zeros((HEAD, LANES), F32)
    for index, ref in enumerate(packet_refs):
        def add_one(p, carry):
            head = ref[p, body_rows:, :].astype(F32)
            for column in range(width // LANES):
                body = ref[p, column * half:(column + 1) * half, :].astype(F32)
                lanes = slice(column * LANES, (column + 1) * LANES)
                for s in range(sec_dev):
                    base_ref[s, :, lanes] += jnp.where(head[0:1] == s, body, 0.0)
            return carry + head
        result = lax.fori_loop(0, ref.shape[0], add_one, jnp.zeros((HEAD, LANES), F32))
        if index < own:
            head_sum = head_sum + result
    return head_sum


def late_sum(packet_refs, s, half, width):
    body_rows = width // LANES * half
    value = jnp.zeros((half, width), F32)
    for ref in views(packet_refs):
        body = jnp.concatenate(
            [ref[c * half:(c + 1) * half].astype(F32) for c in range(width // LANES)], axis=1
        )
        slot = spread(ref[body_rows:].astype(F32)[0:1], width)
        value += jnp.where(slot == s, body, 0.0)
    return value


def first_early_kernel(split, count, *refs):
    packet_refs = refs[:count]
    start_ref, energy_ref, base_ref, scalar_ref = refs[count:]
    sec_dev, half, width = start_ref.shape
    for s in range(sec_dev):
        base_ref[s] = spread(energy_ref[s], width) * start_ref[s].astype(F32)
    head_sum = add_packets(packet_refs, split, half, base_ref)
    norm = head_scalar(head_sum, 0)
    scalar_ref[0:1] = norm
    scalar_ref[1:2] = head_scalar(head_sum, 1) / norm


def first_kernel(count, *refs):
    packet_refs = refs[:count]
    limit_ref, start_ref, base_ref, scalar_ref, first_ref, one_ref = refs[count:-VEC_PARTS]
    vec_refs = refs[-VEC_PARTS:]
    sec_dev, half, width = start_ref.shape
    shift = spread(scalar_ref[1:2], width)
    first_row = lax.axis_index("rep") * half
    cross = jnp.zeros((8, width), F32)
    square = jnp.zeros((8, width), F32)
    for s in range(sec_dev):
        mask = live(limit_ref, s, first_row, (half, width))
        start = start_ref[s].astype(F32)
        one = jnp.where(mask, base_ref[s] + late_sum(packet_refs, s, half, width), 0.0)
        one_ref[s] = one
        first_ref[s] = one.astype(BF16)
        vector = one - shift * start
        part, row = vec_place(s, sec_dev, half)
        vec_refs[part][row:row + half] = vector.astype(BF16)
        cross += fold(start * vector)
        square += fold(vector * vector)
    scalars = (total(cross), total(square))
    more = header(jnp.int32(0), scalars, (MORE_ROWS, width))
    vec_refs[-1][sec_dev // VEC_PARTS * half:] = more


def second_early_kernel(split, count, entries, *refs):
    packet_refs = refs[:count]
    vec_refs = refs[count:count + VEC_PARTS]
    energy_ref, one_ref, scalar_ref, base_ref, scale_ref = refs[count + VEC_PARTS:]
    sec_dev, half, width = one_ref.shape
    for s in range(sec_dev):
        part, row = vec_place(s, sec_dev, half)
        vector = vec_refs[part][row:row + half].astype(F32)
        base_ref[s] = spread(energy_ref[s], width) * vector
    head_sum = add_packets(packet_refs, split, half, base_ref)
    cross = head_scalar(head_sum, 0)
    square = head_scalar(head_sum, 1)
    excess = cross / scalar_ref[0:1]
    resid_sq = jnp.maximum(square - excess * cross, 0.0)
    scale = lax.rsqrt(resid_sq / entries + EPSILON)
    scale_ref[...] = jnp.broadcast_to(scale, scale_ref.shape)
    for s in range(sec_dev):
        base_ref[s] = base_ref[s] - spread(excess, width) * one_ref[s]


def second_kernel(count, *refs):
    packet_refs = refs[:count]
    limit_ref, base_ref, scale_ref, second_ref = refs[count:]
    sec_dev, half, width = base_ref.shape
    scale = spread(scale_ref[0:1], width)
    first_row = lax.axis_index("rep") * half
    for s in range(sec_dev):
        mask = live(limit_ref, s, first_row, (half, width))
        value = scale * (base_ref[s] + late_sum(packet_refs, s, half, width))
        second_ref[s] = jnp.where(mask, value, 0.0).astype(BF16)


def call(kernel, name, outs, *operands, flops=0):
    return pl.pallas_call(
        kernel,
        out_shape=outs,
        in_specs=[whole(pltpu.VMEM)] * len(operands),
        out_specs=[whole(pltpu.VMEM)] * len(outs),
        compiler_params=pltpu.CompilerParams(vmem_limit_bytes=VMEM_BYTES),
        cost_estimate=pl.CostEstimate(flops=flops, bytes_accessed=0, transcendentals=0),
        name=name,
    )(*operands)


def body(psi, left_env, right_env, pairing, block_rows, block_cols, energy):
    sec_count = lax.axis_size("sec")
    op_count = lax.axis_size("op")
    rep_count = lax.axis_size("rep")
    terms, sec_dev, half, width = left_env.shape
    entries = sec_count * sec_dev * rep_count * half * width
    split = sec_count * op_count <= 8
    can_pair = sec_count & (sec_count - 1) == 0
    steps = list(range(1, sec_count))
    first_plan = (False, steps, [[0]] + [[k] for k in steps[:-2]] + [steps[-2:]])
    second_groups = [[0]] + [[k] for k in steps[1:2] + steps[:1] + steps[2:]]
    second_plan = (can_pair, steps[1:2] + steps[:1] + steps[2:], second_groups)
    params = pltpu.CompilerParams(vmem_limit_bytes=VMEM_BYTES)
    vec_shape = (sec_dev, half, width)
    vec_bf16 = jax.ShapeDtypeStruct(vec_shape, BF16)

    def from_others(array):
        arrays = []
        for step in range(1, rep_count):
            turn = [((i + step) % rep_count, i) for i in range(rep_count)]
            arrays.append(lax.ppermute(array, "rep", turn))
        return arrays

    psi_others = from_others(psi)
    level_others = from_others(energy)
    start, left_env, lists, limits, levels, scalars = pl.pallas_call(
        load_kernel,
        out_shape=[
            vec_bf16,
            jax.ShapeDtypeStruct(left_env.shape, BF16),
            jax.ShapeDtypeStruct((sec_count, LANES), jnp.int32),
            jax.ShapeDtypeStruct((2 * sec_dev, LANES), jnp.int32),
            jax.ShapeDtypeStruct((sec_dev, half, LANES), F32),
            jax.ShapeDtypeStruct((16, width), F32),
        ],
        in_specs=[whole(pltpu.HBM)] * 6,
        out_specs=[whole(pltpu.VMEM)] * 6,
        scratch_shapes=[
            pltpu.VMEM(vec_shape, BF16),
            pltpu.VMEM((sec_dev, half), F32),
            pltpu.SMEM((sec_dev,), jnp.int32),
            pltpu.SMEM((sec_dev,), jnp.int32),
            pltpu.SMEM((sec_dev, terms), jnp.int32),
            pltpu.SMEM((sec_count, LANES), jnp.int32),
            pltpu.SMEM((sec_count,), jnp.int32),
            pltpu.SemaphoreType.DMA((6 + terms,)),
        ],
        compiler_params=params,
        name="load",
    )(*(
        pltpu.with_memory_space_constraint(array, pltpu.HBM)
        for array in (psi, left_env, pairing.T, block_rows, block_cols, energy)
    ))

    block_f32 = jax.ShapeDtypeStruct(vec_shape, F32)
    row_f32 = jax.ShapeDtypeStruct((8, LANES), F32)

    packets = sigma_packets(
        True, split, first_plan[0], rep_count, lists, left_env, right_env,
        [start, limits, scalars, *psi_others, *level_others],
    )
    early, late = exchange(packets, split, *first_plan)
    base, scalars = call(
        functools.partial(first_early_kernel, split, len(early)), "combine_first_early",
        [block_f32, row_f32], *early, start, levels, flops=EARLY_FLOPS,
    )
    first, sigma_one, *vector = call(
        functools.partial(first_kernel, len(late)), "combine_first",
        [
            pltpu.VMEM(vec_shape, BF16),
            block_f32,
        ]
        + [
            jax.ShapeDtypeStruct(
                (sec_dev // VEC_PARTS * half + (part + 1) // VEC_PARTS * MORE_ROWS, width), BF16
            )
            for part in range(VEC_PARTS)
        ],
        *late, limits, start, base, scalars,
    )

    *packets, first_out = sigma_packets(
        False, split, second_plan[0], rep_count, lists, left_env, right_env,
        [first, *vector, *sum((list(other) for other in zip(*map(from_others, vector))), [])],
    )
    early, late = exchange(packets, split, *second_plan)
    base, scale = call(
        functools.partial(second_early_kernel, split, len(early), entries),
        "combine_second_early", [block_f32, row_f32], *early, *vector, levels, sigma_one, scalars,
        flops=EARLY_FLOPS,
    )
    (second_out,) = call(
        functools.partial(second_kernel, len(late)), "combine_second", [vec_bf16],
        *late, limits, base, scale,
    )
    return (first_out, second_out)


def solution(mesh):
    return jax.shard_map(
        body,
        mesh=mesh,
        in_specs=(
            P(("grp", "sec"), "rep", None),
            P(("grp", "op"), "sec", "rep", None),
            P(("grp", "op"), None, None),
            P(("grp", "op"), "sec"),
            P(("grp", "sec")),
            P(("grp", "sec")),
            P(("grp", "sec"), "rep"),
        ),
        out_specs=(P(("grp", "sec"), "rep", None), P(("grp", "sec"), "rep", None)),
        check_vma=False,
    )
```

```python
import functools

import jax
import jax.numpy as jnp
from jax import lax
from jax.experimental import pallas as pl
from jax.experimental.pallas import tpu as pltpu
from jax.sharding import PartitionSpec as P

EPSILON = 1e-06
HEAD = 8
PARTS = 3
EARLY_FLOPS = 10**9
MORE_ROWS = 16
LANES = 128
VMEM_BYTES = 24 * 1024 * 1024
F32 = jnp.float32
BF16 = jnp.bfloat16


def whole(space):
    return pl.BlockSpec(memory_space=space)


def live(limit_ref, s, first_row, shape):
    sec_dev = limit_ref.shape[0] // 2
    repeat = shape[1] // LANES
    rows = jnp.concatenate([limit_ref[s:s + 1, :]] * repeat, axis=1)
    cols = jnp.concatenate([limit_ref[sec_dev + s:sec_dev + s + 1, :]] * repeat, axis=1)
    row_ids = first_row + lax.broadcasted_iota(jnp.int32, shape, 0)
    col_ids = lax.broadcasted_iota(jnp.int32, shape, 1)
    return (row_ids < rows) & (col_ids < cols)


def energy_columns(level):
    missing = -level.shape[0] % 8
    if missing:
        level = jnp.concatenate([level, jnp.zeros((missing, level.shape[1]), F32)], axis=0)
    return level.T


def spread(array, width):
    return jnp.concatenate([array] * (width // LANES), axis=1)


def quotient(value, count):
    return value >> (count.bit_length() - 1) if count & (count - 1) == 0 else lax.div(value, count)


def remainder(value, count):
    return value & (count - 1) if count & (count - 1) == 0 else lax.rem(value, count)


def fold(array):
    rows, width = array.shape
    return jnp.sum(array.reshape(rows // 8, 8, width), axis=0)


def total(array):
    return jnp.sum(jnp.sum(array, axis=0, keepdims=True), axis=1, keepdims=True)


def header(slot, scalars, shape=(HEAD, LANES)):
    row_ids = lax.broadcasted_iota(jnp.int32, shape, 0)
    head = jnp.where(row_ids == 0, slot.astype(F32), 0.0)
    row = 1
    for scalar in scalars:
        rest = jnp.broadcast_to(scalar, shape)
        for _ in range(PARTS):
            piece = rest.astype(BF16).astype(F32)
            head = jnp.where(row_ids == row, piece, head)
            rest = rest - piece
            row += 1
    return head.astype(BF16)


def head_scalar(head_sum, index):
    first = 1 + PARTS * index
    return jnp.sum(head_sum[first:first + PARTS], axis=0, keepdims=True)


def most_pairs(pairs, sec_count):
    return pairs // sec_count + 1


def load_kernel(
    psi_hbm, left_hbm, pairing_hbm, rows_hbm, cols_hbm, energy_hbm,
    start_ref, left_ref, list_ref, limit_ref, energy_ref, scalar_ref,
    psi_ref, level_ref, rows_ref, cols_ref, pairing_ref, entry_ref, count_ref, sems,
):
    sec_dev, half, width = psi_ref.shape
    terms = left_ref.shape[0]
    sec_count = list_ref.shape[0]
    cap = most_pairs(terms * sec_dev, sec_count)
    pairs = [
        (rows_hbm, rows_ref), (cols_hbm, cols_ref), (energy_hbm, level_ref),
        (pairing_hbm, pairing_ref), (psi_hbm, psi_ref),
    ]
    for t in range(left_ref.shape[0]):
        pairs.append((left_hbm.at[t], left_ref.at[t]))
    copies = [
        pltpu.make_async_copy(source, target, sems.at[i])
        for i, (source, target) in enumerate(pairs)
    ]
    for copy in copies:
        copy.start()
    for owner in range(sec_count):
        count_ref[owner] = 0
        entry_ref[owner, cap] = 0
        for i in range(cap):
            entry_ref[owner, i] = terms * sec_dev
    for copy in copies[:3]:
        copy.wait()
    for s in range(sec_dev):
        limit_ref[s:s + 1, :] = jnp.full((1, LANES), rows_ref[s], jnp.int32)
        limit_ref[sec_dev + s:sec_dev + s + 1, :] = jnp.full((1, LANES), cols_ref[s], jnp.int32)
    columns = energy_columns(level_ref[...])
    for s in range(sec_dev):
        energy_ref[s] = jnp.broadcast_to(columns[:, s:s + 1], (half, LANES))
    copies[3].wait()
    for t in range(terms):
        for s in range(sec_dev):
            target = pairing_ref[s, t]
            owner = quotient(target, sec_dev)
            count = count_ref[owner]
            entry_ref[owner, count] = t * sec_dev + s
            entry_ref[owner, cap] = remainder(target, sec_dev)
            count_ref[owner] = count + 1
    entries = pltpu.make_async_copy(entry_ref, list_ref, sems.at[len(copies)])
    entries.start()
    copies[4].wait()
    first_row = lax.axis_index("rep") * half
    norm = jnp.zeros((8, width), F32)
    level = jnp.zeros((8, width), F32)
    for s in range(sec_dev):
        vector = jnp.where(
            live(limit_ref, s, first_row, (half, width)), psi_ref[s].astype(F32), 0.0
        )
        start_ref[s] = vector.astype(BF16)
        square = vector * vector
        norm += fold(square)
        level += fold(square * spread(energy_ref[s], width))
    scalar_ref[0:8, :] = norm
    scalar_ref[8:16, :] = level
    for copy in copies[5:]:
        copy.wait()
    entries.wait()


def product_kernel(is_first, split, paired, rep_count, sec_count, *refs):
    refs = list(refs)
    take = lambda count: [refs.pop(0) for _ in range(count)]
    list_ref, left_ref, right_ref = take(3)
    if is_first:
        start_ref, limit_ref, scalar_ref = take(3)
        psi_refs = take(rep_count - 1)
        level_refs = take(rep_count - 1)
    else:
        (first_ref,) = take(1)
        vector_refs = take(rep_count)
    out_refs = take(sec_count if split else 1)
    if not is_first:
        (first_hbm,) = take(1)
    inner_ref, entry_ref, sems = refs
    terms, sec_dev, half, width = left_ref.shape
    pairs = terms * sec_dev
    cap = most_pairs(pairs, sec_count)
    rep = lax.axis_index("rep")
    sec = lax.axis_index("sec")
    fetch = pltpu.make_async_copy(list_ref, entry_ref, sems.at[0])
    fetch.start()
    if not is_first:
        put = pltpu.make_async_copy(first_ref, first_hbm, sems.at[1])
        put.start()
    inner_ref[pairs] = jnp.zeros((half, width), BF16)

    def first_row(step):
        return remainder(rep + step, rep_count) * half

    if is_first:
        folded = [scalar_ref[0:8, :], scalar_ref[8:16, :]]
        columns = [energy_columns(ref[...]) for ref in level_refs]
    for s in range(sec_dev):
        if is_first:
            blocks = [start_ref[s]]
            for step in range(1, rep_count):
                psi = psi_refs[step - 1][s]
                mask = live(limit_ref, s, first_row(step), (half, width))
                blocks.append(jnp.where(mask, psi.astype(F32), 0.0).astype(BF16))
        else:
            blocks = [ref[s * half:(s + 1) * half] for ref in vector_refs]
        vector = jnp.concatenate(blocks, axis=0)
        for turn in range(1, rep_count):
            turned = blocks[rep_count - turn:] + blocks[:rep_count - turn]
            vector = jnp.where(rep == turn, jnp.concatenate(turned, axis=0), vector)
        inner = jnp.dot(
            left_ref[:, s].reshape(terms * half, width), vector, preferred_element_type=F32
        ).astype(BF16)
        for t in range(terms):
            inner_ref[t * sec_dev + s] = inner[t * half:(t + 1) * half]
        if is_first:
            for step in range(1, rep_count):
                block = blocks[step].astype(F32)
                square = block * block
                energy = jnp.broadcast_to(columns[step - 1][:, s:s + 1], (half, width))
                folded = [folded[0] + fold(square), folded[1] + fold(square * energy)]
    if is_first:
        scalars = [total(array) for array in folded]
    else:
        head = sum(ref[sec_dev * half:].astype(F32) for ref in vector_refs)
        scalars = [head_scalar(head, i)[:, :LANES] for i in range(2)]
    fetch.wait()
    for d in range(sec_count):
        if not split:
            owner = d
        elif paired:
            owner = sec ^ d
        else:
            owner = remainder(sec + d, sec_count)
        packet = jnp.zeros((half, width), F32)
        for i in range(cap):
            pair = entry_ref[owner, i]
            term = jnp.minimum(quotient(pair, sec_dev), terms - 1)
            packet += jnp.dot(inner_ref[pair], right_ref[term], preferred_element_type=F32)
        out = out_refs[d] if split else out_refs[0].at[d]
        for column in range(width // LANES):
            out[column * half:(column + 1) * half, :] = packet[
                :, column * LANES:(column + 1) * LANES
            ].astype(BF16)
        out[width // LANES * half:, :] = header(entry_ref[owner, cap], scalars)
    if not is_first:
        put.wait()


def sigma_packets(is_first, split, paired, rep_count, lists, left_env, right_env, more):
    terms, sec_dev, half, width = left_env.shape
    sec_count = lax.axis_size("sec")
    packet = (width // LANES * half + HEAD, LANES)
    if split:
        outs = [jax.ShapeDtypeStruct(packet, BF16)] * sec_count
    else:
        outs = [jax.ShapeDtypeStruct((sec_count,) + packet, BF16)]
    out_specs = [whole(pltpu.VMEM)] * len(outs)
    if not is_first:
        outs.append(jax.ShapeDtypeStruct((sec_dev, half, width), BF16))
        out_specs.append(whole(pltpu.HBM))
    pair_flops = 2 * half * width * width * 2
    operands = [lists, left_env, right_env, *more]
    return pl.pallas_call(
        functools.partial(product_kernel, is_first, split, paired, rep_count, sec_count),
        out_shape=outs,
        in_specs=[whole(pltpu.VMEM)] * len(operands),
        out_specs=out_specs,
        scratch_shapes=[
            pltpu.VMEM((terms * sec_dev + 1, half, width), BF16),
            pltpu.SMEM(lists.shape, jnp.int32),
            pltpu.SemaphoreType.DMA((2,)),
        ],
        compiler_params=pltpu.CompilerParams(vmem_limit_bytes=VMEM_BYTES),
        cost_estimate=pl.CostEstimate(
            flops=terms * sec_dev * pair_flops,
            bytes_accessed=2 * (left_env.size + right_env.size),
            transcendentals=0,
        ),
        name="products_first" if is_first else "products_second",
    )(*operands)


def exchange(packets, split, paired, order, groups, late_count=1):
    sec_count = lax.axis_size("sec")
    op_count = lax.axis_size("op")
    op_turns = [
        [(i, (i + step) % op_count) for i in range(op_count)] for step in range(1, op_count)
    ]
    over_op = lambda packet: [lax.ppermute(packet, "op", turn) for turn in op_turns]
    if not split:
        arrived = lax.all_to_all(packets[0], "sec", split_axis=0, concat_axis=0, tiled=True)
        return [arrived] + over_op(arrived), []
    arrived = {0: packets[0]}
    for step in order:
        reach = (lambda i: i ^ step) if paired else (lambda i: (i + step) % sec_count)
        turn = [(i, reach(i)) for i in range(sec_count)]
        arrived[step] = lax.ppermute(packets[step], "sec", turn)
    crossed = [over_op(jnp.stack([arrived[step] for step in group])) for group in groups]
    early, late = crossed[:-late_count], crossed[-late_count:]
    return [arrived[step] for step in [0, *order]] + sum(early, []), sum(late, [])


def views(refs):
    return [
        view
        for ref in refs
        for view in ([ref] if len(ref.shape) == 2 else [ref.at[i] for i in range(ref.shape[0])])
    ]


def add_packets(packet_refs, split, half, base_ref):
    sec_dev, _, width = base_ref.shape
    own = lax.axis_size("sec") if split else 1
    body_rows = width // LANES * half
    if split:
        packet_refs = views(packet_refs)
        heads = [ref[body_rows:].astype(F32) for ref in packet_refs]
        for column in range(width // LANES):
            lanes = slice(column * LANES, (column + 1) * LANES)
            for s in range(sec_dev):
                part = base_ref[s, :, lanes]
                for ref, head in zip(packet_refs, heads):
                    body = ref[column * half:(column + 1) * half].astype(F32)
                    part += jnp.where(head[0:1] == s, body, 0.0)
                base_ref[s, :, lanes] = part
        return sum(heads[1:own], heads[0])

    head_sum = jnp.zeros((HEAD, LANES), F32)
    for index, ref in enumerate(packet_refs):
        def add_one(p, carry):
            head = ref[p, body_rows:, :].astype(F32)
            for column in range(width // LANES):
                body = ref[p, column * half:(column + 1) * half, :].astype(F32)
                lanes = slice(column * LANES, (column + 1) * LANES)
                for s in range(sec_dev):
                    base_ref[s, :, lanes] += jnp.where(head[0:1] == s, body, 0.0)
            return carry + head
        result = lax.fori_loop(0, ref.shape[0], add_one, jnp.zeros((HEAD, LANES), F32))
        if index < own:
            head_sum = head_sum + result
    return head_sum


def late_sum(packet_refs, s, half, width):
    body_rows = width // LANES * half
    value = jnp.zeros((half, width), F32)
    for ref in views(packet_refs):
        body = jnp.concatenate(
            [ref[c * half:(c + 1) * half].astype(F32) for c in range(width // LANES)], axis=1
        )
        slot = spread(ref[body_rows:].astype(F32)[0:1], width)
        value += jnp.where(slot == s, body, 0.0)
    return value


def first_early_kernel(split, count, *refs):
    packet_refs = refs[:count]
    start_ref, energy_ref, base_ref, scalar_ref = refs[count:]
    sec_dev, half, width = start_ref.shape
    for s in range(sec_dev):
        base_ref[s] = spread(energy_ref[s], width) * start_ref[s].astype(F32)
    head_sum = add_packets(packet_refs, split, half, base_ref)
    norm = head_scalar(head_sum, 0)
    scalar_ref[0:1] = norm
    scalar_ref[1:2] = head_scalar(head_sum, 1) / norm


def first_kernel(count, *refs):
    packet_refs = refs[:count]
    limit_ref, start_ref, base_ref, scalar_ref, first_ref, one_ref, vec_ref = refs[count:]
    sec_dev, half, width = start_ref.shape
    shift = spread(scalar_ref[1:2], width)
    first_row = lax.axis_index("rep") * half
    cross = jnp.zeros((8, width), F32)
    square = jnp.zeros((8, width), F32)
    for s in range(sec_dev):
        mask = live(limit_ref, s, first_row, (half, width))
        start = start_ref[s].astype(F32)
        one = jnp.where(mask, base_ref[s] + late_sum(packet_refs, s, half, width), 0.0)
        one_ref[s] = one
        first_ref[s] = one.astype(BF16)
        vector = one - shift * start
        vec_ref[s * half:(s + 1) * half] = vector.astype(BF16)
        cross += fold(start * vector)
        square += fold(vector * vector)
    scalars = (total(cross), total(square))
    vec_ref[sec_dev * half:] = header(jnp.int32(0), scalars, (MORE_ROWS, width))


def second_early_kernel(split, count, entries, *refs):
    packet_refs = refs[:count]
    vec_ref, energy_ref, one_ref, scalar_ref, base_ref, scale_ref = refs[count:]
    sec_dev, half, width = one_ref.shape
    for s in range(sec_dev):
        vector = vec_ref[s * half:(s + 1) * half].astype(F32)
        base_ref[s] = spread(energy_ref[s], width) * vector
    head_sum = add_packets(packet_refs, split, half, base_ref)
    cross = head_scalar(head_sum, 0)
    square = head_scalar(head_sum, 1)
    excess = cross / scalar_ref[0:1]
    resid_sq = jnp.maximum(square - excess * cross, 0.0)
    scale = lax.rsqrt(resid_sq / entries + EPSILON)
    scale_ref[...] = jnp.broadcast_to(scale, scale_ref.shape)
    for s in range(sec_dev):
        base_ref[s] = base_ref[s] - spread(excess, width) * one_ref[s]


def second_kernel(count, *refs):
    packet_refs = refs[:count]
    limit_ref, base_ref, scale_ref, second_ref = refs[count:]
    sec_dev, half, width = base_ref.shape
    scale = spread(scale_ref[0:1], width)
    first_row = lax.axis_index("rep") * half
    for s in range(sec_dev):
        mask = live(limit_ref, s, first_row, (half, width))
        value = scale * (base_ref[s] + late_sum(packet_refs, s, half, width))
        second_ref[s] = jnp.where(mask, value, 0.0).astype(BF16)


def call(kernel, name, outs, *operands, flops=0):
    return pl.pallas_call(
        kernel,
        out_shape=outs,
        in_specs=[whole(pltpu.VMEM)] * len(operands),
        out_specs=[whole(pltpu.VMEM)] * len(outs),
        compiler_params=pltpu.CompilerParams(vmem_limit_bytes=VMEM_BYTES),
        cost_estimate=pl.CostEstimate(flops=flops, bytes_accessed=0, transcendentals=0),
        name=name,
    )(*operands)


def body(psi, left_env, right_env, pairing, block_rows, block_cols, energy):
    sec_count = lax.axis_size("sec")
    op_count = lax.axis_size("op")
    rep_count = lax.axis_size("rep")
    terms, sec_dev, half, width = left_env.shape
    entries = sec_count * sec_dev * rep_count * half * width
    split = sec_count * op_count <= 8
    can_pair = sec_count & (sec_count - 1) == 0
    steps = list(range(1, sec_count))
    first_plan = (False, steps, [[0]] + [[k] for k in steps[:-2]] + [steps[-2:]])
    second_groups = [[0]] + [[k] for k in steps[1:2] + steps[:1] + steps[2:]]
    second_plan = (can_pair, steps, [[0]] + [[k] for k in steps], 2)
    params = pltpu.CompilerParams(vmem_limit_bytes=VMEM_BYTES)
    vec_shape = (sec_dev, half, width)
    vec_bf16 = jax.ShapeDtypeStruct(vec_shape, BF16)

    def from_others(array):
        arrays = []
        for step in range(1, rep_count):
            turn = [((i + step) % rep_count, i) for i in range(rep_count)]
            arrays.append(lax.ppermute(array, "rep", turn))
        return arrays

    psi_others = from_others(psi)
    level_others = from_others(energy)
    start, left_env, lists, limits, levels, scalars = pl.pallas_call(
        load_kernel,
        out_shape=[
            vec_bf16,
            jax.ShapeDtypeStruct(left_env.shape, BF16),
            jax.ShapeDtypeStruct((sec_count, LANES), jnp.int32),
            jax.ShapeDtypeStruct((2 * sec_dev, LANES), jnp.int32),
            jax.ShapeDtypeStruct((sec_dev, half, LANES), F32),
            jax.ShapeDtypeStruct((16, width), F32),
        ],
        in_specs=[whole(pltpu.HBM)] * 6,
        out_specs=[whole(pltpu.VMEM)] * 6,
        scratch_shapes=[
            pltpu.VMEM(vec_shape, BF16),
            pltpu.VMEM((sec_dev, half), F32),
            pltpu.SMEM((sec_dev,), jnp.int32),
            pltpu.SMEM((sec_dev,), jnp.int32),
            pltpu.SMEM((sec_dev, terms), jnp.int32),
            pltpu.SMEM((sec_count, LANES), jnp.int32),
            pltpu.SMEM((sec_count,), jnp.int32),
            pltpu.SemaphoreType.DMA((6 + terms,)),
        ],
        compiler_params=params,
        name="load",
    )(*(
        pltpu.with_memory_space_constraint(array, pltpu.HBM)
        for array in (psi, left_env, pairing.T, block_rows, block_cols, energy)
    ))

    block_f32 = jax.ShapeDtypeStruct(vec_shape, F32)
    row_f32 = jax.ShapeDtypeStruct((8, LANES), F32)

    packets = sigma_packets(
        True, split, first_plan[0], rep_count, lists, left_env, right_env,
        [start, limits, scalars, *psi_others, *level_others],
    )
    early, late = exchange(packets, split, *first_plan)
    base, scalars = call(
        functools.partial(first_early_kernel, split, len(early)), "combine_first_early",
        [block_f32, row_f32], *early, start, levels, flops=EARLY_FLOPS,
    )
    first, sigma_one, vector = call(
        functools.partial(first_kernel, len(late)), "combine_first",
        [
            pltpu.VMEM(vec_shape, BF16),
            block_f32,
            jax.ShapeDtypeStruct((sec_dev * half + MORE_ROWS, width), BF16),
        ],
        *late, limits, start, base, scalars,
    )

    *packets, first_out = sigma_packets(
        False, split, second_plan[0], rep_count, lists, left_env, right_env,
        [first, vector, *from_others(vector)],
    )
    early, late = exchange(packets, split, *second_plan)
    base, scale = call(
        functools.partial(second_early_kernel, split, len(early), entries),
        "combine_second_early", [block_f32, row_f32], *early, vector, levels, sigma_one, scalars,
        flops=EARLY_FLOPS,
    )
    (second_out,) = call(
        functools.partial(second_kernel, len(late)), "combine_second", [vec_bf16],
        *late, limits, base, scale,
    )
    return (first_out, second_out)


def solution(mesh):
    return jax.shard_map(
        body,
        mesh=mesh,
        in_specs=(
            P(("grp", "sec"), "rep", None),
            P(("grp", "op"), "sec", "rep", None),
            P(("grp", "op"), None, None),
            P(("grp", "op"), "sec"),
            P(("grp", "sec")),
            P(("grp", "sec")),
            P(("grp", "sec"), "rep"),
        ),
        out_specs=(P(("grp", "sec"), "rep", None), P(("grp", "sec"), "rep", None)),
        check_vma=False,
    )
```

```python
import functools

import jax
import jax.numpy as jnp
from jax import lax
from jax.experimental import pallas as pl
from jax.experimental.pallas import tpu as pltpu
from jax.sharding import PartitionSpec as P

EPSILON = 1e-06
HEAD = 8
PARTS = 3
EARLY_FLOPS = 10**9
MORE_ROWS = 16
LANES = 128
VMEM_BYTES = 24 * 1024 * 1024
F32 = jnp.float32
BF16 = jnp.bfloat16


def whole(space):
    return pl.BlockSpec(memory_space=space)


def live(limit_ref, s, first_row, shape):
    sec_dev = limit_ref.shape[0] // 2
    repeat = shape[1] // LANES
    rows = jnp.concatenate([limit_ref[s:s + 1, :]] * repeat, axis=1)
    cols = jnp.concatenate([limit_ref[sec_dev + s:sec_dev + s + 1, :]] * repeat, axis=1)
    row_ids = first_row + lax.broadcasted_iota(jnp.int32, shape, 0)
    col_ids = lax.broadcasted_iota(jnp.int32, shape, 1)
    return (row_ids < rows) & (col_ids < cols)


def energy_columns(level):
    missing = -level.shape[0] % 8
    if missing:
        level = jnp.concatenate([level, jnp.zeros((missing, level.shape[1]), F32)], axis=0)
    return level.T


def spread(array, width):
    return jnp.concatenate([array] * (width // LANES), axis=1)


def quotient(value, count):
    return value >> (count.bit_length() - 1) if count & (count - 1) == 0 else lax.div(value, count)


def remainder(value, count):
    return value & (count - 1) if count & (count - 1) == 0 else lax.rem(value, count)


def fold(array):
    rows, width = array.shape
    return jnp.sum(array.reshape(rows // 8, 8, width), axis=0)


def total(array):
    return jnp.sum(jnp.sum(array, axis=0, keepdims=True), axis=1, keepdims=True)


def header(slot, scalars, shape=(HEAD, LANES)):
    row_ids = lax.broadcasted_iota(jnp.int32, shape, 0)
    head = jnp.where(row_ids == 0, slot.astype(F32), 0.0)
    row = 1
    for scalar in scalars:
        rest = jnp.broadcast_to(scalar, shape)
        for _ in range(PARTS):
            piece = rest.astype(BF16).astype(F32)
            head = jnp.where(row_ids == row, piece, head)
            rest = rest - piece
            row += 1
    return head.astype(BF16)


def head_scalar(head_sum, index):
    first = 1 + PARTS * index
    return jnp.sum(head_sum[first:first + PARTS], axis=0, keepdims=True)


def most_pairs(pairs, sec_count):
    return pairs // sec_count + 1


def load_kernel(
    psi_hbm, left_hbm, pairing_hbm, rows_hbm, cols_hbm, energy_hbm,
    start_ref, left_ref, list_ref, limit_ref, energy_ref, scalar_ref,
    psi_ref, level_ref, rows_ref, cols_ref, pairing_ref, entry_ref, count_ref, sems,
):
    sec_dev, half, width = psi_ref.shape
    terms = left_ref.shape[0]
    sec_count = list_ref.shape[0]
    cap = most_pairs(terms * sec_dev, sec_count)
    pairs = [
        (rows_hbm, rows_ref), (cols_hbm, cols_ref), (energy_hbm, level_ref),
        (pairing_hbm, pairing_ref), (psi_hbm, psi_ref),
    ]
    for t in range(left_ref.shape[0]):
        pairs.append((left_hbm.at[t], left_ref.at[t]))
    copies = [
        pltpu.make_async_copy(source, target, sems.at[i])
        for i, (source, target) in enumerate(pairs)
    ]
    for copy in copies:
        copy.start()
    for owner in range(sec_count):
        count_ref[owner] = 0
        entry_ref[owner, cap] = 0
        for i in range(cap):
            entry_ref[owner, i] = terms * sec_dev
    for copy in copies[:3]:
        copy.wait()
    for s in range(sec_dev):
        limit_ref[s:s + 1, :] = jnp.full((1, LANES), rows_ref[s], jnp.int32)
        limit_ref[sec_dev + s:sec_dev + s + 1, :] = jnp.full((1, LANES), cols_ref[s], jnp.int32)
    columns = energy_columns(level_ref[...])
    for s in range(sec_dev):
        energy_ref[s] = jnp.broadcast_to(columns[:, s:s + 1], (half, LANES))
    copies[3].wait()
    for t in range(terms):
        for s in range(sec_dev):
            target = pairing_ref[s, t]
            owner = quotient(target, sec_dev)
            count = count_ref[owner]
            entry_ref[owner, count] = t * sec_dev + s
            entry_ref[owner, cap] = remainder(target, sec_dev)
            count_ref[owner] = count + 1
    entries = pltpu.make_async_copy(entry_ref, list_ref, sems.at[len(copies)])
    entries.start()
    copies[4].wait()
    first_row = lax.axis_index("rep") * half
    norm = jnp.zeros((8, width), F32)
    level = jnp.zeros((8, width), F32)
    for s in range(sec_dev):
        vector = jnp.where(
            live(limit_ref, s, first_row, (half, width)), psi_ref[s].astype(F32), 0.0
        )
        start_ref[s] = vector.astype(BF16)
        square = vector * vector
        norm += fold(square)
        level += fold(square * spread(energy_ref[s], width))
    scalar_ref[0:8, :] = norm
    scalar_ref[8:16, :] = level
    for copy in copies[5:]:
        copy.wait()
    entries.wait()


def product_kernel(is_first, split, paired, rep_count, sec_count, *refs):
    refs = list(refs)
    take = lambda count: [refs.pop(0) for _ in range(count)]
    list_ref, left_ref, right_ref = take(3)
    if is_first:
        start_ref, limit_ref, scalar_ref = take(3)
        psi_refs = take(rep_count - 1)
        level_refs = take(rep_count - 1)
    else:
        (first_ref,) = take(1)
        vector_refs = take(rep_count)
    out_refs = take(sec_count if split else 1)
    if not is_first:
        (first_hbm,) = take(1)
    inner_ref, entry_ref, sems = refs
    terms, sec_dev, half, width = left_ref.shape
    pairs = terms * sec_dev
    cap = most_pairs(pairs, sec_count)
    rep = lax.axis_index("rep")
    sec = lax.axis_index("sec")
    fetch = pltpu.make_async_copy(list_ref, entry_ref, sems.at[0])
    fetch.start()
    if not is_first:
        put = pltpu.make_async_copy(first_ref, first_hbm, sems.at[1])
        put.start()
    inner_ref[pairs] = jnp.zeros((half, width), BF16)

    def first_row(step):
        return remainder(rep + step, rep_count) * half

    if is_first:
        folded = [scalar_ref[0:8, :], scalar_ref[8:16, :]]
        columns = [energy_columns(ref[...]) for ref in level_refs]
    for s in range(sec_dev):
        if is_first:
            blocks = [start_ref[s]]
            for step in range(1, rep_count):
                psi = psi_refs[step - 1][s]
                mask = live(limit_ref, s, first_row(step), (half, width))
                blocks.append(jnp.where(mask, psi.astype(F32), 0.0).astype(BF16))
        else:
            blocks = [ref[s * half:(s + 1) * half] for ref in vector_refs]
        vector = jnp.concatenate(blocks, axis=0)
        for turn in range(1, rep_count):
            turned = blocks[rep_count - turn:] + blocks[:rep_count - turn]
            vector = jnp.where(rep == turn, jnp.concatenate(turned, axis=0), vector)
        inner = jnp.dot(
            left_ref[:, s].reshape(terms * half, width), vector, preferred_element_type=F32
        ).astype(BF16)
        for t in range(terms):
            inner_ref[t * sec_dev + s] = inner[t * half:(t + 1) * half]
        if is_first:
            for step in range(1, rep_count):
                block = blocks[step].astype(F32)
                square = block * block
                energy = jnp.broadcast_to(columns[step - 1][:, s:s + 1], (half, width))
                folded = [folded[0] + fold(square), folded[1] + fold(square * energy)]
    if is_first:
        scalars = [total(array) for array in folded]
    else:
        head = sum(ref[sec_dev * half:].astype(F32) for ref in vector_refs)
        scalars = [head_scalar(head, i)[:, :LANES] for i in range(2)]
    fetch.wait()
    for d in range(sec_count):
        if not split:
            owner = d
        elif paired:
            owner = sec ^ d
        else:
            owner = remainder(sec + d, sec_count)
        listed = [entry_ref[owner, i] for i in range(cap)]
        picked = [jnp.minimum(quotient(pair, sec_dev), terms - 1) for pair in listed]
        packet = jnp.dot(
            jnp.concatenate([inner_ref[pair] for pair in listed], axis=1),
            jnp.concatenate([right_ref[term] for term in picked], axis=0),
            preferred_element_type=F32,
        )
        out = out_refs[d] if split else out_refs[0].at[d]
        for column in range(width // LANES):
            out[column * half:(column + 1) * half, :] = packet[
                :, column * LANES:(column + 1) * LANES
            ].astype(BF16)
        out[width // LANES * half:, :] = header(entry_ref[owner, cap], scalars)
    if not is_first:
        put.wait()


def sigma_packets(is_first, split, paired, rep_count, lists, left_env, right_env, more):
    terms, sec_dev, half, width = left_env.shape
    sec_count = lax.axis_size("sec")
    packet = (width // LANES * half + HEAD, LANES)
    if split:
        outs = [jax.ShapeDtypeStruct(packet, BF16)] * sec_count
    else:
        outs = [jax.ShapeDtypeStruct((sec_count,) + packet, BF16)]
    out_specs = [whole(pltpu.VMEM)] * len(outs)
    if not is_first:
        outs.append(jax.ShapeDtypeStruct((sec_dev, half, width), BF16))
        out_specs.append(whole(pltpu.HBM))
    pair_flops = 2 * half * width * width * 2
    operands = [lists, left_env, right_env, *more]
    return pl.pallas_call(
        functools.partial(product_kernel, is_first, split, paired, rep_count, sec_count),
        out_shape=outs,
        in_specs=[whole(pltpu.VMEM)] * len(operands),
        out_specs=out_specs,
        scratch_shapes=[
            pltpu.VMEM((terms * sec_dev + 1, half, width), BF16),
            pltpu.SMEM(lists.shape, jnp.int32),
            pltpu.SemaphoreType.DMA((2,)),
        ],
        compiler_params=pltpu.CompilerParams(vmem_limit_bytes=VMEM_BYTES),
        cost_estimate=pl.CostEstimate(
            flops=terms * sec_dev * pair_flops,
            bytes_accessed=2 * (left_env.size + right_env.size),
            transcendentals=0,
        ),
        name="products_first" if is_first else "products_second",
    )(*operands)


def exchange(packets, split, paired, order, groups):
    sec_count = lax.axis_size("sec")
    op_count = lax.axis_size("op")
    op_turns = [
        [(i, (i + step) % op_count) for i in range(op_count)] for step in range(1, op_count)
    ]
    over_op = lambda packet: [lax.ppermute(packet, "op", turn) for turn in op_turns]
    if not split:
        arrived = lax.all_to_all(packets[0], "sec", split_axis=0, concat_axis=0, tiled=True)
        return [arrived] + over_op(arrived), []
    arrived = {0: packets[0]}
    for step in order:
        reach = (lambda i: i ^ step) if paired else (lambda i: (i + step) % sec_count)
        turn = [(i, reach(i)) for i in range(sec_count)]
        arrived[step] = lax.ppermute(packets[step], "sec", turn)
    crossed = [over_op(jnp.stack([arrived[step] for step in group])) for group in groups]
    return [arrived[step] for step in [0, *order]] + sum(crossed[:-1], []), crossed[-1]


def views(refs):
    return [
        view
        for ref in refs
        for view in ([ref] if len(ref.shape) == 2 else [ref.at[i] for i in range(ref.shape[0])])
    ]


def add_packets(packet_refs, split, half, base_ref):
    sec_dev, _, width = base_ref.shape
    own = lax.axis_size("sec") if split else 1
    body_rows = width // LANES * half
    if split:
        packet_refs = views(packet_refs)
        heads = [ref[body_rows:].astype(F32) for ref in packet_refs]
        for column in range(width // LANES):
            lanes = slice(column * LANES, (column + 1) * LANES)
            for s in range(sec_dev):
                part = base_ref[s, :, lanes]
                for ref, head in zip(packet_refs, heads):
                    body = ref[column * half:(column + 1) * half].astype(F32)
                    part += jnp.where(head[0:1] == s, body, 0.0)
                base_ref[s, :, lanes] = part
        return sum(heads[1:own], heads[0])

    head_sum = jnp.zeros((HEAD, LANES), F32)
    for index, ref in enumerate(packet_refs):
        def add_one(p, carry):
            head = ref[p, body_rows:, :].astype(F32)
            for column in range(width // LANES):
                body = ref[p, column * half:(column + 1) * half, :].astype(F32)
                lanes = slice(column * LANES, (column + 1) * LANES)
                for s in range(sec_dev):
                    base_ref[s, :, lanes] += jnp.where(head[0:1] == s, body, 0.0)
            return carry + head
        result = lax.fori_loop(0, ref.shape[0], add_one, jnp.zeros((HEAD, LANES), F32))
        if index < own:
            head_sum = head_sum + result
    return head_sum


def late_sum(packet_refs, s, half, width):
    body_rows = width // LANES * half
    value = jnp.zeros((half, width), F32)
    for ref in views(packet_refs):
        body = jnp.concatenate(
            [ref[c * half:(c + 1) * half].astype(F32) for c in range(width // LANES)], axis=1
        )
        slot = spread(ref[body_rows:].astype(F32)[0:1], width)
        value += jnp.where(slot == s, body, 0.0)
    return value


def first_early_kernel(split, count, *refs):
    packet_refs = refs[:count]
    start_ref, energy_ref, base_ref, scalar_ref = refs[count:]
    sec_dev, half, width = start_ref.shape
    for s in range(sec_dev):
        base_ref[s] = spread(energy_ref[s], width) * start_ref[s].astype(F32)
    head_sum = add_packets(packet_refs, split, half, base_ref)
    norm = head_scalar(head_sum, 0)
    scalar_ref[0:1] = norm
    scalar_ref[1:2] = head_scalar(head_sum, 1) / norm


def first_kernel(count, *refs):
    packet_refs = refs[:count]
    limit_ref, start_ref, base_ref, scalar_ref, first_ref, one_ref, vec_ref = refs[count:]
    sec_dev, half, width = start_ref.shape
    shift = spread(scalar_ref[1:2], width)
    first_row = lax.axis_index("rep") * half
    cross = jnp.zeros((8, width), F32)
    square = jnp.zeros((8, width), F32)
    for s in range(sec_dev):
        mask = live(limit_ref, s, first_row, (half, width))
        start = start_ref[s].astype(F32)
        one = jnp.where(mask, base_ref[s] + late_sum(packet_refs, s, half, width), 0.0)
        one_ref[s] = one
        first_ref[s] = one.astype(BF16)
        vector = one - shift * start
        vec_ref[s * half:(s + 1) * half] = vector.astype(BF16)
        cross += fold(start * vector)
        square += fold(vector * vector)
    scalars = (total(cross), total(square))
    vec_ref[sec_dev * half:] = header(jnp.int32(0), scalars, (MORE_ROWS, width))


def second_early_kernel(split, count, entries, *refs):
    packet_refs = refs[:count]
    vec_ref, energy_ref, one_ref, scalar_ref, base_ref, scale_ref = refs[count:]
    sec_dev, half, width = one_ref.shape
    for s in range(sec_dev):
        vector = vec_ref[s * half:(s + 1) * half].astype(F32)
        base_ref[s] = spread(energy_ref[s], width) * vector
    head_sum = add_packets(packet_refs, split, half, base_ref)
    cross = head_scalar(head_sum, 0)
    square = head_scalar(head_sum, 1)
    excess = cross / scalar_ref[0:1]
    resid_sq = jnp.maximum(square - excess * cross, 0.0)
    scale = lax.rsqrt(resid_sq / entries + EPSILON)
    scale_ref[...] = jnp.broadcast_to(scale, scale_ref.shape)
    for s in range(sec_dev):
        base_ref[s] = base_ref[s] - spread(excess, width) * one_ref[s]


def second_kernel(count, *refs):
    packet_refs = refs[:count]
    limit_ref, base_ref, scale_ref, second_ref = refs[count:]
    sec_dev, half, width = base_ref.shape
    scale = spread(scale_ref[0:1], width)
    first_row = lax.axis_index("rep") * half
    for s in range(sec_dev):
        mask = live(limit_ref, s, first_row, (half, width))
        value = scale * (base_ref[s] + late_sum(packet_refs, s, half, width))
        second_ref[s] = jnp.where(mask, value, 0.0).astype(BF16)


def call(kernel, name, outs, *operands, flops=0):
    return pl.pallas_call(
        kernel,
        out_shape=outs,
        in_specs=[whole(pltpu.VMEM)] * len(operands),
        out_specs=[whole(pltpu.VMEM)] * len(outs),
        compiler_params=pltpu.CompilerParams(vmem_limit_bytes=VMEM_BYTES),
        cost_estimate=pl.CostEstimate(flops=flops, bytes_accessed=0, transcendentals=0),
        name=name,
    )(*operands)


def body(psi, left_env, right_env, pairing, block_rows, block_cols, energy):
    sec_count = lax.axis_size("sec")
    op_count = lax.axis_size("op")
    rep_count = lax.axis_size("rep")
    terms, sec_dev, half, width = left_env.shape
    entries = sec_count * sec_dev * rep_count * half * width
    split = sec_count * op_count <= 8
    can_pair = sec_count & (sec_count - 1) == 0
    steps = list(range(1, sec_count))
    first_plan = (False, steps, [[0]] + [[k] for k in steps[:-2]] + [steps[-2:]])
    second_groups = [[0]] + [[k] for k in steps[1:2] + steps[:1] + steps[2:]]
    second_plan = (can_pair, steps[1:2] + steps[:1] + steps[2:], second_groups)
    params = pltpu.CompilerParams(vmem_limit_bytes=VMEM_BYTES)
    vec_shape = (sec_dev, half, width)
    vec_bf16 = jax.ShapeDtypeStruct(vec_shape, BF16)

    def from_others(array):
        arrays = []
        for step in range(1, rep_count):
            turn = [((i + step) % rep_count, i) for i in range(rep_count)]
            arrays.append(lax.ppermute(array, "rep", turn))
        return arrays

    psi_others = from_others(psi)
    level_others = from_others(energy)
    start, left_env, lists, limits, levels, scalars = pl.pallas_call(
        load_kernel,
        out_shape=[
            vec_bf16,
            jax.ShapeDtypeStruct(left_env.shape, BF16),
            jax.ShapeDtypeStruct((sec_count, LANES), jnp.int32),
            jax.ShapeDtypeStruct((2 * sec_dev, LANES), jnp.int32),
            jax.ShapeDtypeStruct((sec_dev, half, LANES), F32),
            jax.ShapeDtypeStruct((16, width), F32),
        ],
        in_specs=[whole(pltpu.HBM)] * 6,
        out_specs=[whole(pltpu.VMEM)] * 6,
        scratch_shapes=[
            pltpu.VMEM(vec_shape, BF16),
            pltpu.VMEM((sec_dev, half), F32),
            pltpu.SMEM((sec_dev,), jnp.int32),
            pltpu.SMEM((sec_dev,), jnp.int32),
            pltpu.SMEM((sec_dev, terms), jnp.int32),
            pltpu.SMEM((sec_count, LANES), jnp.int32),
            pltpu.SMEM((sec_count,), jnp.int32),
            pltpu.SemaphoreType.DMA((6 + terms,)),
        ],
        compiler_params=params,
        name="load",
    )(*(
        pltpu.with_memory_space_constraint(array, pltpu.HBM)
        for array in (psi, left_env, pairing.T, block_rows, block_cols, energy)
    ))

    block_f32 = jax.ShapeDtypeStruct(vec_shape, F32)
    row_f32 = jax.ShapeDtypeStruct((8, LANES), F32)

    packets = sigma_packets(
        True, split, first_plan[0], rep_count, lists, left_env, right_env,
        [start, limits, scalars, *psi_others, *level_others],
    )
    early, late = exchange(packets, split, *first_plan)
    base, scalars = call(
        functools.partial(first_early_kernel, split, len(early)), "combine_first_early",
        [block_f32, row_f32], *early, start, levels, flops=EARLY_FLOPS,
    )
    first, sigma_one, vector = call(
        functools.partial(first_kernel, len(late)), "combine_first",
        [
            pltpu.VMEM(vec_shape, BF16),
            block_f32,
            jax.ShapeDtypeStruct((sec_dev * half + MORE_ROWS, width), BF16),
        ],
        *late, limits, start, base, scalars,
    )

    *packets, first_out = sigma_packets(
        False, split, second_plan[0], rep_count, lists, left_env, right_env,
        [first, vector, *from_others(vector)],
    )
    early, late = exchange(packets, split, *second_plan)
    base, scale = call(
        functools.partial(second_early_kernel, split, len(early), entries),
        "combine_second_early", [block_f32, row_f32], *early, vector, levels, sigma_one, scalars,
        flops=EARLY_FLOPS,
    )
    (second_out,) = call(
        functools.partial(second_kernel, len(late)), "combine_second", [vec_bf16],
        *late, limits, base, scale,
    )
    return (first_out, second_out)


def solution(mesh):
    return jax.shard_map(
        body,
        mesh=mesh,
        in_specs=(
            P(("grp", "sec"), "rep", None),
            P(("grp", "op"), "sec", "rep", None),
            P(("grp", "op"), None, None),
            P(("grp", "op"), "sec"),
            P(("grp", "sec")),
            P(("grp", "sec")),
            P(("grp", "sec"), "rep"),
        ),
        out_specs=(P(("grp", "sec"), "rep", None), P(("grp", "sec"), "rep", None)),
        check_vma=False,
    )
```

```python
import functools

import jax
import jax.numpy as jnp
from jax import lax
from jax.experimental import pallas as pl
from jax.experimental.pallas import tpu as pltpu
from jax.sharding import PartitionSpec as P

EPSILON = 1e-06
HEAD = 8
PARTS = 3
EARLY_FLOPS = 10**9
MORE_ROWS = 16
LANES = 128
VMEM_BYTES = 24 * 1024 * 1024
F32 = jnp.float32
BF16 = jnp.bfloat16


def whole(space):
    return pl.BlockSpec(memory_space=space)


def live(limit_ref, s, first_row, shape):
    sec_dev = limit_ref.shape[0] // 2
    repeat = shape[1] // LANES
    rows = jnp.concatenate([limit_ref[s:s + 1, :]] * repeat, axis=1)
    cols = jnp.concatenate([limit_ref[sec_dev + s:sec_dev + s + 1, :]] * repeat, axis=1)
    row_ids = first_row + lax.broadcasted_iota(jnp.int32, shape, 0)
    col_ids = lax.broadcasted_iota(jnp.int32, shape, 1)
    return (row_ids < rows) & (col_ids < cols)


def energy_columns(level):
    missing = -level.shape[0] % 8
    if missing:
        level = jnp.concatenate([level, jnp.zeros((missing, level.shape[1]), F32)], axis=0)
    return level.T


def spread(array, width):
    return jnp.concatenate([array] * (width // LANES), axis=1)


def quotient(value, count):
    return value >> (count.bit_length() - 1) if count & (count - 1) == 0 else lax.div(value, count)


def remainder(value, count):
    return value & (count - 1) if count & (count - 1) == 0 else lax.rem(value, count)


def fold(array):
    rows, width = array.shape
    return jnp.sum(array.reshape(rows // 8, 8, width), axis=0)


def total(array):
    return jnp.sum(jnp.sum(array, axis=0, keepdims=True), axis=1, keepdims=True)


def header(slot, scalars, shape=(HEAD, LANES)):
    row_ids = lax.broadcasted_iota(jnp.int32, shape, 0)
    head = jnp.where(row_ids == 0, slot.astype(F32), 0.0)
    row = 1
    for scalar in scalars:
        rest = jnp.broadcast_to(scalar, shape)
        for _ in range(PARTS):
            piece = rest.astype(BF16).astype(F32)
            head = jnp.where(row_ids == row, piece, head)
            rest = rest - piece
            row += 1
    return head.astype(BF16)


def head_scalar(head_sum, index):
    first = 1 + PARTS * index
    return jnp.sum(head_sum[first:first + PARTS], axis=0, keepdims=True)


def most_pairs(pairs, sec_count):
    return pairs // sec_count + 1


def load_kernel(
    psi_hbm, left_hbm, pairing_hbm, rows_hbm, cols_hbm, energy_hbm,
    start_ref, left_ref, list_ref, limit_ref, energy_ref, scalar_ref,
    psi_ref, level_ref, rows_ref, cols_ref, pairing_ref, entry_ref, count_ref, sems,
):
    sec_dev, half, width = psi_ref.shape
    terms = left_ref.shape[0]
    sec_count = list_ref.shape[0]
    cap = most_pairs(terms * sec_dev, sec_count)
    pairs = [
        (rows_hbm, rows_ref), (cols_hbm, cols_ref), (energy_hbm, level_ref),
        (pairing_hbm, pairing_ref), (psi_hbm, psi_ref),
    ]
    for t in range(left_ref.shape[0]):
        pairs.append((left_hbm.at[t], left_ref.at[t]))
    copies = [
        pltpu.make_async_copy(source, target, sems.at[i])
        for i, (source, target) in enumerate(pairs)
    ]
    for copy in copies:
        copy.start()
    for owner in range(sec_count):
        count_ref[owner] = 0
        entry_ref[owner, cap] = 0
        for i in range(cap):
            entry_ref[owner, i] = terms * sec_dev
    for copy in copies[:3]:
        copy.wait()
    for s in range(sec_dev):
        limit_ref[s:s + 1, :] = jnp.full((1, LANES), rows_ref[s], jnp.int32)
        limit_ref[sec_dev + s:sec_dev + s + 1, :] = jnp.full((1, LANES), cols_ref[s], jnp.int32)
    columns = energy_columns(level_ref[...])
    for s in range(sec_dev):
        energy_ref[s] = jnp.broadcast_to(columns[:, s:s + 1], (half, LANES))
    copies[3].wait()
    for t in range(terms):
        for s in range(sec_dev):
            target = pairing_ref[s, t]
            owner = quotient(target, sec_dev)
            count = count_ref[owner]
            entry_ref[owner, count] = t * sec_dev + s
            entry_ref[owner, cap] = remainder(target, sec_dev)
            count_ref[owner] = count + 1
    entries = pltpu.make_async_copy(entry_ref, list_ref, sems.at[len(copies)])
    entries.start()
    copies[4].wait()
    first_row = lax.axis_index("rep") * half
    norm = jnp.zeros((8, width), F32)
    level = jnp.zeros((8, width), F32)
    for s in range(sec_dev):
        vector = jnp.where(
            live(limit_ref, s, first_row, (half, width)), psi_ref[s].astype(F32), 0.0
        )
        start_ref[s] = vector.astype(BF16)
        square = vector * vector
        norm += fold(square)
        level += fold(square * spread(energy_ref[s], width))
    scalar_ref[0:8, :] = norm
    scalar_ref[8:16, :] = level
    for copy in copies[5:]:
        copy.wait()
    entries.wait()


def product_kernel(is_first, split, paired, rep_count, sec_count, *refs):
    refs = list(refs)
    take = lambda count: [refs.pop(0) for _ in range(count)]
    list_ref, left_ref, right_ref = take(3)
    if is_first:
        start_ref, limit_ref, scalar_ref = take(3)
        psi_refs = take(rep_count - 1)
        level_refs = take(rep_count - 1)
    else:
        (first_ref,) = take(1)
        vector_refs = take(rep_count)
    out_refs = take(sec_count if split else 1)
    if not is_first:
        (first_hbm,) = take(1)
    inner_ref, entry_ref, sems = refs
    terms, sec_dev, half, width = left_ref.shape
    pairs = terms * sec_dev
    cap = most_pairs(pairs, sec_count)
    rep = lax.axis_index("rep")
    sec = lax.axis_index("sec")
    fetch = pltpu.make_async_copy(list_ref, entry_ref, sems.at[0])
    fetch.start()
    if not is_first:
        put = pltpu.make_async_copy(first_ref, first_hbm, sems.at[1])
        put.start()
    inner_ref[pairs] = jnp.zeros((half, width), BF16)

    def first_row(step):
        return remainder(rep + step, rep_count) * half

    if is_first:
        folded = [scalar_ref[0:8, :], scalar_ref[8:16, :]]
        columns = [energy_columns(ref[...]) for ref in level_refs]
    for s in range(sec_dev):
        if is_first:
            blocks = [start_ref[s]]
            for step in range(1, rep_count):
                psi = psi_refs[step - 1][s]
                mask = live(limit_ref, s, first_row(step), (half, width))
                blocks.append(jnp.where(mask, psi.astype(F32), 0.0).astype(BF16))
        else:
            blocks = [ref[s * half:(s + 1) * half] for ref in vector_refs]
        vector = jnp.concatenate(blocks, axis=0)
        for turn in range(1, rep_count):
            turned = blocks[rep_count - turn:] + blocks[:rep_count - turn]
            vector = jnp.where(rep == turn, jnp.concatenate(turned, axis=0), vector)
        inner = jnp.dot(
            left_ref[:, s].reshape(terms * half, width), vector, preferred_element_type=F32
        ).astype(BF16)
        for t in range(terms):
            inner_ref[t * sec_dev + s] = inner[t * half:(t + 1) * half]
        if is_first:
            for step in range(1, rep_count):
                block = blocks[step].astype(F32)
                square = block * block
                energy = jnp.broadcast_to(columns[step - 1][:, s:s + 1], (half, width))
                folded = [folded[0] + fold(square), folded[1] + fold(square * energy)]
    if is_first:
        scalars = [total(array) for array in folded]
    else:
        head = sum(ref[sec_dev * half:].astype(F32) for ref in vector_refs)
        scalars = [head_scalar(head, i)[:, :LANES] for i in range(2)]
    fetch.wait()
    for d in range(sec_count):
        if not split:
            owner = d
        elif paired:
            owner = sec ^ d
        else:
            owner = remainder(sec + d, sec_count)
        packet = jnp.zeros((half, width), F32)
        for i in range(cap):
            pair = entry_ref[owner, i]
            term = jnp.minimum(quotient(pair, sec_dev), terms - 1)
            packet += jnp.dot(inner_ref[pair], right_ref[term], preferred_element_type=F32)
        out = out_refs[d] if split else out_refs[0].at[d]
        for column in range(width // LANES):
            out[column * half:(column + 1) * half, :] = packet[
                :, column * LANES:(column + 1) * LANES
            ].astype(BF16)
        out[width // LANES * half:, :] = header(entry_ref[owner, cap], scalars)
    if not is_first:
        put.wait()


def sigma_packets(is_first, split, paired, rep_count, lists, left_env, right_env, more):
    terms, sec_dev, half, width = left_env.shape
    sec_count = lax.axis_size("sec")
    packet = (width // LANES * half + HEAD, LANES)
    if split:
        outs = [jax.ShapeDtypeStruct(packet, BF16)] * sec_count
    else:
        outs = [jax.ShapeDtypeStruct((sec_count,) + packet, BF16)]
    out_specs = [whole(pltpu.VMEM)] * len(outs)
    if not is_first:
        outs.append(jax.ShapeDtypeStruct((sec_dev, half, width), BF16))
        out_specs.append(whole(pltpu.HBM))
    pair_flops = 2 * half * width * width * 2
    operands = [lists, left_env, right_env, *more]
    return pl.pallas_call(
        functools.partial(product_kernel, is_first, split, paired, rep_count, sec_count),
        out_shape=outs,
        in_specs=[whole(pltpu.VMEM)] * len(operands),
        out_specs=out_specs,
        scratch_shapes=[
            pltpu.VMEM((terms * sec_dev + 1, half, width), BF16),
            pltpu.SMEM(lists.shape, jnp.int32),
            pltpu.SemaphoreType.DMA((2,)),
        ],
        compiler_params=pltpu.CompilerParams(vmem_limit_bytes=VMEM_BYTES),
        cost_estimate=pl.CostEstimate(
            flops=terms * sec_dev * pair_flops,
            bytes_accessed=2 * (left_env.size + right_env.size),
            transcendentals=0,
        ),
        name="products_first" if is_first else "products_second",
    )(*operands)


def exchange(packets, split, paired, order, groups):
    sec_count = lax.axis_size("sec")
    op_count = lax.axis_size("op")
    op_turns = [
        [(i, (i + step) % op_count) for i in range(op_count)] for step in range(1, op_count)
    ]
    over_op = lambda packet: [lax.ppermute(packet, "op", turn) for turn in op_turns]
    if not split:
        arrived = lax.all_to_all(packets[0], "sec", split_axis=0, concat_axis=0, tiled=True)
        return [arrived] + over_op(arrived), []
    arrived = {0: packets[0]}
    for step in order:
        reach = (lambda i: i ^ step) if paired else (lambda i: (i + step) % sec_count)
        turn = [(i, reach(i)) for i in range(sec_count)]
        arrived[step] = lax.ppermute(packets[step], "sec", turn)
    crossed = [over_op(jnp.stack([arrived[step] for step in group])) for group in groups]
    return [arrived[step] for step in [0, *order]] + sum(crossed[:-1], []), crossed[-1]


def views(refs):
    return [
        view
        for ref in refs
        for view in ([ref] if len(ref.shape) == 2 else [ref.at[i] for i in range(ref.shape[0])])
    ]


def add_packets(packet_refs, split, half, base_ref):
    sec_dev, _, width = base_ref.shape
    own = lax.axis_size("sec") if split else 1
    body_rows = width // LANES * half
    if split:
        packet_refs = views(packet_refs)
        heads = [ref[body_rows:].astype(F32) for ref in packet_refs]
        for column in range(width // LANES):
            lanes = slice(column * LANES, (column + 1) * LANES)
            for s in range(sec_dev):
                part = base_ref[s, :, lanes]
                for ref, head in zip(packet_refs, heads):
                    body = ref[column * half:(column + 1) * half].astype(F32)
                    part += jnp.where(head[0:1] == s, body, 0.0)
                base_ref[s, :, lanes] = part
        return sum(heads[1:own], heads[0])

    head_sum = jnp.zeros((HEAD, LANES), F32)
    for index, ref in enumerate(packet_refs):
        def add_one(p, carry):
            head = ref[p, body_rows:, :].astype(F32)
            for column in range(width // LANES):
                body = ref[p, column * half:(column + 1) * half, :].astype(F32)
                lanes = slice(column * LANES, (column + 1) * LANES)
                for s in range(sec_dev):
                    base_ref[s, :, lanes] += jnp.where(head[0:1] == s, body, 0.0)
            return carry + head
        result = lax.fori_loop(0, ref.shape[0], add_one, jnp.zeros((HEAD, LANES), F32))
        if index < own:
            head_sum = head_sum + result
    return head_sum


def late_sum(packet_refs, s, half, width):
    body_rows = width // LANES * half
    value = jnp.zeros((half, width), F32)
    for ref in views(packet_refs):
        body = jnp.concatenate(
            [ref[c * half:(c + 1) * half].astype(F32) for c in range(width // LANES)], axis=1
        )
        slot = spread(ref[body_rows:].astype(F32)[0:1], width)
        value += jnp.where(slot == s, body, 0.0)
    return value


def first_early_kernel(split, count, *refs):
    packet_refs = refs[:count]
    start_ref, energy_ref, base_ref, scalar_ref = refs[count:]
    sec_dev, half, width = start_ref.shape
    for s in range(sec_dev):
        base_ref[s] = spread(energy_ref[s], width) * start_ref[s].astype(F32)
    head_sum = add_packets(packet_refs, split, half, base_ref)
    norm = head_scalar(head_sum, 0)
    scalar_ref[0:1] = norm
    scalar_ref[1:2] = head_scalar(head_sum, 1) / norm


def first_kernel(count, *refs):
    packet_refs = refs[:count]
    limit_ref, start_ref, base_ref, scalar_ref, first_ref, one_ref, vec_ref = refs[count:]
    sec_dev, half, width = start_ref.shape
    shift = spread(scalar_ref[1:2], width)
    first_row = lax.axis_index("rep") * half
    cross = jnp.zeros((8, width), F32)
    square = jnp.zeros((8, width), F32)
    for s in range(sec_dev):
        mask = live(limit_ref, s, first_row, (half, width))
        start = start_ref[s].astype(F32)
        one = jnp.where(mask, base_ref[s] + late_sum(packet_refs, s, half, width), 0.0)
        one_ref[s] = one
        first_ref[s] = one.astype(BF16)
        vector = one - shift * start
        vec_ref[s * half:(s + 1) * half] = vector.astype(BF16)
        cross += fold(start * vector)
        square += fold(vector * vector)
    scalars = (total(cross), total(square))
    vec_ref[sec_dev * half:] = header(jnp.int32(0), scalars, (MORE_ROWS, width))


def second_early_kernel(split, count, entries, *refs):
    packet_refs = refs[:count]
    vec_ref, energy_ref, one_ref, scalar_ref, base_ref, scale_ref = refs[count:]
    sec_dev, half, width = one_ref.shape
    for s in range(sec_dev):
        vector = vec_ref[s * half:(s + 1) * half].astype(F32)
        base_ref[s] = spread(energy_ref[s], width) * vector
    head_sum = add_packets(packet_refs, split, half, base_ref)
    cross = head_scalar(head_sum, 0)
    square = head_scalar(head_sum, 1)
    excess = cross / scalar_ref[0:1]
    resid_sq = jnp.maximum(square - excess * cross, 0.0)
    scale = lax.rsqrt(resid_sq / entries + EPSILON)
    scale_ref[...] = jnp.broadcast_to(scale, scale_ref.shape)
    for s in range(sec_dev):
        base_ref[s] = base_ref[s] - spread(excess, width) * one_ref[s]


def second_kernel(count, *refs):
    packet_refs = refs[:count]
    limit_ref, base_ref, scale_ref, second_ref = refs[count:]
    sec_dev, half, width = base_ref.shape
    scale = spread(scale_ref[0:1], width)
    first_row = lax.axis_index("rep") * half
    for s in range(sec_dev):
        mask = live(limit_ref, s, first_row, (half, width))
        value = scale * (base_ref[s] + late_sum(packet_refs, s, half, width))
        second_ref[s] = jnp.where(mask, value, 0.0).astype(BF16)


def call(kernel, name, outs, *operands, flops=0):
    return pl.pallas_call(
        kernel,
        out_shape=outs,
        in_specs=[whole(pltpu.VMEM)] * len(operands),
        out_specs=[whole(pltpu.VMEM)] * len(outs),
        compiler_params=pltpu.CompilerParams(vmem_limit_bytes=VMEM_BYTES),
        cost_estimate=pl.CostEstimate(flops=flops, bytes_accessed=0, transcendentals=0),
        name=name,
    )(*operands)


def body(psi, left_env, right_env, pairing, block_rows, block_cols, energy):
    sec_count = lax.axis_size("sec")
    op_count = lax.axis_size("op")
    rep_count = lax.axis_size("rep")
    terms, sec_dev, half, width = left_env.shape
    entries = sec_count * sec_dev * rep_count * half * width
    split = sec_count * op_count <= 8
    can_pair = sec_count & (sec_count - 1) == 0
    steps = list(range(1, sec_count))
    first_plan = (False, steps, [[0]] + [[k] for k in steps[:-2]] + [steps[-2:]])
    second_groups = [[0]] + [[k] for k in steps[1:2] + steps[:1] + steps[2:]]
    second_plan = (False, steps, [[0]] + [[k] for k in steps[:-2]] + [steps[-2:]])
    params = pltpu.CompilerParams(vmem_limit_bytes=VMEM_BYTES)
    vec_shape = (sec_dev, half, width)
    vec_bf16 = jax.ShapeDtypeStruct(vec_shape, BF16)

    def from_others(array):
        arrays = []
        for step in range(1, rep_count):
            turn = [((i + step) % rep_count, i) for i in range(rep_count)]
            arrays.append(lax.ppermute(array, "rep", turn))
        return arrays

    psi_others = from_others(psi)
    level_others = from_others(energy)
    start, left_env, lists, limits, levels, scalars = pl.pallas_call(
        load_kernel,
        out_shape=[
            vec_bf16,
            jax.ShapeDtypeStruct(left_env.shape, BF16),
            jax.ShapeDtypeStruct((sec_count, LANES), jnp.int32),
            jax.ShapeDtypeStruct((2 * sec_dev, LANES), jnp.int32),
            jax.ShapeDtypeStruct((sec_dev, half, LANES), F32),
            jax.ShapeDtypeStruct((16, width), F32),
        ],
        in_specs=[whole(pltpu.HBM)] * 6,
        out_specs=[whole(pltpu.VMEM)] * 6,
        scratch_shapes=[
            pltpu.VMEM(vec_shape, BF16),
            pltpu.VMEM((sec_dev, half), F32),
            pltpu.SMEM((sec_dev,), jnp.int32),
            pltpu.SMEM((sec_dev,), jnp.int32),
            pltpu.SMEM((sec_dev, terms), jnp.int32),
            pltpu.SMEM((sec_count, LANES), jnp.int32),
            pltpu.SMEM((sec_count,), jnp.int32),
            pltpu.SemaphoreType.DMA((6 + terms,)),
        ],
        compiler_params=params,
        name="load",
    )(*(
        pltpu.with_memory_space_constraint(array, pltpu.HBM)
        for array in (psi, left_env, pairing.T, block_rows, block_cols, energy)
    ))

    block_f32 = jax.ShapeDtypeStruct(vec_shape, F32)
    row_f32 = jax.ShapeDtypeStruct((8, LANES), F32)

    packets = sigma_packets(
        True, split, first_plan[0], rep_count, lists, left_env, right_env,
        [start, limits, scalars, *psi_others, *level_others],
    )
    early, late = exchange(packets, split, *first_plan)
    base, scalars = call(
        functools.partial(first_early_kernel, split, len(early)), "combine_first_early",
        [block_f32, row_f32], *early, start, levels, flops=EARLY_FLOPS,
    )
    first, sigma_one, vector = call(
        functools.partial(first_kernel, len(late)), "combine_first",
        [
            pltpu.VMEM(vec_shape, BF16),
            block_f32,
            jax.ShapeDtypeStruct((sec_dev * half + MORE_ROWS, width), BF16),
        ],
        *late, limits, start, base, scalars,
    )

    *packets, first_out = sigma_packets(
        False, split, second_plan[0], rep_count, lists, left_env, right_env,
        [first, vector, *from_others(vector)],
    )
    early, late = exchange(packets, split, *second_plan)
    base, scale = call(
        functools.partial(second_early_kernel, split, len(early), entries),
        "combine_second_early", [block_f32, row_f32], *early, vector, levels, sigma_one, scalars,
        flops=EARLY_FLOPS,
    )
    (second_out,) = call(
        functools.partial(second_kernel, len(late)), "combine_second", [vec_bf16],
        *late, limits, base, scale,
    )
    return (first_out, second_out)


def solution(mesh):
    return jax.shard_map(
        body,
        mesh=mesh,
        in_specs=(
            P(("grp", "sec"), "rep", None),
            P(("grp", "op"), "sec", "rep", None),
            P(("grp", "op"), None, None),
            P(("grp", "op"), "sec"),
            P(("grp", "sec")),
            P(("grp", "sec")),
            P(("grp", "sec"), "rep"),
        ),
        out_specs=(P(("grp", "sec"), "rep", None), P(("grp", "sec"), "rep", None)),
        check_vma=False,
    )
```

```python
import functools

import jax
import jax.numpy as jnp
from jax import lax
from jax.experimental import pallas as pl
from jax.experimental.pallas import tpu as pltpu
from jax.sharding import PartitionSpec as P

EPSILON = 1e-06
HEAD = 16
PARTS = 3
EARLY_FLOPS = 10**9
MORE_ROWS = 16
LANES = 128
VMEM_BYTES = 24 * 1024 * 1024
F32 = jnp.float32
BF16 = jnp.bfloat16


def whole(space):
    return pl.BlockSpec(memory_space=space)


def live(limit_ref, s, first_row, shape):
    sec_dev = limit_ref.shape[0] // 2
    repeat = shape[1] // LANES
    rows = jnp.concatenate([limit_ref[s:s + 1, :]] * repeat, axis=1)
    cols = jnp.concatenate([limit_ref[sec_dev + s:sec_dev + s + 1, :]] * repeat, axis=1)
    row_ids = first_row + lax.broadcasted_iota(jnp.int32, shape, 0)
    col_ids = lax.broadcasted_iota(jnp.int32, shape, 1)
    return (row_ids < rows) & (col_ids < cols)


def energy_columns(level):
    missing = -level.shape[0] % 8
    if missing:
        level = jnp.concatenate([level, jnp.zeros((missing, level.shape[1]), F32)], axis=0)
    return level.T


def spread(array, width):
    return jnp.concatenate([array] * (width // LANES), axis=1)


def quotient(value, count):
    return value >> (count.bit_length() - 1) if count & (count - 1) == 0 else lax.div(value, count)


def remainder(value, count):
    return value & (count - 1) if count & (count - 1) == 0 else lax.rem(value, count)


def fold(array):
    rows, width = array.shape
    return jnp.sum(array.reshape(rows // 8, 8, width), axis=0)


def total(array):
    return jnp.sum(jnp.sum(array, axis=0, keepdims=True), axis=1, keepdims=True)


def header(slot, scalars, shape=(HEAD, LANES)):
    row_ids = lax.broadcasted_iota(jnp.int32, shape, 0)
    head = jnp.where(row_ids == 0, slot.astype(F32), 0.0)
    row = 1
    for scalar in scalars:
        rest = jnp.broadcast_to(scalar, shape)
        for _ in range(PARTS):
            piece = rest.astype(BF16).astype(F32)
            head = jnp.where(row_ids == row, piece, head)
            rest = rest - piece
            row += 1
    return head.astype(BF16)


def head_scalar(head_sum, index):
    first = 1 + PARTS * index
    return jnp.sum(head_sum[first:first + PARTS], axis=0, keepdims=True)


def most_pairs(pairs, sec_count):
    return pairs // sec_count + 1


def load_kernel(
    psi_hbm, left_hbm, pairing_hbm, rows_hbm, cols_hbm, energy_hbm,
    start_ref, left_ref, list_ref, limit_ref, energy_ref, scalar_ref,
    psi_ref, level_ref, rows_ref, cols_ref, pairing_ref, entry_ref, count_ref, sems,
):
    sec_dev, half, width = psi_ref.shape
    terms = left_ref.shape[0]
    sec_count = list_ref.shape[0]
    cap = most_pairs(terms * sec_dev, sec_count)
    pairs = [
        (rows_hbm, rows_ref), (cols_hbm, cols_ref), (energy_hbm, level_ref),
        (pairing_hbm, pairing_ref), (psi_hbm, psi_ref),
    ]
    for t in range(left_ref.shape[0]):
        pairs.append((left_hbm.at[t], left_ref.at[t]))
    copies = [
        pltpu.make_async_copy(source, target, sems.at[i])
        for i, (source, target) in enumerate(pairs)
    ]
    for copy in copies:
        copy.start()
    for owner in range(sec_count):
        count_ref[owner] = 0
        entry_ref[owner, cap] = 0
        for i in range(cap):
            entry_ref[owner, i] = terms * sec_dev
    for copy in copies[:3]:
        copy.wait()
    for s in range(sec_dev):
        limit_ref[s:s + 1, :] = jnp.full((1, LANES), rows_ref[s], jnp.int32)
        limit_ref[sec_dev + s:sec_dev + s + 1, :] = jnp.full((1, LANES), cols_ref[s], jnp.int32)
    columns = energy_columns(level_ref[...])
    for s in range(sec_dev):
        energy_ref[s] = jnp.broadcast_to(columns[:, s:s + 1], (half, LANES))
    copies[3].wait()
    for t in range(terms):
        for s in range(sec_dev):
            target = pairing_ref[s, t]
            owner = quotient(target, sec_dev)
            count = count_ref[owner]
            entry_ref[owner, count] = t * sec_dev + s
            entry_ref[owner, cap] = remainder(target, sec_dev)
            count_ref[owner] = count + 1
    entries = pltpu.make_async_copy(entry_ref, list_ref, sems.at[len(copies)])
    entries.start()
    copies[4].wait()
    first_row = lax.axis_index("rep") * half
    norm = jnp.zeros((8, width), F32)
    level = jnp.zeros((8, width), F32)
    for s in range(sec_dev):
        vector = jnp.where(
            live(limit_ref, s, first_row, (half, width)), psi_ref[s].astype(F32), 0.0
        )
        start_ref[s] = vector.astype(BF16)
        square = vector * vector
        norm += fold(square)
        level += fold(square * spread(energy_ref[s], width))
    scalar_ref[0:8, :] = norm
    scalar_ref[8:16, :] = level
    for copy in copies[5:]:
        copy.wait()
    entries.wait()


def product_kernel(is_first, split, paired, rep_count, sec_count, *refs):
    refs = list(refs)
    take = lambda count: [refs.pop(0) for _ in range(count)]
    list_ref, left_ref, right_ref = take(3)
    if is_first:
        start_ref, limit_ref, scalar_ref = take(3)
        psi_refs = take(rep_count - 1)
        level_refs = take(rep_count - 1)
    else:
        (first_ref,) = take(1)
        vector_refs = take(rep_count)
    out_refs = take(sec_count if split else 1)
    if not is_first:
        (first_hbm,) = take(1)
    inner_ref, entry_ref, sems = refs
    terms, sec_dev, half, width = left_ref.shape
    pairs = terms * sec_dev
    cap = most_pairs(pairs, sec_count)
    rep = lax.axis_index("rep")
    sec = lax.axis_index("sec")
    fetch = pltpu.make_async_copy(list_ref, entry_ref, sems.at[0])
    fetch.start()
    if not is_first:
        put = pltpu.make_async_copy(first_ref, first_hbm, sems.at[1])
        put.start()
    inner_ref[pairs] = jnp.zeros((half, width), BF16)

    def first_row(step):
        return remainder(rep + step, rep_count) * half

    if is_first:
        folded = [scalar_ref[0:8, :], scalar_ref[8:16, :]]
        columns = [energy_columns(ref[...]) for ref in level_refs]
    for s in range(sec_dev):
        if is_first:
            blocks = [start_ref[s]]
            for step in range(1, rep_count):
                psi = psi_refs[step - 1][s]
                mask = live(limit_ref, s, first_row(step), (half, width))
                blocks.append(jnp.where(mask, psi.astype(F32), 0.0).astype(BF16))
        else:
            blocks = [ref[s * half:(s + 1) * half] for ref in vector_refs]
        vector = jnp.concatenate(blocks, axis=0)
        for turn in range(1, rep_count):
            turned = blocks[rep_count - turn:] + blocks[:rep_count - turn]
            vector = jnp.where(rep == turn, jnp.concatenate(turned, axis=0), vector)
        inner = jnp.dot(
            left_ref[:, s].reshape(terms * half, width), vector, preferred_element_type=F32
        ).astype(BF16)
        for t in range(terms):
            inner_ref[t * sec_dev + s] = inner[t * half:(t + 1) * half]
        if is_first:
            for step in range(1, rep_count):
                block = blocks[step].astype(F32)
                square = block * block
                energy = jnp.broadcast_to(columns[step - 1][:, s:s + 1], (half, width))
                folded = [folded[0] + fold(square), folded[1] + fold(square * energy)]
    if is_first:
        scalars = [total(array) for array in folded]
    else:
        head = sum(ref[sec_dev * half:].astype(F32) for ref in vector_refs)
        scalars = [head_scalar(head, i)[:, :LANES] for i in range(2)]
    fetch.wait()
    for d in range(sec_count):
        if not split:
            owner = d
        elif paired:
            owner = sec ^ d
        else:
            owner = remainder(sec + d, sec_count)
        packet = jnp.zeros((half, width), F32)
        for i in range(cap):
            pair = entry_ref[owner, i]
            term = jnp.minimum(quotient(pair, sec_dev), terms - 1)
            packet += jnp.dot(inner_ref[pair], right_ref[term], preferred_element_type=F32)
        out = out_refs[d] if split else out_refs[0].at[d]
        for column in range(width // LANES):
            out[column * half:(column + 1) * half, :] = packet[
                :, column * LANES:(column + 1) * LANES
            ].astype(BF16)
        out[width // LANES * half:, :] = header(entry_ref[owner, cap], scalars)
    if not is_first:
        put.wait()


def sigma_packets(is_first, split, paired, rep_count, lists, left_env, right_env, more):
    terms, sec_dev, half, width = left_env.shape
    sec_count = lax.axis_size("sec")
    packet = (width // LANES * half + HEAD, LANES)
    if split:
        outs = [jax.ShapeDtypeStruct(packet, BF16)] * sec_count
    else:
        outs = [jax.ShapeDtypeStruct((sec_count,) + packet, BF16)]
    out_specs = [whole(pltpu.VMEM)] * len(outs)
    if not is_first:
        outs.append(jax.ShapeDtypeStruct((sec_dev, half, width), BF16))
        out_specs.append(whole(pltpu.HBM))
    pair_flops = 2 * half * width * width * 2
    operands = [lists, left_env, right_env, *more]
    return pl.pallas_call(
        functools.partial(product_kernel, is_first, split, paired, rep_count, sec_count),
        out_shape=outs,
        in_specs=[whole(pltpu.VMEM)] * len(operands),
        out_specs=out_specs,
        scratch_shapes=[
            pltpu.VMEM((terms * sec_dev + 1, half, width), BF16),
            pltpu.SMEM(lists.shape, jnp.int32),
            pltpu.SemaphoreType.DMA((2,)),
        ],
        compiler_params=pltpu.CompilerParams(vmem_limit_bytes=VMEM_BYTES),
        cost_estimate=pl.CostEstimate(
            flops=terms * sec_dev * pair_flops,
            bytes_accessed=2 * (left_env.size + right_env.size),
            transcendentals=0,
        ),
        name="products_first" if is_first else "products_second",
    )(*operands)


def exchange(packets, split, paired, order, groups, late_count=1):
    sec_count = lax.axis_size("sec")
    op_count = lax.axis_size("op")
    op_turns = [
        [(i, (i + step) % op_count) for i in range(op_count)] for step in range(1, op_count)
    ]
    over_op = lambda packet: [lax.ppermute(packet, "op", turn) for turn in op_turns]
    if not split:
        arrived = lax.all_to_all(packets[0], "sec", split_axis=0, concat_axis=0, tiled=True)
        return [arrived] + over_op(arrived), []
    arrived = {0: packets[0]}
    for step in order:
        reach = (lambda i: i ^ step) if paired else (lambda i: (i + step) % sec_count)
        turn = [(i, reach(i)) for i in range(sec_count)]
        arrived[step] = lax.ppermute(packets[step], "sec", turn)
    crossed = [over_op(jnp.stack([arrived[step] for step in group])) for group in groups]
    early, late = crossed[:-late_count], crossed[-late_count:]
    return [arrived[step] for step in [0, *order]] + sum(early, []), sum(late, [])


def views(refs):
    return [
        view
        for ref in refs
        for view in ([ref] if len(ref.shape) == 2 else [ref.at[i] for i in range(ref.shape[0])])
    ]


def add_packets(packet_refs, split, half, base_ref):
    sec_dev, _, width = base_ref.shape
    own = lax.axis_size("sec") if split else 1
    body_rows = width // LANES * half
    if split:
        packet_refs = views(packet_refs)
        heads = [ref[body_rows:].astype(F32) for ref in packet_refs]
        for column in range(width // LANES):
            lanes = slice(column * LANES, (column + 1) * LANES)
            for s in range(sec_dev):
                part = base_ref[s, :, lanes]
                for ref, head in zip(packet_refs, heads):
                    body = ref[column * half:(column + 1) * half].astype(F32)
                    part += jnp.where(head[0:1] == s, body, 0.0)
                base_ref[s, :, lanes] = part
        return sum(heads[1:own], heads[0])

    head_sum = jnp.zeros((HEAD, LANES), F32)
    for index, ref in enumerate(packet_refs):
        def add_one(p, carry):
            head = ref[p, body_rows:, :].astype(F32)
            for column in range(width // LANES):
                body = ref[p, column * half:(column + 1) * half, :].astype(F32)
                lanes = slice(column * LANES, (column + 1) * LANES)
                for s in range(sec_dev):
                    base_ref[s, :, lanes] += jnp.where(head[0:1] == s, body, 0.0)
            return carry + head
        result = lax.fori_loop(0, ref.shape[0], add_one, jnp.zeros((HEAD, LANES), F32))
        if index < own:
            head_sum = head_sum + result
    return head_sum


def late_sum(packet_refs, s, half, width):
    body_rows = width // LANES * half
    value = jnp.zeros((half, width), F32)
    for ref in views(packet_refs):
        body = jnp.concatenate(
            [ref[c * half:(c + 1) * half].astype(F32) for c in range(width // LANES)], axis=1
        )
        slot = spread(ref[body_rows:].astype(F32)[0:1], width)
        value += jnp.where(slot == s, body, 0.0)
    return value


def first_early_kernel(split, count, *refs):
    packet_refs = refs[:count]
    start_ref, energy_ref, base_ref, scalar_ref = refs[count:]
    sec_dev, half, width = start_ref.shape
    for s in range(sec_dev):
        base_ref[s] = spread(energy_ref[s], width) * start_ref[s].astype(F32)
    head_sum = add_packets(packet_refs, split, half, base_ref)
    norm = head_scalar(head_sum, 0)
    scalar_ref[0:1] = norm
    scalar_ref[1:2] = head_scalar(head_sum, 1) / norm


def first_kernel(count, *refs):
    packet_refs = refs[:count]
    limit_ref, start_ref, base_ref, scalar_ref, first_ref, one_ref, vec_ref = refs[count:]
    sec_dev, half, width = start_ref.shape
    shift = spread(scalar_ref[1:2], width)
    first_row = lax.axis_index("rep") * half
    cross = jnp.zeros((8, width), F32)
    square = jnp.zeros((8, width), F32)
    for s in range(sec_dev):
        mask = live(limit_ref, s, first_row, (half, width))
        start = start_ref[s].astype(F32)
        one = jnp.where(mask, base_ref[s] + late_sum(packet_refs, s, half, width), 0.0)
        one_ref[s] = one
        first_ref[s] = one.astype(BF16)
        vector = one - shift * start
        vec_ref[s * half:(s + 1) * half] = vector.astype(BF16)
        cross += fold(start * vector)
        square += fold(vector * vector)
    scalars = (total(cross), total(square))
    vec_ref[sec_dev * half:] = header(jnp.int32(0), scalars, (MORE_ROWS, width))


def second_early_kernel(split, count, entries, *refs):
    packet_refs = refs[:count]
    vec_ref, energy_ref, one_ref, scalar_ref, base_ref, scale_ref = refs[count:]
    sec_dev, half, width = one_ref.shape
    for s in range(sec_dev):
        vector = vec_ref[s * half:(s + 1) * half].astype(F32)
        base_ref[s] = spread(energy_ref[s], width) * vector
    head_sum = add_packets(packet_refs, split, half, base_ref)
    cross = head_scalar(head_sum, 0)
    square = head_scalar(head_sum, 1)
    excess = cross / scalar_ref[0:1]
    resid_sq = jnp.maximum(square - excess * cross, 0.0)
    scale = lax.rsqrt(resid_sq / entries + EPSILON)
    scale_ref[...] = jnp.broadcast_to(scale, scale_ref.shape)
    for s in range(sec_dev):
        base_ref[s] = base_ref[s] - spread(excess, width) * one_ref[s]


def second_kernel(count, *refs):
    packet_refs = refs[:count]
    limit_ref, base_ref, scale_ref, second_ref = refs[count:]
    sec_dev, half, width = base_ref.shape
    scale = spread(scale_ref[0:1], width)
    first_row = lax.axis_index("rep") * half
    for s in range(sec_dev):
        mask = live(limit_ref, s, first_row, (half, width))
        value = scale * (base_ref[s] + late_sum(packet_refs, s, half, width))
        second_ref[s] = jnp.where(mask, value, 0.0).astype(BF16)


def call(kernel, name, outs, *operands, flops=0):
    return pl.pallas_call(
        kernel,
        out_shape=outs,
        in_specs=[whole(pltpu.VMEM)] * len(operands),
        out_specs=[whole(pltpu.VMEM)] * len(outs),
        compiler_params=pltpu.CompilerParams(vmem_limit_bytes=VMEM_BYTES),
        cost_estimate=pl.CostEstimate(flops=flops, bytes_accessed=0, transcendentals=0),
        name=name,
    )(*operands)


def body(psi, left_env, right_env, pairing, block_rows, block_cols, energy):
    sec_count = lax.axis_size("sec")
    op_count = lax.axis_size("op")
    rep_count = lax.axis_size("rep")
    terms, sec_dev, half, width = left_env.shape
    entries = sec_count * sec_dev * rep_count * half * width
    split = sec_count * op_count <= 8
    can_pair = sec_count & (sec_count - 1) == 0
    steps = list(range(1, sec_count))
    first_plan = (False, steps, [[0]] + [[k] for k in steps[:-2]] + [steps[-2:]])
    second_groups = [[0]] + [[k] for k in steps[1:2] + steps[:1] + steps[2:]]
    second_plan = (can_pair, steps[1:2] + steps[:1] + steps[2:], second_groups, 2)
    params = pltpu.CompilerParams(vmem_limit_bytes=VMEM_BYTES)
    vec_shape = (sec_dev, half, width)
    vec_bf16 = jax.ShapeDtypeStruct(vec_shape, BF16)

    def from_others(array):
        arrays = []
        for step in range(1, rep_count):
            turn = [((i + step) % rep_count, i) for i in range(rep_count)]
            arrays.append(lax.ppermute(array, "rep", turn))
        return arrays

    psi_others = from_others(psi)
    level_others = from_others(energy)
    start, left_env, lists, limits, levels, scalars = pl.pallas_call(
        load_kernel,
        out_shape=[
            vec_bf16,
            jax.ShapeDtypeStruct(left_env.shape, BF16),
            jax.ShapeDtypeStruct((sec_count, LANES), jnp.int32),
            jax.ShapeDtypeStruct((2 * sec_dev, LANES), jnp.int32),
            jax.ShapeDtypeStruct((sec_dev, half, LANES), F32),
            jax.ShapeDtypeStruct((16, width), F32),
        ],
        in_specs=[whole(pltpu.HBM)] * 6,
        out_specs=[whole(pltpu.VMEM)] * 6,
        scratch_shapes=[
            pltpu.VMEM(vec_shape, BF16),
            pltpu.VMEM((sec_dev, half), F32),
            pltpu.SMEM((sec_dev,), jnp.int32),
            pltpu.SMEM((sec_dev,), jnp.int32),
            pltpu.SMEM((sec_dev, terms), jnp.int32),
            pltpu.SMEM((sec_count, LANES), jnp.int32),
            pltpu.SMEM((sec_count,), jnp.int32),
            pltpu.SemaphoreType.DMA((6 + terms,)),
        ],
        compiler_params=params,
        name="load",
    )(*(
        pltpu.with_memory_space_constraint(array, pltpu.HBM)
        for array in (psi, left_env, pairing.T, block_rows, block_cols, energy)
    ))

    block_f32 = jax.ShapeDtypeStruct(vec_shape, F32)
    row_f32 = jax.ShapeDtypeStruct((8, LANES), F32)

    packets = sigma_packets(
        True, split, first_plan[0], rep_count, lists, left_env, right_env,
        [start, limits, scalars, *psi_others, *level_others],
    )
    early, late = exchange(packets, split, *first_plan)
    base, scalars = call(
        functools.partial(first_early_kernel, split, len(early)), "combine_first_early",
        [block_f32, row_f32], *early, start, levels, flops=EARLY_FLOPS,
    )
    first, sigma_one, vector = call(
        functools.partial(first_kernel, len(late)), "combine_first",
        [
            pltpu.VMEM(vec_shape, BF16),
            block_f32,
            jax.ShapeDtypeStruct((sec_dev * half + MORE_ROWS, width), BF16),
        ],
        *late, limits, start, base, scalars,
    )

    *packets, first_out = sigma_packets(
        False, split, second_plan[0], rep_count, lists, left_env, right_env,
        [first, vector, *from_others(vector)],
    )
    early, late = exchange(packets, split, *second_plan)
    base, scale = call(
        functools.partial(second_early_kernel, split, len(early), entries),
        "combine_second_early", [block_f32, row_f32], *early, vector, levels, sigma_one, scalars,
        flops=EARLY_FLOPS,
    )
    (second_out,) = call(
        functools.partial(second_kernel, len(late)), "combine_second", [vec_bf16],
        *late, limits, base, scale,
    )
    return (first_out, second_out)


def solution(mesh):
    return jax.shard_map(
        body,
        mesh=mesh,
        in_specs=(
            P(("grp", "sec"), "rep", None),
            P(("grp", "op"), "sec", "rep", None),
            P(("grp", "op"), None, None),
            P(("grp", "op"), "sec"),
            P(("grp", "sec")),
            P(("grp", "sec")),
            P(("grp", "sec"), "rep"),
        ),
        out_specs=(P(("grp", "sec"), "rep", None), P(("grp", "sec"), "rep", None)),
        check_vma=False,
    )
```

```python
import functools

import jax
import jax.numpy as jnp
from jax import lax
from jax.experimental import pallas as pl
from jax.experimental.pallas import tpu as pltpu
from jax.sharding import PartitionSpec as P

EPSILON = 1e-06
HEAD = 8
PARTS = 3
EARLY_FLOPS = 10**9
SLOT_ROW = 2
MORE_ROWS = 16
LANES = 128
VMEM_BYTES = 24 * 1024 * 1024
F32 = jnp.float32
BF16 = jnp.bfloat16


def whole(space):
    return pl.BlockSpec(memory_space=space)


def live(limit_ref, s, first_row, shape):
    sec_dev = limit_ref.shape[0] // 2
    repeat = shape[1] // LANES
    rows = jnp.concatenate([limit_ref[s:s + 1, :]] * repeat, axis=1)
    cols = jnp.concatenate([limit_ref[sec_dev + s:sec_dev + s + 1, :]] * repeat, axis=1)
    row_ids = first_row + lax.broadcasted_iota(jnp.int32, shape, 0)
    col_ids = lax.broadcasted_iota(jnp.int32, shape, 1)
    return (row_ids < rows) & (col_ids < cols)


def energy_columns(level):
    missing = -level.shape[0] % 8
    if missing:
        level = jnp.concatenate([level, jnp.zeros((missing, level.shape[1]), F32)], axis=0)
    return level.T


def spread(array, width):
    return jnp.concatenate([array] * (width // LANES), axis=1)


def quotient(value, count):
    return value >> (count.bit_length() - 1) if count & (count - 1) == 0 else lax.div(value, count)


def remainder(value, count):
    return value & (count - 1) if count & (count - 1) == 0 else lax.rem(value, count)


def fold(array):
    rows, width = array.shape
    return jnp.sum(array.reshape(rows // 8, 8, width), axis=0)


def total(array):
    return jnp.sum(jnp.sum(array, axis=0, keepdims=True), axis=1, keepdims=True)


def header(slot, scalars, shape=(HEAD, LANES)):
    row_ids = lax.broadcasted_iota(jnp.int32, shape, 0)
    head = jnp.where(row_ids == 0, slot.astype(F32), 0.0)
    row = 1
    for scalar in scalars:
        rest = jnp.broadcast_to(scalar, shape)
        for _ in range(PARTS):
            piece = rest.astype(BF16).astype(F32)
            head = jnp.where(row_ids == row, piece, head)
            rest = rest - piece
            row += 1
    return head.astype(BF16)


def head_scalar(head_sum, index):
    first = 1 + PARTS * index
    return jnp.sum(head_sum[first:first + PARTS], axis=0, keepdims=True)


def most_pairs(pairs, sec_count):
    return pairs // sec_count + 1


def load_kernel(
    psi_hbm, left_hbm, pairing_hbm, rows_hbm, cols_hbm, energy_hbm,
    start_ref, left_ref, list_ref, limit_ref, energy_ref, scalar_ref,
    psi_ref, level_ref, rows_ref, cols_ref, pairing_ref, entry_ref, count_ref, sems,
):
    sec_dev, half, width = psi_ref.shape
    terms = left_ref.shape[0]
    sec_count = list_ref.shape[0]
    cap = most_pairs(terms * sec_dev, sec_count)
    pairs = [
        (rows_hbm, rows_ref), (cols_hbm, cols_ref), (energy_hbm, level_ref),
        (pairing_hbm, pairing_ref), (psi_hbm, psi_ref),
    ]
    for t in range(left_ref.shape[0]):
        pairs.append((left_hbm.at[t], left_ref.at[t]))
    copies = [
        pltpu.make_async_copy(source, target, sems.at[i])
        for i, (source, target) in enumerate(pairs)
    ]
    for copy in copies:
        copy.start()
    for owner in range(sec_count):
        count_ref[owner] = 0
        entry_ref[owner, cap] = 0
        for i in range(cap):
            entry_ref[owner, i] = terms * sec_dev
    for copy in copies[:3]:
        copy.wait()
    for s in range(sec_dev):
        limit_ref[s:s + 1, :] = jnp.full((1, LANES), rows_ref[s], jnp.int32)
        limit_ref[sec_dev + s:sec_dev + s + 1, :] = jnp.full((1, LANES), cols_ref[s], jnp.int32)
    columns = energy_columns(level_ref[...])
    for s in range(sec_dev):
        energy_ref[s] = jnp.broadcast_to(columns[:, s:s + 1], (half, LANES))
    copies[3].wait()
    for t in range(terms):
        for s in range(sec_dev):
            target = pairing_ref[s, t]
            owner = quotient(target, sec_dev)
            count = count_ref[owner]
            entry_ref[owner, count] = t * sec_dev + s
            entry_ref[owner, cap] = remainder(target, sec_dev)
            count_ref[owner] = count + 1
    entries = pltpu.make_async_copy(entry_ref, list_ref, sems.at[len(copies)])
    entries.start()
    copies[4].wait()
    first_row = lax.axis_index("rep") * half
    norm = jnp.zeros((8, width), F32)
    level = jnp.zeros((8, width), F32)
    for s in range(sec_dev):
        vector = jnp.where(
            live(limit_ref, s, first_row, (half, width)), psi_ref[s].astype(F32), 0.0
        )
        start_ref[s] = vector.astype(BF16)
        square = vector * vector
        norm += fold(square)
        level += fold(square * spread(energy_ref[s], width))
    scalar_ref[0:8, :] = norm
    scalar_ref[8:16, :] = level
    for copy in copies[5:]:
        copy.wait()
    entries.wait()


def product_kernel(is_first, split, paired, rep_count, sec_count, *refs):
    refs = list(refs)
    take = lambda count: [refs.pop(0) for _ in range(count)]
    list_ref, left_ref, right_ref = take(3)
    if is_first:
        start_ref, limit_ref, scalar_ref = take(3)
        psi_refs = take(rep_count - 1)
        level_refs = take(rep_count - 1)
    else:
        (first_ref,) = take(1)
        vector_refs = take(rep_count)
    out_refs = take(sec_count if split else 1)
    if not is_first:
        (first_hbm,) = take(1)
    inner_ref, entry_ref, sems = refs
    terms, sec_dev, half, width = left_ref.shape
    pairs = terms * sec_dev
    cap = most_pairs(pairs, sec_count)
    rep = lax.axis_index("rep")
    sec = lax.axis_index("sec")
    fetch = pltpu.make_async_copy(list_ref, entry_ref, sems.at[0])
    fetch.start()
    if not is_first:
        put = pltpu.make_async_copy(first_ref, first_hbm, sems.at[1])
        put.start()
    inner_ref[pairs] = jnp.zeros((half, width), BF16)

    def first_row(step):
        return remainder(rep + step, rep_count) * half

    if is_first:
        folded = [scalar_ref[0:8, :], scalar_ref[8:16, :]]
        columns = [energy_columns(ref[...]) for ref in level_refs]
    for s in range(sec_dev):
        if is_first:
            blocks = [start_ref[s]]
            for step in range(1, rep_count):
                psi = psi_refs[step - 1][s]
                mask = live(limit_ref, s, first_row(step), (half, width))
                blocks.append(jnp.where(mask, psi.astype(F32), 0.0).astype(BF16))
        else:
            blocks = [ref[s * half:(s + 1) * half] for ref in vector_refs]
        vector = jnp.concatenate(blocks, axis=0)
        for turn in range(1, rep_count):
            turned = blocks[rep_count - turn:] + blocks[:rep_count - turn]
            vector = jnp.where(rep == turn, jnp.concatenate(turned, axis=0), vector)
        inner = jnp.dot(
            left_ref[:, s].reshape(terms * half, width), vector, preferred_element_type=F32
        ).astype(BF16)
        for t in range(terms):
            inner_ref[t * sec_dev + s] = inner[t * half:(t + 1) * half]
        if is_first:
            for step in range(1, rep_count):
                block = blocks[step].astype(F32)
                square = block * block
                energy = jnp.broadcast_to(columns[step - 1][:, s:s + 1], (half, width))
                folded = [folded[0] + fold(square), folded[1] + fold(square * energy)]
    if is_first:
        scalars = [total(array) for array in folded]
    else:
        head = sum(ref[sec_dev * half:].astype(F32) for ref in vector_refs)
        scalars = [head_scalar(head, i)[:, :LANES] for i in range(2)]
    fetch.wait()
    for d in range(sec_count):
        if not split:
            owner = d
        elif paired:
            owner = sec ^ d
        else:
            owner = remainder(sec + d, sec_count)
        packet = jnp.zeros((half, width), F32)
        for i in range(cap):
            pair = entry_ref[owner, i]
            term = jnp.minimum(quotient(pair, sec_dev), terms - 1)
            packet += jnp.dot(inner_ref[pair], right_ref[term], preferred_element_type=F32)
        out = out_refs[d] if split else out_refs[0].at[d]
        for column in range(width // LANES):
            out[column * half:(column + 1) * half, :] = packet[
                :, column * LANES:(column + 1) * LANES
            ].astype(BF16)
        out[width // LANES * half:, :] = header(entry_ref[owner, cap], scalars)
    if not is_first:
        put.wait()


def sigma_packets(is_first, split, paired, rep_count, lists, left_env, right_env, more):
    terms, sec_dev, half, width = left_env.shape
    sec_count = lax.axis_size("sec")
    packet = (width // LANES * half + HEAD, LANES)
    if split:
        outs = [jax.ShapeDtypeStruct(packet, BF16)] * sec_count
    else:
        outs = [jax.ShapeDtypeStruct((sec_count,) + packet, BF16)]
    out_specs = [whole(pltpu.VMEM)] * len(outs)
    if not is_first:
        outs.append(jax.ShapeDtypeStruct((sec_dev, half, width), BF16))
        out_specs.append(whole(pltpu.HBM))
    pair_flops = 2 * half * width * width * 2
    operands = [lists, left_env, right_env, *more]
    return pl.pallas_call(
        functools.partial(product_kernel, is_first, split, paired, rep_count, sec_count),
        out_shape=outs,
        in_specs=[whole(pltpu.VMEM)] * len(operands),
        out_specs=out_specs,
        scratch_shapes=[
            pltpu.VMEM((terms * sec_dev + 1, half, width), BF16),
            pltpu.SMEM(lists.shape, jnp.int32),
            pltpu.SemaphoreType.DMA((2,)),
        ],
        compiler_params=pltpu.CompilerParams(vmem_limit_bytes=VMEM_BYTES),
        cost_estimate=pl.CostEstimate(
            flops=terms * sec_dev * pair_flops,
            bytes_accessed=2 * (left_env.size + right_env.size),
            transcendentals=0,
        ),
        name="products_first" if is_first else "products_second",
    )(*operands)


def exchange(packets, split, paired, order, groups, bare=0):
    sec_count = lax.axis_size("sec")
    op_count = lax.axis_size("op")
    op_turns = [
        [(i, (i + step) % op_count) for i in range(op_count)] for step in range(1, op_count)
    ]
    over_op = lambda packet: [lax.ppermute(packet, "op", turn) for turn in op_turns]
    if not split:
        arrived = lax.all_to_all(packets[0], "sec", split_axis=0, concat_axis=0, tiled=True)
        return [arrived] + over_op(arrived), []
    arrived = {0: packets[0]}
    for step in order:
        reach = (lambda i: i ^ step) if paired else (lambda i: (i + step) % sec_count)
        turn = [(i, reach(i)) for i in range(sec_count)]
        arrived[step] = lax.ppermute(packets[step], "sec", turn)
    crossed = [
        over_op(jnp.stack([arrived[step][:bare or None] for step in group])) for group in groups
    ]
    return [arrived[step] for step in [0, *order]] + sum(crossed[:-1], []), crossed[-1]


def views(refs):
    return [
        view
        for ref in refs
        for view in ([ref] if len(ref.shape) == 2 else [ref.at[i] for i in range(ref.shape[0])])
    ]


def add_packets(packet_refs, split, half, base_ref, slots=()):
    sec_dev, _, width = base_ref.shape
    own = lax.axis_size("sec") if split else 1
    body_rows = width // LANES * half
    if split:
        packet_refs = views(packet_refs)
        with_head = packet_refs[:len(packet_refs) - len(slots)]
        heads = [ref[body_rows:].astype(F32) for ref in with_head]
        heads += slots
        for column in range(width // LANES):
            lanes = slice(column * LANES, (column + 1) * LANES)
            for s in range(sec_dev):
                part = base_ref[s, :, lanes]
                for ref, head in zip(packet_refs, heads):
                    body = ref[column * half:(column + 1) * half].astype(F32)
                    part += jnp.where(head[0:1] == s, body, 0.0)
                base_ref[s, :, lanes] = part
        return sum(heads[1:own], heads[0])

    head_sum = jnp.zeros((HEAD, LANES), F32)
    for index, ref in enumerate(packet_refs):
        def add_one(p, carry):
            head = ref[p, body_rows:, :].astype(F32)
            for column in range(width // LANES):
                body = ref[p, column * half:(column + 1) * half, :].astype(F32)
                lanes = slice(column * LANES, (column + 1) * LANES)
                for s in range(sec_dev):
                    base_ref[s, :, lanes] += jnp.where(head[0:1] == s, body, 0.0)
            return carry + head
        result = lax.fori_loop(0, ref.shape[0], add_one, jnp.zeros((HEAD, LANES), F32))
        if index < own:
            head_sum = head_sum + result
    return head_sum


def late_sum(packet_refs, s, half, width, slots=()):
    body_rows = width // LANES * half
    value = jnp.zeros((half, width), F32)
    for i, ref in enumerate(views(packet_refs)):
        body = jnp.concatenate(
            [ref[c * half:(c + 1) * half].astype(F32) for c in range(width // LANES)], axis=1
        )
        slot = slots[i] if slots else ref[body_rows:].astype(F32)[0:1]
        slot = spread(slot, width)
        value += jnp.where(slot == s, body, 0.0)
    return value


def first_early_kernel(split, count, *refs):
    packet_refs = refs[:count]
    start_ref, energy_ref, base_ref, scalar_ref = refs[count:]
    sec_dev, half, width = start_ref.shape
    for s in range(sec_dev):
        base_ref[s] = spread(energy_ref[s], width) * start_ref[s].astype(F32)
    head_sum = add_packets(packet_refs, split, half, base_ref)
    norm = head_scalar(head_sum, 0)
    scalar_ref[0:1] = norm
    scalar_ref[1:2] = head_scalar(head_sum, 1) / norm
    if split:
        crossed = views(packet_refs)[lax.axis_size("sec"):]
        for i, ref in enumerate(crossed):
            scalar_ref[SLOT_ROW + i:SLOT_ROW + i + 1] = crossed_slot(ref, half, width)


def crossed_slot(ref, half, width):
    return ref[width // LANES * half:].astype(F32)[0:1]


def known_slots(slot_ref, steps):
    sec_count = lax.axis_size("sec")
    sec = lax.axis_index("sec")
    rows = [remainder(sec - (sec ^ step) + sec_count, sec_count) for step in steps]
    return [slot_ref[pl.ds(row, 1), :] for row in rows]


def first_kernel(count, *refs):
    packet_refs = refs[:count]
    limit_ref, start_ref, base_ref, scalar_ref, first_ref, one_ref, vec_ref, slot_ref = refs[count:]
    sec_dev, half, width = start_ref.shape
    late = views(packet_refs)
    early_count = lax.axis_size("sec") - len(late)
    slot_ref[...] = jnp.zeros_like(slot_ref)
    if late:
        slot_ref[0:early_count] = scalar_ref[SLOT_ROW:SLOT_ROW + early_count]
        for i, ref in enumerate(late):
            row = early_count + i
            slot_ref[row:row + 1] = crossed_slot(ref, half, width)
    shift = spread(scalar_ref[1:2], width)
    first_row = lax.axis_index("rep") * half
    cross = jnp.zeros((8, width), F32)
    square = jnp.zeros((8, width), F32)
    for s in range(sec_dev):
        mask = live(limit_ref, s, first_row, (half, width))
        start = start_ref[s].astype(F32)
        one = jnp.where(mask, base_ref[s] + late_sum(packet_refs, s, half, width), 0.0)
        one_ref[s] = one
        first_ref[s] = one.astype(BF16)
        vector = one - shift * start
        vec_ref[s * half:(s + 1) * half] = vector.astype(BF16)
        cross += fold(start * vector)
        square += fold(vector * vector)
    scalars = (total(cross), total(square))
    vec_ref[sec_dev * half:] = header(jnp.int32(0), scalars, (MORE_ROWS, width))


def second_early_kernel(split, count, entries, steps, *refs):
    packet_refs = refs[:count]
    slot_ref, vec_ref, energy_ref, one_ref, scalar_ref, base_ref, scale_ref = refs[count:]
    sec_dev, half, width = one_ref.shape
    for s in range(sec_dev):
        vector = vec_ref[s * half:(s + 1) * half].astype(F32)
        base_ref[s] = spread(energy_ref[s], width) * vector
    head_sum = add_packets(packet_refs, split, half, base_ref, known_slots(slot_ref, steps))
    cross = head_scalar(head_sum, 0)
    square = head_scalar(head_sum, 1)
    excess = cross / scalar_ref[0:1]
    resid_sq = jnp.maximum(square - excess * cross, 0.0)
    scale = lax.rsqrt(resid_sq / entries + EPSILON)
    scale_ref[...] = jnp.broadcast_to(scale, scale_ref.shape)
    for s in range(sec_dev):
        base_ref[s] = base_ref[s] - spread(excess, width) * one_ref[s]


def second_kernel(count, steps, *refs):
    packet_refs = refs[:count]
    slot_ref, limit_ref, base_ref, scale_ref, second_ref = refs[count:]
    sec_dev, half, width = base_ref.shape
    scale = spread(scale_ref[0:1], width)
    slots = known_slots(slot_ref, steps)
    first_row = lax.axis_index("rep") * half
    for s in range(sec_dev):
        mask = live(limit_ref, s, first_row, (half, width))
        value = scale * (base_ref[s] + late_sum(packet_refs, s, half, width, slots))
        second_ref[s] = jnp.where(mask, value, 0.0).astype(BF16)


def call(kernel, name, outs, *operands, flops=0):
    return pl.pallas_call(
        kernel,
        out_shape=outs,
        in_specs=[whole(pltpu.VMEM)] * len(operands),
        out_specs=[whole(pltpu.VMEM)] * len(outs),
        compiler_params=pltpu.CompilerParams(vmem_limit_bytes=VMEM_BYTES),
        cost_estimate=pl.CostEstimate(flops=flops, bytes_accessed=0, transcendentals=0),
        name=name,
    )(*operands)


def body(psi, left_env, right_env, pairing, block_rows, block_cols, energy):
    sec_count = lax.axis_size("sec")
    op_count = lax.axis_size("op")
    rep_count = lax.axis_size("rep")
    terms, sec_dev, half, width = left_env.shape
    entries = sec_count * sec_dev * rep_count * half * width
    split = sec_count * op_count <= 8
    can_pair = sec_count & (sec_count - 1) == 0
    steps = list(range(1, sec_count))
    first_plan = (False, steps, [[0]] + [[k] for k in steps[:-2]] + [steps[-2:]])
    second_groups = [[0]] + [[k] for k in steps[1:2] + steps[:1] + steps[2:]]
    second_plan = (can_pair, steps[1:2] + steps[:1] + steps[2:], second_groups)
    known = split and can_pair and op_count == 2 and sec_count <= 4
    params = pltpu.CompilerParams(vmem_limit_bytes=VMEM_BYTES)
    vec_shape = (sec_dev, half, width)
    vec_bf16 = jax.ShapeDtypeStruct(vec_shape, BF16)

    def from_others(array):
        arrays = []
        for step in range(1, rep_count):
            turn = [((i + step) % rep_count, i) for i in range(rep_count)]
            arrays.append(lax.ppermute(array, "rep", turn))
        return arrays

    psi_others = from_others(psi)
    level_others = from_others(energy)
    start, left_env, lists, limits, levels, scalars = pl.pallas_call(
        load_kernel,
        out_shape=[
            vec_bf16,
            jax.ShapeDtypeStruct(left_env.shape, BF16),
            jax.ShapeDtypeStruct((sec_count, LANES), jnp.int32),
            jax.ShapeDtypeStruct((2 * sec_dev, LANES), jnp.int32),
            jax.ShapeDtypeStruct((sec_dev, half, LANES), F32),
            jax.ShapeDtypeStruct((16, width), F32),
        ],
        in_specs=[whole(pltpu.HBM)] * 6,
        out_specs=[whole(pltpu.VMEM)] * 6,
        scratch_shapes=[
            pltpu.VMEM(vec_shape, BF16),
            pltpu.VMEM((sec_dev, half), F32),
            pltpu.SMEM((sec_dev,), jnp.int32),
            pltpu.SMEM((sec_dev,), jnp.int32),
            pltpu.SMEM((sec_dev, terms), jnp.int32),
            pltpu.SMEM((sec_count, LANES), jnp.int32),
            pltpu.SMEM((sec_count,), jnp.int32),
            pltpu.SemaphoreType.DMA((6 + terms,)),
        ],
        compiler_params=params,
        name="load",
    )(*(
        pltpu.with_memory_space_constraint(array, pltpu.HBM)
        for array in (psi, left_env, pairing.T, block_rows, block_cols, energy)
    ))

    block_f32 = jax.ShapeDtypeStruct(vec_shape, F32)
    row_f32 = jax.ShapeDtypeStruct((8, LANES), F32)

    packets = sigma_packets(
        True, split, first_plan[0], rep_count, lists, left_env, right_env,
        [start, limits, scalars, *psi_others, *level_others],
    )
    early, late = exchange(packets, split, *first_plan)
    base, scalars = call(
        functools.partial(first_early_kernel, split, len(early)), "combine_first_early",
        [block_f32, row_f32], *early, start, levels, flops=EARLY_FLOPS,
    )
    first, sigma_one, vector, slots = call(
        functools.partial(first_kernel, len(late)), "combine_first",
        [
            pltpu.VMEM(vec_shape, BF16),
            block_f32,
            jax.ShapeDtypeStruct((sec_dev * half + MORE_ROWS, width), BF16),
            row_f32,
        ],
        *late, limits, start, base, scalars,
    )

    *packets, first_out = sigma_packets(
        False, split, second_plan[0], rep_count, lists, left_env, right_env,
        [first, vector, *from_others(vector)],
    )
    bare = width // LANES * half if known else 0
    early, late = exchange(packets, split, *second_plan, bare)
    crossed = sum(second_plan[2], []) if known else []
    late_steps = second_plan[2][-1] if known else []
    base, scale = call(
        functools.partial(
            second_early_kernel, split, len(early), entries, crossed[:len(crossed) - len(late_steps)]
        ),
        "combine_second_early", [block_f32, row_f32], *early, slots, vector, levels, sigma_one, scalars,
        flops=EARLY_FLOPS,
    )
    (second_out,) = call(
        functools.partial(second_kernel, len(late), late_steps), "combine_second", [vec_bf16],
        *late, slots, limits, base, scale,
    )
    return (first_out, second_out)


def solution(mesh):
    return jax.shard_map(
        body,
        mesh=mesh,
        in_specs=(
            P(("grp", "sec"), "rep", None),
            P(("grp", "op"), "sec", "rep", None),
            P(("grp", "op"), None, None),
            P(("grp", "op"), "sec"),
            P(("grp", "sec")),
            P(("grp", "sec")),
            P(("grp", "sec"), "rep"),
        ),
        out_specs=(P(("grp", "sec"), "rep", None), P(("grp", "sec"), "rep", None)),
        check_vma=False,
    )
```

```python
import functools

import jax
import jax.numpy as jnp
from jax import lax
from jax.experimental import pallas as pl
from jax.experimental.pallas import tpu as pltpu
from jax.sharding import PartitionSpec as P

EPSILON = 1e-06
HEAD = 8
PARTS = 3
EARLY_FLOPS = 10**9
SLOT_ROW = 2
MORE_ROWS = 16
LANES = 128
VMEM_BYTES = 24 * 1024 * 1024
F32 = jnp.float32
BF16 = jnp.bfloat16


def whole(space):
    return pl.BlockSpec(memory_space=space)


def live(limit_ref, s, first_row, shape):
    sec_dev = limit_ref.shape[0] // 2
    repeat = shape[1] // LANES
    rows = jnp.concatenate([limit_ref[s:s + 1, :]] * repeat, axis=1)
    cols = jnp.concatenate([limit_ref[sec_dev + s:sec_dev + s + 1, :]] * repeat, axis=1)
    row_ids = first_row + lax.broadcasted_iota(jnp.int32, shape, 0)
    col_ids = lax.broadcasted_iota(jnp.int32, shape, 1)
    return (row_ids < rows) & (col_ids < cols)


def energy_columns(level):
    missing = -level.shape[0] % 8
    if missing:
        level = jnp.concatenate([level, jnp.zeros((missing, level.shape[1]), F32)], axis=0)
    return level.T


def spread(array, width):
    return jnp.concatenate([array] * (width // LANES), axis=1)


def quotient(value, count):
    return value >> (count.bit_length() - 1) if count & (count - 1) == 0 else lax.div(value, count)


def remainder(value, count):
    return value & (count - 1) if count & (count - 1) == 0 else lax.rem(value, count)


def fold(array):
    rows, width = array.shape
    return jnp.sum(array.reshape(rows // 8, 8, width), axis=0)


def total(array):
    return jnp.sum(jnp.sum(array, axis=0, keepdims=True), axis=1, keepdims=True)


def header(slot, scalars, shape=(HEAD, LANES)):
    row_ids = lax.broadcasted_iota(jnp.int32, shape, 0)
    head = jnp.where(row_ids == 0, slot.astype(F32), 0.0)
    row = 1
    for scalar in scalars:
        rest = jnp.broadcast_to(scalar, shape)
        for _ in range(PARTS):
            piece = rest.astype(BF16).astype(F32)
            head = jnp.where(row_ids == row, piece, head)
            rest = rest - piece
            row += 1
    return head.astype(BF16)


def head_scalar(head_sum, index):
    first = 1 + PARTS * index
    return jnp.sum(head_sum[first:first + PARTS], axis=0, keepdims=True)


def most_pairs(pairs, sec_count):
    return pairs // sec_count + 1


def load_kernel(
    psi_hbm, left_hbm, pairing_hbm, rows_hbm, cols_hbm, energy_hbm,
    start_ref, left_ref, list_ref, limit_ref, energy_ref, scalar_ref,
    psi_ref, level_ref, rows_ref, cols_ref, pairing_ref, entry_ref, count_ref, sems,
):
    sec_dev, half, width = psi_ref.shape
    terms = left_ref.shape[0]
    sec_count = list_ref.shape[0]
    cap = most_pairs(terms * sec_dev, sec_count)
    pairs = [
        (rows_hbm, rows_ref), (cols_hbm, cols_ref), (energy_hbm, level_ref),
        (pairing_hbm, pairing_ref), (psi_hbm, psi_ref),
    ]
    for t in range(left_ref.shape[0]):
        pairs.append((left_hbm.at[t], left_ref.at[t]))
    copies = [
        pltpu.make_async_copy(source, target, sems.at[i])
        for i, (source, target) in enumerate(pairs)
    ]
    for copy in copies:
        copy.start()
    for owner in range(sec_count):
        count_ref[owner] = 0
        entry_ref[owner, cap] = 0
        for i in range(cap):
            entry_ref[owner, i] = terms * sec_dev
    for copy in copies[:3]:
        copy.wait()
    for s in range(sec_dev):
        limit_ref[s:s + 1, :] = jnp.full((1, LANES), rows_ref[s], jnp.int32)
        limit_ref[sec_dev + s:sec_dev + s + 1, :] = jnp.full((1, LANES), cols_ref[s], jnp.int32)
    columns = energy_columns(level_ref[...])
    for s in range(sec_dev):
        energy_ref[s] = jnp.broadcast_to(columns[:, s:s + 1], (half, LANES))
    copies[3].wait()
    for t in range(terms):
        for s in range(sec_dev):
            target = pairing_ref[s, t]
            owner = quotient(target, sec_dev)
            count = count_ref[owner]
            entry_ref[owner, count] = t * sec_dev + s
            entry_ref[owner, cap] = remainder(target, sec_dev)
            count_ref[owner] = count + 1
    entries = pltpu.make_async_copy(entry_ref, list_ref, sems.at[len(copies)])
    entries.start()
    copies[4].wait()
    first_row = lax.axis_index("rep") * half
    norm = jnp.zeros((8, width), F32)
    level = jnp.zeros((8, width), F32)
    for s in range(sec_dev):
        vector = jnp.where(
            live(limit_ref, s, first_row, (half, width)), psi_ref[s].astype(F32), 0.0
        )
        start_ref[s] = vector.astype(BF16)
        square = vector * vector
        norm += fold(square)
        level += fold(square * spread(energy_ref[s], width))
    scalar_ref[0:8, :] = norm
    scalar_ref[8:16, :] = level
    for copy in copies[5:]:
        copy.wait()
    entries.wait()


def product_kernel(is_first, split, paired, rep_count, sec_count, *refs):
    refs = list(refs)
    take = lambda count: [refs.pop(0) for _ in range(count)]
    list_ref, left_ref, right_ref = take(3)
    if is_first:
        start_ref, limit_ref, scalar_ref = take(3)
        psi_refs = take(rep_count - 1)
        level_refs = take(rep_count - 1)
    else:
        (first_ref,) = take(1)
        vector_refs = take(rep_count)
    out_refs = take(sec_count if split else 1)
    if not is_first:
        (first_hbm,) = take(1)
    inner_ref, entry_ref, sems = refs
    terms, sec_dev, half, width = left_ref.shape
    pairs = terms * sec_dev
    cap = most_pairs(pairs, sec_count)
    rep = lax.axis_index("rep")
    sec = lax.axis_index("sec")
    fetch = pltpu.make_async_copy(list_ref, entry_ref, sems.at[0])
    fetch.start()
    if not is_first:
        put = pltpu.make_async_copy(first_ref, first_hbm, sems.at[1])
        put.start()
    inner_ref[pairs] = jnp.zeros((half, width), BF16)

    def first_row(step):
        return remainder(rep + step, rep_count) * half

    if is_first:
        folded = [scalar_ref[0:8, :], scalar_ref[8:16, :]]
        columns = [energy_columns(ref[...]) for ref in level_refs]
    for s in range(sec_dev):
        if is_first:
            blocks = [start_ref[s]]
            for step in range(1, rep_count):
                psi = psi_refs[step - 1][s]
                mask = live(limit_ref, s, first_row(step), (half, width))
                blocks.append(jnp.where(mask, psi.astype(F32), 0.0).astype(BF16))
        else:
            blocks = [ref[s * half:(s + 1) * half] for ref in vector_refs]
        vector = jnp.concatenate(blocks, axis=0)
        for turn in range(1, rep_count):
            turned = blocks[rep_count - turn:] + blocks[:rep_count - turn]
            vector = jnp.where(rep == turn, jnp.concatenate(turned, axis=0), vector)
        inner = jnp.dot(
            left_ref[:, s].reshape(terms * half, width), vector, preferred_element_type=F32
        ).astype(BF16)
        for t in range(terms):
            inner_ref[t * sec_dev + s] = inner[t * half:(t + 1) * half]
        if is_first:
            for step in range(1, rep_count):
                block = blocks[step].astype(F32)
                square = block * block
                energy = jnp.broadcast_to(columns[step - 1][:, s:s + 1], (half, width))
                folded = [folded[0] + fold(square), folded[1] + fold(square * energy)]
    if is_first:
        scalars = [total(array) for array in folded]
    else:
        head = sum(ref[sec_dev * half:].astype(F32) for ref in vector_refs)
        scalars = [head_scalar(head, i)[:, :LANES] for i in range(2)]
    fetch.wait()
    for d in range(sec_count):
        if not split:
            owner = d
        elif paired:
            owner = sec ^ d
        else:
            owner = remainder(sec + d, sec_count)
        packet = jnp.zeros((half, width), F32)
        for i in range(cap):
            pair = entry_ref[owner, i]
            term = jnp.minimum(quotient(pair, sec_dev), terms - 1)
            packet += jnp.dot(inner_ref[pair], right_ref[term], preferred_element_type=F32)
        out = out_refs[d] if split else out_refs[0].at[d]
        for column in range(width // LANES):
            out[column * half:(column + 1) * half, :] = packet[
                :, column * LANES:(column + 1) * LANES
            ].astype(BF16)
        out[width // LANES * half:, :] = header(entry_ref[owner, cap], scalars)
    if not is_first:
        put.wait()


def sigma_packets(is_first, split, paired, rep_count, lists, left_env, right_env, more):
    terms, sec_dev, half, width = left_env.shape
    sec_count = lax.axis_size("sec")
    packet = (width // LANES * half + HEAD, LANES)
    if split:
        outs = [jax.ShapeDtypeStruct(packet, BF16)] * sec_count
    else:
        outs = [jax.ShapeDtypeStruct((sec_count,) + packet, BF16)]
    out_specs = [whole(pltpu.VMEM)] * len(outs)
    if not is_first:
        outs.append(jax.ShapeDtypeStruct((sec_dev, half, width), BF16))
        out_specs.append(whole(pltpu.HBM))
    pair_flops = 2 * half * width * width * 2
    operands = [lists, left_env, right_env, *more]
    return pl.pallas_call(
        functools.partial(product_kernel, is_first, split, paired, rep_count, sec_count),
        out_shape=outs,
        in_specs=[whole(pltpu.VMEM)] * len(operands),
        out_specs=out_specs,
        scratch_shapes=[
            pltpu.VMEM((terms * sec_dev + 1, half, width), BF16),
            pltpu.SMEM(lists.shape, jnp.int32),
            pltpu.SemaphoreType.DMA((2,)),
        ],
        compiler_params=pltpu.CompilerParams(vmem_limit_bytes=VMEM_BYTES),
        cost_estimate=pl.CostEstimate(
            flops=terms * sec_dev * pair_flops,
            bytes_accessed=2 * (left_env.size + right_env.size),
            transcendentals=0,
        ),
        name="products_first" if is_first else "products_second",
    )(*operands)


def exchange(packets, split, paired, order, groups, bare=0):
    sec_count = lax.axis_size("sec")
    op_count = lax.axis_size("op")
    op_turns = [
        [(i, (i + step) % op_count) for i in range(op_count)] for step in range(1, op_count)
    ]
    over_op = lambda packet: [lax.ppermute(packet, "op", turn) for turn in op_turns]
    if not split:
        arrived = lax.all_to_all(packets[0], "sec", split_axis=0, concat_axis=0, tiled=True)
        return [arrived] + over_op(arrived), []
    arrived = {0: packets[0]}
    for step in order:
        reach = (lambda i: i ^ step) if paired else (lambda i: (i + step) % sec_count)
        turn = [(i, reach(i)) for i in range(sec_count)]
        arrived[step] = lax.ppermute(packets[step], "sec", turn)
    crossed = []
    for group in groups:
        rows = bare if bare and group != [0] else None
        crossed.append(over_op(jnp.stack([arrived[step][:rows] for step in group])))
    return [arrived[step] for step in [0, *order]] + sum(crossed[:-1], []), crossed[-1]


def views(refs):
    return [
        view
        for ref in refs
        for view in ([ref] if len(ref.shape) == 2 else [ref.at[i] for i in range(ref.shape[0])])
    ]


def add_packets(packet_refs, split, half, base_ref, slots=()):
    sec_dev, _, width = base_ref.shape
    own = lax.axis_size("sec") if split else 1
    body_rows = width // LANES * half
    if split:
        packet_refs = views(packet_refs)
        with_head = packet_refs[:len(packet_refs) - len(slots)]
        heads = [ref[body_rows:].astype(F32) for ref in with_head]
        heads += slots
        for column in range(width // LANES):
            lanes = slice(column * LANES, (column + 1) * LANES)
            for s in range(sec_dev):
                part = base_ref[s, :, lanes]
                for ref, head in zip(packet_refs, heads):
                    body = ref[column * half:(column + 1) * half].astype(F32)
                    part += jnp.where(head[0:1] == s, body, 0.0)
                base_ref[s, :, lanes] = part
        return sum(heads[1:own], heads[0])

    head_sum = jnp.zeros((HEAD, LANES), F32)
    for index, ref in enumerate(packet_refs):
        def add_one(p, carry):
            head = ref[p, body_rows:, :].astype(F32)
            for column in range(width // LANES):
                body = ref[p, column * half:(column + 1) * half, :].astype(F32)
                lanes = slice(column * LANES, (column + 1) * LANES)
                for s in range(sec_dev):
                    base_ref[s, :, lanes] += jnp.where(head[0:1] == s, body, 0.0)
            return carry + head
        result = lax.fori_loop(0, ref.shape[0], add_one, jnp.zeros((HEAD, LANES), F32))
        if index < own:
            head_sum = head_sum + result
    return head_sum


def late_sum(packet_refs, s, half, width, slots=()):
    body_rows = width // LANES * half
    value = jnp.zeros((half, width), F32)
    for i, ref in enumerate(views(packet_refs)):
        body = jnp.concatenate(
            [ref[c * half:(c + 1) * half].astype(F32) for c in range(width // LANES)], axis=1
        )
        slot = slots[i] if slots else ref[body_rows:].astype(F32)[0:1]
        slot = spread(slot, width)
        value += jnp.where(slot == s, body, 0.0)
    return value


def first_early_kernel(split, count, *refs):
    packet_refs = refs[:count]
    start_ref, energy_ref, base_ref, scalar_ref = refs[count:]
    sec_dev, half, width = start_ref.shape
    for s in range(sec_dev):
        base_ref[s] = spread(energy_ref[s], width) * start_ref[s].astype(F32)
    head_sum = add_packets(packet_refs, split, half, base_ref)
    norm = head_scalar(head_sum, 0)
    scalar_ref[0:1] = norm
    scalar_ref[1:2] = head_scalar(head_sum, 1) / norm
    if split:
        crossed = views(packet_refs)[lax.axis_size("sec"):]
        for i, ref in enumerate(crossed):
            scalar_ref[SLOT_ROW + i:SLOT_ROW + i + 1] = crossed_slot(ref, half, width)


def crossed_slot(ref, half, width):
    return ref[width // LANES * half:].astype(F32)[0:1]


def known_slots(slot_ref, steps):
    sec_count = lax.axis_size("sec")
    sec = lax.axis_index("sec")
    rows = [remainder(sec - (sec ^ step) + sec_count, sec_count) for step in steps]
    return [slot_ref[pl.ds(row, 1), :] for row in rows]


def first_kernel(count, *refs):
    packet_refs = refs[:count]
    limit_ref, start_ref, base_ref, scalar_ref, first_ref, one_ref, vec_ref, slot_ref = refs[count:]
    sec_dev, half, width = start_ref.shape
    late = views(packet_refs)
    early_count = lax.axis_size("sec") - len(late)
    slot_ref[...] = jnp.zeros_like(slot_ref)
    if late:
        slot_ref[0:early_count] = scalar_ref[SLOT_ROW:SLOT_ROW + early_count]
        for i, ref in enumerate(late):
            row = early_count + i
            slot_ref[row:row + 1] = crossed_slot(ref, half, width)
    shift = spread(scalar_ref[1:2], width)
    first_row = lax.axis_index("rep") * half
    cross = jnp.zeros((8, width), F32)
    square = jnp.zeros((8, width), F32)
    for s in range(sec_dev):
        mask = live(limit_ref, s, first_row, (half, width))
        start = start_ref[s].astype(F32)
        one = jnp.where(mask, base_ref[s] + late_sum(packet_refs, s, half, width), 0.0)
        one_ref[s] = one
        first_ref[s] = one.astype(BF16)
        vector = one - shift * start
        vec_ref[s * half:(s + 1) * half] = vector.astype(BF16)
        cross += fold(start * vector)
        square += fold(vector * vector)
    scalars = (total(cross), total(square))
    vec_ref[sec_dev * half:] = header(jnp.int32(0), scalars, (MORE_ROWS, width))


def second_early_kernel(split, count, entries, steps, *refs):
    packet_refs = refs[:count]
    slot_ref, vec_ref, energy_ref, one_ref, scalar_ref, base_ref, scale_ref = refs[count:]
    sec_dev, half, width = one_ref.shape
    for s in range(sec_dev):
        vector = vec_ref[s * half:(s + 1) * half].astype(F32)
        base_ref[s] = spread(energy_ref[s], width) * vector
    head_sum = add_packets(packet_refs, split, half, base_ref, known_slots(slot_ref, steps))
    cross = head_scalar(head_sum, 0)
    square = head_scalar(head_sum, 1)
    excess = cross / scalar_ref[0:1]
    resid_sq = jnp.maximum(square - excess * cross, 0.0)
    scale = lax.rsqrt(resid_sq / entries + EPSILON)
    scale_ref[...] = jnp.broadcast_to(scale, scale_ref.shape)
    for s in range(sec_dev):
        base_ref[s] = base_ref[s] - spread(excess, width) * one_ref[s]


def second_kernel(count, steps, *refs):
    packet_refs = refs[:count]
    slot_ref, limit_ref, base_ref, scale_ref, second_ref = refs[count:]
    sec_dev, half, width = base_ref.shape
    scale = spread(scale_ref[0:1], width)
    slots = known_slots(slot_ref, steps)
    first_row = lax.axis_index("rep") * half
    for s in range(sec_dev):
        mask = live(limit_ref, s, first_row, (half, width))
        value = scale * (base_ref[s] + late_sum(packet_refs, s, half, width, slots))
        second_ref[s] = jnp.where(mask, value, 0.0).astype(BF16)


def call(kernel, name, outs, *operands, flops=0):
    return pl.pallas_call(
        kernel,
        out_shape=outs,
        in_specs=[whole(pltpu.VMEM)] * len(operands),
        out_specs=[whole(pltpu.VMEM)] * len(outs),
        compiler_params=pltpu.CompilerParams(vmem_limit_bytes=VMEM_BYTES),
        cost_estimate=pl.CostEstimate(flops=flops, bytes_accessed=0, transcendentals=0),
        name=name,
    )(*operands)


def body(psi, left_env, right_env, pairing, block_rows, block_cols, energy):
    sec_count = lax.axis_size("sec")
    op_count = lax.axis_size("op")
    rep_count = lax.axis_size("rep")
    terms, sec_dev, half, width = left_env.shape
    entries = sec_count * sec_dev * rep_count * half * width
    split = sec_count * op_count <= 8
    can_pair = sec_count & (sec_count - 1) == 0
    steps = list(range(1, sec_count))
    first_plan = (False, steps, [[0]] + [[k] for k in steps[:-2]] + [steps[-2:]])
    second_groups = [[0]] + [[k] for k in steps[1:2] + steps[:1] + steps[2:]]
    second_plan = (can_pair, steps[1:2] + steps[:1] + steps[2:], second_groups)
    known = split and can_pair and op_count == 2 and sec_count <= 4
    params = pltpu.CompilerParams(vmem_limit_bytes=VMEM_BYTES)
    vec_shape = (sec_dev, half, width)
    vec_bf16 = jax.ShapeDtypeStruct(vec_shape, BF16)

    def from_others(array):
        arrays = []
        for step in range(1, rep_count):
            turn = [((i + step) % rep_count, i) for i in range(rep_count)]
            arrays.append(lax.ppermute(array, "rep", turn))
        return arrays

    psi_others = from_others(psi)
    level_others = from_others(energy)
    start, left_env, lists, limits, levels, scalars = pl.pallas_call(
        load_kernel,
        out_shape=[
            vec_bf16,
            jax.ShapeDtypeStruct(left_env.shape, BF16),
            jax.ShapeDtypeStruct((sec_count, LANES), jnp.int32),
            jax.ShapeDtypeStruct((2 * sec_dev, LANES), jnp.int32),
            jax.ShapeDtypeStruct((sec_dev, half, LANES), F32),
            jax.ShapeDtypeStruct((16, width), F32),
        ],
        in_specs=[whole(pltpu.HBM)] * 6,
        out_specs=[whole(pltpu.VMEM)] * 6,
        scratch_shapes=[
            pltpu.VMEM(vec_shape, BF16),
            pltpu.VMEM((sec_dev, half), F32),
            pltpu.SMEM((sec_dev,), jnp.int32),
            pltpu.SMEM((sec_dev,), jnp.int32),
            pltpu.SMEM((sec_dev, terms), jnp.int32),
            pltpu.SMEM((sec_count, LANES), jnp.int32),
            pltpu.SMEM((sec_count,), jnp.int32),
            pltpu.SemaphoreType.DMA((6 + terms,)),
        ],
        compiler_params=params,
        name="load",
    )(*(
        pltpu.with_memory_space_constraint(array, pltpu.HBM)
        for array in (psi, left_env, pairing.T, block_rows, block_cols, energy)
    ))

    block_f32 = jax.ShapeDtypeStruct(vec_shape, F32)
    row_f32 = jax.ShapeDtypeStruct((8, LANES), F32)

    packets = sigma_packets(
        True, split, first_plan[0], rep_count, lists, left_env, right_env,
        [start, limits, scalars, *psi_others, *level_others],
    )
    early, late = exchange(packets, split, *first_plan)
    base, scalars = call(
        functools.partial(first_early_kernel, split, len(early)), "combine_first_early",
        [block_f32, row_f32], *early, start, levels, flops=EARLY_FLOPS,
    )
    first, sigma_one, vector, slots = call(
        functools.partial(first_kernel, len(late)), "combine_first",
        [
            pltpu.VMEM(vec_shape, BF16),
            block_f32,
            jax.ShapeDtypeStruct((sec_dev * half + MORE_ROWS, width), BF16),
            row_f32,
        ],
        *late, limits, start, base, scalars,
    )

    *packets, first_out = sigma_packets(
        False, split, second_plan[0], rep_count, lists, left_env, right_env,
        [first, vector, *from_others(vector)],
    )
    bare = width // LANES * half if known else 0
    early, late = exchange(packets, split, *second_plan, bare)
    crossed = sum(second_plan[2], []) if known else []
    late_steps = second_plan[2][-1] if known else []
    base, scale = call(
        functools.partial(
            second_early_kernel, split, len(early), entries, crossed[:len(crossed) - len(late_steps)]
        ),
        "combine_second_early", [block_f32, row_f32], *early, slots, vector, levels, sigma_one, scalars,
        flops=EARLY_FLOPS,
    )
    (second_out,) = call(
        functools.partial(second_kernel, len(late), late_steps), "combine_second", [vec_bf16],
        *late, slots, limits, base, scale,
    )
    return (first_out, second_out)


def solution(mesh):
    return jax.shard_map(
        body,
        mesh=mesh,
        in_specs=(
            P(("grp", "sec"), "rep", None),
            P(("grp", "op"), "sec", "rep", None),
            P(("grp", "op"), None, None),
            P(("grp", "op"), "sec"),
            P(("grp", "sec")),
            P(("grp", "sec")),
            P(("grp", "sec"), "rep"),
        ),
        out_specs=(P(("grp", "sec"), "rep", None), P(("grp", "sec"), "rep", None)),
        check_vma=False,
    )
```
